32 devices in a mesh: expert: 4 (over x, core), fsdp: 8 (over z, y).
Axes of the slice: x: 2, y: 2, z: 4, core: 2. Of those that a mesh axis runs over, the one named last changes fastest.
Arguments:
- layer_input: bfloat16 [8, 1024, 2048], P('fsdp', 'expert')
- doc_ids: int32 [8, 1024], P('fsdp'), may hold values from 0 to 2, as said below
- expert_ids: int32 [8, 1024, 8], P('fsdp', 'expert'), may hold values from 0 to 31, all different within a row; in each aligned block of 256 rows (0 to 255, 256 to 511, ..., all dimensions but the last counted through in order) at most 76 rows name the same one
- w_query: bfloat16 [2048, 4096], P('fsdp'), may hold values from -0.125 to 0.125
- w_key: bfloat16 [2048, 512], P('fsdp'), may hold values from -0.125 to 0.125
- w_value: bfloat16 [2048, 512], P('fsdp'), may hold values from -0.125 to 0.125
- w_out: bfloat16 [4096, 2048], P('fsdp'), may hold values from -1.5 to 1.5
- w_router: bfloat16 [2048, 32], P('fsdp'), may hold values from -0.0625 to 0.0625
- gain_attn: bfloat16 [2048], P('fsdp'), may hold values from 0.099609375 to 1.8984375
- gain_ffn: bfloat16 [2048], P('fsdp'), may hold values from 0.099609375 to 1.8984375
- gain_query: bfloat16 [128], P('fsdp'), may hold values from 0.099609375 to 1.8984375
- gain_key: bfloat16 [128], P('fsdp'), may hold values from 0.099609375 to 1.8984375
- w_gate: bfloat16 [32, 2048, 768], P(('expert', 'fsdp')), may hold values from -0.125 to 0.125
- w_up: bfloat16 [32, 2048, 768], P(('expert', 'fsdp')), may hold values from -0.125 to 0.125
- w_down: bfloat16 [32, 768, 2048], P(('expert', 'fsdp')), may hold values from -0.875 to 0.875
- grad_output: float32 [8, 1024, 2048], P('fsdp', 'expert'), may hold values from -6 to 6
Outputs:
- layer_output: float32 [8, 1024, 2048], P('fsdp', 'expert')
- grad_input: float32 [8, 1024, 2048], P('fsdp', 'expert')
- grad_w_query: float32 [2048, 4096], P('fsdp')
- grad_w_key: float32 [2048, 512], P('fsdp')
- grad_w_value: float32 [2048, 512], P('fsdp')
- grad_w_out: float32 [4096, 2048], P('fsdp')
- grad_w_router: float32 [2048, 32], P('fsdp')
- grad_gain_attn: float32 [2048], P('fsdp')
- grad_gain_ffn: float32 [2048], P('fsdp')
- grad_gain_query: float32 [128], P('fsdp')
- grad_gain_key: float32 [128], P('fsdp')
- grad_w_gate: float32 [32, 2048, 768], P(('expert', 'fsdp'))
- grad_w_up: float32 [32, 2048, 768], P(('expert', 'fsdp'))
- grad_w_down: float32 [32, 768, 2048], P(('expert', 'fsdp'))
The draws below stay inside these ranges and needn't reach their ends.
Inputs may be any that keep to these rules, and one draw needn't show every extreme that they name: `expert_ids`: each row names 8 different experts; in each aligned block of 256 rows (the rows of one device) no expert is named by more than 76 rows. `doc_ids`: in each sequence the numbers never fall; document 1 begins at a position from 1 to 255 and ends before a position from 769 to 1023, documents 0 and 2 lie before and after it.
All inputs are finite; a program needn't handle non-finite values.
Results may differ from the reference program's by a relative error of at most 0.023.
Values may be sent and summed in bfloat16 or wider, within the bound.
A program may use at most 448 MiB of HBM per device.

```python
import math
import jax
import jax.numpy as jnp
import numpy as np
from jax import lax

D = 2048
QUERY_HEADS = 32
KEY_VALUE_HEADS = 4
HEAD_SIZE = 128
FF = 768
TOP = 8
SEQUENCE_TOKENS = 1024
TOK = 256
SEQS = 8
TOKENS = 8192
QW = 4096
KW = 512
EXPERTS = 32
CAP = 76
DEVICES = 32


def draw_layer_input(key, part):
    key = jax.random.fold_in(key, 5)
    key_rows, key_cols, key_base = jax.random.split(key, 3)
    row_scale = jnp.exp(jax.random.uniform(key_rows, (SEQS, SEQUENCE_TOKENS, 1), jnp.float32, -1.15, 1.15))
    col_scale = jnp.exp(jax.random.uniform(key_cols, (1, 1, D), jnp.float32, -1.15, 1.15))
    base = jax.random.normal(key_base, (SEQS, SEQUENCE_TOKENS, D), jnp.float32)
    return (base * row_scale * col_scale).astype(jnp.bfloat16)


def draw_doc_ids(key, part):
    key = jax.random.fold_in(key, 11)
    key_first, key_last = jax.random.split(key)
    first = jax.random.randint(key_first, (SEQS, 1), 1, TOK)
    last = jax.random.randint(key_last, (SEQS, 1), SEQUENCE_TOKENS - TOK + 1, SEQUENCE_TOKENS)
    places = jnp.arange(SEQUENCE_TOKENS, dtype=jnp.int32)[None, :]
    return (places >= first).astype(jnp.int32) + (places >= last).astype(jnp.int32)


def levels(stream_key, extent, cuts, smallest, high):
    def one(axis_at, blocks):
        heights = jax.random.uniform(jax.random.fold_in(jax.random.fold_in(stream_key, 6), axis_at), (blocks,), jnp.float32, smallest / len(cuts), high / len(cuts))
        return jnp.repeat(jnp.exp(heights), extent[axis_at] // blocks).reshape((-1,) + (1,) * (len(extent) - axis_at - 1))

    loudness = one(*cuts[0])
    for cut in cuts[1:]:
        loudness = loudness * one(*cut)
    return loudness


def assign_block(stream_key, own, number, rows, amount, top, limit, slope):
    sequence = jax.random.permutation(stream_key, amount)
    packed, common = portions_of(amount, rows * top, limit, slope, True), portions_of(amount, rows * top, limit, slope, False)
    places = jnp.arange(amount)

    def named(lengths, rotation):
        used = int((lengths > 0).sum())
        fixed = max(1, used // 4)
        moved = fixed + (places - fixed + rotation * (used - fixed)) % max(1, amount - fixed)
        return jnp.zeros((amount,), jnp.int32).at[sequence[jnp.where(places < fixed, places, moved)]].set(jnp.asarray(lengths, jnp.int32))

    lengths = jnp.where(number % 4 == 0, named(packed, number // 4), named(common, number - number // 4 - 1))
    mixed = jax.random.permutation(jax.random.fold_in(own, 3), amount)
    source_of, taker = mixed[0:amount // 2 * 2:2], mixed[1:amount // 2 * 2:2]
    room = jnp.minimum(lengths[source_of] - 1, limit - lengths[taker]) // 2
    room = jnp.where((source_of == sequence[0]) | (taker == sequence[0]) | (lengths[taker] == 0), 0, jnp.maximum(room, 0))
    moved = jax.random.randint(jax.random.fold_in(own, 4), (amount // 2,), 0, 1 << 20) % (room + 1)
    lengths = lengths.at[source_of].add(-moved).at[taker].add(moved)
    items = jnp.searchsorted(jnp.cumsum(lengths), jnp.arange(rows * top), side="right").astype(jnp.int32)
    listing = items.reshape(top, rows).T
    listing = listing[jax.random.permutation(jax.random.fold_in(own, 1), rows)]
    rotation = jax.random.randint(jax.random.fold_in(own, 2), (rows, 1), 0, top)
    return jnp.take_along_axis(listing, (jnp.arange(top)[None, :] + rotation) % top, axis=1)


def portions_of(amount, total, limit, slope, full):
    weights = [(1 << 20) // math.isqrt(standing ** slope) + 1 for standing in range(1, amount + 1)]
    largest = limit if full else min(limit, max(-(-total // amount), total * weights[0] // sum(weights)))
    least = 1 if total - largest >= amount - 1 else 0
    holding, spare = [largest] + [least] * (amount - 1), total - largest - least * (amount - 1)
    while spare > 0:
        free = [i for i in range(1, amount) if holding[i] < largest] or [i for i in range(1, amount) if holding[i] < limit]
        mass, budget = sum([weights[i] for i in free]), spare
        for i in free:
            more = min(limit - holding[i], max(1, budget * weights[i] // mass), spare)
            holding[i] = holding[i] + more
            spare = spare - more
    return np.array(holding)


def bell_draw(rng, extent, scale, most, shards=(), kind=jnp.bfloat16):
    values = scale * jax.random.normal(rng, extent, jnp.float32)
    if shards:
        values = values * levels(rng, extent, shards, -0.22, 0.18)
    return jnp.clip(values, -most, most).astype(kind)


def setup_inputs(seed: int = 0) -> dict:
    splits = jax.random.split(jax.random.key(seed), 17)
    layer_input = draw_layer_input(jax.random.fold_in(splits[16], 71), 0)
    doc_ids = draw_doc_ids(jax.random.fold_in(splits[16], 71), 0)
    expert_ids_keys = jax.random.split(jax.random.fold_in(splits[2], 1), SEQS * SEQUENCE_TOKENS // TOK)
    expert_ids_turns = jax.random.permutation(jax.random.fold_in(splits[2], 3), SEQS * SEQUENCE_TOKENS // TOK)
    expert_ids = jax.vmap(lambda own, number: assign_block(jax.random.fold_in(splits[2], 2), own, number, TOK, EXPERTS, TOP, CAP, 2))(expert_ids_keys, expert_ids_turns).reshape((SEQS, SEQUENCE_TOKENS, TOP))
    w_query = bell_draw(splits[3], (D, QW), D ** -0.5, 0.125, ((0, 8),))
    w_key = bell_draw(splits[4], (D, KW), D ** -0.5, 0.125, ((0, 8),))
    w_value = bell_draw(splits[5], (D, KW), D ** -0.5, 0.125, ((0, 8),))
    w_out = bell_draw(splits[6], (QW, D), (QW // 256) ** -0.5, 1.5, ((0, 8),))
    w_router = bell_draw(splits[7], (D, EXPERTS), (0.5 * D ** -0.5), 0.0625, ((0, 8),))
    gain_attn = jnp.clip(1.0 + 0.18 * jax.random.normal(splits[8], (D,), jnp.float32), 0.099609375, 1.8984375).astype(jnp.bfloat16)
    gain_ffn = jnp.clip(1.0 + 0.18 * jax.random.normal(splits[9], (D,), jnp.float32), 0.099609375, 1.8984375).astype(jnp.bfloat16)
    gain_query = jnp.clip(1.0 + 0.18 * jax.random.normal(splits[10], (HEAD_SIZE,), jnp.float32), 0.099609375, 1.8984375).astype(jnp.bfloat16)
    gain_key = jnp.clip(1.0 + 0.18 * jax.random.normal(splits[11], (HEAD_SIZE,), jnp.float32), 0.099609375, 1.8984375).astype(jnp.bfloat16)
    w_gate = bell_draw(splits[12], (EXPERTS, D, FF), D ** -0.5, 0.125, ((0, 32),))
    w_up = bell_draw(splits[13], (EXPERTS, D, FF), D ** -0.5, 0.125, ((0, 32),))
    w_down = bell_draw(splits[14], (EXPERTS, FF, D), (FF // 16) ** -0.5, 0.875, ((0, 32),))
    grad_output = bell_draw(splits[15], (SEQS, SEQUENCE_TOKENS, D), 1.0, 6.0, ((0, 8), (1, 4)), jnp.float32)
    return {"layer_input": layer_input, "doc_ids": doc_ids, "expert_ids": expert_ids, "w_query": w_query, "w_key": w_key, "w_value": w_value, "w_out": w_out, "w_router": w_router, "gain_attn": gain_attn, "gain_ffn": gain_ffn, "gain_query": gain_query, "gain_key": gain_key, "w_gate": w_gate, "w_up": w_up, "w_down": w_down, "grad_output": grad_output}


EPS = 1e-06
THETA = 1000000.0
HIGHEST = lax.Precision.HIGHEST

@jax.custom_vjp
def reduced_precision(v):
    return lax.optimization_barrier(v.astype(jnp.bfloat16)).astype(jnp.float32)

@jax.custom_vjp
def reduced_precision_backward(v):
    return v

def low_keep(v):
    return (reduced_precision(v), None)

def low_pass(kept, grad):
    return (grad,)

def back_keep(v):
    return (v, None)

def back_low(kept, grad):
    return (reduced_precision(grad),)
reduced_precision.defvjp(low_keep, low_pass)
reduced_precision_backward.defvjp(back_keep, back_low)

def apply_rms_norm(value_rows_local, gain):
    return value_rows_local * lax.rsqrt(lax.optimization_barrier(jnp.mean(value_rows_local * value_rows_local, -1, keepdims=True)) + EPS) * gain

def apply_rotary(value_rows_local, cosine_table, sine_table):
    half = value_rows_local.shape[-1] // 2
    turned = jnp.concatenate([-value_rows_local[..., half:], value_rows_local[..., :half]], -1)
    return value_rows_local * cosine_table + turned * sine_table

def angles(positions):
    freq = THETA ** (-(jnp.arange(HEAD_SIZE // 2, dtype=jnp.float32) * 2.0) / HEAD_SIZE)
    turn = positions.astype(jnp.float32)[:, None] * freq[None, :]
    turn = jnp.concatenate([turn, turn], -1)
    return (jnp.cos(turn), jnp.sin(turn))

def matrix_product(left, right):
    return jnp.dot(left, right, precision=HIGHEST, preferred_element_type=jnp.float32)

def reference(layer_input, doc_ids, expert_ids, w_query, w_key, w_value, w_out, w_router, gain_attn, gain_ffn, gain_query, gain_key, w_gate, w_up, w_down, grad_output):
    query_groups = QUERY_HEADS // KEY_VALUE_HEADS
    scale = HEAD_SIZE ** (-0.5)
    pairs = TOKENS * TOP
    slots = DEVICES * CAP
    positions = jnp.arange(SEQUENCE_TOKENS, dtype=jnp.int32)
    cosine_table, sine_table = angles(positions)
    cosine_table = cosine_table[:, None, :]
    sine_table = sine_table[:, None, :]
    causal = positions[:, None] >= positions[None, :]
    flat_routes = expert_ids.reshape(-1).astype(jnp.int32)
    order = jnp.argsort(flat_routes, stable=True).astype(jnp.int32)
    counts = jax.ops.segment_sum(jnp.ones_like(flat_routes), flat_routes, EXPERTS).astype(jnp.int32)
    starts = (jnp.cumsum(counts) - counts).astype(jnp.int32)
    offsets = jnp.arange(slots, dtype=jnp.int32)
    picked = order[jnp.minimum(starts[:, None] + offsets[None, :], pairs - 1)].astype(jnp.int32)
    filled = (offsets[None, :] < counts[:, None]).astype(jnp.float32)
    owners = (picked // TOP).astype(jnp.int32)
    selector = (expert_ids[..., None] == jnp.arange(EXPERTS, dtype=jnp.int32)).astype(jnp.float32).reshape(TOKENS, TOP, EXPERTS)

    def forward(inputs, wq, key_weight, value_weight, wo, wr, g_attn, g_ffn, query_gain_vector, g_key, gate_all, up_all, down_all):

        def attend(pieces):
            seq_tokens, seq_ids = pieces
            normalized_input = reduced_precision(apply_rms_norm(seq_tokens, g_attn))
            query_rows_local = reduced_precision_backward(matrix_product(normalized_input, wq)).reshape(SEQUENCE_TOKENS, QUERY_HEADS, HEAD_SIZE)
            key_rows_local = reduced_precision_backward(matrix_product(normalized_input, key_weight)).reshape(SEQUENCE_TOKENS, KEY_VALUE_HEADS, HEAD_SIZE)
            value_rows_local = reduced_precision(reduced_precision_backward(matrix_product(normalized_input, value_weight))).reshape(SEQUENCE_TOKENS, KEY_VALUE_HEADS, HEAD_SIZE)
            query_rows_local = reduced_precision(apply_rotary(apply_rms_norm(query_rows_local, query_gain_vector), cosine_table, sine_table)).reshape(SEQUENCE_TOKENS, KEY_VALUE_HEADS, query_groups, HEAD_SIZE)
            key_rows_local = reduced_precision(apply_rotary(apply_rms_norm(key_rows_local, g_key), cosine_table, sine_table))
            scores = reduced_precision_backward(scale * jnp.einsum('tkgd,skd->kgts', query_rows_local, key_rows_local, precision=HIGHEST))
            allowed = causal & (seq_ids[:, None] == seq_ids[None, :])
            scores = jnp.where(allowed, scores, -1e+30)
            shifted = jnp.exp(scores - lax.optimization_barrier(jnp.max(scores, -1, keepdims=True)))
            weights = reduced_precision(shifted / lax.optimization_barrier(jnp.sum(shifted, -1, keepdims=True)))
            mixed = jnp.einsum('kgts,skd->tkgd', weights, value_rows_local, precision=HIGHEST).reshape(SEQUENCE_TOKENS, QUERY_HEADS * HEAD_SIZE)
            mixed = reduced_precision(reduced_precision_backward(mixed))
            return reduced_precision_backward(matrix_product(mixed, wo))
        branch = lax.map(jax.checkpoint(attend), (inputs, doc_ids))
        hidden = inputs + branch
        normed_two = reduced_precision(apply_rms_norm(hidden, g_ffn)).reshape(TOKENS, D)
        logits = reduced_precision_backward(matrix_product(normed_two, wr))
        chosen = jnp.einsum('tke,te->tk', selector, logits, precision=HIGHEST)
        gates = jax.nn.softmax(chosen, -1).reshape(pairs)

        def expert_layer(pieces):
            gate_w, up_w, down_w, members, live = pieces
            rows_in = reduced_precision_backward(normed_two[members // TOP] * live[:, None])
            gate_pre = reduced_precision_backward(matrix_product(rows_in, gate_w))
            up_pre = reduced_precision_backward(matrix_product(rows_in, up_w))
            inner = reduced_precision(jax.nn.silu(gate_pre) * up_pre)
            result = reduced_precision(reduced_precision_backward(matrix_product(inner, down_w)))
            return result * gates[members][:, None]
        weighted = lax.map(jax.checkpoint(expert_layer), (gate_all, up_all, down_all, picked, filled))
        combined = jax.ops.segment_sum(weighted.reshape(-1, D), owners.reshape(-1), TOKENS)
        return hidden + combined.reshape(SEQS, SEQUENCE_TOKENS, D)
    primal = (layer_input.astype(jnp.float32), w_query.astype(jnp.float32), w_key.astype(jnp.float32), w_value.astype(jnp.float32), w_out.astype(jnp.float32), w_router.astype(jnp.float32), gain_attn.astype(jnp.float32), gain_ffn.astype(jnp.float32), gain_query.astype(jnp.float32), gain_key.astype(jnp.float32), w_gate.astype(jnp.float32), w_up.astype(jnp.float32), w_down.astype(jnp.float32))
    result_out, pullback = jax.vjp(forward, *primal)
    grads = pullback(grad_output.astype(jnp.float32))
    return (result_out, grads[0], grads[1], grads[2], grads[3], grads[4], grads[5], grads[6], grads[7], grads[8], grads[9], grads[10], grads[11], grads[12])
```

```python
import functools

import jax
import jax.numpy as jnp
from jax import lax
from jax.experimental import pallas as pl
from jax.experimental.pallas import tpu as pltpu
from jax.sharding import PartitionSpec as P

EXPERT = "expert"
FSDP = "fsdp"
UP, DOWN, ABOVE, BELOW = "up", "down", "above", "below"
QUERY_HEADS = 32
KEY_VALUE_HEADS = 4
HEAD_SIZE = 128
TOP = 8


EPS = 1e-06
THETA = 1000000.0
HIGHEST = lax.Precision.HIGHEST


def angles(positions):
    freq = THETA ** (-(jnp.arange(HEAD_SIZE // 2, dtype=jnp.float32) * 2.0) / HEAD_SIZE)
    turn = positions.astype(jnp.float32)[:, None] * freq[None, :]
    turn = jnp.concatenate([turn, turn], -1)
    return (jnp.cos(turn), jnp.sin(turn))


def apply_rotary(value_rows_local, cosine_table, sine_table):
    half = value_rows_local.shape[-1] // 2
    turned = jnp.concatenate([-value_rows_local[..., half:], value_rows_local[..., :half]], -1)
    return value_rows_local * cosine_table + turned * sine_table


def unrotate(grads, cosine_table, sine_table):
    half = grads.shape[-1] // 2
    scaled = grads * sine_table
    turned = jnp.concatenate([-scaled[..., half:], scaled[..., :half]], -1)
    return grads * cosine_table - turned


def inverse_rms(value_rows_local):
    return lax.rsqrt(jnp.mean(value_rows_local * value_rows_local, -1, keepdims=True) + EPS)


def norm_backward(grad, value_rows_local, inverse, gain):
    scaled = grad * gain
    return inverse * scaled - inverse * inverse * inverse * value_rows_local * jnp.mean(
        scaled * value_rows_local, -1, keepdims=True
    )


MESH = pl.DeviceIdType.MESH
PATHS = ("zxy", "zyx", "xzy", "yzx")
CHIPS = 16
SLOTS = 80


def part_rows(rows):
    small = rows * 3 // 16
    large = rows // 2 - small
    starts = (0, small, 2 * small, 2 * small + large)
    return starts, (small, small, large, large)


class Place:
    def __init__(self):
        self.e = lax.axis_index(EXPERT)
        self.f = lax.axis_index(FSDP)
        self.x, self.c = self.e // 2, self.e % 2
        self.z, self.y = self.f // 2, self.f % 2

    def device(self, axis):
        if axis == "c":
            return (self.x * 2 + 1 - self.c, self.f)
        if axis == "x":
            return ((1 - self.x) * 2 + self.c, self.f)
        if axis == "y":
            return (self.e, self.z * 2 + 1 - self.y)
        if axis == UP:
            return (self.e, jnp.minimum(self.z + 1, 3) * 2 + self.y)
        return (self.e, jnp.maximum(self.z - 1, 0) * 2 + self.y)

    def ranked(self, j):
        inner = (1, 0, 2, 3)[j]
        end = (self.z == 0) | (self.z == 3)
        low = jnp.where(end, j, inner)
        return jnp.where(self.z < 2, low, 3 - low)

    def chip(self, zs, xr, yr):
        xs = 1 - self.x if xr else self.x
        ys = 1 - self.y if yr else self.y
        return xs * 8 + zs * 2 + ys


def greet(place, axes=("c", "x", "y")):
    barrier = pltpu.get_barrier_semaphore()
    for axis in axes:
        pl.semaphore_signal(barrier, 1, device_id=place.device(axis), device_id_type=MESH)

    @pl.when(place.z < 3)
    def _():
        pl.semaphore_signal(barrier, 1, device_id=place.device(UP), device_id_type=MESH)

    @pl.when(place.z > 0)
    def _():
        pl.semaphore_signal(barrier, 1, device_id=place.device(DOWN), device_id_type=MESH)

    inner = (place.z > 0) & (place.z < 3)
    pl.semaphore_wait(barrier, len(axes) + jnp.where(inner, 2, 1))


def greet_all(place, experts, shards):
    barrier = pltpu.get_barrier_semaphore()
    count = experts * shards

    def one(i, carry):
        target = lax.rem(place.e * shards + place.f + i, count)
        pl.semaphore_signal(
            barrier, 1, device_id=(target // shards, lax.rem(target, shards)), device_id_type=MESH
        )
        return carry

    lax.fori_loop(1, count, one, 0)
    pl.semaphore_wait(barrier, count - 1)


def items():
    found = [(j, xr, yr) for j in range(4) for xr in range(2) for yr in range(2)]
    return sorted(found, key=lambda it: (it[0] + it[1] + it[2], -it[0]))


def onward(path, j, xr, yr):
    differs = {"z": j > 0, "x": xr > 0, "y": yr > 0}
    last = -1
    for i, axis in enumerate(path):
        if differs[axis]:
            last = i
    out = []
    if last >= 0 and path[last] == "z":
        out.append("z+")
    for axis in path[last + 1 :]:
        out.append("z*" if axis == "z" else axis)
    return out


def links(place, path, j, xr, yr, zs):
    out = []
    for axis in onward(path, j, xr, yr):
        if axis == "z+":
            out.append((UP, (zs < place.z) & (place.z < 3)))
            out.append((DOWN, (zs > place.z) & (place.z > 0)))
        elif axis == "z*":
            out.append((UP, place.z < 3))
            out.append((DOWN, place.z > 0))
        else:
            out.append((axis, None))
    return out


def run(condition, action):
    if condition is None:
        action()
    else:
        pl.when(condition)(action)


LINK = {"x": 0, "y": 1, UP: 2, DOWN: 3}


def dispatch_kernel(dims, tok, sel, *rest):
    experts, shards, extra = dims
    if extra:
        (
            small, picked, small_all, held, own, other, arrive, leave, swap_out, swap_in, local,
            small_out, small_in,
        ) = rest
    else:
        picked, held, own, other, arrive, leave, swap_out, swap_in, local = rest
    place = Place()
    rows, width = tok.shape
    starts, sizes = part_rows(rows)
    if extra:
        greet_all(place, experts, shards)
        me = place.e * shards + place.f

        def send_small(i, carry):
            target = lax.rem(me + i, experts * shards)
            pltpu.make_async_remote_copy(
                src_ref=small,
                dst_ref=small_all.at[me],
                send_sem=small_out.at[i],
                recv_sem=small_in.at[me],
                device_id=(target // shards, lax.rem(target, shards)),
                device_id_type=MESH,
            ).start()
            return carry

        lax.fori_loop(1, experts * shards, send_small, 0)
        keep_small = pltpu.make_async_copy(small, small_all.at[me], local.at[CHIPS + 1])
        keep_small.start()
    else:
        greet(place)
    mine = place.chip(place.z, 0, 0)
    keep = pltpu.make_async_copy(tok, held.at[mine], local.at[CHIPS])
    keep.start()
    pending = []
    finish = []

    def multiply(chip):
        def tile(i, carry):
            columns = pl.ds(pl.multiple_of(i * 512, 512), 512)
            rows_here = jnp.dot(
                sel[chip], held[chip, :, columns], preferred_element_type=jnp.float32
            ).astype(jnp.bfloat16)
            own[chip, :, columns] = rows_here[:SLOTS]
            other[chip, :, columns] = rows_here[SLOTS:]
            return carry

        lax.fori_loop(0, width // 512, tile, 0)
        away = pltpu.make_async_remote_copy(
            src_ref=other.at[chip],
            dst_ref=picked.at[place.c, chip],
            send_sem=swap_out.at[chip],
            recv_sem=swap_in.at[chip],
            device_id=place.device("c"),
            device_id_type=MESH,
        )
        away.start()
        stay = pltpu.make_async_copy(own.at[chip], picked.at[place.c, chip], local.at[chip])
        stay.start()
        finish.append((away, stay))

    waiting = []
    for j, xr, yr in items():
        zs = place.ranked(j)
        chip = place.chip(zs, xr, yr)
        first = j == 0 and xr == 0 and yr == 0
        for p, path in enumerate(PATHS):
            window = held.at[chip, pl.ds(starts[p], sizes[p])]
            source = tok.at[pl.ds(starts[p], sizes[p])] if first else window
            if not first:
                pltpu.make_async_remote_copy(
                    src_ref=window,
                    dst_ref=window,
                    send_sem=leave.at[p, chip, 0],
                    recv_sem=arrive.at[p, chip],
                    device_id=place.device("c"),
                    device_id_type=MESH,
                ).wait_recv()
            for axis, condition in links(place, path, j, xr, yr, zs):
                copy = pltpu.make_async_remote_copy(
                    src_ref=source,
                    dst_ref=window,
                    send_sem=leave.at[p, chip, LINK[axis]],
                    recv_sem=arrive.at[p, chip],
                    device_id=place.device(axis),
                    device_id_type=MESH,
                )
                run(condition, copy.start)
                pending.append((condition, copy))
        if first:
            keep.wait()
        waiting.append(chip)
        if len(waiting) > 1:
            multiply(waiting.pop(0))
    while waiting:
        multiply(waiting.pop(0))
    for condition, copy in pending:
        run(condition, copy.wait_send)
    for away, stay in finish:
        away.wait()
        stay.wait()
    if extra:
        keep_small.wait()

        def wait_small(i, carry):
            source = lax.rem(me + i, experts * shards)
            copy = pltpu.make_async_remote_copy(
                src_ref=small,
                dst_ref=small_all.at[source],
                send_sem=small_out.at[i],
                recv_sem=small_in.at[source],
                device_id=(place.e, place.f),
                device_id_type=MESH,
            )
            copy.wait_send()
            copy.wait_recv()
            return carry

        lax.fori_loop(1, experts * shards, wait_small, 0)


def dispatch(experts, shards, number, tok, sel, small=None):
    rows, width = tok.shape
    devices = experts * shards
    any_space = pl.BlockSpec(memory_space=pl.ANY)
    vmem = pl.BlockSpec(memory_space=pltpu.VMEM)
    out_shape = [jax.ShapeDtypeStruct((2, CHIPS, SLOTS, width), jnp.bfloat16)]
    scratch = [
        pltpu.VMEM((CHIPS, rows, width), jnp.bfloat16),
        pltpu.VMEM((CHIPS, SLOTS, width), jnp.bfloat16),
        pltpu.VMEM((CHIPS, SLOTS, width), jnp.bfloat16),
        pltpu.SemaphoreType.DMA((4, CHIPS)),
        pltpu.SemaphoreType.DMA((4, CHIPS, 4)),
        pltpu.SemaphoreType.DMA((CHIPS,)),
        pltpu.SemaphoreType.DMA((CHIPS,)),
        pltpu.SemaphoreType.DMA((CHIPS + 2,)),
    ]
    operands = [tok, sel]
    in_specs = [any_space, vmem]
    if small is not None:
        operands.append(small)
        in_specs.append(any_space)
        out_shape.append(jax.ShapeDtypeStruct((devices,) + small.shape, small.dtype))
        scratch += [pltpu.SemaphoreType.DMA((devices,)), pltpu.SemaphoreType.DMA((devices,))]
    out = pl.pallas_call(
        functools.partial(dispatch_kernel, (experts, shards, small is not None)),
        out_shape=out_shape,
        in_specs=in_specs,
        out_specs=[any_space] * len(out_shape),
        scratch_shapes=scratch,
        compiler_params=pltpu.CompilerParams(
            collective_id=number, has_side_effects=True, vmem_limit_bytes=56 * 2**20
        ),
        name="dispatch",
    )(*operands)
    return out if small is not None else out[0]


def child_slots():
    table = {}
    top = 0
    _, sizes = part_rows(256)
    for p, path in enumerate(PATHS):
        for axis in "xyz":
            place_of = path.index(axis)
            before = path[:place_of]
            count = 1
            for other in before:
                count *= 4 if other == "z" else 2
            lines = count * (5 if axis == "z" else 1)
            table[p, axis] = (top, before)
            top += lines * sizes[p]
    return table, top


def combine_kernel(dims, weighted, sel, *rest):
    experts, shards, extra = dims
    if extra:
        (
            small, total, small_all, near, far, acc, slots, near_in, far_in, far_out, arrive, leave,
            small_out, small_in, local,
        ) = rest
    else:
        total, near, far, acc, slots, near_in, far_in, far_out, arrive, leave = rest
    place = Place()
    rows, width = total.shape
    starts, sizes = part_rows(rows)
    table, _ = child_slots()
    if extra:
        greet_all(place, experts, shards)
        me = place.e * shards + place.f

        def send_small(i, carry):
            target = lax.rem(me + i, experts * shards)
            pltpu.make_async_remote_copy(
                src_ref=small.at[target],
                dst_ref=small_all.at[me],
                send_sem=small_out.at[i],
                recv_sem=small_in.at[me],
                device_id=(target // shards, lax.rem(target, shards)),
                device_id_type=MESH,
            ).start()
            return carry

        lax.fori_loop(1, experts * shards, send_small, 0)
        keep_small = pltpu.make_async_copy(small.at[me], small_all.at[me], local)
        keep_small.start()
    else:
        greet(place)
    order = items()[::-1]

    def far_copy(chip):
        return pltpu.make_async_remote_copy(
            src_ref=weighted.at[1 - place.c, chip],
            dst_ref=far.at[chip],
            send_sem=far_out.at[chip],
            recv_sem=far_in.at[chip],
            device_id=place.device("c"),
            device_id_type=MESH,
        )

    def near_copy(chip):
        return pltpu.make_async_copy(weighted.at[place.c, chip], near.at[chip], near_in.at[chip])

    for j, xr, yr in order:
        chip = place.chip(place.ranked(j), xr, yr)
        far_copy(chip).start()
        near_copy(chip).start()

    def slot(p, axis, side, zd, xd, yd):
        top, before = table[p, axis]
        index = 0
        for other in before:
            if other == "z":
                index = index * 4 + zd
            else:
                index = index * 2 + (xd if other == "x" else yd)
        if axis == "z":
            index = index * 5 + (jnp.where(zd == place.z, 4, zd) if side == BELOW else zd)
        return slots.at[pl.ds(pl.multiple_of(top + index * sizes[p], 16), sizes[p])]

    def far_slot(p, axis, side, zd, xd, yd, zhere):
        top, before = table[p, axis]
        index = 0
        for other in before:
            if other == "z":
                index = index * 4 + zd
            else:
                index = index * 2 + (xd if other == "x" else yd)
        if axis == "z":
            index = index * 5 + (jnp.where(zd == zhere, 4, zd) if side == BELOW else zd)
        return slots.at[pl.ds(pl.multiple_of(top + index * sizes[p], 16), sizes[p])]

    pending = []
    for j, xr, yr in order:
        zd = place.ranked(j)
        xd = 1 - place.x if xr else place.x
        yd = 1 - place.y if yr else place.y
        chip = place.chip(zd, xr, yr)
        last = j == 0 and xr == 0 and yr == 0
        far_copy(chip).wait_recv()
        near_copy(chip).wait()

        def tile(i, carry):
            columns = pl.ds(pl.multiple_of(i * 512, 512), 512)
            dense = jnp.dot(
                sel[chip, :, :SLOTS], near[chip, :, columns], preferred_element_type=jnp.float32
            ) + jnp.dot(
                sel[chip, :, SLOTS:], far[chip, :, columns], preferred_element_type=jnp.float32
            )
            acc[chip, :, columns] = dense.astype(jnp.bfloat16)
            return carry

        lax.fori_loop(0, width // 512, tile, 0)
        for p, path in enumerate(PATHS):
            children = []
            for axis in onward(path, j, xr, yr):
                if axis == "z+":
                    children.append(("z", ABOVE, (zd < place.z) & (place.z < 3)))
                    children.append(("z", BELOW, (zd > place.z) & (place.z > 0)))
                elif axis == "z*":
                    children.append(("z", ABOVE, place.z < 3))
                    children.append(("z", BELOW, place.z > 0))
                else:
                    children.append((axis, None, None))
            for axis, side, condition in children:
                link = {"x": 0, "y": 1}[axis] if axis != "z" else (2 if side == ABOVE else 3)
                window = slot(p, axis, side, zd, xd, yd)
                got = pltpu.make_async_remote_copy(
                    src_ref=window,
                    dst_ref=window,
                    send_sem=leave.at[p, chip],
                    recv_sem=arrive.at[p, chip, link],
                    device_id=place.device("c"),
                    device_id_type=MESH,
                )

                def take(got=got, window=window):
                    got.wait_recv()

                    def add(i, carry):
                        here = pl.ds(pl.multiple_of(i * 16, 16), 16)
                        at = pl.ds(pl.multiple_of(starts[p] + i * 16, 16), 16)
                        acc[chip, at] = (
                            acc[chip, at].astype(jnp.float32) + window[here].astype(jnp.float32)
                        ).astype(jnp.bfloat16)
                        return carry

                    lax.fori_loop(0, sizes[p] // 16, add, 0)

                run(condition, take)
            if last:
                continue
            differs = {"z": j > 0, "x": xr > 0, "y": yr > 0}
            parent = [axis for axis in path if differs[axis]][-1]
            window = acc.at[chip, pl.ds(starts[p], sizes[p])]

            def send(axis, link, side, condition):
                zhere = place.z + (0 if side is None else (-1 if side == ABOVE else 1))
                copy = pltpu.make_async_remote_copy(
                    src_ref=window,
                    dst_ref=far_slot(p, axis, side, zd, xd, yd, zhere),
                    send_sem=leave.at[p, chip],
                    recv_sem=arrive.at[p, chip, link],
                    device_id=place.device(
                        axis if side is None else (DOWN if side == ABOVE else UP)
                    ),
                    device_id_type=MESH,
                )
                run(condition, copy.start)
                pending.append((condition, copy))

            if parent == "z":
                send("z", 2, ABOVE, zd < place.z)
                send("z", 3, BELOW, zd > place.z)
            else:
                send(parent, {"x": 0, "y": 1}[parent], None, None)
    mine = place.chip(place.z, 0, 0)

    def put(i, carry):
        here = pl.ds(pl.multiple_of(i * 16, 16), 16)
        total[here] = acc[mine, here].astype(jnp.float32)
        return carry

    lax.fori_loop(0, rows // 16, put, 0)
    for condition, copy in pending:
        run(condition, copy.wait_send)
    for j, xr, yr in order:
        far_copy(place.chip(place.ranked(j), xr, yr)).wait_send()
    if extra:
        keep_small.wait()

        def wait_small(i, carry):
            source = lax.rem(me + i, experts * shards)
            copy = pltpu.make_async_remote_copy(
                src_ref=small.at[source],
                dst_ref=small_all.at[source],
                send_sem=small_out.at[i],
                recv_sem=small_in.at[source],
                device_id=(place.e, place.f),
                device_id_type=MESH,
            )
            copy.wait_send()
            copy.wait_recv()
            return carry

        lax.fori_loop(1, experts * shards, wait_small, 0)


def combine(experts, shards, number, weighted, sel, small=None):
    rows = sel.shape[1]
    width = weighted.shape[-1]
    devices = experts * shards
    any_space = pl.BlockSpec(memory_space=pl.ANY)
    vmem = pl.BlockSpec(memory_space=pltpu.VMEM)
    _, top = child_slots()
    out_shape = [jax.ShapeDtypeStruct((rows, width), jnp.float32)]
    out_specs = [vmem]
    scratch = [
        pltpu.VMEM((CHIPS, SLOTS, width), jnp.bfloat16),
        pltpu.VMEM((CHIPS, SLOTS, width), jnp.bfloat16),
        pltpu.VMEM((CHIPS, rows, width), jnp.bfloat16),
        pltpu.VMEM((top, width), jnp.bfloat16),
        pltpu.SemaphoreType.DMA((CHIPS,)),
        pltpu.SemaphoreType.DMA((CHIPS,)),
        pltpu.SemaphoreType.DMA((CHIPS,)),
        pltpu.SemaphoreType.DMA((4, CHIPS, 4)),
        pltpu.SemaphoreType.DMA((4, CHIPS)),
    ]
    operands = [weighted, sel]
    in_specs = [any_space, vmem]
    if small is not None:
        operands.append(small)
        in_specs.append(any_space)
        out_shape.append(jax.ShapeDtypeStruct(small.shape, small.dtype))
        out_specs.append(any_space)
        scratch += [
            pltpu.SemaphoreType.DMA((devices,)),
            pltpu.SemaphoreType.DMA((devices,)),
            pltpu.SemaphoreType.DMA,
        ]
    out = pl.pallas_call(
        functools.partial(combine_kernel, (experts, shards, small is not None)),
        out_shape=out_shape,
        in_specs=in_specs,
        out_specs=out_specs,
        scratch_shapes=scratch,
        compiler_params=pltpu.CompilerParams(
            collective_id=number, has_side_effects=True, vmem_limit_bytes=60 * 2**20
        ),
        name="combine",
    )(*operands)
    return out if small is not None else out[0]


def remote(src, dst, send_sem, recv_sem, device):
    return pltpu.make_async_remote_copy(
        src_ref=src,
        dst_ref=dst,
        send_sem=send_sem,
        recv_sem=recv_sem,
        device_id=device,
        device_id_type=MESH,
    )


FLAT = ("zy", "yz")
CHUNKS = 4


def flat_parts(rows):
    return (0, rows * 3 // 4), (rows * 3 // 4, rows - rows * 3 // 4)


def send_around(place, experts, shards, src_of, dst, out_sems, in_sems, across):
    count = experts * shards if across else shards
    me = place.e * shards + place.f if across else place.f

    def copy(i, sending):
        other = lax.rem(me + i, count)
        if across:
            device = (other // shards, lax.rem(other, shards))
        else:
            device = (place.e, other)
        source = me if sending else other
        return remote(src_of(other), dst.at[source], out_sems.at[i], in_sems.at[source], device)

    def start(i, carry):
        copy(i, True).start()
        return carry

    def finish(i, carry):
        done = copy(i, False)
        done.wait_send()
        done.wait_recv()
        return carry

    lax.fori_loop(1, count, start, 0)
    return lambda: lax.fori_loop(1, count, finish, 0)


def gather_kernel(
    dims, flat, tall, tok, pack, ids, flat_all, tall_all, tok_all, pack_all, ids_all,
    flat_in, flat_out, tall_in, tall_out, tok_in, tok_out, pack_in, pack_out, ids_in, ids_out, local,
):
    experts, shards = dims
    place = Place()
    greet_all(place, experts, shards)
    me = place.e * shards + place.f
    starts, sizes = flat_parts(flat.shape[0])
    chunk = tall.shape[0] // CHUNKS
    pending = []
    keeps = [
        pltpu.make_async_copy(flat, flat_all.at[place.f], local.at[0]),
        pltpu.make_async_copy(tok, tok_all.at[place.e], local.at[1]),
        pltpu.make_async_copy(pack, pack_all.at[place.f], local.at[2]),
        pltpu.make_async_copy(ids, ids_all.at[me], local.at[3]),
    ]

    def go(condition, copy):
        run(condition, copy.start)
        pending.append((condition, copy))

    def both(a, b):
        return b if a is None else (a if b is None else a & b)

    def flat_item(p, j, yr):
        zs = place.ranked(j)
        source = zs * 2 + (1 - place.y if yr else place.y)
        first = j == 0 and yr == 0
        window = flat_all.at[source, pl.ds(starts[p], sizes[p])]
        src = flat.at[pl.ds(starts[p], sizes[p])] if first else window
        if not first:
            remote(
                window, window, flat_out.at[p, source, 0], flat_in.at[p, source], place.device("c")
            ).wait_recv()
        for axis, condition in links(place, FLAT[p], j, 0, yr, zs):
            go(
                condition,
                remote(
                    src,
                    window,
                    flat_out.at[p, source, LINK[axis]],
                    flat_in.at[p, source],
                    place.device(axis),
                ),
            )

    owner = place.z == place.e

    def tall_item(k):
        piece = pl.ds(k * chunk, chunk)
        window = tall_all.at[place.y, piece]

        @pl.when(~owner)
        def _():
            remote(window, window, tall_out.at[k, 0], tall_in.at[0, k], place.device("c")).wait_recv()

        for mine in (True, False):
            src = tall.at[piece] if mine else window
            role = owner if mine else ~owner
            for axis, condition in (
                ("y", None),
                (UP, (place.z >= place.e) & (place.z < 3)),
                (DOWN, (place.z <= place.e) & (place.z > 0)),
            ):
                go(
                    both(role, condition),
                    remote(
                        src,
                        window,
                        tall_out.at[k, LINK[axis]],
                        tall_in.at[1 if axis == "y" else 0, k],
                        place.device(axis),
                    ),
                )

    flat_item(0, 0, 0)
    flat_item(1, 0, 0)
    go(None, remote(tok, tok_all.at[place.e], tok_out.at[0], tok_in.at[place.e], place.device("x")))
    go(None, remote(tok, tok_all.at[place.e], tok_out.at[1], tok_in.at[place.e], place.device("c")))
    end_pack = send_around(
        place, experts, shards, lambda i: pack, pack_all, pack_out, pack_in, False
    )
    end_ids = send_around(place, experts, shards, lambda i: ids, ids_all, ids_out, ids_in, True)
    for keep in keeps:
        keep.start()
    keep_tall = pltpu.make_async_copy(tall, tall_all.at[place.y], local.at[4])
    run(owner, keep_tall.start)
    across = (1 - place.x) * 2 + place.c
    flat_item(1, 0, 1)
    tall_item(0)
    flat_item(0, 1, 0)
    tall_item(1)
    flat_item(1, 1, 0)
    flat_item(1, 1, 1)
    tall_item(2)
    flat_item(0, 2, 0)
    tall_item(3)
    window = tok_all.at[across]
    relay = remote(window, window, tok_out.at[2], tok_in.at[across], place.device("c"))
    relay.wait_recv()
    go(None, relay)
    flat_item(1, 2, 0)
    flat_item(1, 2, 1)
    flat_item(0, 3, 0)
    flat_item(1, 3, 0)
    flat_item(1, 3, 1)
    for j in range(4):
        flat_item(0, j, 1)
    for k in range(CHUNKS):
        window = tall_all.at[1 - place.y, pl.ds(k * chunk, chunk)]
        remote(window, window, tall_out.at[k, 0], tall_in.at[1, k], place.device("c")).wait_recv()
    for source in (place.x * 2 + 1 - place.c, (1 - place.x) * 2 + 1 - place.c):
        window = tok_all.at[source]
        remote(window, window, tok_out.at[2], tok_in.at[source], place.device("c")).wait_recv()
    for condition, copy in pending:
        run(condition, copy.wait_send)
    end_pack()
    end_ids()
    for keep in keeps:
        keep.wait()
    run(owner, keep_tall.wait)


def gather(experts, shards, number, flat, tall, tok, pack, ids):
    space = pl.BlockSpec(memory_space=pl.ANY)
    dma = pltpu.SemaphoreType.DMA
    devices = experts * shards

    def shape(lead, a):
        return jax.ShapeDtypeStruct((lead,) + a.shape, a.dtype)

    return pl.pallas_call(
        functools.partial(gather_kernel, (experts, shards)),
        out_shape=[
            shape(shards, flat),
            shape(2, tall),
            shape(experts, tok),
            shape(shards, pack),
            shape(devices, ids),
        ],
        in_specs=[space] * 5,
        out_specs=[space] * 5,
        scratch_shapes=[
            dma((2, shards)),
            dma((2, shards, 4)),
            dma((2, CHUNKS)),
            dma((CHUNKS, 4)),
            dma((experts,)),
            dma((3,)),
            dma((shards,)),
            dma((shards,)),
            dma((devices,)),
            dma((devices,)),
            dma((5,)),
        ],
        compiler_params=pltpu.CompilerParams(
            collective_id=number, has_side_effects=True, vmem_limit_bytes=16 * 2**20
        ),
        name="gather",
    )(flat, tall, tok, pack, ids)


def add_rows(acc, first, window, rows, step=16):
    def add(i, carry):
        here = pl.ds(pl.multiple_of(i * step, step), step)
        at = pl.ds(pl.multiple_of(first + i * step, step), step)
        acc[at] = (acc[at].astype(jnp.float32) + window[here].astype(jnp.float32)).astype(acc.dtype)
        return carry

    lax.fori_loop(0, rows // step, add, 0)


def reduce_kernel(
    dims, flat, tall, pack, flat_all, tall_out, pack_all,
    acc, tacc, yslot, zslot, yone, zall, ty, tz,
    load, yin, zin, yone_in, zall_in, ty_in, tz_in, flat_send, tall_send, spread_in, spread_out,
    tall_in, pack_in, pack_out, keep_tall, local,
):
    experts, shards = dims
    place = Place()
    greet_all(place, experts, shards)
    me = place.e * shards + place.f
    tall_keeps = []
    owner = place.z == place.e
    home = place.x == place.z // 2
    same = place.c == place.z % 2
    starts, sizes = flat_parts(flat.shape[1])
    height = tall.shape[1]
    chunk = height // CHUNKS
    pending = []

    def go(condition, copy):
        run(condition, copy.start)
        pending.append((condition, copy))

    def both(a, b):
        return a if b is None else a & b

    load_tall = pltpu.make_async_copy(tall, tacc, load.at[0])
    load_flat = pltpu.make_async_copy(flat, acc, load.at[1])
    for k in range(CHUNKS):
        piece = pl.ds(k * chunk, chunk)
        go(
            None,
            remote(tall.at[1 - place.y, piece], ty.at[piece], tall_send.at[0, k], ty_in.at[k], place.device("y")),
        )
    order = (3, 2, 1, 0)
    for j in order:
        zd = place.ranked(j)
        target = zd * 2 + 1 - place.y
        go(
            None,
            remote(
                flat.at[target, pl.ds(starts[0], sizes[0])],
                yslot.at[zd],
                flat_send.at[0, target],
                yin.at[zd],
                place.device("y"),
            ),
        )
    load_tall.start()
    load_flat.start()
    end_pack = send_around(
        place, experts, shards, lambda i: pack.at[lax.rem(i, shards)], pack_all, pack_out, pack_in, True
    )
    keep_pack = pltpu.make_async_copy(pack.at[place.f], pack_all.at[me], local.at[0])
    keep_pack.start()
    load_tall.wait()
    load_flat.wait()

    def into(slots, sems, zd, side):
        index = jnp.where(zd == place.z, 4, zd) if side == BELOW else zd
        return slots.at[index], sems.at[index]

    def out_to(slots, sems, zd, side):
        there = place.z - 1 if side == ABOVE else place.z + 1
        index = jnp.where(zd == there, 4, zd) if side == BELOW else zd
        return slots.at[index], sems.at[index]

    def line(j, p, first, slots, sems, send_sem, target):
        zd = place.ranked(j)
        rows = sizes[p]
        for side, condition in (
            (ABOVE, (zd <= place.z) & (place.z < 3)),
            (BELOW, (zd >= place.z) & (place.z > 0)),
        ):
            window, sem = into(slots, sems, zd, side)

            def take(window=window, sem=sem):
                remote(window, window, send_sem, sem, place.device("c")).wait_recv()
                add_rows(acc.at[target], first, window, rows)

            if j == 0:
                condition = place.z < 3 if side == ABOVE else place.z > 0
            run(condition, take)
        if j == 0:
            return
        for side, axis, condition in ((ABOVE, DOWN, zd < place.z), (BELOW, UP, zd > place.z)):
            window, sem = out_to(slots, sems, zd, side)
            go(
                condition,
                remote(acc.at[target, pl.ds(first, rows)], window, send_sem, sem, place.device(axis)),
            )

    def tall_line(k):
        piece = pl.ds(k * chunk, chunk)
        remote(ty.at[piece], ty.at[piece], tall_send.at[0, k], ty_in.at[k], place.device("c")).wait_recv()
        add_rows(tacc.at[place.y], k * chunk, ty.at[piece], chunk)
        for side, index, condition in (
            (ABOVE, 0, (place.z >= place.e) & (place.z < 3)),
            (BELOW, 1, (place.z <= place.e) & (place.z > 0)),
        ):
            window = tz.at[index, piece]

            def take(window=window, index=index):
                remote(window, window, tall_send.at[1, k], tz_in.at[index, k], place.device("c")).wait_recv()
                add_rows(tacc.at[place.y], k * chunk, window, chunk)

            run(condition, take)
        for index, axis, condition in ((0, DOWN, place.z > place.e), (1, UP, place.z < place.e)):
            go(
                condition,
                remote(
                    tacc.at[place.y, piece], tz.at[index, piece], tall_send.at[1, k], tz_in.at[index, k],
                    place.device(axis),
                ),
            )
        piece_out = tall_out.at[piece]
        keep = pltpu.make_async_copy(tacc.at[place.y, piece], piece_out, keep_tall.at[k])
        run(owner, keep.start)
        tall_keeps.append(keep)
        for row, axis in ((2, "x"), (3, "c")):
            go(
                owner,
                remote(
                    tacc.at[place.y, piece], piece_out, tall_send.at[row, k], tall_in.at[k],
                    place.device(axis),
                ),
            )

    def flat_first(j):
        zd = place.ranked(j)
        target = zd * 2 + place.y
        window = yslot.at[zd]
        remote(window, window, flat_send.at[0, target], yin.at[zd], place.device("c")).wait_recv()
        add_rows(acc.at[target], starts[0], window, sizes[0])
        line(j, 0, starts[0], zslot, zin, flat_send.at[0, target], target)

    def flat_second(j, yr):
        zd = place.ranked(j)
        target = zd * 2 + (1 - place.y if yr else place.y)
        line(j, 1, starts[1], zall.at[yr], zall_in.at[yr], flat_send.at[1, target], target)

    for j in order[:-1]:
        flat_second(j, 1)
        flat_second(j, 0)
        flat_first(j)
        tall_line(3 - j)
    flat_second(0, 1)
    other = place.z * 2 + 1 - place.y
    go(
        None,
        remote(
            acc.at[other, pl.ds(starts[1], sizes[1])], yone, flat_send.at[1, other], yone_in.at[0],
            place.device("y"),
        ),
    )
    flat_second(0, 0)
    flat_first(0)
    remote(yone, yone, flat_send.at[1, other], yone_in.at[0], place.device("c")).wait_recv()
    add_rows(acc.at[place.f], starts[1], yone, sizes[1])
    keep_flat = pltpu.make_async_copy(acc.at[place.f], flat_all.at[place.e], local.at[1])
    keep_flat.start()
    for axis in ("x", "c"):
        go(
            None,
            remote(
                acc.at[place.f], flat_all.at[place.e], spread_out.at[0 if axis == "x" else 1],
                spread_in.at[place.e], place.device(axis),
            ),
        )
    tall_line(CHUNKS - 1)
    across = (1 - place.x) * 2 + place.c
    window = flat_all.at[across]
    relay = remote(window, window, spread_out.at[2], spread_in.at[across], place.device("c"))
    relay.wait_recv()
    go(None, relay)
    for k in range(CHUNKS):
        window = tall_out.at[pl.ds(k * chunk, chunk)]
        tall_relay = remote(window, window, tall_send.at[4, k], tall_in.at[k], place.device("c"))
        run(~owner, tall_relay.wait_recv)
        go(~home & same, tall_relay)
    for source in (place.x * 2 + 1 - place.c, (1 - place.x) * 2 + 1 - place.c):
        window = flat_all.at[source]
        remote(window, window, spread_out.at[2], spread_in.at[source], place.device("c")).wait_recv()
    for condition, copy in pending:
        run(condition, copy.wait_send)
    end_pack()
    keep_pack.wait()
    keep_flat.wait()
    for keep in tall_keeps:
        run(owner, keep.wait)


def reduce(experts, shards, number, flat, tall, pack):
    space = pl.BlockSpec(memory_space=pl.ANY)
    dma = pltpu.SemaphoreType.DMA
    devices = experts * shards
    _, sizes = flat_parts(flat.shape[1])
    width, wide = flat.shape[2], tall.shape[2]
    low = jnp.bfloat16
    return pl.pallas_call(
        functools.partial(reduce_kernel, (experts, shards)),
        out_shape=[
            jax.ShapeDtypeStruct((experts,) + flat.shape[1:], low),
            jax.ShapeDtypeStruct(tall.shape[1:], low),
            jax.ShapeDtypeStruct((devices,) + pack.shape[1:], pack.dtype),
        ],
        in_specs=[space] * 3,
        out_specs=[space] * 3,
        scratch_shapes=[
            pltpu.VMEM(flat.shape, low),
            pltpu.VMEM(tall.shape, low),
            pltpu.VMEM((4, sizes[0], width), low),
            pltpu.VMEM((5, sizes[0], width), low),
            pltpu.VMEM((sizes[1], width), low),
            pltpu.VMEM((2, 5, sizes[1], width), low),
            pltpu.VMEM(tall.shape[1:], low),
            pltpu.VMEM((2,) + tall.shape[1:], low),
            dma((2,)),
            dma((4,)),
            dma((5,)),
            dma((1,)),
            dma((2, 5)),
            dma((CHUNKS,)),
            dma((2, CHUNKS)),
            dma((2, shards)),
            dma((5, CHUNKS)),
            dma((experts,)),
            dma((3,)),
            dma((CHUNKS,)),
            dma((devices,)),
            dma((devices,)),
            dma((CHUNKS,)),
            dma((2,)),
        ],
        compiler_params=pltpu.CompilerParams(
            collective_id=number, has_side_effects=True, vmem_limit_bytes=48 * 2**20
        ),
        name="reduce",
    )(flat, tall, pack)


def group_gather_kernel(tok, out, x_out, x_in, c_out, c_in, relay_out, relay_in, local):
    place = Place()
    greet(place)
    across = (1 - place.x) * 2 + place.c
    chunk = tok.shape[0] // CHUNKS
    keep = pltpu.make_async_copy(tok, out.at[place.e], local.at[0])
    near = remote(tok, out.at[place.e], c_out.at[0], c_in.at[0], place.device("c"))
    copies = []
    for k in range(CHUNKS):
        piece = pl.ds(k * chunk, chunk)
        copies.append(
            remote(tok.at[piece], out.at[place.e, piece], x_out.at[k], x_in.at[k], place.device("x"))
        )
        copies[-1].start()
    near.start()
    keep.start()
    for k in range(CHUNKS):
        window = out.at[across, pl.ds(k * chunk, chunk)]
        remote(window, window, x_out.at[k], x_in.at[k], place.device("c")).wait_recv()
        relay = remote(window, window, relay_out.at[k], relay_in.at[k], place.device("c"))
        relay.start()
        copies.append(relay)
    for k in range(CHUNKS):
        window = out.at[(1 - place.x) * 2 + 1 - place.c, pl.ds(k * chunk, chunk)]
        remote(window, window, relay_out.at[k], relay_in.at[k], place.device("c")).wait_recv()
    near.wait()
    keep.wait()
    for copy in copies:
        copy.wait_send()


def group_gather(number, tok):
    space = pl.BlockSpec(memory_space=pl.ANY)
    dma = pltpu.SemaphoreType.DMA
    return pl.pallas_call(
        group_gather_kernel,
        out_shape=jax.ShapeDtypeStruct((4,) + tok.shape, tok.dtype),
        in_specs=[space],
        out_specs=space,
        scratch_shapes=[
            dma((CHUNKS,)), dma((CHUNKS,)), dma((1,)), dma((1,)), dma((CHUNKS,)), dma((CHUNKS,)), dma((1,)),
        ],
        compiler_params=pltpu.CompilerParams(
            collective_id=number, has_side_effects=True, vmem_limit_bytes=16 * 2**20
        ),
        name="group_gather",
    )(tok)


def group_scatter_kernel(
    partial, total, acc, near, cross, load_in, near_out, near_in, x_out, x_in
):
    place = Place()
    greet(place)
    rows = partial.shape[1]
    chunk = rows // CHUNKS
    sends = []
    loads = []
    for half in (1 - place.x, place.x):
        for k in range(CHUNKS):
            piece = pl.ds(k * chunk, chunk)
            copy = remote(
                partial.at[half * 2 + 1 - place.c, piece], near.at[half, piece], near_out.at[half, k],
                near_in.at[half, k], place.device("c"),
            )
            copy.start()
            sends.append(copy)
            load = pltpu.make_async_copy(
                partial.at[half * 2 + place.c, piece], acc.at[half, piece], load_in.at[half, k]
            )
            load.start()
            loads.append(load)
    for index, half in enumerate((1 - place.x, place.x)):
        for k in range(CHUNKS):
            piece = pl.ds(k * chunk, chunk)
            window = near.at[half, piece]
            loads[index * CHUNKS + k].wait()
            remote(window, window, near_out.at[half, k], near_in.at[half, k], place.device("c")).wait_recv()
            add_rows(acc.at[half], k * chunk, window, chunk)
            if index == 0:
                copy = remote(
                    acc.at[half, piece], cross.at[piece], x_out.at[k], x_in.at[k], place.device("x")
                )
                copy.start()
                sends.append(copy)
    for k in range(CHUNKS):
        window = cross.at[pl.ds(k * chunk, chunk)]
        remote(window, window, x_out.at[k], x_in.at[k], place.device("c")).wait_recv()

        def add(i, carry):
            here = pl.ds(pl.multiple_of(k * chunk + i * 16, 16), 16)
            total[here] = acc[place.x, here].astype(jnp.float32) + cross[here].astype(jnp.float32)
            return carry

        lax.fori_loop(0, chunk // 16, add, 0)
    for copy in sends:
        copy.wait_send()


def group_scatter(number, partial):
    dma = pltpu.SemaphoreType.DMA
    rows, width = partial.shape[1:]
    low = jnp.bfloat16
    return pl.pallas_call(
        group_scatter_kernel,
        out_shape=jax.ShapeDtypeStruct((rows, width), jnp.float32),
        in_specs=[pl.BlockSpec(memory_space=pl.ANY)],
        out_specs=pl.BlockSpec(memory_space=pltpu.VMEM),
        scratch_shapes=[
            pltpu.VMEM((2, rows, width), low),
            pltpu.VMEM((2, rows, width), low),
            pltpu.VMEM((rows, width), low),
            dma((2, CHUNKS)),
            dma((2, CHUNKS)),
            dma((2, CHUNKS)),
            dma((CHUNKS,)),
            dma((CHUNKS,)),
        ],
        compiler_params=pltpu.CompilerParams(
            collective_id=number, has_side_effects=True, vmem_limit_bytes=16 * 2**20
        ),
        name="group_scatter",
    )(partial)


def local(
    layer_input,
    doc_ids,
    expert_ids,
    w_query,
    w_key,
    w_value,
    w_out,
    w_router,
    gain_attn,
    gain_ffn,
    gain_query,
    gain_key,
    w_gate,
    w_up,
    w_down,
    grad_output,
):
    single_float = jnp.float32
    brain_float_half = jnp.bfloat16
    row_count = layer_input.shape[1]
    width = layer_input.shape[2]
    length_total = doc_ids.shape[1]
    query_groups = QUERY_HEADS // KEY_VALUE_HEADS
    scale = HEAD_SIZE ** (-0.5)
    experts = w_router.shape[1]
    capacity = max(2, 6 * row_count * TOP // (5 * experts))
    pairs = row_count * TOP
    (
        full_query,
        gathered_key,
        full_value,
        full_out,
        full_router,
        gain_one,
        gain_two,
        gain_q,
        key_gain_vector,
    ) = (
        lax.all_gather(w_query, FSDP, axis=0, tiled=True),
        lax.all_gather(w_key, FSDP, axis=0, tiled=True),
        lax.all_gather(w_value, FSDP, axis=0, tiled=True),
        lax.all_gather(w_out, FSDP, axis=0, tiled=True),
        lax.all_gather(w_router, FSDP, axis=0, tiled=True),
        lax.all_gather(gain_attn, FSDP, axis=0, tiled=True),
        lax.all_gather(gain_ffn, FSDP, axis=0, tiled=True),
        lax.all_gather(gain_query, FSDP, axis=0, tiled=True),
        lax.all_gather(gain_key, FSDP, axis=0, tiled=True),
    )
    gain_one = gain_one.astype(single_float)
    gain_two = gain_two.astype(single_float)
    gain_q = gain_q.astype(single_float)
    key_gain_vector = key_gain_vector.astype(single_float)
    inputs = layer_input[0].astype(single_float)
    offset = lax.axis_index(EXPERT) * row_count
    own_pos = offset + jnp.arange(row_count, dtype=jnp.int32)
    all_pos = jnp.arange(length_total, dtype=jnp.int32)
    seq_ids = doc_ids[0]
    own_ids = lax.dynamic_slice_in_dim(seq_ids, offset, row_count)
    allowed = (own_ids[:, None] == seq_ids[None, :]) & (own_pos[:, None] >= all_pos[None, :])
    cosine_table, sine_table = angles(own_pos)
    cosine_table = cosine_table[:, None, :]
    sine_table = sine_table[:, None, :]
    scale_one = inverse_rms(inputs)
    normalized_input = (inputs * scale_one * gain_one).astype(brain_float_half)
    query_raw = jnp.dot(normalized_input, full_query, preferred_element_type=single_float).reshape(
        row_count, QUERY_HEADS, HEAD_SIZE
    )
    key_unnormalized = jnp.dot(
        normalized_input, gathered_key, preferred_element_type=single_float
    ).reshape(row_count, KEY_VALUE_HEADS, HEAD_SIZE)
    value_low = jnp.dot(normalized_input, full_value, preferred_element_type=single_float).astype(
        brain_float_half
    )
    query_scale = inverse_rms(query_raw)
    key_norm_scale = inverse_rms(key_unnormalized)
    query_rot = (
        apply_rotary(query_raw * query_scale * gain_q, cosine_table, sine_table)
        .astype(brain_float_half)
        .reshape(row_count, KEY_VALUE_HEADS, query_groups, HEAD_SIZE)
    )
    key_rotated = apply_rotary(
        key_unnormalized * key_norm_scale * key_gain_vector, cosine_table, sine_table
    ).astype(brain_float_half)
    key_gathered_rows, value_gathered_rows = (
        lax.all_gather(
            key_rotated.reshape(row_count, KEY_VALUE_HEADS * HEAD_SIZE),
            EXPERT,
            axis=0,
            tiled=True,
        ),
        lax.all_gather(value_low, EXPERT, axis=0, tiled=True),
    )
    key_gathered_rows = key_gathered_rows.reshape(length_total, KEY_VALUE_HEADS, HEAD_SIZE)
    value_gathered_rows = value_gathered_rows.reshape(length_total, KEY_VALUE_HEADS, HEAD_SIZE)

    def masked_scores():
        raw = (
            jnp.einsum(
                "tkgd,skd->kgts", query_rot, key_gathered_rows, preferred_element_type=single_float
            )
            * scale
        )
        return jnp.where(allowed, raw, -1e30)

    scores = masked_scores()
    peak = jnp.max(scores, -1, keepdims=True)
    shifted = jnp.exp(scores - peak)
    totals = jnp.sum(shifted, -1, keepdims=True)
    weights_low = (shifted / totals).astype(brain_float_half)
    log_total = peak + jnp.log(totals)
    mixed = (
        jnp.einsum(
            "kgts,skd->tkgd", weights_low, value_gathered_rows, preferred_element_type=single_float
        )
        .reshape(row_count, QUERY_HEADS * HEAD_SIZE)
        .astype(brain_float_half)
    )
    hidden = inputs + jnp.dot(mixed, full_out, preferred_element_type=single_float)
    scale_two = inverse_rms(hidden)
    normed_two = (hidden * scale_two * gain_two).astype(brain_float_half)
    logits = jnp.dot(normed_two, full_router, preferred_element_type=single_float)
    selector = (expert_ids[0][:, :, None] == jnp.arange(experts, dtype=jnp.int32)).astype(
        single_float
    )
    chosen = jnp.einsum("tke,te->tk", selector, logits, precision=HIGHEST)
    gates = jax.nn.softmax(chosen, -1)
    flat_routes = expert_ids[0].reshape(pairs)
    hits = (flat_routes[:, None] == jnp.arange(experts, dtype=jnp.int32)).astype(jnp.int32)
    before = jnp.cumsum(hits, 0) - hits
    ranks = jnp.sum(before * hits, 1)
    slot_index = flat_routes * capacity + ranks
    owner_rows = jnp.arange(pairs, dtype=jnp.int32) // TOP
    outgoing = (
        jnp.zeros((experts * capacity, width), brain_float_half)
        .at[slot_index]
        .set(normed_two[owner_rows])
    )
    arrived = lax.all_to_all(
        outgoing.reshape(experts, capacity, width),
        (EXPERT, FSDP),
        split_axis=0,
        concat_axis=0,
        tiled=True,
    ).reshape(experts * capacity, width)
    gate_pre = jnp.dot(arrived, w_gate[0], preferred_element_type=single_float)
    up_pre = jnp.dot(arrived, w_up[0], preferred_element_type=single_float)
    activated = jax.nn.silu(gate_pre)
    inner = (activated * up_pre).astype(brain_float_half)
    result = jnp.dot(inner, w_down[0], preferred_element_type=single_float).astype(brain_float_half)
    returned = lax.all_to_all(
        result.reshape(experts, capacity, width),
        (EXPERT, FSDP),
        split_axis=0,
        concat_axis=0,
        tiled=True,
    ).reshape(experts * capacity, width)
    expert_rows = returned[slot_index].astype(single_float).reshape(row_count, TOP, width)
    output = hidden + jnp.einsum("tk,tkd->td", gates, expert_rows, precision=HIGHEST)
    grad_top = grad_output[0]
    grad_gates = jnp.einsum("tkd,td->tk", expert_rows, grad_top, precision=HIGHEST)
    grad_pairs = (
        (gates[:, :, None] * grad_top[:, None, :]).astype(brain_float_half).reshape(pairs, width)
    )
    grad_send = (
        jnp.zeros((experts * capacity, width), brain_float_half).at[slot_index].set(grad_pairs)
    )
    grad_arrived = lax.all_to_all(
        grad_send.reshape(experts, capacity, width),
        (EXPERT, FSDP),
        split_axis=0,
        concat_axis=0,
        tiled=True,
    ).reshape(experts * capacity, width)
    grad_down = jnp.einsum("rf,rd->fd", inner, grad_arrived, preferred_element_type=single_float)
    grad_inner = jnp.einsum(
        "rd,fd->rf", grad_arrived, w_down[0], preferred_element_type=single_float
    )
    sigmoid_gate = jax.nn.sigmoid(gate_pre)
    slope = sigmoid_gate * (1.0 + gate_pre * (1.0 - sigmoid_gate))
    grad_gate_pre = (grad_inner * up_pre * slope).astype(brain_float_half)
    grad_up_pre = (grad_inner * activated).astype(brain_float_half)
    grad_gate_w = jnp.einsum(
        "rd,rf->df", arrived, grad_gate_pre, preferred_element_type=single_float
    )
    grad_up_w = jnp.einsum("rd,rf->df", arrived, grad_up_pre, preferred_element_type=single_float)
    grad_rows = (
        jnp.einsum("rf,df->rd", grad_gate_pre, w_gate[0], preferred_element_type=single_float)
        + jnp.einsum("rf,df->rd", grad_up_pre, w_up[0], preferred_element_type=single_float)
    ).astype(brain_float_half)
    grad_back = lax.all_to_all(
        grad_rows.reshape(experts, capacity, width),
        (EXPERT, FSDP),
        split_axis=0,
        concat_axis=0,
        tiled=True,
    ).reshape(experts * capacity, width)
    grad_normed_two = jnp.sum(
        grad_back[slot_index].astype(single_float).reshape(row_count, TOP, width), 1
    )
    grad_chosen = gates * (grad_gates - jnp.sum(gates * grad_gates, -1, keepdims=True))
    grad_logits = jnp.einsum("tke,tk->te", selector, grad_chosen, precision=HIGHEST).astype(
        brain_float_half
    )
    grad_normed_two = grad_normed_two + jnp.einsum(
        "te,de->td", grad_logits, full_router, preferred_element_type=single_float
    )
    grad_router = jnp.einsum(
        "td,te->de", normed_two, grad_logits, preferred_element_type=single_float
    )
    grad_gain_two = jnp.sum(grad_normed_two * hidden * scale_two, 0)
    grad_hidden = grad_top + norm_backward(grad_normed_two, hidden, scale_two, gain_two)
    grad_branch = grad_hidden.astype(brain_float_half)
    grad_out_w = jnp.einsum("tq,td->qd", mixed, grad_branch, preferred_element_type=single_float)
    grad_mixed = (
        jnp.einsum("td,qd->tq", grad_branch, full_out, preferred_element_type=single_float)
        .astype(brain_float_half)
        .reshape(row_count, KEY_VALUE_HEADS, query_groups, HEAD_SIZE)
    )
    again = masked_scores()
    weights = jnp.exp(again - log_total)
    weights_again = weights.astype(brain_float_half)
    grad_weights = jnp.einsum(
        "tkgd,skd->kgts", grad_mixed, value_gathered_rows, preferred_element_type=single_float
    )
    spread = jnp.sum(weights * grad_weights, -1, keepdims=True)
    grad_scores = (weights * (grad_weights - spread)).astype(brain_float_half)
    grad_query_rot = (
        jnp.einsum(
            "kgts,skd->tkgd", grad_scores, key_gathered_rows, preferred_element_type=single_float
        )
        * scale
    ).reshape(row_count, QUERY_HEADS, HEAD_SIZE)
    grad_key_all = (
        jnp.einsum("kgts,tkgd->skd", grad_scores, query_rot, preferred_element_type=single_float)
        * scale
    ).reshape(length_total, KEY_VALUE_HEADS * HEAD_SIZE)
    grad_value_all = jnp.einsum(
        "kgts,tkgd->skd", weights_again, grad_mixed, preferred_element_type=single_float
    ).reshape(length_total, KEY_VALUE_HEADS * HEAD_SIZE)
    gradient_key_rotated, grad_value = (
        lax.psum_scatter(
            grad_key_all.astype(jnp.bfloat16), EXPERT, scatter_dimension=0, tiled=True
        ).astype(jnp.float32),
        lax.psum_scatter(
            grad_value_all.astype(jnp.bfloat16), EXPERT, scatter_dimension=0, tiled=True
        ).astype(jnp.float32),
    )
    gradient_key_rotated = gradient_key_rotated.reshape(row_count, KEY_VALUE_HEADS, HEAD_SIZE)
    grad_query_unit = unrotate(grad_query_rot, cosine_table, sine_table)
    gradient_key_normalized = unrotate(gradient_key_rotated, cosine_table, sine_table)
    grad_gain_q = jnp.sum(grad_query_unit * query_raw * query_scale, (0, 1))
    grad_gain_k = jnp.sum(gradient_key_normalized * key_unnormalized * key_norm_scale, (0, 1))
    grad_query = (
        norm_backward(grad_query_unit, query_raw, query_scale, gain_q)
        .reshape(row_count, QUERY_HEADS * HEAD_SIZE)
        .astype(brain_float_half)
    )
    grad_key = (
        norm_backward(gradient_key_normalized, key_unnormalized, key_norm_scale, key_gain_vector)
        .reshape(row_count, KEY_VALUE_HEADS * HEAD_SIZE)
        .astype(brain_float_half)
    )
    grad_value_low = grad_value.astype(brain_float_half)
    grad_query_w = jnp.einsum(
        "td,tq->dq", normalized_input, grad_query, preferred_element_type=single_float
    )
    grad_key_w = jnp.einsum(
        "td,tq->dq", normalized_input, grad_key, preferred_element_type=single_float
    )
    grad_value_w = jnp.einsum(
        "td,tq->dq", normalized_input, grad_value_low, preferred_element_type=single_float
    )
    grad_normed = (
        jnp.einsum("tq,dq->td", grad_query, full_query, preferred_element_type=single_float)
        + jnp.einsum("tq,dq->td", grad_key, gathered_key, preferred_element_type=single_float)
        + jnp.einsum("tq,dq->td", grad_value_low, full_value, preferred_element_type=single_float)
    )
    grad_gain_one = jnp.sum(grad_normed * inputs * scale_one, 0)
    grad_inputs = grad_hidden + norm_backward(grad_normed, inputs, scale_one, gain_one)
    local_grads = (
        grad_query_w,
        grad_key_w,
        grad_value_w,
        grad_out_w,
        grad_router,
        grad_gain_one,
        grad_gain_two,
        grad_gain_q,
        grad_gain_k,
    )
    shards = (
        lax.psum_scatter(
            local_grads[0].astype(jnp.bfloat16), FSDP, scatter_dimension=0, tiled=True
        ).astype(jnp.float32),
        lax.psum_scatter(
            local_grads[1].astype(jnp.bfloat16), FSDP, scatter_dimension=0, tiled=True
        ).astype(jnp.float32),
        lax.psum_scatter(
            local_grads[2].astype(jnp.bfloat16), FSDP, scatter_dimension=0, tiled=True
        ).astype(jnp.float32),
        lax.psum_scatter(
            local_grads[3].astype(jnp.bfloat16), FSDP, scatter_dimension=0, tiled=True
        ).astype(jnp.float32),
        lax.psum_scatter(
            local_grads[4].astype(jnp.bfloat16), FSDP, scatter_dimension=0, tiled=True
        ).astype(jnp.float32),
        lax.psum_scatter(
            local_grads[5].astype(jnp.bfloat16), FSDP, scatter_dimension=0, tiled=True
        ).astype(jnp.float32),
        lax.psum_scatter(
            local_grads[6].astype(jnp.bfloat16), FSDP, scatter_dimension=0, tiled=True
        ).astype(jnp.float32),
        lax.psum_scatter(
            local_grads[7].astype(jnp.bfloat16), FSDP, scatter_dimension=0, tiled=True
        ).astype(jnp.float32),
        lax.psum_scatter(
            local_grads[8].astype(jnp.bfloat16), FSDP, scatter_dimension=0, tiled=True
        ).astype(jnp.float32),
    )
    shards = (
        lax.psum(shards[0].astype(jnp.bfloat16), EXPERT).astype(jnp.float32),
        lax.psum(shards[1].astype(jnp.bfloat16), EXPERT).astype(jnp.float32),
        lax.psum(shards[2].astype(jnp.bfloat16), EXPERT).astype(jnp.float32),
        lax.psum(shards[3].astype(jnp.bfloat16), EXPERT).astype(jnp.float32),
        lax.psum(shards[4].astype(jnp.bfloat16), EXPERT).astype(jnp.float32),
        lax.psum(shards[5].astype(jnp.bfloat16), EXPERT).astype(jnp.float32),
        lax.psum(shards[6].astype(jnp.bfloat16), EXPERT).astype(jnp.float32),
        lax.psum(shards[7].astype(jnp.bfloat16), EXPERT).astype(jnp.float32),
        lax.psum(shards[8].astype(jnp.bfloat16), EXPERT).astype(jnp.float32),
    )
    return (
        output[None],
        grad_inputs[None],
        shards[0],
        shards[1],
        shards[2],
        shards[3],
        shards[4],
        shards[5],
        shards[6],
        shards[7],
        shards[8],
        grad_gate_w[None],
        grad_up_w[None],
        grad_down[None],
    )


def by_core(blocks):
    return blocks.reshape((2, 2, CHIPS // 2) + blocks.shape[1:]).swapaxes(0, 1).reshape(
        (2, CHIPS) + blocks.shape[1:]
    )


def by_device(blocks):
    return blocks.reshape((2, 2, CHIPS // 2) + blocks.shape[2:]).swapaxes(0, 1).reshape(
        (2 * CHIPS,) + blocks.shape[2:]
    )


def routes(every):
    rows = every.shape[1]
    expert = lax.axis_index(EXPERT)
    shards = lax.axis_size(FSDP)
    core = expert % 2
    me = expert * shards + lax.axis_index(FSDP)
    neighbour = me + (1 - 2 * core) * shards
    every = by_core(every)
    earlier = (jnp.arange(rows)[:, None] < jnp.arange(rows)[None, :]).astype(jnp.bfloat16)

    def chosen(number, blocks):
        hit = jnp.any(blocks == number, -1)
        rank = jnp.dot(
            hit.astype(jnp.bfloat16), earlier, preferred_element_type=jnp.float32
        ).astype(jnp.int32)
        places = jnp.arange(SLOTS, dtype=jnp.int32)
        return (hit[..., None, :] & (rank[..., None, :] == places[:, None])).astype(jnp.bfloat16)

    mine = chosen(me, every)
    near = lax.dynamic_index_in_dim(mine, core, 0, keepdims=False)
    far = chosen(neighbour, lax.dynamic_index_in_dim(every, core, 0, keepdims=False))
    pick = jnp.concatenate([near, far], 1)

    def gate_rows(gates):
        values = by_core(gates.reshape(-1, rows, TOP))
        values = jnp.sum(jnp.where(every == me, values, 0.0), -1)
        return jnp.sum(mine.astype(jnp.float32) * values[:, :, None, :], -1).reshape(-1, 1)

    def back(values):
        values = values.reshape(2, CHIPS, SLOTS, 1)
        dense = by_device(jnp.sum(mine.astype(jnp.float32) * values, 2))
        dense = dense.reshape(2 * CHIPS, rows // 128, 128)
        return jnp.pad(dense, ((0, 0), (0, 8 - rows // 128), (0, 0)))

    return pick, pick.swapaxes(1, 2), gate_rows, back


def packed(pieces, lead, rows):
    flat = jnp.concatenate([piece.reshape(lead, -1) for piece in pieces], 1)
    flat = jnp.pad(flat, ((0, 0), (0, rows * 128 - flat.shape[1])))
    return flat.reshape(lead, rows, 128)


def local_staged(
    layer_input,
    doc_ids,
    expert_ids,
    w_query,
    w_key,
    w_value,
    w_out,
    w_router,
    gain_attn,
    gain_ffn,
    gain_query,
    gain_key,
    w_gate,
    w_up,
    w_down,
    grad_output,
):
    f32 = jnp.float32
    low = jnp.bfloat16
    rows, width = layer_input.shape[1:]
    length = doc_ids.shape[1]
    depth = w_router.shape[0]
    groups, shards = lax.axis_size(EXPERT), lax.axis_size(FSDP)
    experts = w_router.shape[1]
    heads = QUERY_HEADS // groups
    span = heads * HEAD_SIZE
    scale = HEAD_SIZE ** (-0.5)
    mine = lax.axis_index(EXPERT)

    def columns(weight, count):
        return lax.dynamic_slice_in_dim(weight, mine * count, count, 1)

    flat = jnp.concatenate(
        [columns(w_query, span), columns(w_key, HEAD_SIZE), columns(w_value, HEAD_SIZE)], 1
    )
    pack = packed([w_router, gain_attn, gain_ffn, gain_query, gain_key], 1, 80)[0]
    w_qkv, w_mix, tokens, pack_all, ids_all = gather(
        groups,
        shards,
        5,
        flat,
        w_out,
        layer_input[0],
        pack,
        expert_ids[0].reshape(-1, 128),
    )
    w_qkv = w_qkv.reshape(width, span + 2 * HEAD_SIZE)
    w_mix = w_mix.reshape(span, width)
    tokens = tokens.reshape(length, width).astype(f32)
    pack_all = pack_all.reshape(shards, -1)
    at = depth * experts
    full_router = pack_all[:, :at].reshape(width, experts)
    gain_one = pack_all[:, at : at + depth].reshape(width).astype(f32)
    gain_two = pack_all[:, at + depth : at + 2 * depth].reshape(width).astype(f32)
    at += 2 * depth
    small = HEAD_SIZE // shards
    gain_q = pack_all[:, at : at + small].reshape(HEAD_SIZE).astype(f32)
    gain_k = pack_all[:, at + small : at + 2 * small].reshape(HEAD_SIZE).astype(f32)
    pick, spread, gate_rows, back = routes(ids_all.reshape(groups * shards, rows, TOP))
    grad_top = grad_output[0]
    grads_in = dispatch(groups, shards, 1, grad_top.astype(low), pick)

    place = jnp.arange(length, dtype=jnp.int32)
    documents = doc_ids[0]
    allowed = (documents[:, None] == documents[None, :]) & (place[:, None] >= place[None, :])
    cosine_table, sine_table = angles(place)
    cosine_heads, sine_heads = cosine_table[:, None, :], sine_table[:, None, :]
    scale_one = inverse_rms(tokens)
    normed_one = (tokens * scale_one * gain_one).astype(low)
    raw = jnp.dot(normed_one, w_qkv, preferred_element_type=f32)
    query_raw = raw[:, :span].reshape(length, heads, HEAD_SIZE)
    key_raw = raw[:, span : span + HEAD_SIZE]
    value = raw[:, span + HEAD_SIZE :].astype(low)
    query_scale = inverse_rms(query_raw)
    key_scale = inverse_rms(key_raw)
    query_rot = apply_rotary(query_raw * query_scale * gain_q, cosine_heads, sine_heads).astype(low)
    key_rot = apply_rotary(key_raw * key_scale * gain_k, cosine_table, sine_table).astype(low)

    def masked_scores():
        products = jnp.einsum("tgd,sd->gts", query_rot, key_rot, preferred_element_type=f32)
        return jnp.where(allowed, products * scale, -1e30)

    scores = masked_scores()
    peak = jnp.max(scores, -1, keepdims=True)
    shifted = jnp.exp(scores - peak)
    totals = jnp.sum(shifted, -1, keepdims=True)
    weights_low = (shifted / totals).astype(low)
    log_total = peak + jnp.log(totals)
    mixed = jnp.einsum("gts,sd->tgd", weights_low, value, preferred_element_type=f32)
    mixed = mixed.reshape(length, span).astype(low)
    branch = jnp.dot(mixed, w_mix, preferred_element_type=f32).astype(low)
    inputs = layer_input[0].astype(f32)
    hidden = inputs + group_scatter(8, branch.reshape(groups, rows, width))
    scale_two = inverse_rms(hidden)
    normed_two = (hidden * scale_two * gain_two).astype(low)
    logits = jnp.dot(normed_two, full_router, preferred_element_type=f32)
    selector = (expert_ids[0][:, :, None] == jnp.arange(experts, dtype=jnp.int32)).astype(f32)
    gates = jax.nn.softmax(jnp.sum(selector * logits[:, None, :], -1), -1)
    arrived, gates_all = dispatch(groups, shards, 2, normed_two, pick, gates.reshape(-1, 128))
    gate_here = gate_rows(gates_all)
    arrived = arrived.reshape(-1, width)
    grads_in = grads_in.reshape(-1, width)

    gate_pre = jnp.dot(arrived, w_gate[0], preferred_element_type=f32)
    up_pre = jnp.dot(arrived, w_up[0], preferred_element_type=f32)
    activated = jax.nn.silu(gate_pre)
    inner = (activated * up_pre).astype(low)
    result = jnp.dot(inner, w_down[0], preferred_element_type=f32)
    gate_grads = jnp.sum(result * grads_in.astype(f32), -1)
    weighted = (result * gate_here).astype(low)
    combined, gates_back = combine(
        groups, shards, 3, weighted.reshape(2, CHIPS, SLOTS, width), spread, back(gate_grads)
    )
    output = hidden + combined
    gates_back = gates_back[:, : rows // 128].reshape(experts, rows)
    grad_gates = jnp.sum(selector * gates_back.T[:, None, :], -1)
    grad_arrived = (grads_in.astype(f32) * gate_here).astype(low)
    grad_down = jnp.einsum("rf,rd->fd", inner, grad_arrived, preferred_element_type=f32)
    grad_inner = jnp.einsum("rd,fd->rf", grad_arrived, w_down[0], preferred_element_type=f32)
    sigmoid_gate = jax.nn.sigmoid(gate_pre)
    slope = sigmoid_gate * (1.0 + gate_pre * (1.0 - sigmoid_gate))
    grad_gate_pre = (grad_inner * up_pre * slope).astype(low)
    grad_up_pre = (grad_inner * activated).astype(low)
    grad_gate_w = jnp.einsum("rd,rf->df", arrived, grad_gate_pre, preferred_element_type=f32)
    grad_up_w = jnp.einsum("rd,rf->df", arrived, grad_up_pre, preferred_element_type=f32)
    grad_rows = (
        jnp.einsum("rf,df->rd", grad_gate_pre, w_gate[0], preferred_element_type=f32)
        + jnp.einsum("rf,df->rd", grad_up_pre, w_up[0], preferred_element_type=f32)
    ).astype(low)
    grad_normed_two = combine(
        groups, shards, 4, grad_rows.reshape(2, CHIPS, SLOTS, width), spread
    )

    grad_chosen = gates * (grad_gates - jnp.sum(gates * grad_gates, -1, keepdims=True))
    grad_logits = jnp.sum(selector * grad_chosen[:, :, None], 1).astype(low)
    grad_normed_two = grad_normed_two + jnp.einsum(
        "te,de->td", grad_logits, full_router, preferred_element_type=f32
    )
    grad_router = jnp.einsum("td,te->de", normed_two, grad_logits, preferred_element_type=f32)
    grad_gain_two = jnp.sum(grad_normed_two * hidden * scale_two, 0)
    grad_hidden = grad_top + norm_backward(grad_normed_two, hidden, scale_two, gain_two)
    grad_branch = group_gather(7, grad_hidden.astype(low)).reshape(length, width)
    grad_mix = jnp.einsum("tq,td->qd", mixed, grad_branch, preferred_element_type=f32).astype(low)
    grad_mixed = jnp.einsum("td,qd->tq", grad_branch, w_mix, preferred_element_type=f32)
    grad_mixed = grad_mixed.astype(low).reshape(length, heads, HEAD_SIZE)

    weights = jnp.exp(masked_scores() - log_total)
    grad_weights = jnp.einsum("tgd,sd->gts", grad_mixed, value, preferred_element_type=f32)
    balance = jnp.sum(weights * grad_weights, -1, keepdims=True)
    grad_scores = (weights * (grad_weights - balance)).astype(low)
    grad_query_rot = scale * jnp.einsum(
        "gts,sd->tgd", grad_scores, key_rot, preferred_element_type=f32
    )
    grad_key_rot = scale * jnp.einsum(
        "gts,tgd->sd", grad_scores, query_rot, preferred_element_type=f32
    )
    grad_value = jnp.einsum(
        "gts,tgd->sd", weights.astype(low), grad_mixed, preferred_element_type=f32
    )
    grad_query_unit = unrotate(grad_query_rot, cosine_heads, sine_heads)
    grad_key_unit = unrotate(grad_key_rot, cosine_table, sine_table)
    grad_gain_q = jnp.sum(grad_query_unit * query_raw * query_scale, (0, 1))
    grad_gain_k = jnp.sum(grad_key_unit * key_raw * key_scale, 0)
    grad_query = norm_backward(grad_query_unit, query_raw, query_scale, gain_q)
    grad_key = norm_backward(grad_key_unit, key_raw, key_scale, gain_k)
    grad_raw = jnp.concatenate(
        [grad_query.reshape(length, span).astype(low), grad_key.astype(low), grad_value.astype(low)],
        1,
    )
    grad_qkv = jnp.einsum("td,tq->dq", normed_one, grad_raw, preferred_element_type=f32).astype(low)
    grad_normed_one = jnp.einsum("tq,dq->td", grad_raw, w_qkv, preferred_element_type=f32)
    grad_normed_one = group_scatter(9, grad_normed_one.astype(low).reshape(groups, rows, width))
    scale_own = inverse_rms(inputs)
    grad_gain_one = jnp.sum(grad_normed_one * inputs * scale_own, 0)
    grad_inputs = grad_hidden + norm_backward(grad_normed_one, inputs, scale_own, gain_one)

    sums = packed([grad_router, grad_gain_one, grad_gain_two, grad_gain_q, grad_gain_k], shards, 72)
    flat_sum, tall_sum, pack_sum = reduce(
        groups,
        shards,
        6,
        grad_qkv.reshape(shards, depth, -1),
        grad_mix.reshape(2, -1, width),
        sums,
    )
    flat_sum = flat_sum.swapaxes(0, 1).astype(f32)
    pack_sum = jnp.sum(pack_sum, 0).reshape(-1)
    at = depth * experts
    return (
        output[None],
        grad_inputs[None],
        flat_sum[:, :, :span].reshape(depth, groups * span),
        flat_sum[:, :, span : span + HEAD_SIZE].reshape(depth, groups * HEAD_SIZE),
        flat_sum[:, :, span + HEAD_SIZE :].reshape(depth, groups * HEAD_SIZE),
        tall_sum.astype(f32),
        pack_sum[:at].reshape(depth, experts),
        pack_sum[at : at + depth],
        pack_sum[at + depth : at + 2 * depth],
        pack_sum[at + 2 * depth : at + 2 * depth + small],
        pack_sum[at + 2 * depth + small : at + 2 * depth + 2 * small],
        grad_gate_w[None],
        grad_up_w[None],
        grad_down[None],
    )


def solution(mesh):
    in_specs = (
        P(FSDP, EXPERT, None),
        P(FSDP, None),
        P(FSDP, EXPERT, None),
        P(FSDP, None),
        P(FSDP, None),
        P(FSDP, None),
        P(FSDP, None),
        P(FSDP, None),
        P(FSDP),
        P(FSDP),
        P(FSDP),
        P(FSDP),
        P((EXPERT, FSDP), None, None),
        P((EXPERT, FSDP), None, None),
        P((EXPERT, FSDP), None, None),
        P(FSDP, EXPERT, None),
    )
    out_specs = (
        P(FSDP, EXPERT, None),
        P(FSDP, EXPERT, None),
        P(FSDP, None),
        P(FSDP, None),
        P(FSDP, None),
        P(FSDP, None),
        P(FSDP, None),
        P(FSDP),
        P(FSDP),
        P(FSDP),
        P(FSDP),
        P((EXPERT, FSDP), None, None),
        P((EXPERT, FSDP), None, None),
        P((EXPERT, FSDP), None, None),
    )
    staged = mesh.shape[EXPERT] == 4 and mesh.shape[FSDP] == 8
    return jax.shard_map(local_staged if staged else local, mesh=mesh, in_specs=in_specs, out_specs=out_specs, check_vma=False)
```

```python
import functools

import jax
import jax.numpy as jnp
import numpy as np
from jax import lax
from jax.experimental import pallas as pl
from jax.experimental.pallas import tpu as pltpu
from jax.sharding import PartitionSpec as P

EXPERT = "expert"
FSDP = "fsdp"
UP, DOWN, ABOVE, BELOW = "up", "down", "above", "below"
QUERY_HEADS = 32
KEY_VALUE_HEADS = 4
HEAD_SIZE = 128
TOP = 8


EPS = 1e-06
THETA = 1000000.0
HIGHEST = lax.Precision.HIGHEST


def angles(positions):
    freq = THETA ** (-(jnp.arange(HEAD_SIZE // 2, dtype=jnp.float32) * 2.0) / HEAD_SIZE)
    turn = positions.astype(jnp.float32)[:, None] * freq[None, :]
    turn = jnp.concatenate([turn, turn], -1)
    return (jnp.cos(turn), jnp.sin(turn))


def apply_rotary(value_rows_local, cosine_table, sine_table):
    half = value_rows_local.shape[-1] // 2
    turned = jnp.concatenate([-value_rows_local[..., half:], value_rows_local[..., :half]], -1)
    return value_rows_local * cosine_table + turned * sine_table


def unrotate(grads, cosine_table, sine_table):
    half = grads.shape[-1] // 2
    scaled = grads * sine_table
    turned = jnp.concatenate([-scaled[..., half:], scaled[..., :half]], -1)
    return grads * cosine_table - turned


def inverse_rms(value_rows_local):
    return lax.rsqrt(jnp.mean(value_rows_local * value_rows_local, -1, keepdims=True) + EPS)


def norm_backward(grad, value_rows_local, inverse, gain):
    scaled = grad * gain
    return inverse * scaled - inverse * inverse * inverse * value_rows_local * jnp.mean(
        scaled * value_rows_local, -1, keepdims=True
    )


MESH = pl.DeviceIdType.MESH
SLOTS = 80
FAR_FIRST = ((1, 3), (1, 2), (0, 3), (1, 1), (0, 2), (0, 1), (1, 0), (0, 0))
BACK = FAR_FIRST
AHEAD = 2
HALVES = 2


class Place:
    def __init__(self):
        self.e = lax.axis_index(EXPERT)
        self.f = lax.axis_index(FSDP)
        self.x, self.c = self.e // 2, self.e % 2
        self.z, self.y = self.f // 2, self.f % 2

    def device(self, axis):
        if axis == "c":
            return (self.x * 2 + 1 - self.c, self.f)
        if axis == "x":
            return ((1 - self.x) * 2 + self.c, self.f)
        if axis == "y":
            return (self.e, self.z * 2 + 1 - self.y)
        if axis == UP:
            return (self.e, jnp.minimum(self.z + 1, 3) * 2 + self.y)
        return (self.e, jnp.maximum(self.z - 1, 0) * 2 + self.y)

    def ranked(self, j):
        inner = (1, 0, 2, 3)[j]
        end = (self.z == 0) | (self.z == 3)
        low = jnp.where(end, j, inner)
        return jnp.where(self.z < 2, low, 3 - low)

    def line(self):
        x, y, even = self.x, self.y, self.c == 0
        near = (jnp.where(even, 1 - x, x), jnp.where(even, y, 1 - y))
        far = (jnp.where(even, x, 1 - x), jnp.where(even, 1 - y, y))
        return near, far

    def at(self, chip, core):
        return (chip[0] * 2 + core, self.z * 2 + chip[1])


def block_number(chip, core, ar, zs):
    x, y = chip
    xs = jnp.where(core == 0, 1 - x, x) if ar else x
    ys = jnp.where(core == 0, y, 1 - y) if ar else y
    return (xs * 2 + core) * 8 + zs * 2 + ys


def greet(place):
    barrier = pltpu.get_barrier_semaphore()
    beside = [place.device("c")]
    for chip in ((1 - place.x, place.y), (place.x, 1 - place.y)):
        beside += [place.at(chip, 0), place.at(chip, 1)]
    for device in beside:
        pl.semaphore_signal(barrier, 1, device_id=device, device_id_type=MESH)

    @pl.when(place.z < 3)
    def _():
        pl.semaphore_signal(barrier, 1, device_id=place.device(UP), device_id_type=MESH)

    @pl.when(place.z > 0)
    def _():
        pl.semaphore_signal(barrier, 1, device_id=place.device(DOWN), device_id_type=MESH)

    inner = (place.z > 0) & (place.z < 3)
    pl.semaphore_wait(barrier, len(beside) + jnp.where(inner, 2, 1))


def greet_all(place, experts, shards):
    barrier = pltpu.get_barrier_semaphore()
    count = experts * shards

    def one(i, carry):
        target = lax.rem(place.e * shards + place.f + i, count)
        pl.semaphore_signal(
            barrier, 1, device_id=(target // shards, lax.rem(target, shards)), device_id_type=MESH
        )
        return carry

    lax.fori_loop(1, count, one, 0)
    pl.semaphore_wait(barrier, count - 1)


def onward(path, j, xr, yr):
    differs = {"z": j > 0, "x": xr > 0, "y": yr > 0}
    last = -1
    for i, axis in enumerate(path):
        if differs[axis]:
            last = i
    out = []
    if last >= 0 and path[last] == "z":
        out.append("z+")
    for axis in path[last + 1 :]:
        out.append("z*" if axis == "z" else axis)
    return out


def links(place, path, j, xr, yr, zs):
    out = []
    for axis in onward(path, j, xr, yr):
        if axis == "z+":
            out.append((UP, (zs < place.z) & (place.z < 3)))
            out.append((DOWN, (zs > place.z) & (place.z > 0)))
        elif axis == "z*":
            out.append((UP, place.z < 3))
            out.append((DOWN, place.z > 0))
        else:
            out.append((axis, None))
    return out


def run(condition, action):
    if condition is None:
        action()
    else:
        pl.when(condition)(action)


LINK = {"x": 0, "y": 1, UP: 2, DOWN: 3}


def remote(src, dst, send_sem, recv_sem, device):
    return pltpu.make_async_remote_copy(
        src_ref=src,
        dst_ref=dst,
        send_sem=send_sem,
        recv_sem=recv_sem,
        device_id=device,
        device_id_type=MESH,
    )


class Side:
    def __init__(self, steps, events):
        self.steps, self.events = list(steps), events
        self.total, self.seen = len(self.steps), 0

    def event(self):
        self.seen += 1
        left = self.total - self.total * min(self.seen, self.events) // self.events
        while len(self.steps) > left:
            self.steps.pop(0)()


class Extra:
    def __init__(self, operands=(), in_specs=(), outs=(), out_specs=(), scratch=(), steps=None):
        self.operands, self.in_specs = list(operands), list(in_specs)
        self.outs, self.out_specs, self.scratch = list(outs), list(out_specs), list(scratch)
        self.steps = steps if steps is not None else lambda *refs: []


def split(refs, counts):
    out = []
    for count in counts:
        out.append(refs[:count])
        refs = refs[count:]
    return out


def exchange_small(place, dims, src_of, dst, sems_out, sems_in, sem):
    experts, shards = dims
    count = experts * shards
    me = place.e * shards + place.f
    keep = pltpu.make_async_copy(src_of(me), dst.at[me], sem)
    keep.start()

    def copy(i, sending):
        other = lax.rem(me + i, count)
        source = me if sending else other
        device = (other // shards, lax.rem(other, shards))
        return remote(src_of(other), dst.at[source], sems_out.at[i], sems_in.at[source], device)

    def start(i, carry):
        copy(i, True).start()
        return carry

    def finish(i, carry):
        done = copy(i, False)
        done.wait_send()
        done.wait_recv()
        return carry

    lax.fori_loop(1, count, start, 0)

    def end():
        keep.wait()
        lax.fori_loop(1, count, finish, 0)

    return end


def dispatch_kernel(dims, has_small, extra, *refs):
    counts = (
        2 + has_small, len(extra.operands), 1 + has_small, len(extra.outs), 7 + 3 * has_small,
        len(extra.scratch),
    )
    ins, more_in, outs, more_out, scratch, more_scratch = split(refs, counts)
    tok, sel = ins[:2]
    picked = outs[0]
    held, stage, arrive, leave, pick_out, pick_in, local = scratch[:7]
    place = Place()
    width = tok.shape[1]
    near, far = place.line()
    mine = (place.x, place.y)
    if has_small:
        greet_all(place, *dims)
        end_small = exchange_small(
            place, dims, lambda i: ins[2], outs[1], scratch[7], scratch[8], scratch[9].at[0]
        )
    else:
        greet(place)
    side = Side(extra.steps(*more_in, *more_out, *more_scratch), 8)
    keep = pltpu.make_async_copy(tok, held.at[place.z], local.at[8])
    keep.start()
    pending = []
    finish = []
    targets = (place.device("c"), place.at(far, place.c), place.at(far, 1 - place.c))

    def pick(ar, zs):
        block = ar * 4 + zs
        number = block_number(mine, place.c, ar, zs)

        def tile(i, carry):
            columns = pl.ds(pl.multiple_of(i * 512, 512), 512)
            stage[block, :, columns] = jnp.dot(
                sel[block], held[block, :, columns], preferred_element_type=jnp.float32
            ).astype(jnp.bfloat16)
            return carry

        lax.fori_loop(0, width // 512, tile, 0)
        for k in (2, 1, 0):
            away = remote(
                stage.at[block, pl.ds((k + 1) * SLOTS, SLOTS)], picked.at[number],
                pick_out.at[block, k], pick_in.at[number], targets[k],
            )
            away.start()
            finish.append(away)
        stay = pltpu.make_async_copy(
            stage.at[block, pl.ds(0, SLOTS)], picked.at[number], local.at[block]
        )
        stay.start()
        finish.append(stay)

    half = tok.shape[0] // HALVES
    for ar, j in FAR_FIRST[::-1]:
        zs = place.ranked(j)
        block = ar * 4 + zs
        for h in range(HALVES):
            part = pl.ds(h * half, half)
            window = held.at[block, part]
            if ar or j:
                remote(
                    window, window, leave.at[zs, 0, h], arrive.at[block, h], place.device("c")
                ).wait_recv()
            if ar:
                continue
            source = tok.at[part] if j == 0 else window
            onward = (
                (UP, zs, 0, (zs <= place.z) & (place.z < 3)),
                (DOWN, zs, 1, (zs >= place.z) & (place.z > 0)),
                ("near", 4 + zs, 2, None),
            )
            for axis, there, k, condition in onward:
                device = place.at(near, place.c) if axis == "near" else place.device(axis)
                copy = remote(
                    source, held.at[there, part], leave.at[zs, k, h], arrive.at[there, h], device
                )
                run(condition, copy.start)
                pending.append((condition, copy))
        if not ar and j == 0:
            keep.wait()
        pick(ar, zs)
        side.event()
    for condition, copy in pending:
        run(condition, copy.wait_send)

    def arrived(i, carry):
        xs, cs, ys = i // 16, i // 8 % 2, i % 2
        inside = (cs == place.c) & jnp.where(place.c == 0, ys == place.y, xs == place.x)

        @pl.when(~inside)
        def _():
            window = picked.at[i]
            remote(window, window, pick_out.at[0, 0], pick_in.at[i], place.device("c")).wait_recv()

        return carry

    lax.fori_loop(0, 32, arrived, 0)
    for k, copy in enumerate(finish):
        if k % 4 == 3:
            copy.wait()
        else:
            copy.wait_send()
    if has_small:
        end_small()


def dispatch(experts, shards, number, tok, sel, small=None, extra=None):
    rows, width = tok.shape
    devices = experts * shards
    extra = extra or Extra()
    space = pl.BlockSpec(memory_space=pl.ANY)
    vmem = pl.BlockSpec(memory_space=pltpu.VMEM)
    dma = pltpu.SemaphoreType.DMA
    has_small = int(small is not None)
    operands, in_specs = [tok, sel], [space, vmem]
    out_shape = [jax.ShapeDtypeStruct((devices, SLOTS, width), jnp.bfloat16)]
    scratch = [
        pltpu.VMEM((8, rows, width), jnp.bfloat16),
        pltpu.VMEM((8, 4 * SLOTS, width), jnp.bfloat16),
        dma((8, HALVES)),
        dma((4, 3, HALVES)),
        dma((8, 3)),
        dma((devices,)),
        dma((9,)),
    ]
    if has_small:
        operands.append(small)
        in_specs.append(space)
        out_shape.append(jax.ShapeDtypeStruct((devices,) + small.shape, small.dtype))
        scratch += [dma((devices,)), dma((devices,)), dma((1,))]
    return pl.pallas_call(
        functools.partial(dispatch_kernel, (experts, shards), has_small, extra),
        out_shape=out_shape + extra.outs,
        in_specs=in_specs + extra.in_specs,
        out_specs=[space] * len(out_shape) + extra.out_specs,
        scratch_shapes=scratch + extra.scratch,
        compiler_params=pltpu.CompilerParams(
            collective_id=number, has_side_effects=True, vmem_limit_bytes=60 * 2**20
        ),
        name="dispatch",
    )(*operands, *extra.operands)


def combine_kernel(dims, has_small, extra, *refs):
    counts = (
        2 + has_small, len(extra.operands), 1 + has_small, len(extra.outs), 10 + 3 * has_small,
        len(extra.scratch),
    )
    ins, more_in, outs, more_out, scratch, more_scratch = split(refs, counts)
    weighted, sel = ins[:2]
    total = outs[0]
    rows4, acc, beside, chain, rows_in, rows_out, beside_in, beside_out, chain_in, chain_out = scratch[:10]
    place = Place()
    width = total.shape[1]
    near, far = place.line()
    mine = (place.x, place.y)
    if has_small:
        greet_all(place, *dims)
        end_small = exchange_small(
            place, dims, lambda i: ins[2].at[i], outs[1], scratch[10], scratch[11], scratch[12].at[0]
        )
    else:
        greet(place)
    side = Side(extra.steps(*more_in, *more_out, *more_scratch), 8)
    other = 1 - place.c
    homes = ((mine, place.c), (mine, other), (far, place.c), (near, other))

    def row_copy(ar, zs, k):
        chip, core = homes[k]
        source = weighted.at[block_number(chip, core, ar, zs)]
        block = ar * 4 + zs
        window = rows4.at[block, pl.ds(k * SLOTS, SLOTS)]
        if k == 0:
            return pltpu.make_async_copy(source, window, rows_in.at[block, 0])
        return remote(
            source, window, rows_out.at[block, k - 1], rows_in.at[block, k], place.at(chip, core)
        )

    def send_rows(i):
        ar, j = BACK[i]
        for k in (2, 3, 1, 0):
            row_copy(ar, place.ranked(j), k).start()

    for i in range(AHEAD):
        send_rows(i)
    pending = []
    half = total.shape[0] // HALVES
    for i, (ar, j) in enumerate(BACK):
        zs = place.ranked(j)
        block = ar * 4 + zs
        for k in range(4):
            copy = row_copy(ar, zs, k)
            if k == 0:
                copy.wait()
            else:
                copy.wait_recv()
                copy.wait_send()
        if i + AHEAD < 8:
            send_rows(i + AHEAD)
        last = not ar and j == 0
        above = (zs <= place.z) & (place.z < 3)
        below = (zs >= place.z) & (place.z > 0)
        below_slot = jnp.where(zs == place.z, 4, zs)
        for h in range(HALVES):
            part = pl.ds(h * half, half)
            if not ar:
                window = beside.at[zs, part]
                remote(
                    window, window, beside_out.at[zs, h], beside_in.at[zs, h], place.device("c")
                ).wait_recv()
                for condition, slot in ((above, zs), (below, below_slot)):
                    window = chain.at[slot, part]
                    got = remote(
                        window, window, chain_out.at[0, h], chain_in.at[slot, h], place.device("c")
                    )
                    run(condition, got.wait_recv)

            def tile(t, carry):
                columns = pl.ds(pl.multiple_of(t * 512, 512), 512)
                dense = jnp.dot(
                    sel[block, part], rows4[block, :, columns], preferred_element_type=jnp.float32
                )
                if not ar:
                    dense = dense + beside[zs, part, columns].astype(jnp.float32)
                if last:
                    total[part, columns] = dense
                else:
                    acc[block, part, columns] = dense.astype(jnp.bfloat16)
                return carry

            lax.fori_loop(0, width // 512, tile, 0)
            if not ar:

                def add(slot):
                    def step(t, carry):
                        here = pl.ds(pl.multiple_of(h * half + t * 16, 16), 16)
                        more = chain[slot, here].astype(jnp.float32)
                        if last:
                            total[here] += more
                        else:
                            acc[block, here] = (acc[block, here].astype(jnp.float32) + more).astype(
                                jnp.bfloat16
                            )
                        return carry

                    lax.fori_loop(0, half // 16, step, 0)

                run(above, functools.partial(add, zs))
                run(below, functools.partial(add, below_slot))
            if ar:
                copy = remote(
                    acc.at[block, part], beside.at[zs, part], beside_out.at[zs, h],
                    beside_in.at[zs, h], place.at(near, place.c),
                )
                copy.start()
                pending.append((None, copy))
            elif not last:
                there = jnp.where(zs == place.z + 1, 4, zs)
                for condition, axis, slot in (
                    (zs < place.z, DOWN, zs),
                    (zs > place.z, UP, there),
                ):
                    copy = remote(
                        acc.at[block, part], chain.at[slot, part], chain_out.at[zs, h],
                        chain_in.at[slot, h], place.device(axis),
                    )
                    run(condition, copy.start)
                    pending.append((condition, copy))
        side.event()
    for condition, copy in pending:
        run(condition, copy.wait_send)
    if has_small:
        end_small()


def combine(experts, shards, number, weighted, sel, small=None, extra=None):
    rows = sel.shape[1]
    width = weighted.shape[-1]
    devices = experts * shards
    extra = extra or Extra()
    space = pl.BlockSpec(memory_space=pl.ANY)
    vmem = pl.BlockSpec(memory_space=pltpu.VMEM)
    dma = pltpu.SemaphoreType.DMA
    low = jnp.bfloat16
    has_small = int(small is not None)
    operands, in_specs = [weighted, sel], [space, vmem]
    out_shape, out_specs = [jax.ShapeDtypeStruct((rows, width), jnp.float32)], [vmem]
    scratch = [
        pltpu.VMEM((8, 4 * SLOTS, width), low),
        pltpu.VMEM((8, rows, width), low),
        pltpu.VMEM((4, rows, width), low),
        pltpu.VMEM((5, rows, width), low),
        dma((8, 4)),
        dma((8, 3)),
        dma((4, HALVES)),
        dma((4, HALVES)),
        dma((5, HALVES)),
        dma((4, HALVES)),
    ]
    if has_small:
        operands.append(small)
        in_specs.append(space)
        out_shape.append(jax.ShapeDtypeStruct(small.shape, small.dtype))
        out_specs.append(space)
        scratch += [dma((devices,)), dma((devices,)), dma((1,))]
    return pl.pallas_call(
        functools.partial(combine_kernel, (experts, shards), has_small, extra),
        out_shape=out_shape + extra.outs,
        in_specs=in_specs + extra.in_specs,
        out_specs=out_specs + extra.out_specs,
        scratch_shapes=scratch + extra.scratch,
        compiler_params=pltpu.CompilerParams(
            collective_id=number, has_side_effects=True, vmem_limit_bytes=60 * 2**20
        ),
        name="combine",
    )(*operands, *extra.operands)


FLAT = ("zy", "yz")
CHUNKS = 4


def flat_parts(rows):
    return (0, rows * 3 // 4), (rows * 3 // 4, rows - rows * 3 // 4)


def send_around(place, experts, shards, src_of, dst, out_sems, in_sems, across):
    count = experts * shards if across else shards
    me = place.e * shards + place.f if across else place.f

    def copy(i, sending):
        other = lax.rem(me + i, count)
        if across:
            device = (other // shards, lax.rem(other, shards))
        else:
            device = (place.e, other)
        source = me if sending else other
        return remote(src_of(other), dst.at[source], out_sems.at[i], in_sems.at[source], device)

    def start(i, carry):
        copy(i, True).start()
        return carry

    def finish(i, carry):
        done = copy(i, False)
        done.wait_send()
        done.wait_recv()
        return carry

    lax.fori_loop(1, count, start, 0)
    return lambda: lax.fori_loop(1, count, finish, 0)


def gather_kernel(
    dims, flat, tall, tok, pack, ids, flat_all, tall_all, tok_all, pack_all, ids_all,
    flat_in, flat_out, tall_in, tall_out, tok_in, tok_out, pack_in, pack_out, ids_in, ids_out, local,
):
    experts, shards = dims
    place = Place()
    greet_all(place, experts, shards)
    me = place.e * shards + place.f
    starts, sizes = flat_parts(flat.shape[0])
    chunk = tall.shape[0] // CHUNKS
    pending = []
    keeps = [
        pltpu.make_async_copy(flat, flat_all.at[place.f], local.at[0]),
        pltpu.make_async_copy(tok, tok_all.at[place.e], local.at[1]),
        pltpu.make_async_copy(pack, pack_all.at[place.f], local.at[2]),
        pltpu.make_async_copy(ids, ids_all.at[me], local.at[3]),
    ]

    def go(condition, copy):
        run(condition, copy.start)
        pending.append((condition, copy))

    def both(a, b):
        return b if a is None else (a if b is None else a & b)

    def flat_item(p, j, yr):
        zs = place.ranked(j)
        source = zs * 2 + (1 - place.y if yr else place.y)
        first = j == 0 and yr == 0
        window = flat_all.at[source, pl.ds(starts[p], sizes[p])]
        src = flat.at[pl.ds(starts[p], sizes[p])] if first else window
        if not first:
            remote(
                window, window, flat_out.at[p, source, 0], flat_in.at[p, source], place.device("c")
            ).wait_recv()
        for axis, condition in links(place, FLAT[p], j, 0, yr, zs):
            go(
                condition,
                remote(
                    src,
                    window,
                    flat_out.at[p, source, LINK[axis]],
                    flat_in.at[p, source],
                    place.device(axis),
                ),
            )

    owner = place.z == place.e

    def tall_item(k):
        piece = pl.ds(k * chunk, chunk)
        window = tall_all.at[place.y, piece]

        @pl.when(~owner)
        def _():
            remote(window, window, tall_out.at[k, 0], tall_in.at[0, k], place.device("c")).wait_recv()

        for mine in (True, False):
            src = tall.at[piece] if mine else window
            role = owner if mine else ~owner
            for axis, condition in (
                ("y", None),
                (UP, (place.z >= place.e) & (place.z < 3)),
                (DOWN, (place.z <= place.e) & (place.z > 0)),
            ):
                go(
                    both(role, condition),
                    remote(
                        src,
                        window,
                        tall_out.at[k, LINK[axis]],
                        tall_in.at[1 if axis == "y" else 0, k],
                        place.device(axis),
                    ),
                )

    flat_item(0, 0, 0)
    flat_item(1, 0, 0)
    go(None, remote(tok, tok_all.at[place.e], tok_out.at[0], tok_in.at[place.e], place.device("x")))
    go(None, remote(tok, tok_all.at[place.e], tok_out.at[1], tok_in.at[place.e], place.device("c")))
    end_pack = send_around(
        place, experts, shards, lambda i: pack, pack_all, pack_out, pack_in, False
    )
    end_ids = send_around(place, experts, shards, lambda i: ids, ids_all, ids_out, ids_in, True)
    for keep in keeps:
        keep.start()
    keep_tall = pltpu.make_async_copy(tall, tall_all.at[place.y], local.at[4])
    run(owner, keep_tall.start)
    across = (1 - place.x) * 2 + place.c
    flat_item(1, 0, 1)
    tall_item(0)
    flat_item(0, 1, 0)
    tall_item(1)
    flat_item(1, 1, 0)
    flat_item(1, 1, 1)
    tall_item(2)
    flat_item(0, 2, 0)
    tall_item(3)
    window = tok_all.at[across]
    relay = remote(window, window, tok_out.at[2], tok_in.at[across], place.device("c"))
    relay.wait_recv()
    go(None, relay)
    flat_item(1, 2, 0)
    flat_item(1, 2, 1)
    flat_item(0, 3, 0)
    flat_item(1, 3, 0)
    flat_item(1, 3, 1)
    for j in range(4):
        flat_item(0, j, 1)
    for k in range(CHUNKS):
        window = tall_all.at[1 - place.y, pl.ds(k * chunk, chunk)]
        remote(window, window, tall_out.at[k, 0], tall_in.at[1, k], place.device("c")).wait_recv()
    for source in (place.x * 2 + 1 - place.c, (1 - place.x) * 2 + 1 - place.c):
        window = tok_all.at[source]
        remote(window, window, tok_out.at[2], tok_in.at[source], place.device("c")).wait_recv()
    for condition, copy in pending:
        run(condition, copy.wait_send)
    end_pack()
    end_ids()
    for keep in keeps:
        keep.wait()
    run(owner, keep_tall.wait)


def gather(experts, shards, number, flat, tall, tok, pack, ids):
    space = pl.BlockSpec(memory_space=pl.ANY)
    dma = pltpu.SemaphoreType.DMA
    devices = experts * shards

    def shape(lead, a):
        return jax.ShapeDtypeStruct((lead,) + a.shape, a.dtype)

    return pl.pallas_call(
        functools.partial(gather_kernel, (experts, shards)),
        out_shape=[
            shape(shards, flat),
            shape(2, tall),
            shape(experts, tok),
            shape(shards, pack),
            shape(devices, ids),
        ],
        in_specs=[space] * 5,
        out_specs=[space] * 5,
        scratch_shapes=[
            dma((2, shards)),
            dma((2, shards, 4)),
            dma((2, CHUNKS)),
            dma((CHUNKS, 4)),
            dma((experts,)),
            dma((3,)),
            dma((shards,)),
            dma((shards,)),
            dma((devices,)),
            dma((devices,)),
            dma((5,)),
        ],
        compiler_params=pltpu.CompilerParams(
            collective_id=number, has_side_effects=True, vmem_limit_bytes=16 * 2**20
        ),
        name="gather",
    )(flat, tall, tok, pack, ids)


def add_rows(acc, first, window, rows, step=16):
    def add(i, carry):
        here = pl.ds(pl.multiple_of(i * step, step), step)
        at = pl.ds(pl.multiple_of(first + i * step, step), step)
        acc[at] = (acc[at].astype(jnp.float32) + window[here].astype(jnp.float32)).astype(acc.dtype)
        return carry

    lax.fori_loop(0, rows // step, add, 0)


def reduce_kernel(
    dims, flat, tall, pack, out_q, out_k, out_v, tall_out, pack_all,
    acc, tacc, yslot, zslot, yone, zall, ty, tz,
    load, yin, zin, yone_in, zall_in, ty_in, tz_in, flat_send, tall_send, spread_in, spread_out,
    tall_in, pack_in, pack_out, keep_tall, local,
):
    experts, shards = dims
    place = Place()
    greet_all(place, experts, shards)
    me = place.e * shards + place.f
    tall_keeps = []
    owner = place.z == place.e
    home = place.x == place.z // 2
    same = place.c == place.z % 2
    starts, sizes = flat_parts(flat.shape[1])
    height = tall.shape[1]
    chunk = height // CHUNKS
    pending = []

    def go(condition, copy):
        run(condition, copy.start)
        pending.append((condition, copy))

    def both(a, b):
        return a if b is None else a & b

    load_tall = pltpu.make_async_copy(tall, tacc, load.at[0])
    load_flat = pltpu.make_async_copy(flat, acc, load.at[1])
    across_y = []
    order = (3, 2, 1, 0)
    for j in order:
        k = 3 - j
        target = place.ranked(j) * 2 + 1 - place.y
        across_y.append(
            remote(
                flat.at[target, pl.ds(starts[0], sizes[0])],
                yslot.at[place.ranked(j)],
                flat_send.at[0, target],
                yin.at[place.ranked(j)],
                place.device("y"),
            )
        )
        piece = pl.ds(k * chunk, chunk)
        across_y.append(
            remote(
                tall.at[1 - place.y, piece], ty.at[piece], tall_send.at[0, k], ty_in.at[k],
                place.device("y"),
            )
        )
    started = [0]

    def feed(count):
        while started[0] < min(count + 2, len(across_y)):
            if started[0] >= 2:
                across_y[started[0] - 2].wait_send()
            across_y[started[0]].start()
            started[0] += 1

    feed(0)
    load_tall.start()
    load_flat.start()
    end_pack = send_around(
        place, experts, shards, lambda i: pack.at[lax.rem(i, shards)], pack_all, pack_out, pack_in, True
    )
    keep_pack = pltpu.make_async_copy(pack.at[place.f], pack_all.at[me], local.at[0])
    keep_pack.start()
    load_tall.wait()
    load_flat.wait()

    def into(slots, sems, zd, side):
        index = jnp.where(zd == place.z, 4, zd) if side == BELOW else zd
        return slots.at[index], sems.at[index]

    def out_to(slots, sems, zd, side):
        there = place.z - 1 if side == ABOVE else place.z + 1
        index = jnp.where(zd == there, 4, zd) if side == BELOW else zd
        return slots.at[index], sems.at[index]

    def line(j, p, first, slots, sems, send_sem, target):
        zd = place.ranked(j)
        rows = sizes[p]
        for side, condition in (
            (ABOVE, (zd <= place.z) & (place.z < 3)),
            (BELOW, (zd >= place.z) & (place.z > 0)),
        ):
            window, sem = into(slots, sems, zd, side)

            def take(window=window, sem=sem):
                remote(window, window, send_sem, sem, place.device("c")).wait_recv()
                add_rows(acc.at[target], first, window, rows)

            if j == 0:
                condition = place.z < 3 if side == ABOVE else place.z > 0
            run(condition, take)
        if j == 0:
            return
        for side, axis, condition in ((ABOVE, DOWN, zd < place.z), (BELOW, UP, zd > place.z)):
            window, sem = out_to(slots, sems, zd, side)
            go(
                condition,
                remote(acc.at[target, pl.ds(first, rows)], window, send_sem, sem, place.device(axis)),
            )

    def tall_line(k):
        piece = pl.ds(k * chunk, chunk)
        remote(ty.at[piece], ty.at[piece], tall_send.at[0, k], ty_in.at[k], place.device("c")).wait_recv()
        add_rows(tacc.at[place.y], k * chunk, ty.at[piece], chunk)
        for side, index, condition in (
            (ABOVE, 0, (place.z >= place.e) & (place.z < 3)),
            (BELOW, 1, (place.z <= place.e) & (place.z > 0)),
        ):
            window = tz.at[index, piece]

            def take(window=window, index=index):
                remote(window, window, tall_send.at[1, k], tz_in.at[index, k], place.device("c")).wait_recv()
                add_rows(tacc.at[place.y], k * chunk, window, chunk)

            run(condition, take)
        for index, axis, condition in ((0, DOWN, place.z > place.e), (1, UP, place.z < place.e)):
            go(
                condition,
                remote(
                    tacc.at[place.y, piece], tz.at[index, piece], tall_send.at[1, k], tz_in.at[index, k],
                    place.device(axis),
                ),
            )
        piece_out = tall_out.at[piece]
        keep = pltpu.make_async_copy(tacc.at[place.y, piece], piece_out, keep_tall.at[k])
        run(owner, keep.start)
        tall_keeps.append(keep)
        for row, axis in ((2, "x"), (3, "c")):
            go(
                owner,
                remote(
                    tacc.at[place.y, piece], piece_out, tall_send.at[row, k], tall_in.at[k],
                    place.device(axis),
                ),
            )

    def flat_first(j):
        zd = place.ranked(j)
        target = zd * 2 + place.y
        window = yslot.at[zd]
        remote(window, window, flat_send.at[0, target], yin.at[zd], place.device("c")).wait_recv()
        add_rows(acc.at[target], starts[0], window, sizes[0])
        line(j, 0, starts[0], zslot, zin, flat_send.at[0, target], target)

    def flat_second(j, yr):
        zd = place.ranked(j)
        target = zd * 2 + (1 - place.y if yr else place.y)
        line(j, 1, starts[1], zall.at[yr], zall_in.at[yr], flat_send.at[1, target], target)

    for j in order[:-1]:
        flat_second(j, 1)
        flat_second(j, 0)
        feed(2 * (3 - j))
        flat_first(j)
        feed(2 * (3 - j) + 1)
        tall_line(3 - j)
    feed(6)
    flat_second(0, 1)
    other = place.z * 2 + 1 - place.y
    go(
        None,
        remote(
            acc.at[other, pl.ds(starts[1], sizes[1])], yone, flat_send.at[1, other], yone_in.at[0],
            place.device("y"),
        ),
    )
    flat_second(0, 0)
    flat_first(0)
    remote(yone, yone, flat_send.at[1, other], yone_in.at[0], place.device("c")).wait_recv()
    add_rows(acc.at[place.f], starts[1], yone, sizes[1])
    feed(7)
    cuts = []
    first = 0
    for out in (out_q, out_k, out_v):
        wide = out.shape[1] // experts
        cuts.append((out, first, wide))
        first += wide

    def window_of(i, source):
        out, _, wide = cuts[i]
        return out.at[:, pl.ds(pl.multiple_of(source * wide, 128), wide)]

    flat_keeps = []
    for i, (out, first, wide) in enumerate(cuts):
        done = acc.at[place.f, :, pl.ds(first, wide)]
        keep = pltpu.make_async_copy(done, window_of(i, place.e), local.at[1 + i])
        keep.start()
        flat_keeps.append(keep)
        for row, axis in enumerate(("x", "c")):
            go(
                None,
                remote(
                    done, window_of(i, place.e), spread_out.at[row, i], spread_in.at[place.e, i],
                    place.device(axis),
                ),
            )
    tall_line(CHUNKS - 1)
    across = (1 - place.x) * 2 + place.c
    for i in range(3):
        window = window_of(i, across)
        relay = remote(window, window, spread_out.at[2, i], spread_in.at[across, i], place.device("c"))
        relay.wait_recv()
        go(None, relay)
    for k in range(CHUNKS):
        window = tall_out.at[pl.ds(k * chunk, chunk)]
        tall_relay = remote(window, window, tall_send.at[4, k], tall_in.at[k], place.device("c"))
        run(~owner, tall_relay.wait_recv)
        go(~home & same, tall_relay)
    for source in (place.x * 2 + 1 - place.c, (1 - place.x) * 2 + 1 - place.c):
        for i in range(3):
            window = window_of(i, source)
            remote(
                window, window, spread_out.at[2, i], spread_in.at[source, i], place.device("c")
            ).wait_recv()
    for copy in across_y[-2:]:
        copy.wait_send()
    for condition, copy in pending:
        run(condition, copy.wait_send)
    end_pack()
    keep_pack.wait()
    for keep in flat_keeps:
        keep.wait()
    for keep in tall_keeps:
        run(owner, keep.wait)


def reduce(experts, shards, number, flat, tall, pack):
    space = pl.BlockSpec(memory_space=pl.ANY)
    dma = pltpu.SemaphoreType.DMA
    devices = experts * shards
    _, sizes = flat_parts(flat.shape[1])
    width, wide = flat.shape[2], tall.shape[2]
    low = jnp.bfloat16
    return pl.pallas_call(
        functools.partial(reduce_kernel, (experts, shards)),
        out_shape=[
            jax.ShapeDtypeStruct((flat.shape[1], experts * (width - 2 * HEAD_SIZE)), low),
            jax.ShapeDtypeStruct((flat.shape[1], experts * HEAD_SIZE), low),
            jax.ShapeDtypeStruct((flat.shape[1], experts * HEAD_SIZE), low),
            jax.ShapeDtypeStruct(tall.shape[1:], low),
            jax.ShapeDtypeStruct((devices,) + pack.shape[1:], pack.dtype),
        ],
        in_specs=[space] * 3,
        out_specs=[space] * 5,
        scratch_shapes=[
            pltpu.VMEM(flat.shape, low),
            pltpu.VMEM(tall.shape, low),
            pltpu.VMEM((4, sizes[0], width), low),
            pltpu.VMEM((5, sizes[0], width), low),
            pltpu.VMEM((sizes[1], width), low),
            pltpu.VMEM((2, 5, sizes[1], width), low),
            pltpu.VMEM(tall.shape[1:], low),
            pltpu.VMEM((2,) + tall.shape[1:], low),
            dma((2,)),
            dma((4,)),
            dma((5,)),
            dma((1,)),
            dma((2, 5)),
            dma((CHUNKS,)),
            dma((2, CHUNKS)),
            dma((2, shards)),
            dma((5, CHUNKS)),
            dma((experts, 3)),
            dma((3, 3)),
            dma((CHUNKS,)),
            dma((devices,)),
            dma((devices,)),
            dma((CHUNKS,)),
            dma((4,)),
        ],
        compiler_params=pltpu.CompilerParams(
            collective_id=number, has_side_effects=True, vmem_limit_bytes=48 * 2**20
        ),
        name="reduce",
    )(flat, tall, pack)


def group_gather_kernel(tok, out, x_out, x_in, c_out, c_in, relay_out, relay_in, local):
    place = Place()
    greet(place)
    across = (1 - place.x) * 2 + place.c
    chunk = tok.shape[0] // CHUNKS
    keep = pltpu.make_async_copy(tok, out.at[place.e], local.at[0])
    near = remote(tok, out.at[place.e], c_out.at[0], c_in.at[0], place.device("c"))
    copies = []
    for k in range(CHUNKS):
        piece = pl.ds(k * chunk, chunk)
        copies.append(
            remote(tok.at[piece], out.at[place.e, piece], x_out.at[k], x_in.at[k], place.device("x"))
        )
        copies[-1].start()
    near.start()
    keep.start()
    for k in range(CHUNKS):
        window = out.at[across, pl.ds(k * chunk, chunk)]
        remote(window, window, x_out.at[k], x_in.at[k], place.device("c")).wait_recv()
        relay = remote(window, window, relay_out.at[k], relay_in.at[k], place.device("c"))
        relay.start()
        copies.append(relay)
    for k in range(CHUNKS):
        window = out.at[(1 - place.x) * 2 + 1 - place.c, pl.ds(k * chunk, chunk)]
        remote(window, window, relay_out.at[k], relay_in.at[k], place.device("c")).wait_recv()
    near.wait()
    keep.wait()
    for copy in copies:
        copy.wait_send()


def group_gather(number, tok):
    space = pl.BlockSpec(memory_space=pl.ANY)
    dma = pltpu.SemaphoreType.DMA
    return pl.pallas_call(
        group_gather_kernel,
        out_shape=jax.ShapeDtypeStruct((4,) + tok.shape, tok.dtype),
        in_specs=[space],
        out_specs=space,
        scratch_shapes=[
            dma((CHUNKS,)), dma((CHUNKS,)), dma((1,)), dma((1,)), dma((CHUNKS,)), dma((CHUNKS,)), dma((1,)),
        ],
        compiler_params=pltpu.CompilerParams(
            collective_id=number, has_side_effects=True, vmem_limit_bytes=16 * 2**20
        ),
        name="group_gather",
    )(tok)


def group_scatter_kernel(
    partial, total, acc, near, cross, load_in, near_out, near_in, x_out, x_in
):
    place = Place()
    greet(place)
    rows = partial.shape[1]
    chunk = rows // CHUNKS
    sends = []
    loads = []
    for half in (1 - place.x, place.x):
        for k in range(CHUNKS):
            piece = pl.ds(k * chunk, chunk)
            copy = remote(
                partial.at[half * 2 + 1 - place.c, piece], near.at[half, piece], near_out.at[half, k],
                near_in.at[half, k], place.device("c"),
            )
            copy.start()
            sends.append(copy)
            load = pltpu.make_async_copy(
                partial.at[half * 2 + place.c, piece], acc.at[half, piece], load_in.at[half, k]
            )
            load.start()
            loads.append(load)
    for index, half in enumerate((1 - place.x, place.x)):
        for k in range(CHUNKS):
            piece = pl.ds(k * chunk, chunk)
            window = near.at[half, piece]
            loads[index * CHUNKS + k].wait()
            remote(window, window, near_out.at[half, k], near_in.at[half, k], place.device("c")).wait_recv()
            add_rows(acc.at[half], k * chunk, window, chunk)
            if index == 0:
                copy = remote(
                    acc.at[half, piece], cross.at[piece], x_out.at[k], x_in.at[k], place.device("x")
                )
                copy.start()
                sends.append(copy)
    for k in range(CHUNKS):
        window = cross.at[pl.ds(k * chunk, chunk)]
        remote(window, window, x_out.at[k], x_in.at[k], place.device("c")).wait_recv()

        def add(i, carry):
            here = pl.ds(pl.multiple_of(k * chunk + i * 16, 16), 16)
            total[here] = acc[place.x, here].astype(jnp.float32) + cross[here].astype(jnp.float32)
            return carry

        lax.fori_loop(0, chunk // 16, add, 0)
    for copy in sends:
        copy.wait_send()


def group_scatter(number, partial):
    dma = pltpu.SemaphoreType.DMA
    rows, width = partial.shape[1:]
    low = jnp.bfloat16
    return pl.pallas_call(
        group_scatter_kernel,
        out_shape=jax.ShapeDtypeStruct((rows, width), jnp.float32),
        in_specs=[pl.BlockSpec(memory_space=pl.ANY)],
        out_specs=pl.BlockSpec(memory_space=pltpu.VMEM),
        scratch_shapes=[
            pltpu.VMEM((2, rows, width), low),
            pltpu.VMEM((2, rows, width), low),
            pltpu.VMEM((rows, width), low),
            dma((2, CHUNKS)),
            dma((2, CHUNKS)),
            dma((2, CHUNKS)),
            dma((CHUNKS,)),
            dma((CHUNKS,)),
        ],
        compiler_params=pltpu.CompilerParams(
            collective_id=number, has_side_effects=True, vmem_limit_bytes=16 * 2**20
        ),
        name="group_scatter",
    )(partial)


BLOCK = 256


def dot_last(a, b):
    return lax.dot_general(a, b, (((1,), (1,)), ((), ())), preferred_element_type=jnp.float32)


def dot(a, b):
    return jnp.dot(a, b, preferred_element_type=jnp.float32)


def turn(rows):
    lane = lax.broadcasted_iota(jnp.int32, rows.shape, 1)
    half = HEAD_SIZE // 2
    return pltpu.roll(rows, half, 1) * jnp.where(lane < half, -1.0, 1.0)


def mask_block(r, count, ids_column, ids_row, bias):
    queries = pl.ds(r * BLOCK, BLOCK)

    def part(i, carry):
        keys = pl.ds(pl.multiple_of(i * BLOCK, BLOCK), BLOCK)
        key_at = lax.broadcasted_iota(jnp.int32, (BLOCK, BLOCK), 0) + i * BLOCK
        query_at = lax.broadcasted_iota(jnp.int32, (BLOCK, BLOCK), 1) + r * BLOCK
        allowed = (ids_column[keys] == ids_row[:, queries]) & (key_at <= query_at)
        bias[keys] = jnp.where(allowed, 0.0, -1e30)
        return carry

    lax.fori_loop(0, count // BLOCK, part, 0)


def project_steps(
    tok, w_qkv, gain_one, gain_q, gain_k, cosine, sine, normed, raw, query_rot, key_rot, value
):
    heads = query_rot.shape[1] // HEAD_SIZE
    low = jnp.bfloat16

    def rotated(v, rows, gain):
        u = v * inverse_rms(v) * gain
        return (u * cosine[rows] + turn(u) * sine[rows]).astype(low)

    def norm(r):
        def part(i, carry):
            here = pl.ds(pl.multiple_of(r * BLOCK + i * 16, 16), 16)
            x = tok[here].astype(jnp.float32)
            normed[here] = (x * inverse_rms(x) * gain_one[...]).astype(low)
            return carry

        lax.fori_loop(0, BLOCK // 16, part, 0, unroll=2)

    def multiply(r):
        rows = pl.ds(r * BLOCK, BLOCK)

        def pair(i, carry):
            column = pl.ds(pl.multiple_of(i * 2 * HEAD_SIZE, 2 * HEAD_SIZE), 2 * HEAD_SIZE)
            both = dot(normed[rows], w_qkv[:, column])
            raw[rows, column] = both
            for k in range(2):
                at = pl.ds(pl.multiple_of((2 * i + k) * HEAD_SIZE, HEAD_SIZE), HEAD_SIZE)
                one = both[:, k * HEAD_SIZE : (k + 1) * HEAD_SIZE]
                query_rot[rows, at] = rotated(one, rows, gain_q[...])
            return carry

        lax.fori_loop(0, heads // 2, pair, 0)
        last = pl.ds(heads * HEAD_SIZE, 2 * HEAD_SIZE)
        both = dot(normed[rows], w_qkv[:, last])
        raw[rows, last] = both
        key_rot[rows] = rotated(both[:, :HEAD_SIZE], rows, gain_k[...])
        value[rows] = both[:, HEAD_SIZE:].astype(low)

    steps = []
    for r in range(tok.shape[0] // BLOCK):
        steps.append(functools.partial(norm, r))
        steps.append(functools.partial(multiply, r))
    return steps


def attend_steps(query_rot, key_rot, value, ids_column, ids_row, mixed, bias, value_t):
    length = key_rot.shape[0]
    heads = query_rot.shape[1] // HEAD_SIZE
    scale = HEAD_SIZE ** (-0.5)

    def prepare(r):
        if r == 0:
            value_t[...] = value[...].T
        mask_block(r, (r + 1) * BLOCK, ids_column, ids_row, bias)

    def heads_of(r, first, some):
        rows = pl.ds(r * BLOCK, BLOCK)
        count = (r + 1) * BLOCK

        def head(h, carry):
            column = pl.ds(pl.multiple_of(h * HEAD_SIZE, HEAD_SIZE), HEAD_SIZE)
            scores = dot_last(key_rot[:count], query_rot[rows, column]) * scale + bias[:count]
            shifted = jnp.exp(scores - jnp.max(scores, 0, keepdims=True))
            weights = shifted * (1.0 / jnp.sum(shifted, 0, keepdims=True))
            out = dot(value_t[:, :count], weights.astype(jnp.bfloat16))
            mixed[rows, column] = out.T.astype(jnp.bfloat16)
            return carry

        lax.fori_loop(first, first + some, head, 0, unroll=2)

    steps = []
    for r in range(length // BLOCK):
        steps.append(functools.partial(prepare, r))
        some = heads if r == 0 else heads // 2
        for first in range(0, heads, some):
            steps.append(functools.partial(heads_of, r, first, some))
    return steps


def load(pairs, sems):
    copies = [pltpu.make_async_copy(a, b, sems.at[i]) for i, (a, b) in enumerate(pairs)]
    for copy in copies:
        copy.start()
    return copies


def attention(tokens, w_qkv, gain_one, gain_q, gain_k, cosine, sine, ids_column, ids_row, heads):
    length, width = tokens.shape
    wide = w_qkv.shape[1]
    span = heads * HEAD_SIZE
    low, f32 = jnp.bfloat16, jnp.float32
    space, vmem = pl.BlockSpec(memory_space=pl.ANY), pl.BlockSpec(memory_space=pltpu.VMEM)
    shapes = [
        ((length, width), low),
        ((length, wide), f32),
        ((length, span), low),
        ((length, HEAD_SIZE), low),
        ((length, HEAD_SIZE), low),
        ((length, span), low),
    ]

    def steps(*refs):
        ins, outs, scratch = split(refs, (9, 6, 12))
        tok, weight, in_sems, out_sems, bias, value_t = scratch[:6]
        results = scratch[6:]
        copies = load([(ins[0], tok), (ins[1], weight)], in_sems)

        def begin():
            for copy in copies:
                copy.wait()

        saved = []

        def save(picks):
            for i in picks:
                copy = pltpu.make_async_copy(results[i], outs[i], out_sems.at[i])
                copy.start()
                saved.append(copy)

        def end():
            save((5,))
            for copy in saved:
                copy.wait()

        return (
            [begin]
            + project_steps(tok, weight, *ins[2:7], *results[:5])
            + [functools.partial(save, range(5))]
            + attend_steps(*results[2:5], *ins[7:9], results[5], bias, value_t)
            + [end]
        )

    return Extra(
        (tokens, w_qkv, gain_one, gain_q, gain_k, cosine, sine, ids_column, ids_row),
        [space, space] + [vmem] * 7,
        [jax.ShapeDtypeStruct(*shape) for shape in shapes],
        [space] * 6,
        [
            pltpu.VMEM(tokens.shape, low),
            pltpu.VMEM(w_qkv.shape, low),
            pltpu.SemaphoreType.DMA((2,)),
            pltpu.SemaphoreType.DMA((6,)),
            pltpu.VMEM((length, BLOCK), f32),
            pltpu.VMEM((HEAD_SIZE, length), low),
        ]
        + [pltpu.VMEM(*shape) for shape in shapes],
        steps,
    )


def attend_back_steps(
    query_rot, key_rot, value, raw, grad_mixed, ids_column, ids_row, gain_q, gain_k, cosine, sine,
    grad_raw, grad_gains, bias, key_t, grad_key, grad_value, sums,
):
    length = key_rot.shape[0]
    heads = query_rot.shape[1] // HEAD_SIZE
    scale = HEAD_SIZE ** (-0.5)
    low = jnp.bfloat16

    def back(grad, rows, column, gain, index):
        unit = grad * cosine[rows] - turn(grad * sine[rows])
        v = raw[rows, column]
        inverse = inverse_rms(v)
        sums[index] += jnp.sum((unit * v * inverse).reshape(-1, 8, HEAD_SIZE), 0)
        grad_raw[rows, column] = norm_backward(unit, v, inverse, gain).astype(low)

    def prepare(r):
        if r == 0:
            key_t[...] = key_rot[...].T
            grad_key[...] = jnp.zeros_like(grad_key)
            grad_value[...] = jnp.zeros_like(grad_value)
            sums[...] = jnp.zeros_like(sums)
        mask_block(r, (r + 1) * BLOCK, ids_column, ids_row, bias)

    def heads_of(r, first, some):
        rows = pl.ds(r * BLOCK, BLOCK)
        count = (r + 1) * BLOCK

        def head(h, carry):
            column = pl.ds(pl.multiple_of(h * HEAD_SIZE, HEAD_SIZE), HEAD_SIZE)
            query = query_rot[rows, column]
            grad_out = grad_mixed[rows, column]
            scores = dot_last(key_rot[:count], query) * scale + bias[:count]
            shifted = jnp.exp(scores - jnp.max(scores, 0, keepdims=True))
            weights = shifted * (1.0 / jnp.sum(shifted, 0, keepdims=True))
            grad_value[:count] += dot(weights.astype(low), grad_out)
            grad_weights = dot_last(value[:count], grad_out)
            spread = jnp.sum(weights * grad_weights, 0, keepdims=True)
            grad_scores = (weights * (grad_weights - spread)).astype(low)
            grad_key[:count] += dot(grad_scores, query)
            grad_query = dot(key_t[:, :count], grad_scores).T * scale
            back(grad_query, rows, column, gain_q[...], 0)
            return carry

        lax.fori_loop(first, first + some, head, 0, unroll=2)

    def last():
        column = pl.ds(heads * HEAD_SIZE, HEAD_SIZE)
        for r in range(length // BLOCK):
            rows = pl.ds(r * BLOCK, BLOCK)
            back(grad_key[rows] * scale, rows, column, gain_k[...], 1)
            grad_raw[rows, pl.ds((heads + 1) * HEAD_SIZE, HEAD_SIZE)] = grad_value[rows].astype(low)
        grad_gains[...] = jnp.sum(sums[...], 1)

    steps = []
    for r in range(length // BLOCK):
        steps.append(functools.partial(prepare, r))
        some = heads if r == 0 else (heads // 2 if r == 1 else heads // 4)
        for first in range(0, heads, some):
            steps.append(functools.partial(heads_of, r, first, some))
    return steps + [last]


def attention_back(
    query_rot, key_rot, value, raw, grad_mixed, ids_column, ids_row, gain_q, gain_k, cosine, sine
):
    length = key_rot.shape[0]
    low, f32 = jnp.bfloat16, jnp.float32
    space, vmem = pl.BlockSpec(memory_space=pl.ANY), pl.BlockSpec(memory_space=pltpu.VMEM)
    operands = (
        query_rot, key_rot, value, raw, grad_mixed, ids_column, ids_row, gain_q, gain_k, cosine, sine,
    )

    def steps(*refs):
        ins, outs, scratch = split(refs, (11, 2, 13))
        held, (in_sems, out_sems, result), work = split(scratch, (5, 3, 5))
        copies = load(list(zip(ins[:5], held)), in_sems)

        def begin():
            for copy in copies:
                copy.wait()

        def end():
            copy = pltpu.make_async_copy(result, outs[0], out_sems.at[0])
            copy.start()
            copy.wait()

        return [begin] + attend_back_steps(*held, *ins[5:], result, outs[1], *work) + [end]

    return Extra(
        operands,
        [space] * 5 + [vmem] * 6,
        [jax.ShapeDtypeStruct(raw.shape, low), jax.ShapeDtypeStruct((2, HEAD_SIZE), f32)],
        [space, vmem],
        [pltpu.VMEM(a.shape, a.dtype) for a in operands[:5]]
        + [
            pltpu.SemaphoreType.DMA((5,)),
            pltpu.SemaphoreType.DMA((1,)),
            pltpu.VMEM(raw.shape, low),
            pltpu.VMEM((length, BLOCK), f32),
            pltpu.VMEM((HEAD_SIZE, length), low),
            pltpu.VMEM((length, HEAD_SIZE), f32),
            pltpu.VMEM((length, HEAD_SIZE), f32),
            pltpu.VMEM((2, 8, HEAD_SIZE), f32),
        ],
        steps,
    )


def weight_grads(rows, grad_result, inner, grad_a, grad_b):
    count, width = rows.shape
    inside = inner.shape[1]
    low, f32 = jnp.bfloat16, jnp.float32
    space = pl.BlockSpec(memory_space=pl.ANY)
    tiles = width // BLOCK

    def dot_first(a, b):
        return lax.dot_general(a, b, (((0,), (0,)), ((), ())), preferred_element_type=f32)

    def steps(*refs):
        ins, outs, scratch = split(refs, (5, 3, 9))
        a_held, b_held, inner_held, tile, wide, tall, in_sems, tile_sems, out_sems = scratch
        copies = load([(ins[3], a_held), (ins[4], b_held), (ins[2], inner_held)], in_sems)

        def fetch(i):
            source = ins[0] if i < tiles else ins[1]
            columns = pl.ds((i % tiles) * BLOCK, BLOCK)
            return pltpu.make_async_copy(source.at[:, columns], tile.at[i % 2], tile_sems.at[i % 2])

        def store(i, k):
            at = pl.ds((i % tiles) * BLOCK, BLOCK)
            if i < tiles:
                return pltpu.make_async_copy(wide.at[k, i % 2], outs[k].at[at], out_sems.at[k, i % 2])
            return pltpu.make_async_copy(tall.at[i % 2], outs[2].at[:, at], out_sems.at[2, i % 2])

        def begin():
            fetch(0).start()
            for copy in copies:
                copy.wait()

        def prepare(i):
            fetch(i).wait()
            if i + 1 < 2 * tiles:
                fetch(i + 1).start()

        def first(i, k):
            if k == 0:
                prepare(i)
            if i >= 2:
                store(i - 2, k).wait()
            wide[k, i % 2] = dot_first(tile[i % 2], (a_held, b_held)[k][...])
            store(i, k).start()

        def second(i):
            prepare(i)
            if i >= tiles + 2:
                store(i - 2, 2).wait()
            tall[i % 2] = dot_first(inner_held[...], tile[i % 2])
            store(i, 2).start()

        def end():
            for i in (tiles - 2, tiles - 1):
                store(i, 0).wait()
                store(i, 1).wait()
            for i in (2 * tiles - 2, 2 * tiles - 1):
                store(i, 2).wait()

        found = [begin]
        for i in range(tiles):
            found += [functools.partial(first, i, 0), functools.partial(first, i, 1)]
        for i in range(tiles, 2 * tiles):
            found.append(functools.partial(second, i))
        return found + [end]

    return Extra(
        (rows, grad_result, inner, grad_a, grad_b),
        [space] * 5,
        [
            jax.ShapeDtypeStruct((width, inside), f32),
            jax.ShapeDtypeStruct((width, inside), f32),
            jax.ShapeDtypeStruct((inside, width), f32),
        ],
        [space] * 3,
        [
            pltpu.VMEM((count, inside), low),
            pltpu.VMEM((count, inside), low),
            pltpu.VMEM((count, inside), low),
            pltpu.VMEM((2, count, BLOCK), low),
            pltpu.VMEM((2, 2, BLOCK, inside), f32),
            pltpu.VMEM((2, inside, BLOCK), f32),
            pltpu.SemaphoreType.DMA((3,)),
            pltpu.SemaphoreType.DMA((2,)),
            pltpu.SemaphoreType.DMA((3, 2)),
        ],
        steps,
    )


def expert_kernel(
    x, g, picks, values, w_gate, w_up, w_down,
    weighted, grad_result, inner, grad_a, grad_b, grad_rows, gate_grad,
):
    low = jnp.bfloat16
    sources = picks.shape[0]
    rows = x[...]
    a = dot(rows, w_gate[0])
    b = dot(rows, w_up[0])
    sigmoid = jax.nn.sigmoid(a)
    active = a * sigmoid
    inner_low = (active * b).astype(low)
    inner[...] = inner_low
    here = jnp.concatenate(
        [
            jnp.sum(picks[s].astype(jnp.float32) * values[s], -1, keepdims=True)
            for s in range(sources)
        ],
        0,
    )
    grads = g[...].astype(jnp.float32)
    grad_low = (grads * here).astype(low)
    grad_result[...] = grad_low
    grad_inner = dot_last(grad_low, w_down[0])
    a_low = (grad_inner * b * (sigmoid * (1.0 + a * (1.0 - sigmoid)))).astype(low)
    b_low = (grad_inner * active).astype(low)
    grad_a[...] = a_low
    grad_b[...] = b_low
    grad_rows[...] = (dot_last(a_low, w_gate[0]) + dot_last(b_low, w_up[0])).astype(low)
    result = dot(inner_low, w_down[0])
    found = jnp.sum(result * grads, -1, keepdims=True)
    for s in range(sources):
        part = picks[s].astype(jnp.float32) * found[s * SLOTS : (s + 1) * SLOTS]
        gate_grad[s] = jnp.broadcast_to(jnp.sum(part, 0, keepdims=True), gate_grad.shape[1:])
    weighted[...] = (result * here).astype(low)


def expert(x, g, picks, values, w_gate, w_up, w_down):
    count, width = x.shape
    devices, _, tokens = picks.shape
    inside = w_gate.shape[2]
    sources = 4
    low = jnp.bfloat16

    def rows(columns):
        return pl.BlockSpec((sources * SLOTS, columns), lambda i: (i, 0))

    def each(a, b):
        return pl.BlockSpec((sources, a, b), lambda i: (i, 0, 0))

    def whole(a):
        return pl.BlockSpec(a.shape, lambda i: (0, 0, 0), pipeline_mode=pl.Buffered(1))

    columns = [width, width, inside, inside, inside, width]
    return pl.pallas_call(
        expert_kernel,
        grid=(devices // sources,),
        out_shape=[jax.ShapeDtypeStruct((count, n), low) for n in columns]
        + [jax.ShapeDtypeStruct((devices, 8, tokens), jnp.float32)],
        in_specs=[
            rows(width),
            rows(width),
            each(SLOTS, tokens),
            each(1, tokens),
            whole(w_gate),
            whole(w_up),
            whole(w_down),
        ],
        out_specs=[rows(n) for n in columns] + [each(8, tokens)],
        compiler_params=pltpu.CompilerParams(vmem_limit_bytes=56 * 2**20),
        name=EXPERT,
    )(x, g, picks, values, w_gate, w_up, w_down)


def local(
    layer_input,
    doc_ids,
    expert_ids,
    w_query,
    w_key,
    w_value,
    w_out,
    w_router,
    gain_attn,
    gain_ffn,
    gain_query,
    gain_key,
    w_gate,
    w_up,
    w_down,
    grad_output,
):
    single_float = jnp.float32
    brain_float_half = jnp.bfloat16
    row_count = layer_input.shape[1]
    width = layer_input.shape[2]
    length_total = doc_ids.shape[1]
    query_groups = QUERY_HEADS // KEY_VALUE_HEADS
    scale = HEAD_SIZE ** (-0.5)
    experts = w_router.shape[1]
    capacity = max(2, 6 * row_count * TOP // (5 * experts))
    pairs = row_count * TOP
    (
        full_query,
        gathered_key,
        full_value,
        full_out,
        full_router,
        gain_one,
        gain_two,
        gain_q,
        key_gain_vector,
    ) = (
        lax.all_gather(w_query, FSDP, axis=0, tiled=True),
        lax.all_gather(w_key, FSDP, axis=0, tiled=True),
        lax.all_gather(w_value, FSDP, axis=0, tiled=True),
        lax.all_gather(w_out, FSDP, axis=0, tiled=True),
        lax.all_gather(w_router, FSDP, axis=0, tiled=True),
        lax.all_gather(gain_attn, FSDP, axis=0, tiled=True),
        lax.all_gather(gain_ffn, FSDP, axis=0, tiled=True),
        lax.all_gather(gain_query, FSDP, axis=0, tiled=True),
        lax.all_gather(gain_key, FSDP, axis=0, tiled=True),
    )
    gain_one = gain_one.astype(single_float)
    gain_two = gain_two.astype(single_float)
    gain_q = gain_q.astype(single_float)
    key_gain_vector = key_gain_vector.astype(single_float)
    inputs = layer_input[0].astype(single_float)
    offset = lax.axis_index(EXPERT) * row_count
    own_pos = offset + jnp.arange(row_count, dtype=jnp.int32)
    all_pos = jnp.arange(length_total, dtype=jnp.int32)
    seq_ids = doc_ids[0]
    own_ids = lax.dynamic_slice_in_dim(seq_ids, offset, row_count)
    allowed = (own_ids[:, None] == seq_ids[None, :]) & (own_pos[:, None] >= all_pos[None, :])
    cosine_table, sine_table = angles(own_pos)
    cosine_table = cosine_table[:, None, :]
    sine_table = sine_table[:, None, :]
    scale_one = inverse_rms(inputs)
    normalized_input = (inputs * scale_one * gain_one).astype(brain_float_half)
    query_raw = jnp.dot(normalized_input, full_query, preferred_element_type=single_float).reshape(
        row_count, QUERY_HEADS, HEAD_SIZE
    )
    key_unnormalized = jnp.dot(
        normalized_input, gathered_key, preferred_element_type=single_float
    ).reshape(row_count, KEY_VALUE_HEADS, HEAD_SIZE)
    value_low = jnp.dot(normalized_input, full_value, preferred_element_type=single_float).astype(
        brain_float_half
    )
    query_scale = inverse_rms(query_raw)
    key_norm_scale = inverse_rms(key_unnormalized)
    query_rot = (
        apply_rotary(query_raw * query_scale * gain_q, cosine_table, sine_table)
        .astype(brain_float_half)
        .reshape(row_count, KEY_VALUE_HEADS, query_groups, HEAD_SIZE)
    )
    key_rotated = apply_rotary(
        key_unnormalized * key_norm_scale * key_gain_vector, cosine_table, sine_table
    ).astype(brain_float_half)
    key_gathered_rows, value_gathered_rows = (
        lax.all_gather(
            key_rotated.reshape(row_count, KEY_VALUE_HEADS * HEAD_SIZE),
            EXPERT,
            axis=0,
            tiled=True,
        ),
        lax.all_gather(value_low, EXPERT, axis=0, tiled=True),
    )
    key_gathered_rows = key_gathered_rows.reshape(length_total, KEY_VALUE_HEADS, HEAD_SIZE)
    value_gathered_rows = value_gathered_rows.reshape(length_total, KEY_VALUE_HEADS, HEAD_SIZE)

    def masked_scores():
        raw = (
            jnp.einsum(
                "tkgd,skd->kgts", query_rot, key_gathered_rows, preferred_element_type=single_float
            )
            * scale
        )
        return jnp.where(allowed, raw, -1e30)

    scores = masked_scores()
    peak = jnp.max(scores, -1, keepdims=True)
    shifted = jnp.exp(scores - peak)
    totals = jnp.sum(shifted, -1, keepdims=True)
    weights_low = (shifted / totals).astype(brain_float_half)
    log_total = peak + jnp.log(totals)
    mixed = (
        jnp.einsum(
            "kgts,skd->tkgd", weights_low, value_gathered_rows, preferred_element_type=single_float
        )
        .reshape(row_count, QUERY_HEADS * HEAD_SIZE)
        .astype(brain_float_half)
    )
    hidden = inputs + jnp.dot(mixed, full_out, preferred_element_type=single_float)
    scale_two = inverse_rms(hidden)
    normed_two = (hidden * scale_two * gain_two).astype(brain_float_half)
    logits = jnp.dot(normed_two, full_router, preferred_element_type=single_float)
    selector = (expert_ids[0][:, :, None] == jnp.arange(experts, dtype=jnp.int32)).astype(
        single_float
    )
    chosen = jnp.einsum("tke,te->tk", selector, logits, precision=HIGHEST)
    gates = jax.nn.softmax(chosen, -1)
    flat_routes = expert_ids[0].reshape(pairs)
    hits = (flat_routes[:, None] == jnp.arange(experts, dtype=jnp.int32)).astype(jnp.int32)
    before = jnp.cumsum(hits, 0) - hits
    ranks = jnp.sum(before * hits, 1)
    slot_index = flat_routes * capacity + ranks
    owner_rows = jnp.arange(pairs, dtype=jnp.int32) // TOP
    outgoing = (
        jnp.zeros((experts * capacity, width), brain_float_half)
        .at[slot_index]
        .set(normed_two[owner_rows])
    )
    arrived = lax.all_to_all(
        outgoing.reshape(experts, capacity, width),
        (EXPERT, FSDP),
        split_axis=0,
        concat_axis=0,
        tiled=True,
    ).reshape(experts * capacity, width)
    gate_pre = jnp.dot(arrived, w_gate[0], preferred_element_type=single_float)
    up_pre = jnp.dot(arrived, w_up[0], preferred_element_type=single_float)
    activated = jax.nn.silu(gate_pre)
    inner = (activated * up_pre).astype(brain_float_half)
    result = jnp.dot(inner, w_down[0], preferred_element_type=single_float).astype(brain_float_half)
    returned = lax.all_to_all(
        result.reshape(experts, capacity, width),
        (EXPERT, FSDP),
        split_axis=0,
        concat_axis=0,
        tiled=True,
    ).reshape(experts * capacity, width)
    expert_rows = returned[slot_index].astype(single_float).reshape(row_count, TOP, width)
    output = hidden + jnp.einsum("tk,tkd->td", gates, expert_rows, precision=HIGHEST)
    grad_top = grad_output[0]
    grad_gates = jnp.einsum("tkd,td->tk", expert_rows, grad_top, precision=HIGHEST)
    grad_pairs = (
        (gates[:, :, None] * grad_top[:, None, :]).astype(brain_float_half).reshape(pairs, width)
    )
    grad_send = (
        jnp.zeros((experts * capacity, width), brain_float_half).at[slot_index].set(grad_pairs)
    )
    grad_arrived = lax.all_to_all(
        grad_send.reshape(experts, capacity, width),
        (EXPERT, FSDP),
        split_axis=0,
        concat_axis=0,
        tiled=True,
    ).reshape(experts * capacity, width)
    grad_down = jnp.einsum("rf,rd->fd", inner, grad_arrived, preferred_element_type=single_float)
    grad_inner = jnp.einsum(
        "rd,fd->rf", grad_arrived, w_down[0], preferred_element_type=single_float
    )
    sigmoid_gate = jax.nn.sigmoid(gate_pre)
    slope = sigmoid_gate * (1.0 + gate_pre * (1.0 - sigmoid_gate))
    grad_gate_pre = (grad_inner * up_pre * slope).astype(brain_float_half)
    grad_up_pre = (grad_inner * activated).astype(brain_float_half)
    grad_gate_w = jnp.einsum(
        "rd,rf->df", arrived, grad_gate_pre, preferred_element_type=single_float
    )
    grad_up_w = jnp.einsum("rd,rf->df", arrived, grad_up_pre, preferred_element_type=single_float)
    grad_rows = (
        jnp.einsum("rf,df->rd", grad_gate_pre, w_gate[0], preferred_element_type=single_float)
        + jnp.einsum("rf,df->rd", grad_up_pre, w_up[0], preferred_element_type=single_float)
    ).astype(brain_float_half)
    grad_back = lax.all_to_all(
        grad_rows.reshape(experts, capacity, width),
        (EXPERT, FSDP),
        split_axis=0,
        concat_axis=0,
        tiled=True,
    ).reshape(experts * capacity, width)
    grad_normed_two = jnp.sum(
        grad_back[slot_index].astype(single_float).reshape(row_count, TOP, width), 1
    )
    grad_chosen = gates * (grad_gates - jnp.sum(gates * grad_gates, -1, keepdims=True))
    grad_logits = jnp.einsum("tke,tk->te", selector, grad_chosen, precision=HIGHEST).astype(
        brain_float_half
    )
    grad_normed_two = grad_normed_two + jnp.einsum(
        "te,de->td", grad_logits, full_router, preferred_element_type=single_float
    )
    grad_router = jnp.einsum(
        "td,te->de", normed_two, grad_logits, preferred_element_type=single_float
    )
    grad_gain_two = jnp.sum(grad_normed_two * hidden * scale_two, 0)
    grad_hidden = grad_top + norm_backward(grad_normed_two, hidden, scale_two, gain_two)
    grad_branch = grad_hidden.astype(brain_float_half)
    grad_out_w = jnp.einsum("tq,td->qd", mixed, grad_branch, preferred_element_type=single_float)
    grad_mixed = (
        jnp.einsum("td,qd->tq", grad_branch, full_out, preferred_element_type=single_float)
        .astype(brain_float_half)
        .reshape(row_count, KEY_VALUE_HEADS, query_groups, HEAD_SIZE)
    )
    again = masked_scores()
    weights = jnp.exp(again - log_total)
    weights_again = weights.astype(brain_float_half)
    grad_weights = jnp.einsum(
        "tkgd,skd->kgts", grad_mixed, value_gathered_rows, preferred_element_type=single_float
    )
    spread = jnp.sum(weights * grad_weights, -1, keepdims=True)
    grad_scores = (weights * (grad_weights - spread)).astype(brain_float_half)
    grad_query_rot = (
        jnp.einsum(
            "kgts,skd->tkgd", grad_scores, key_gathered_rows, preferred_element_type=single_float
        )
        * scale
    ).reshape(row_count, QUERY_HEADS, HEAD_SIZE)
    grad_key_all = (
        jnp.einsum("kgts,tkgd->skd", grad_scores, query_rot, preferred_element_type=single_float)
        * scale
    ).reshape(length_total, KEY_VALUE_HEADS * HEAD_SIZE)
    grad_value_all = jnp.einsum(
        "kgts,tkgd->skd", weights_again, grad_mixed, preferred_element_type=single_float
    ).reshape(length_total, KEY_VALUE_HEADS * HEAD_SIZE)
    gradient_key_rotated, grad_value = (
        lax.psum_scatter(
            grad_key_all.astype(jnp.bfloat16), EXPERT, scatter_dimension=0, tiled=True
        ).astype(jnp.float32),
        lax.psum_scatter(
            grad_value_all.astype(jnp.bfloat16), EXPERT, scatter_dimension=0, tiled=True
        ).astype(jnp.float32),
    )
    gradient_key_rotated = gradient_key_rotated.reshape(row_count, KEY_VALUE_HEADS, HEAD_SIZE)
    grad_query_unit = unrotate(grad_query_rot, cosine_table, sine_table)
    gradient_key_normalized = unrotate(gradient_key_rotated, cosine_table, sine_table)
    grad_gain_q = jnp.sum(grad_query_unit * query_raw * query_scale, (0, 1))
    grad_gain_k = jnp.sum(gradient_key_normalized * key_unnormalized * key_norm_scale, (0, 1))
    grad_query = (
        norm_backward(grad_query_unit, query_raw, query_scale, gain_q)
        .reshape(row_count, QUERY_HEADS * HEAD_SIZE)
        .astype(brain_float_half)
    )
    grad_key = (
        norm_backward(gradient_key_normalized, key_unnormalized, key_norm_scale, key_gain_vector)
        .reshape(row_count, KEY_VALUE_HEADS * HEAD_SIZE)
        .astype(brain_float_half)
    )
    grad_value_low = grad_value.astype(brain_float_half)
    grad_query_w = jnp.einsum(
        "td,tq->dq", normalized_input, grad_query, preferred_element_type=single_float
    )
    grad_key_w = jnp.einsum(
        "td,tq->dq", normalized_input, grad_key, preferred_element_type=single_float
    )
    grad_value_w = jnp.einsum(
        "td,tq->dq", normalized_input, grad_value_low, preferred_element_type=single_float
    )
    grad_normed = (
        jnp.einsum("tq,dq->td", grad_query, full_query, preferred_element_type=single_float)
        + jnp.einsum("tq,dq->td", grad_key, gathered_key, preferred_element_type=single_float)
        + jnp.einsum("tq,dq->td", grad_value_low, full_value, preferred_element_type=single_float)
    )
    grad_gain_one = jnp.sum(grad_normed * inputs * scale_one, 0)
    grad_inputs = grad_hidden + norm_backward(grad_normed, inputs, scale_one, gain_one)
    local_grads = (
        grad_query_w,
        grad_key_w,
        grad_value_w,
        grad_out_w,
        grad_router,
        grad_gain_one,
        grad_gain_two,
        grad_gain_q,
        grad_gain_k,
    )
    shards = (
        lax.psum_scatter(
            local_grads[0].astype(jnp.bfloat16), FSDP, scatter_dimension=0, tiled=True
        ).astype(jnp.float32),
        lax.psum_scatter(
            local_grads[1].astype(jnp.bfloat16), FSDP, scatter_dimension=0, tiled=True
        ).astype(jnp.float32),
        lax.psum_scatter(
            local_grads[2].astype(jnp.bfloat16), FSDP, scatter_dimension=0, tiled=True
        ).astype(jnp.float32),
        lax.psum_scatter(
            local_grads[3].astype(jnp.bfloat16), FSDP, scatter_dimension=0, tiled=True
        ).astype(jnp.float32),
        lax.psum_scatter(
            local_grads[4].astype(jnp.bfloat16), FSDP, scatter_dimension=0, tiled=True
        ).astype(jnp.float32),
        lax.psum_scatter(
            local_grads[5].astype(jnp.bfloat16), FSDP, scatter_dimension=0, tiled=True
        ).astype(jnp.float32),
        lax.psum_scatter(
            local_grads[6].astype(jnp.bfloat16), FSDP, scatter_dimension=0, tiled=True
        ).astype(jnp.float32),
        lax.psum_scatter(
            local_grads[7].astype(jnp.bfloat16), FSDP, scatter_dimension=0, tiled=True
        ).astype(jnp.float32),
        lax.psum_scatter(
            local_grads[8].astype(jnp.bfloat16), FSDP, scatter_dimension=0, tiled=True
        ).astype(jnp.float32),
    )
    shards = (
        lax.psum(shards[0].astype(jnp.bfloat16), EXPERT).astype(jnp.float32),
        lax.psum(shards[1].astype(jnp.bfloat16), EXPERT).astype(jnp.float32),
        lax.psum(shards[2].astype(jnp.bfloat16), EXPERT).astype(jnp.float32),
        lax.psum(shards[3].astype(jnp.bfloat16), EXPERT).astype(jnp.float32),
        lax.psum(shards[4].astype(jnp.bfloat16), EXPERT).astype(jnp.float32),
        lax.psum(shards[5].astype(jnp.bfloat16), EXPERT).astype(jnp.float32),
        lax.psum(shards[6].astype(jnp.bfloat16), EXPERT).astype(jnp.float32),
        lax.psum(shards[7].astype(jnp.bfloat16), EXPERT).astype(jnp.float32),
        lax.psum(shards[8].astype(jnp.bfloat16), EXPERT).astype(jnp.float32),
    )
    return (
        output[None],
        grad_inputs[None],
        shards[0],
        shards[1],
        shards[2],
        shards[3],
        shards[4],
        shards[5],
        shards[6],
        shards[7],
        shards[8],
        grad_gate_w[None],
        grad_up_w[None],
        grad_down[None],
    )


def angle_tables(length):
    power = -(np.arange(HEAD_SIZE // 2, dtype=np.float32) * np.float32(2.0)) / np.float32(HEAD_SIZE)
    freq = np.power(np.float32(THETA), power).astype(np.float32)
    turns = np.arange(length, dtype=np.float32)[:, None] * freq[None, :]
    turns = np.concatenate([turns, turns], -1)
    return jnp.asarray(np.cos(turns)), jnp.asarray(np.sin(turns))


def one_hots(ids, numbers):
    rows = ids.shape[2]
    hit = jnp.any(ids[:, None] == numbers[None, :, None, None], 2)
    earlier = (jnp.arange(rows)[:, None] < jnp.arange(rows)[None, :]).astype(jnp.bfloat16)
    rank = jnp.dot(hit.astype(jnp.bfloat16), earlier, preferred_element_type=jnp.float32)
    places = jnp.arange(SLOTS, dtype=jnp.int32)[:, None]
    taken = hit[:, :, None, :] & (rank.astype(jnp.int32)[:, :, None, :] == places)
    return taken.astype(jnp.bfloat16)


def routes(ids):
    place = Place()
    _, far = place.line()
    mine = (place.x, place.y)
    me = place.e * lax.axis_size(FSDP) + place.f
    numbers = []
    for chip, core in ((mine, place.c), (mine, 1 - place.c), (far, place.c), (far, 1 - place.c)):
        expert_at, shard_at = place.at(chip, core)
        numbers.append(expert_at * lax.axis_size(FSDP) + shard_at)
    blocks = [block_number(mine, place.c, ar, zs) for ar in range(2) for zs in range(4)]
    near = jnp.stack([lax.dynamic_index_in_dim(ids, i, 0, keepdims=False) for i in blocks])
    pick = one_hots(near, jnp.stack(numbers)).reshape(8, 4 * SLOTS, -1)
    return me, one_hots(ids, me[None])[:, 0], pick, pick.swapaxes(1, 2)


def packed(pieces, lead, rows):
    flat = jnp.concatenate([piece.reshape(lead, -1) for piece in pieces], 1)
    flat = jnp.pad(flat, ((0, 0), (0, rows * 128 - flat.shape[1])))
    return flat.reshape(lead, rows, 128)


def local_staged(
    layer_input,
    doc_ids,
    expert_ids,
    w_query,
    w_key,
    w_value,
    w_out,
    w_router,
    gain_attn,
    gain_ffn,
    gain_query,
    gain_key,
    w_gate,
    w_up,
    w_down,
    grad_output,
):
    f32 = jnp.float32
    low = jnp.bfloat16
    rows, width = layer_input.shape[1:]
    length = doc_ids.shape[1]
    depth = w_router.shape[0]
    groups, shards = lax.axis_size(EXPERT), lax.axis_size(FSDP)
    experts = w_router.shape[1]
    heads = QUERY_HEADS // groups
    span = heads * HEAD_SIZE
    mine = lax.axis_index(EXPERT)

    def columns(weight, count):
        return lax.dynamic_slice_in_dim(weight, mine * count, count, 1)

    flat = jnp.concatenate(
        [columns(w_query, span), columns(w_key, HEAD_SIZE), columns(w_value, HEAD_SIZE)], 1
    )
    pack = packed([w_router, gain_attn, gain_ffn, gain_query, gain_key], 1, 80)[0]
    w_qkv, w_mix, tokens, pack_all, ids_all = gather(
        groups,
        shards,
        5,
        flat,
        w_out,
        layer_input[0],
        pack,
        expert_ids[0].T,
    )
    w_qkv = w_qkv.reshape(width, span + 2 * HEAD_SIZE)
    w_mix = w_mix.reshape(span, width)
    tokens = tokens.reshape(length, width)
    pack_all = pack_all.reshape(shards, -1)
    at = depth * experts
    full_router = pack_all[:, :at].reshape(width, experts)
    gain_one = pack_all[:, at : at + depth].reshape(width).astype(f32)
    gain_two = pack_all[:, at + depth : at + 2 * depth].reshape(width).astype(f32)
    at += 2 * depth
    small = HEAD_SIZE // shards
    gain_q = pack_all[:, at : at + small].reshape(HEAD_SIZE).astype(f32)
    gain_k = pack_all[:, at + small : at + 2 * small].reshape(HEAD_SIZE).astype(f32)
    me, mine_picks, pick, spread = routes(ids_all)
    grad_top = grad_output[0]
    ids_column, ids_row = doc_ids[0][:, None], doc_ids[0][None, :]
    cosine, sine = angle_tables(length)
    gain_q, gain_k = gain_q[None], gain_k[None]
    attend = attention(
        tokens, w_qkv, gain_one[None], gain_q, gain_k, cosine, sine, ids_column, ids_row, heads
    )
    grads_in, normed_one, raw, query_rot, key_rot, value, mixed = dispatch(
        groups, shards, 1, grad_top.astype(low), pick, extra=attend
    )
    branch = jnp.dot(mixed, w_mix, preferred_element_type=f32).astype(low)
    inputs = layer_input[0].astype(f32)
    hidden = inputs + group_scatter(8, branch.reshape(groups, rows, width))
    scale_two = inverse_rms(hidden)
    normed_two = (hidden * scale_two * gain_two).astype(low)
    logits = jnp.dot(normed_two, full_router, preferred_element_type=f32)
    selector = (expert_ids[0][:, :, None] == jnp.arange(experts, dtype=jnp.int32)).astype(f32)
    gates = jax.nn.softmax(jnp.sum(selector * logits[:, None, :], -1), -1)
    arrived, gates_all = dispatch(groups, shards, 2, normed_two, pick, gates.T)
    gate_values = jnp.sum(jnp.where(ids_all == me, gates_all, 0.0), 1, keepdims=True)
    arrived = arrived.reshape(-1, width)
    weighted, grad_arrived, inner, grad_a, grad_b, grad_rows, gate_grads = expert(
        arrived, grads_in.reshape(-1, width), mine_picks, gate_values, w_gate, w_up, w_down
    )
    grad_normed_two, gates_back, grad_gate_w, grad_up_w, grad_down = combine(
        groups,
        shards,
        3,
        grad_rows.reshape(experts, SLOTS, width),
        spread,
        gate_grads,
        weight_grads(arrived, grad_arrived, inner, grad_a, grad_b),
    )
    grad_gates = jnp.sum(selector * gates_back[:, 0].T[:, None, :], -1)
    grad_chosen = gates * (grad_gates - jnp.sum(gates * grad_gates, -1, keepdims=True))
    grad_logits = jnp.sum(selector * grad_chosen[:, :, None], 1).astype(low)
    grad_normed_two = grad_normed_two + jnp.einsum(
        "te,de->td", grad_logits, full_router, preferred_element_type=f32
    )
    grad_router = jnp.einsum("td,te->de", normed_two, grad_logits, preferred_element_type=f32)
    grad_gain_two = jnp.sum(grad_normed_two * hidden * scale_two, 0)
    grad_hidden = grad_top + norm_backward(grad_normed_two, hidden, scale_two, gain_two)
    grad_branch = group_gather(7, grad_hidden.astype(low)).reshape(length, width)
    grad_mix = jnp.einsum("tq,td->qd", mixed, grad_branch, preferred_element_type=f32).astype(low)
    grad_mixed = jnp.einsum("td,qd->tq", grad_branch, w_mix, preferred_element_type=f32)
    grad_mixed = grad_mixed.astype(low)

    back = attention_back(
        query_rot, key_rot, value, raw, grad_mixed, ids_column, ids_row, gain_q, gain_k, cosine, sine
    )
    combined, grad_raw, gain_grads = combine(
        groups, shards, 4, weighted.reshape(experts, SLOTS, width), spread, extra=back
    )
    output = hidden + combined
    grad_qkv = jnp.einsum("td,tq->dq", normed_one, grad_raw, preferred_element_type=f32).astype(low)
    grad_normed_one = jnp.einsum("tq,dq->td", grad_raw, w_qkv, preferred_element_type=f32)
    grad_normed_one = group_scatter(9, grad_normed_one.astype(low).reshape(groups, rows, width))
    scale_own = inverse_rms(inputs)
    grad_gain_one = jnp.sum(grad_normed_one * inputs * scale_own, 0)
    grad_inputs = grad_hidden + norm_backward(grad_normed_one, inputs, scale_own, gain_one)

    sums = packed([grad_router, grad_gain_one, grad_gain_two, gain_grads[0], gain_grads[1]], shards, 72)
    query_sum, key_sum, value_sum, tall_sum, pack_sum = reduce(
        groups,
        shards,
        6,
        grad_qkv.reshape(shards, depth, -1),
        grad_mix.reshape(2, -1, width),
        sums,
    )
    pack_sum = jnp.sum(pack_sum, 0).reshape(-1)
    at = depth * experts
    return (
        output[None],
        grad_inputs[None],
        query_sum.astype(f32),
        key_sum.astype(f32),
        value_sum.astype(f32),
        tall_sum.astype(f32),
        pack_sum[:at].reshape(depth, experts),
        pack_sum[at : at + depth],
        pack_sum[at + depth : at + 2 * depth],
        pack_sum[at + 2 * depth : at + 2 * depth + small],
        pack_sum[at + 2 * depth + small : at + 2 * depth + 2 * small],
        grad_gate_w[None],
        grad_up_w[None],
        grad_down[None],
    )


def solution(mesh):
    in_specs = (
        P(FSDP, EXPERT, None),
        P(FSDP, None),
        P(FSDP, EXPERT, None),
        P(FSDP, None),
        P(FSDP, None),
        P(FSDP, None),
        P(FSDP, None),
        P(FSDP, None),
        P(FSDP),
        P(FSDP),
        P(FSDP),
        P(FSDP),
        P((EXPERT, FSDP), None, None),
        P((EXPERT, FSDP), None, None),
        P((EXPERT, FSDP), None, None),
        P(FSDP, EXPERT, None),
    )
    out_specs = (
        P(FSDP, EXPERT, None),
        P(FSDP, EXPERT, None),
        P(FSDP, None),
        P(FSDP, None),
        P(FSDP, None),
        P(FSDP, None),
        P(FSDP, None),
        P(FSDP),
        P(FSDP),
        P(FSDP),
        P(FSDP),
        P((EXPERT, FSDP), None, None),
        P((EXPERT, FSDP), None, None),
        P((EXPERT, FSDP), None, None),
    )
    staged = mesh.shape[EXPERT] == 4 and mesh.shape[FSDP] == 8
    return jax.shard_map(local_staged if staged else local, mesh=mesh, in_specs=in_specs, out_specs=out_specs, check_vma=False)
```

```python
import functools

import jax
import jax.numpy as jnp
import numpy as np
from jax import lax
from jax.experimental import pallas as pl
from jax.experimental.pallas import tpu as pltpu
from jax.sharding import PartitionSpec as P

EXPERT = "expert"
FSDP = "fsdp"
UP, DOWN, ABOVE, BELOW = "up", "down", "above", "below"
QUERY_HEADS = 32
KEY_VALUE_HEADS = 4
HEAD_SIZE = 128
TOP = 8


EPS = 1e-06
THETA = 1000000.0
HIGHEST = lax.Precision.HIGHEST


def angles(positions):
    freq = THETA ** (-(jnp.arange(HEAD_SIZE // 2, dtype=jnp.float32) * 2.0) / HEAD_SIZE)
    turn = positions.astype(jnp.float32)[:, None] * freq[None, :]
    turn = jnp.concatenate([turn, turn], -1)
    return (jnp.cos(turn), jnp.sin(turn))


def apply_rotary(value_rows_local, cosine_table, sine_table):
    half = value_rows_local.shape[-1] // 2
    turned = jnp.concatenate([-value_rows_local[..., half:], value_rows_local[..., :half]], -1)
    return value_rows_local * cosine_table + turned * sine_table


def unrotate(grads, cosine_table, sine_table):
    half = grads.shape[-1] // 2
    scaled = grads * sine_table
    turned = jnp.concatenate([-scaled[..., half:], scaled[..., :half]], -1)
    return grads * cosine_table - turned


def inverse_rms(value_rows_local):
    return lax.rsqrt(jnp.mean(value_rows_local * value_rows_local, -1, keepdims=True) + EPS)


def norm_backward(grad, value_rows_local, inverse, gain):
    scaled = grad * gain
    return inverse * scaled - inverse * inverse * inverse * value_rows_local * jnp.mean(
        scaled * value_rows_local, -1, keepdims=True
    )


MESH = pl.DeviceIdType.MESH
SLOTS = 80
FAR_FIRST = ((1, 3), (1, 2), (0, 3), (1, 1), (0, 2), (0, 1), (1, 0), (0, 0))
BACK = FAR_FIRST
AHEAD = 2
HALVES = 2


class Place:
    def __init__(self):
        self.e = lax.axis_index(EXPERT)
        self.f = lax.axis_index(FSDP)
        self.x, self.c = self.e // 2, self.e % 2
        self.z, self.y = self.f // 2, self.f % 2

    def device(self, axis):
        if axis == "c":
            return (self.x * 2 + 1 - self.c, self.f)
        if axis == "x":
            return ((1 - self.x) * 2 + self.c, self.f)
        if axis == "y":
            return (self.e, self.z * 2 + 1 - self.y)
        if axis == UP:
            return (self.e, jnp.minimum(self.z + 1, 3) * 2 + self.y)
        return (self.e, jnp.maximum(self.z - 1, 0) * 2 + self.y)

    def ranked(self, j):
        inner = (1, 0, 2, 3)[j]
        end = (self.z == 0) | (self.z == 3)
        low = jnp.where(end, j, inner)
        return jnp.where(self.z < 2, low, 3 - low)

    def line(self):
        x, y, even = self.x, self.y, self.c == 0
        near = (jnp.where(even, 1 - x, x), jnp.where(even, y, 1 - y))
        far = (jnp.where(even, x, 1 - x), jnp.where(even, 1 - y, y))
        return near, far

    def at(self, chip, core):
        return (chip[0] * 2 + core, self.z * 2 + chip[1])


def block_number(chip, core, ar, zs):
    x, y = chip
    xs = jnp.where(core == 0, 1 - x, x) if ar else x
    ys = jnp.where(core == 0, y, 1 - y) if ar else y
    return (xs * 2 + core) * 8 + zs * 2 + ys


def greet(place):
    barrier = pltpu.get_barrier_semaphore()
    beside = [place.device("c")]
    for chip in ((1 - place.x, place.y), (place.x, 1 - place.y)):
        beside += [place.at(chip, 0), place.at(chip, 1)]
    for device in beside:
        pl.semaphore_signal(barrier, 1, device_id=device, device_id_type=MESH)

    @pl.when(place.z < 3)
    def _():
        pl.semaphore_signal(barrier, 1, device_id=place.device(UP), device_id_type=MESH)

    @pl.when(place.z > 0)
    def _():
        pl.semaphore_signal(barrier, 1, device_id=place.device(DOWN), device_id_type=MESH)

    inner = (place.z > 0) & (place.z < 3)
    pl.semaphore_wait(barrier, len(beside) + jnp.where(inner, 2, 1))


def greet_all(place, experts, shards):
    barrier = pltpu.get_barrier_semaphore()
    count = experts * shards

    def one(i, carry):
        target = lax.rem(place.e * shards + place.f + i, count)
        pl.semaphore_signal(
            barrier, 1, device_id=(target // shards, lax.rem(target, shards)), device_id_type=MESH
        )
        return carry

    lax.fori_loop(1, count, one, 0)
    pl.semaphore_wait(barrier, count - 1)


def onward(path, j, xr, yr):
    differs = {"z": j > 0, "x": xr > 0, "y": yr > 0}
    last = -1
    for i, axis in enumerate(path):
        if differs[axis]:
            last = i
    out = []
    if last >= 0 and path[last] == "z":
        out.append("z+")
    for axis in path[last + 1 :]:
        out.append("z*" if axis == "z" else axis)
    return out


def links(place, path, j, xr, yr, zs):
    out = []
    for axis in onward(path, j, xr, yr):
        if axis == "z+":
            out.append((UP, (zs < place.z) & (place.z < 3)))
            out.append((DOWN, (zs > place.z) & (place.z > 0)))
        elif axis == "z*":
            out.append((UP, place.z < 3))
            out.append((DOWN, place.z > 0))
        else:
            out.append((axis, None))
    return out


def run(condition, action):
    if condition is None:
        action()
    else:
        pl.when(condition)(action)


LINK = {"x": 0, "y": 1, UP: 2, DOWN: 3}


def remote(src, dst, send_sem, recv_sem, device):
    return pltpu.make_async_remote_copy(
        src_ref=src,
        dst_ref=dst,
        send_sem=send_sem,
        recv_sem=recv_sem,
        device_id=device,
        device_id_type=MESH,
    )


class Side:
    def __init__(self, steps, events):
        self.steps, self.events = list(steps), events
        self.total, self.seen = len(self.steps), 0

    def event(self):
        self.seen += 1
        left = self.total - self.total * min(self.seen, self.events) // self.events
        while len(self.steps) > left:
            self.steps.pop(0)()


class Extra:
    def __init__(self, operands=(), in_specs=(), outs=(), out_specs=(), scratch=(), steps=None):
        self.operands, self.in_specs = list(operands), list(in_specs)
        self.outs, self.out_specs, self.scratch = list(outs), list(out_specs), list(scratch)
        self.steps = steps if steps is not None else lambda *refs: []


def split(refs, counts):
    out = []
    for count in counts:
        out.append(refs[:count])
        refs = refs[count:]
    return out


def exchange_small(place, dims, src_of, dst, sems_out, sems_in, sem):
    experts, shards = dims
    count = experts * shards
    me = place.e * shards + place.f
    keep = pltpu.make_async_copy(src_of(me), dst.at[me], sem)
    keep.start()

    def copy(i, sending):
        other = lax.rem(me + i, count)
        source = me if sending else other
        device = (other // shards, lax.rem(other, shards))
        return remote(src_of(other), dst.at[source], sems_out.at[i], sems_in.at[source], device)

    def start(i, carry):
        copy(i, True).start()
        return carry

    def finish(i, carry):
        done = copy(i, False)
        done.wait_send()
        done.wait_recv()
        return carry

    lax.fori_loop(1, count, start, 0)

    def end():
        keep.wait()
        lax.fori_loop(1, count, finish, 0)

    return end


def dispatch_kernel(dims, has_small, extra, *refs):
    counts = (
        2 + has_small, len(extra.operands), 1 + has_small, len(extra.outs), 7 + 3 * has_small,
        len(extra.scratch),
    )
    ins, more_in, outs, more_out, scratch, more_scratch = split(refs, counts)
    tok, sel = ins[:2]
    picked = outs[0]
    held, stage, arrive, leave, pick_out, pick_in, local = scratch[:7]
    place = Place()
    width = tok.shape[1]
    near, far = place.line()
    mine = (place.x, place.y)
    if has_small:
        greet_all(place, *dims)
        end_small = exchange_small(
            place, dims, lambda i: ins[2], outs[1], scratch[7], scratch[8], scratch[9].at[0]
        )
    else:
        greet(place)
    side = Side(extra.steps(*more_in, *more_out, *more_scratch), 8)
    keep = pltpu.make_async_copy(tok, held.at[place.z], local.at[8])
    keep.start()
    pending = []
    finish = []
    targets = (place.device("c"), place.at(far, place.c), place.at(far, 1 - place.c))

    def pick(ar, zs):
        block = ar * 4 + zs
        number = block_number(mine, place.c, ar, zs)

        def tile(i, carry):
            columns = pl.ds(pl.multiple_of(i * 512, 512), 512)
            stage[block, :, columns] = jnp.dot(
                sel[block], held[block, :, columns], preferred_element_type=jnp.float32
            ).astype(jnp.bfloat16)
            return carry

        lax.fori_loop(0, width // 512, tile, 0)
        for k in (2, 1, 0):
            away = remote(
                stage.at[block, pl.ds((k + 1) * SLOTS, SLOTS)], picked.at[number],
                pick_out.at[block, k], pick_in.at[number], targets[k],
            )
            away.start()
            finish.append(away)
        stay = pltpu.make_async_copy(
            stage.at[block, pl.ds(0, SLOTS)], picked.at[number], local.at[block]
        )
        stay.start()
        finish.append(stay)

    half = tok.shape[0] // HALVES
    for ar, j in FAR_FIRST[::-1]:
        zs = place.ranked(j)
        block = ar * 4 + zs
        for h in range(HALVES):
            part = pl.ds(h * half, half)
            window = held.at[block, part]
            if ar or j:
                remote(
                    window, window, leave.at[zs, 0, h], arrive.at[block, h], place.device("c")
                ).wait_recv()
            if ar:
                continue
            source = tok.at[part] if j == 0 else window
            onward = (
                (UP, zs, 0, (zs <= place.z) & (place.z < 3)),
                (DOWN, zs, 1, (zs >= place.z) & (place.z > 0)),
                ("near", 4 + zs, 2, None),
            )
            for axis, there, k, condition in onward:
                device = place.at(near, place.c) if axis == "near" else place.device(axis)
                copy = remote(
                    source, held.at[there, part], leave.at[zs, k, h], arrive.at[there, h], device
                )
                run(condition, copy.start)
                pending.append((condition, copy))
        if not ar and j == 0:
            keep.wait()
        pick(ar, zs)
        side.event()
    for condition, copy in pending:
        run(condition, copy.wait_send)

    def arrived(i, carry):
        xs, cs, ys = i // 16, i // 8 % 2, i % 2
        inside = (cs == place.c) & jnp.where(place.c == 0, ys == place.y, xs == place.x)

        @pl.when(~inside)
        def _():
            window = picked.at[i]
            remote(window, window, pick_out.at[0, 0], pick_in.at[i], place.device("c")).wait_recv()

        return carry

    lax.fori_loop(0, 32, arrived, 0)
    for k, copy in enumerate(finish):
        if k % 4 == 3:
            copy.wait()
        else:
            copy.wait_send()
    if has_small:
        end_small()


def dispatch(experts, shards, number, tok, sel, small=None, extra=None):
    rows, width = tok.shape
    devices = experts * shards
    extra = extra or Extra()
    space = pl.BlockSpec(memory_space=pl.ANY)
    vmem = pl.BlockSpec(memory_space=pltpu.VMEM)
    dma = pltpu.SemaphoreType.DMA
    has_small = int(small is not None)
    operands, in_specs = [tok, sel], [space, vmem]
    out_shape = [jax.ShapeDtypeStruct((devices, SLOTS, width), jnp.bfloat16)]
    scratch = [
        pltpu.VMEM((8, rows, width), jnp.bfloat16),
        pltpu.VMEM((8, 4 * SLOTS, width), jnp.bfloat16),
        dma((8, HALVES)),
        dma((4, 3, HALVES)),
        dma((8, 3)),
        dma((devices,)),
        dma((9,)),
    ]
    if has_small:
        operands.append(small)
        in_specs.append(space)
        out_shape.append(jax.ShapeDtypeStruct((devices,) + small.shape, small.dtype))
        scratch += [dma((devices,)), dma((devices,)), dma((1,))]
    return pl.pallas_call(
        functools.partial(dispatch_kernel, (experts, shards), has_small, extra),
        out_shape=out_shape + extra.outs,
        in_specs=in_specs + extra.in_specs,
        out_specs=[space] * len(out_shape) + extra.out_specs,
        scratch_shapes=scratch + extra.scratch,
        compiler_params=pltpu.CompilerParams(
            collective_id=number, has_side_effects=True, vmem_limit_bytes=60 * 2**20
        ),
        name="dispatch",
    )(*operands, *extra.operands)


def combine_kernel(dims, has_small, extra, *refs):
    counts = (
        2 + has_small, len(extra.operands), 1 + has_small, len(extra.outs), 10 + 3 * has_small,
        len(extra.scratch),
    )
    ins, more_in, outs, more_out, scratch, more_scratch = split(refs, counts)
    weighted, sel = ins[:2]
    total = outs[0]
    rows4, acc, beside, chain, rows_in, rows_out, beside_in, beside_out, chain_in, chain_out = scratch[:10]
    place = Place()
    width = total.shape[1]
    near, far = place.line()
    mine = (place.x, place.y)
    if has_small:
        greet_all(place, *dims)
        end_small = exchange_small(
            place, dims, lambda i: ins[2].at[i], outs[1], scratch[10], scratch[11], scratch[12].at[0]
        )
    else:
        greet(place)
    side = Side(extra.steps(*more_in, *more_out, *more_scratch), 8)
    other = 1 - place.c
    homes = ((mine, place.c), (mine, other), (far, place.c), (near, other))

    def row_copy(ar, zs, k):
        chip, core = homes[k]
        source = weighted.at[block_number(chip, core, ar, zs)]
        block = ar * 4 + zs
        window = rows4.at[block, pl.ds(k * SLOTS, SLOTS)]
        if k == 0:
            return pltpu.make_async_copy(source, window, rows_in.at[block, 0])
        return remote(
            source, window, rows_out.at[block, k - 1], rows_in.at[block, k], place.at(chip, core)
        )

    def send_rows(i):
        ar, j = BACK[i]
        for k in (2, 3, 1, 0):
            row_copy(ar, place.ranked(j), k).start()

    for i in range(AHEAD):
        send_rows(i)
    pending = []
    half = total.shape[0] // HALVES
    for i, (ar, j) in enumerate(BACK):
        zs = place.ranked(j)
        block = ar * 4 + zs
        for k in range(4):
            copy = row_copy(ar, zs, k)
            if k == 0:
                copy.wait()
            else:
                copy.wait_recv()
                copy.wait_send()
        if i + AHEAD < 8:
            send_rows(i + AHEAD)
        last = not ar and j == 0
        above = (zs <= place.z) & (place.z < 3)
        below = (zs >= place.z) & (place.z > 0)
        below_slot = jnp.where(zs == place.z, 4, zs)
        for h in range(HALVES):
            part = pl.ds(h * half, half)
            if not ar:
                window = beside.at[zs, part]
                remote(
                    window, window, beside_out.at[zs, h], beside_in.at[zs, h], place.device("c")
                ).wait_recv()
                for condition, slot in ((above, zs), (below, below_slot)):
                    window = chain.at[slot, part]
                    got = remote(
                        window, window, chain_out.at[0, h], chain_in.at[slot, h], place.device("c")
                    )
                    run(condition, got.wait_recv)

            def tile(t, carry):
                columns = pl.ds(pl.multiple_of(t * 512, 512), 512)
                dense = jnp.dot(
                    sel[block, part], rows4[block, :, columns], preferred_element_type=jnp.float32
                )
                if not ar:
                    dense = dense + beside[zs, part, columns].astype(jnp.float32)
                if last:
                    total[part, columns] = dense
                else:
                    acc[block, part, columns] = dense.astype(jnp.bfloat16)
                return carry

            lax.fori_loop(0, width // 512, tile, 0)
            if not ar:

                def add(slot):
                    def step(t, carry):
                        here = pl.ds(pl.multiple_of(h * half + t * 16, 16), 16)
                        more = chain[slot, here].astype(jnp.float32)
                        if last:
                            total[here] += more
                        else:
                            acc[block, here] = (acc[block, here].astype(jnp.float32) + more).astype(
                                jnp.bfloat16
                            )
                        return carry

                    lax.fori_loop(0, half // 16, step, 0)

                run(above, functools.partial(add, zs))
                run(below, functools.partial(add, below_slot))
            if ar:
                copy = remote(
                    acc.at[block, part], beside.at[zs, part], beside_out.at[zs, h],
                    beside_in.at[zs, h], place.at(near, place.c),
                )
                copy.start()
                pending.append((None, copy))
            elif not last:
                there = jnp.where(zs == place.z + 1, 4, zs)
                for condition, axis, slot in (
                    (zs < place.z, DOWN, zs),
                    (zs > place.z, UP, there),
                ):
                    copy = remote(
                        acc.at[block, part], chain.at[slot, part], chain_out.at[zs, h],
                        chain_in.at[slot, h], place.device(axis),
                    )
                    run(condition, copy.start)
                    pending.append((condition, copy))
        side.event()
    for condition, copy in pending:
        run(condition, copy.wait_send)
    if has_small:
        end_small()


def combine(experts, shards, number, weighted, sel, small=None, extra=None):
    rows = sel.shape[1]
    width = weighted.shape[-1]
    devices = experts * shards
    extra = extra or Extra()
    space = pl.BlockSpec(memory_space=pl.ANY)
    vmem = pl.BlockSpec(memory_space=pltpu.VMEM)
    dma = pltpu.SemaphoreType.DMA
    low = jnp.bfloat16
    has_small = int(small is not None)
    operands, in_specs = [weighted, sel], [space, vmem]
    out_shape, out_specs = [jax.ShapeDtypeStruct((rows, width), jnp.float32)], [vmem]
    scratch = [
        pltpu.VMEM((8, 4 * SLOTS, width), low),
        pltpu.VMEM((8, rows, width), low),
        pltpu.VMEM((4, rows, width), low),
        pltpu.VMEM((5, rows, width), low),
        dma((8, 4)),
        dma((8, 3)),
        dma((4, HALVES)),
        dma((4, HALVES)),
        dma((5, HALVES)),
        dma((4, HALVES)),
    ]
    if has_small:
        operands.append(small)
        in_specs.append(space)
        out_shape.append(jax.ShapeDtypeStruct(small.shape, small.dtype))
        out_specs.append(space)
        scratch += [dma((devices,)), dma((devices,)), dma((1,))]
    return pl.pallas_call(
        functools.partial(combine_kernel, (experts, shards), has_small, extra),
        out_shape=out_shape + extra.outs,
        in_specs=in_specs + extra.in_specs,
        out_specs=out_specs + extra.out_specs,
        scratch_shapes=scratch + extra.scratch,
        compiler_params=pltpu.CompilerParams(
            collective_id=number, has_side_effects=True, vmem_limit_bytes=60 * 2**20
        ),
        name="combine",
    )(*operands, *extra.operands)


FLAT = ("zy", "yz")
CHUNKS = 4


def flat_parts(rows):
    return (0, rows * 3 // 4), (rows * 3 // 4, rows - rows * 3 // 4)


def send_around(place, experts, shards, src_of, dst, out_sems, in_sems, across):
    count = experts * shards if across else shards
    me = place.e * shards + place.f if across else place.f

    def copy(i, sending):
        other = lax.rem(me + i, count)
        if across:
            device = (other // shards, lax.rem(other, shards))
        else:
            device = (place.e, other)
        source = me if sending else other
        return remote(src_of(other), dst.at[source], out_sems.at[i], in_sems.at[source], device)

    def start(i, carry):
        copy(i, True).start()
        return carry

    def finish(i, carry):
        done = copy(i, False)
        done.wait_send()
        done.wait_recv()
        return carry

    lax.fori_loop(1, count, start, 0)
    return lambda: lax.fori_loop(1, count, finish, 0)


def gather_kernel(
    dims, flat, tall, tok, pack, ids, flat_all, tall_all, tok_all, pack_all, ids_all,
    flat_in, flat_out, tall_in, tall_out, tok_in, tok_out, pack_in, pack_out, ids_in, ids_out, local,
):
    experts, shards = dims
    place = Place()
    greet_all(place, experts, shards)
    me = place.e * shards + place.f
    starts, sizes = flat_parts(flat.shape[0])
    chunk = tall.shape[0] // CHUNKS
    pending = []
    keeps = [
        pltpu.make_async_copy(flat, flat_all.at[place.f], local.at[0]),
        pltpu.make_async_copy(tok, tok_all.at[place.e], local.at[1]),
        pltpu.make_async_copy(pack, pack_all.at[place.f], local.at[2]),
        pltpu.make_async_copy(ids, ids_all.at[me], local.at[3]),
    ]

    def go(condition, copy):
        run(condition, copy.start)
        pending.append((condition, copy))

    def both(a, b):
        return b if a is None else (a if b is None else a & b)

    def flat_item(p, j, yr):
        zs = place.ranked(j)
        source = zs * 2 + (1 - place.y if yr else place.y)
        first = j == 0 and yr == 0
        window = flat_all.at[source, pl.ds(starts[p], sizes[p])]
        src = flat.at[pl.ds(starts[p], sizes[p])] if first else window
        if not first:
            remote(
                window, window, flat_out.at[p, source, 0], flat_in.at[p, source], place.device("c")
            ).wait_recv()
        for axis, condition in links(place, FLAT[p], j, 0, yr, zs):
            go(
                condition,
                remote(
                    src,
                    window,
                    flat_out.at[p, source, LINK[axis]],
                    flat_in.at[p, source],
                    place.device(axis),
                ),
            )

    owner = place.z == place.e

    distance = jnp.abs(place.z - place.e)

    def tall_round(r):
        k = r - distance
        live = (k >= 0) & (k < CHUNKS)
        k = jnp.clip(k, 0, CHUNKS - 1)
        piece = pl.ds(pl.multiple_of(k * chunk, chunk), chunk)
        window = tall_all.at[place.y, piece]

        @pl.when(live & ~owner)
        def _():
            remote(window, window, tall_out.at[k, 0], tall_in.at[0, k], place.device("c")).wait_recv()

        for mine in (True, False):
            src = tall.at[piece] if mine else window
            role = live & (owner if mine else ~owner)
            for axis, condition in (
                (UP, (place.z >= place.e) & (place.z < 3)),
                (DOWN, (place.z <= place.e) & (place.z > 0)),
                ("y", None),
            ):
                go(
                    both(role, condition),
                    remote(
                        src,
                        window,
                        tall_out.at[k, LINK[axis]],
                        tall_in.at[1 if axis == "y" else 0, k],
                        place.device(axis),
                    ),
                )

    flat_item(0, 0, 0)
    flat_item(1, 0, 0)
    go(None, remote(tok, tok_all.at[place.e], tok_out.at[0], tok_in.at[place.e], place.device("x")))
    go(None, remote(tok, tok_all.at[place.e], tok_out.at[1], tok_in.at[place.e], place.device("c")))
    end_pack = send_around(
        place, experts, shards, lambda i: pack, pack_all, pack_out, pack_in, False
    )
    end_ids = send_around(place, experts, shards, lambda i: ids, ids_all, ids_out, ids_in, True)
    for keep in keeps:
        keep.start()
    keep_tall = pltpu.make_async_copy(tall, tall_all.at[place.y], local.at[4])
    run(owner, keep_tall.start)
    across = (1 - place.x) * 2 + place.c
    window = tok_all.at[across]
    relay = remote(window, window, tok_out.at[2], tok_in.at[across], place.device("c"))
    tall_round(0)
    flat_item(1, 0, 1)
    flat_item(0, 1, 0)
    tall_round(1)
    flat_item(0, 2, 0)
    tall_round(2)
    flat_item(1, 1, 0)
    flat_item(1, 1, 1)
    relay.wait_recv()
    go(None, relay)
    flat_item(0, 3, 0)
    tall_round(3)
    flat_item(1, 2, 0)
    flat_item(1, 2, 1)
    tall_round(4)
    flat_item(1, 3, 0)
    flat_item(1, 3, 1)
    tall_round(5)
    tall_round(6)
    for j in range(4):
        flat_item(0, j, 1)
    for k in range(CHUNKS):
        window = tall_all.at[1 - place.y, pl.ds(k * chunk, chunk)]
        remote(window, window, tall_out.at[k, 0], tall_in.at[1, k], place.device("c")).wait_recv()
    for source in (place.x * 2 + 1 - place.c, (1 - place.x) * 2 + 1 - place.c):
        window = tok_all.at[source]
        remote(window, window, tok_out.at[2], tok_in.at[source], place.device("c")).wait_recv()
    for condition, copy in pending:
        run(condition, copy.wait_send)
    end_pack()
    end_ids()
    for keep in keeps:
        keep.wait()
    run(owner, keep_tall.wait)


def gather(experts, shards, number, flat, tall, tok, pack, ids):
    space = pl.BlockSpec(memory_space=pl.ANY)
    dma = pltpu.SemaphoreType.DMA
    devices = experts * shards

    def shape(lead, a):
        return jax.ShapeDtypeStruct((lead,) + a.shape, a.dtype)

    return pl.pallas_call(
        functools.partial(gather_kernel, (experts, shards)),
        out_shape=[
            shape(shards, flat),
            shape(2, tall),
            shape(experts, tok),
            shape(shards, pack),
            shape(devices, ids),
        ],
        in_specs=[space] * 5,
        out_specs=[space] * 5,
        scratch_shapes=[
            dma((2, shards)),
            dma((2, shards, 4)),
            dma((2, CHUNKS)),
            dma((CHUNKS, 4)),
            dma((experts,)),
            dma((3,)),
            dma((shards,)),
            dma((shards,)),
            dma((devices,)),
            dma((devices,)),
            dma((5,)),
        ],
        compiler_params=pltpu.CompilerParams(
            collective_id=number, has_side_effects=True, vmem_limit_bytes=16 * 2**20
        ),
        name="gather",
    )(flat, tall, tok, pack, ids)


def add_rows(acc, first, window, rows, step=16):
    def add(i, carry):
        here = pl.ds(pl.multiple_of(i * step, step), step)
        at = pl.ds(pl.multiple_of(first + i * step, step), step)
        acc[at] = (acc[at].astype(jnp.float32) + window[here].astype(jnp.float32)).astype(acc.dtype)
        return carry

    lax.fori_loop(0, rows // step, add, 0)


def reduce_kernel(
    dims, flat, tall, pack, partial, out_q, out_k, out_v, tall_out, pack_all, total,
    acc, tacc, yslot, zslot, yone, zall, ty, tz,
    load, yin, zin, yone_in, zall_in, ty_in, tz_in, flat_send, tall_send, spread_in, spread_out,
    tall_in, keep_tall, local,
    group_acc, group_near, group_cross, group_load, group_out, group_in, cross_out, cross_in,
):
    experts, shards = dims
    place = Place()
    greet_all(place, experts, shards)
    me = place.e * shards + place.f
    tall_keeps = []
    owner = place.z == place.e
    home = place.x == place.z // 2
    same = place.c == place.z % 2
    starts, sizes = flat_parts(flat.shape[1])
    sizes = (sizes[0], sizes[1] + pack.shape[1])
    height = tall.shape[1]
    chunk = height // CHUNKS
    part = partial.shape[1] // CHUNKS
    pending = []

    def go(condition, copy):
        run(condition, copy.start)
        pending.append((condition, copy))

    def both(a, b):
        return a if b is None else a & b

    load_tall = pltpu.make_async_copy(tall, tacc, load.at[0])
    load_flat = pltpu.make_async_copy(flat, acc.at[:, pl.ds(0, flat.shape[1])], load.at[1])
    load_pack = pltpu.make_async_copy(
        pack, acc.at[:, pl.ds(flat.shape[1], pack.shape[1])], load.at[2]
    )
    across_y = []
    order = (3, 2, 1, 0)

    def add_tall(k):
        piece = pl.ds(k * chunk, chunk)
        across_y.append(
            remote(
                tall.at[1 - place.y, piece], ty.at[piece], tall_send.at[0, k], ty_in.at[k],
                place.device("y"),
            )
        )

    def add_flat(j):
        target = place.ranked(j) * 2 + 1 - place.y
        across_y.append(
            remote(
                flat.at[target, pl.ds(starts[0], sizes[0])],
                yslot.at[place.ranked(j)],
                flat_send.at[0, target],
                yin.at[place.ranked(j)],
                place.device("y"),
            )
        )

    add_tall(0)
    add_tall(1)
    add_flat(3)
    add_tall(2)
    add_flat(2)
    add_tall(3)
    add_flat(1)
    add_flat(0)
    started = [0]

    def feed(count):
        while started[0] < min(count + 2, len(across_y)):
            if started[0] >= 2:
                across_y[started[0] - 2].wait_send()
            across_y[started[0]].start()
            started[0] += 1

    feed(0)
    load_tall.start()
    load_flat.start()
    load_pack.start()
    group_sends = []
    group_loads = []
    for half in (1 - place.x, place.x):
        for i in range(CHUNKS):
            piece = pl.ds(i * part, part)
            copy = remote(
                partial.at[half * 2 + 1 - place.c, piece], group_near.at[half, piece],
                group_out.at[half, i], group_in.at[half, i], place.device("c"),
            )
            copy.start()
            group_sends.append(copy)
            copy = pltpu.make_async_copy(
                partial.at[half * 2 + place.c, piece], group_acc.at[half, piece],
                group_load.at[half, i],
            )
            copy.start()
            group_loads.append(copy)

    def group_half(index, half):
        for i in range(CHUNKS):
            piece = pl.ds(i * part, part)
            window = group_near.at[half, piece]
            group_loads[index * CHUNKS + i].wait()
            remote(
                window, window, group_out.at[half, i], group_in.at[half, i], place.device("c")
            ).wait_recv()
            add_rows(group_acc.at[half], i * part, window, part)
            if index == 0:
                copy = remote(
                    group_acc.at[half, piece], group_cross.at[piece], cross_out.at[i],
                    cross_in.at[i], place.device("x"),
                )
                copy.start()
                group_sends.append(copy)

    def group_end():
        for i in range(CHUNKS):
            window = group_cross.at[pl.ds(i * part, part)]
            remote(window, window, cross_out.at[i], cross_in.at[i], place.device("c")).wait_recv()

            def add(t, carry):
                here = pl.ds(pl.multiple_of(i * part + t * 16, 16), 16)
                own = group_acc[place.x, here].astype(jnp.float32)
                total[here] = own + group_cross[here].astype(jnp.float32)
                return carry

            lax.fori_loop(0, part // 16, add, 0)

    load_tall.wait()
    load_flat.wait()
    load_pack.wait()

    def into(slots, sems, zd, side):
        index = jnp.where(zd == place.z, 4, zd) if side == BELOW else zd
        return slots.at[index], sems.at[index]

    def out_to(slots, sems, zd, side):
        there = place.z - 1 if side == ABOVE else place.z + 1
        index = jnp.where(zd == there, 4, zd) if side == BELOW else zd
        return slots.at[index], sems.at[index]

    def line(j, p, first, slots, sems, send_sem, target):
        zd = place.ranked(j)
        rows = sizes[p]
        for side, condition in (
            (ABOVE, (zd <= place.z) & (place.z < 3)),
            (BELOW, (zd >= place.z) & (place.z > 0)),
        ):
            window, sem = into(slots, sems, zd, side)

            def take(window=window, sem=sem):
                remote(window, window, send_sem, sem, place.device("c")).wait_recv()
                add_rows(acc.at[target], first, window, rows)

            if j == 0:
                condition = place.z < 3 if side == ABOVE else place.z > 0
            run(condition, take)
        if j == 0:
            return
        for side, axis, condition in ((ABOVE, DOWN, zd < place.z), (BELOW, UP, zd > place.z)):
            window, sem = out_to(slots, sems, zd, side)
            go(
                condition,
                remote(acc.at[target, pl.ds(first, rows)], window, send_sem, sem, place.device(axis)),
            )

    above_e, below_e = place.z > place.e, place.z < place.e
    hops = jnp.where(above_e, 3 - place.z, jnp.where(below_e, place.z, jnp.maximum(place.e, 3 - place.e)))

    def tall_round(r):
        k = r - hops
        live = (k >= 0) & (k < CHUNKS)
        k = jnp.clip(k, 0, CHUNKS - 1)
        first = pl.multiple_of(k * chunk, chunk)
        piece = pl.ds(first, chunk)

        @pl.when(live)
        def _():
            remote(
                ty.at[piece], ty.at[piece], tall_send.at[0, k], ty_in.at[k], place.device("c")
            ).wait_recv()
            add_rows(tacc.at[place.y], first, ty.at[piece], chunk)

        for index, condition in (
            (0, (place.z >= place.e) & (place.z < 3)),
            (1, (place.z <= place.e) & (place.z > 0)),
        ):
            window = tz.at[index, piece]

            def take(window=window, index=index):
                remote(
                    window, window, tall_send.at[1, k], tz_in.at[index, k], place.device("c")
                ).wait_recv()
                add_rows(tacc.at[place.y], first, window, chunk)

            run(live & condition, take)
        for index, axis, condition in ((0, DOWN, above_e), (1, UP, below_e)):
            go(
                live & condition,
                remote(
                    tacc.at[place.y, piece], tz.at[index, piece], tall_send.at[1, k],
                    tz_in.at[index, k], place.device(axis),
                ),
            )
        piece_out = tall_out.at[piece]
        keep = pltpu.make_async_copy(tacc.at[place.y, piece], piece_out, keep_tall.at[k])
        run(live & owner, keep.start)
        tall_keeps.append((live & owner, keep))
        for row, axis in ((2, "x"), (3, "c")):
            go(
                live & owner,
                remote(
                    tacc.at[place.y, piece], piece_out, tall_send.at[row, k], tall_in.at[k],
                    place.device(axis),
                ),
            )

    def flat_first(j):
        zd = place.ranked(j)
        target = zd * 2 + place.y
        window = yslot.at[zd]
        remote(window, window, flat_send.at[0, target], yin.at[zd], place.device("c")).wait_recv()
        add_rows(acc.at[target], starts[0], window, sizes[0])
        line(j, 0, starts[0], zslot, zin, flat_send.at[0, target], target)

    def flat_second(j, yr):
        zd = place.ranked(j)
        target = zd * 2 + (1 - place.y if yr else place.y)
        line(j, 1, starts[1], zall.at[yr], zall_in.at[yr], flat_send.at[1, target], target)

    flat_second(3, 1)
    flat_second(3, 0)
    tall_round(0)
    feed(1)
    tall_round(1)
    feed(2)
    flat_second(2, 1)
    flat_second(2, 0)
    flat_first(3)
    feed(3)
    group_half(0, 1 - place.x)
    tall_round(2)
    feed(4)
    flat_second(1, 1)
    flat_second(1, 0)
    flat_first(2)
    feed(5)
    tall_round(3)
    feed(6)
    flat_first(1)
    group_half(1, place.x)
    flat_second(0, 1)
    other = place.z * 2 + 1 - place.y
    go(
        None,
        remote(
            acc.at[other, pl.ds(starts[1], sizes[1])], yone, flat_send.at[1, other], yone_in.at[0],
            place.device("y"),
        ),
    )
    flat_second(0, 0)
    flat_first(0)
    remote(yone, yone, flat_send.at[1, other], yone_in.at[0], place.device("c")).wait_recv()
    add_rows(acc.at[place.f], starts[1], yone, sizes[1])
    cuts = []
    first = 0
    for out in (out_q, out_k, out_v):
        wide = out.shape[1] // experts
        cuts.append((out, pl.ds(0, flat.shape[1]), pl.ds(first, wide)))
        first += wide
    cuts.append((pack_all, pl.ds(flat.shape[1], pack.shape[1]), pl.ds(0, first)))

    def window_of(i, source):
        out = cuts[i][0]
        if i == 3:
            return out.at[source]
        wide = out.shape[1] // experts
        return out.at[:, pl.ds(pl.multiple_of(source * wide, 128), wide)]

    flat_keeps = []
    for i, (out, high, wide) in enumerate(cuts):
        done = acc.at[place.f, high, wide]
        keep = pltpu.make_async_copy(done, window_of(i, place.e), local.at[1 + i])
        keep.start()
        flat_keeps.append(keep)
        for row, axis in enumerate(("x", "c")):
            go(
                None,
                remote(
                    done, window_of(i, place.e), spread_out.at[row, i], spread_in.at[place.e, i],
                    place.device(axis),
                ),
            )
    tall_round(4)
    tall_round(5)
    tall_round(6)
    group_end()
    across = (1 - place.x) * 2 + place.c
    for i in range(4):
        window = window_of(i, across)
        relay = remote(window, window, spread_out.at[2, i], spread_in.at[across, i], place.device("c"))
        relay.wait_recv()
        go(None, relay)
    for k in range(CHUNKS):
        window = tall_out.at[pl.ds(k * chunk, chunk)]
        tall_relay = remote(window, window, tall_send.at[4, k], tall_in.at[k], place.device("c"))
        run(~owner, tall_relay.wait_recv)
        go(~home & same, tall_relay)
    for source in (place.x * 2 + 1 - place.c, (1 - place.x) * 2 + 1 - place.c):
        for i in range(4):
            window = window_of(i, source)
            remote(
                window, window, spread_out.at[2, i], spread_in.at[source, i], place.device("c")
            ).wait_recv()
    for copy in across_y[-2:]:
        copy.wait_send()
    for condition, copy in pending:
        run(condition, copy.wait_send)
    for keep in flat_keeps:
        keep.wait()
    for condition, keep in tall_keeps:
        run(condition, keep.wait)
    for copy in group_sends:
        copy.wait_send()


def reduce(experts, shards, number, flat, tall, pack, partial):
    space = pl.BlockSpec(memory_space=pl.ANY)
    dma = pltpu.SemaphoreType.DMA
    _, sizes = flat_parts(flat.shape[1])
    more = sizes[1] + pack.shape[1]
    width, wide = flat.shape[2], tall.shape[2]
    low = jnp.bfloat16
    return pl.pallas_call(
        functools.partial(reduce_kernel, (experts, shards)),
        out_shape=[
            jax.ShapeDtypeStruct((flat.shape[1], experts * (width - 2 * HEAD_SIZE)), low),
            jax.ShapeDtypeStruct((flat.shape[1], experts * HEAD_SIZE), low),
            jax.ShapeDtypeStruct((flat.shape[1], experts * HEAD_SIZE), low),
            jax.ShapeDtypeStruct(tall.shape[1:], low),
            jax.ShapeDtypeStruct((experts,) + pack.shape[1:], low),
            jax.ShapeDtypeStruct(partial.shape[1:], jnp.float32),
        ],
        in_specs=[space] * 4,
        out_specs=[space] * 5 + [pl.BlockSpec(memory_space=pltpu.VMEM)],
        scratch_shapes=[
            pltpu.VMEM((shards, flat.shape[1] + pack.shape[1], width), low),
            pltpu.VMEM(tall.shape, low),
            pltpu.VMEM((4, sizes[0], width), low),
            pltpu.VMEM((5, sizes[0], width), low),
            pltpu.VMEM((more, width), low),
            pltpu.VMEM((2, 5, more, width), low),
            pltpu.VMEM(tall.shape[1:], low),
            pltpu.VMEM((2,) + tall.shape[1:], low),
            dma((3,)),
            dma((4,)),
            dma((5,)),
            dma((1,)),
            dma((2, 5)),
            dma((CHUNKS,)),
            dma((2, CHUNKS)),
            dma((2, shards)),
            dma((5, CHUNKS)),
            dma((experts, 4)),
            dma((3, 4)),
            dma((CHUNKS,)),
            dma((CHUNKS,)),
            dma((5,)),
            pltpu.VMEM((2,) + partial.shape[1:], low),
            pltpu.VMEM((2,) + partial.shape[1:], low),
            pltpu.VMEM(partial.shape[1:], low),
            dma((2, CHUNKS)),
            dma((2, CHUNKS)),
            dma((2, CHUNKS)),
            dma((CHUNKS,)),
            dma((CHUNKS,)),
        ],
        compiler_params=pltpu.CompilerParams(
            collective_id=number, has_side_effects=True, vmem_limit_bytes=48 * 2**20
        ),
        name="reduce",
    )(flat, tall, pack, partial)


def group_gather_kernel(tok, out, x_out, x_in, c_out, c_in, relay_out, relay_in, local):
    place = Place()
    greet(place)
    across = (1 - place.x) * 2 + place.c
    chunk = tok.shape[0] // CHUNKS
    keep = pltpu.make_async_copy(tok, out.at[place.e], local.at[0])
    near = remote(tok, out.at[place.e], c_out.at[0], c_in.at[0], place.device("c"))
    copies = []
    for k in range(CHUNKS):
        piece = pl.ds(k * chunk, chunk)
        copies.append(
            remote(tok.at[piece], out.at[place.e, piece], x_out.at[k], x_in.at[k], place.device("x"))
        )
        copies[-1].start()
    near.start()
    keep.start()
    for k in range(CHUNKS):
        window = out.at[across, pl.ds(k * chunk, chunk)]
        remote(window, window, x_out.at[k], x_in.at[k], place.device("c")).wait_recv()
        relay = remote(window, window, relay_out.at[k], relay_in.at[k], place.device("c"))
        relay.start()
        copies.append(relay)
    for k in range(CHUNKS):
        window = out.at[(1 - place.x) * 2 + 1 - place.c, pl.ds(k * chunk, chunk)]
        remote(window, window, relay_out.at[k], relay_in.at[k], place.device("c")).wait_recv()
    near.wait()
    keep.wait()
    for copy in copies:
        copy.wait_send()


def group_gather(number, tok):
    space = pl.BlockSpec(memory_space=pl.ANY)
    dma = pltpu.SemaphoreType.DMA
    return pl.pallas_call(
        group_gather_kernel,
        out_shape=jax.ShapeDtypeStruct((4,) + tok.shape, tok.dtype),
        in_specs=[space],
        out_specs=space,
        scratch_shapes=[
            dma((CHUNKS,)), dma((CHUNKS,)), dma((1,)), dma((1,)), dma((CHUNKS,)), dma((CHUNKS,)), dma((1,)),
        ],
        compiler_params=pltpu.CompilerParams(
            collective_id=number, has_side_effects=True, vmem_limit_bytes=16 * 2**20
        ),
        name="group_gather",
    )(tok)


def group_scatter_kernel(
    partial, total, acc, near, cross, load_in, near_out, near_in, x_out, x_in
):
    place = Place()
    greet(place)
    rows = partial.shape[1]
    chunk = rows // CHUNKS
    sends = []
    loads = []
    for half in (1 - place.x, place.x):
        for k in range(CHUNKS):
            piece = pl.ds(k * chunk, chunk)
            copy = remote(
                partial.at[half * 2 + 1 - place.c, piece], near.at[half, piece], near_out.at[half, k],
                near_in.at[half, k], place.device("c"),
            )
            copy.start()
            sends.append(copy)
            load = pltpu.make_async_copy(
                partial.at[half * 2 + place.c, piece], acc.at[half, piece], load_in.at[half, k]
            )
            load.start()
            loads.append(load)
    for index, half in enumerate((1 - place.x, place.x)):
        for k in range(CHUNKS):
            piece = pl.ds(k * chunk, chunk)
            window = near.at[half, piece]
            loads[index * CHUNKS + k].wait()
            remote(window, window, near_out.at[half, k], near_in.at[half, k], place.device("c")).wait_recv()
            add_rows(acc.at[half], k * chunk, window, chunk)
            if index == 0:
                copy = remote(
                    acc.at[half, piece], cross.at[piece], x_out.at[k], x_in.at[k], place.device("x")
                )
                copy.start()
                sends.append(copy)
    for k in range(CHUNKS):
        window = cross.at[pl.ds(k * chunk, chunk)]
        remote(window, window, x_out.at[k], x_in.at[k], place.device("c")).wait_recv()

        def add(i, carry):
            here = pl.ds(pl.multiple_of(k * chunk + i * 16, 16), 16)
            total[here] = acc[place.x, here].astype(jnp.float32) + cross[here].astype(jnp.float32)
            return carry

        lax.fori_loop(0, chunk // 16, add, 0)
    for copy in sends:
        copy.wait_send()


def group_scatter(number, partial):
    dma = pltpu.SemaphoreType.DMA
    rows, width = partial.shape[1:]
    low = jnp.bfloat16
    return pl.pallas_call(
        group_scatter_kernel,
        out_shape=jax.ShapeDtypeStruct((rows, width), jnp.float32),
        in_specs=[pl.BlockSpec(memory_space=pl.ANY)],
        out_specs=pl.BlockSpec(memory_space=pltpu.VMEM),
        scratch_shapes=[
            pltpu.VMEM((2, rows, width), low),
            pltpu.VMEM((2, rows, width), low),
            pltpu.VMEM((rows, width), low),
            dma((2, CHUNKS)),
            dma((2, CHUNKS)),
            dma((2, CHUNKS)),
            dma((CHUNKS,)),
            dma((CHUNKS,)),
        ],
        compiler_params=pltpu.CompilerParams(
            collective_id=number, has_side_effects=True, vmem_limit_bytes=16 * 2**20
        ),
        name="group_scatter",
    )(partial)


BLOCK = 256


def dot_last(a, b):
    return lax.dot_general(a, b, (((1,), (1,)), ((), ())), preferred_element_type=jnp.float32)


def dot(a, b):
    return jnp.dot(a, b, preferred_element_type=jnp.float32)


def turn(rows):
    lane = lax.broadcasted_iota(jnp.int32, rows.shape, 1)
    half = HEAD_SIZE // 2
    return pltpu.roll(rows, half, 1) * jnp.where(lane < half, -1.0, 1.0)


def mask_block(r, count, ids_column, ids_row, bias):
    queries = pl.ds(r * BLOCK, BLOCK)

    def part(i, carry):
        keys = pl.ds(pl.multiple_of(i * BLOCK, BLOCK), BLOCK)
        key_at = lax.broadcasted_iota(jnp.int32, (BLOCK, BLOCK), 0) + i * BLOCK
        query_at = lax.broadcasted_iota(jnp.int32, (BLOCK, BLOCK), 1) + r * BLOCK
        allowed = (ids_column[keys] == ids_row[:, queries]) & (key_at <= query_at)
        bias[keys] = jnp.where(allowed, 0.0, -1e30)
        return carry

    lax.fori_loop(0, count // BLOCK, part, 0)


def project_steps(
    tok, w_qkv, gain_one, gain_q, gain_k, cosine, sine, normed, raw, query_rot, key_rot, value
):
    heads = query_rot.shape[1] // HEAD_SIZE
    low = jnp.bfloat16

    def rotated(v, rows, gain):
        u = v * inverse_rms(v) * gain
        return (u * cosine[rows] + turn(u) * sine[rows]).astype(low)

    def norm(r):
        def part(i, carry):
            here = pl.ds(pl.multiple_of(r * BLOCK + i * 16, 16), 16)
            x = tok[here].astype(jnp.float32)
            normed[here] = (x * inverse_rms(x) * gain_one[...]).astype(low)
            return carry

        lax.fori_loop(0, BLOCK // 16, part, 0, unroll=2)

    def multiply(r):
        rows = pl.ds(r * BLOCK, BLOCK)

        def pair(i, carry):
            column = pl.ds(pl.multiple_of(i * 2 * HEAD_SIZE, 2 * HEAD_SIZE), 2 * HEAD_SIZE)
            both = dot(normed[rows], w_qkv[:, column])
            raw[rows, column] = both
            for k in range(2):
                at = pl.ds(pl.multiple_of((2 * i + k) * HEAD_SIZE, HEAD_SIZE), HEAD_SIZE)
                one = both[:, k * HEAD_SIZE : (k + 1) * HEAD_SIZE]
                query_rot[rows, at] = rotated(one, rows, gain_q[...])
            return carry

        lax.fori_loop(0, heads // 2, pair, 0)
        last = pl.ds(heads * HEAD_SIZE, 2 * HEAD_SIZE)
        both = dot(normed[rows], w_qkv[:, last])
        raw[rows, last] = both
        key_rot[rows] = rotated(both[:, :HEAD_SIZE], rows, gain_k[...])
        value[rows] = both[:, HEAD_SIZE:].astype(low)

    steps = []
    for r in range(tok.shape[0] // BLOCK):
        steps.append(functools.partial(norm, r))
        steps.append(functools.partial(multiply, r))
    return steps


def attend_steps(query_rot, key_rot, value, ids_column, ids_row, mixed, bias, value_t):
    length = key_rot.shape[0]
    heads = query_rot.shape[1] // HEAD_SIZE
    scale = HEAD_SIZE ** (-0.5)

    def prepare(r):
        if r == 0:
            value_t[...] = value[...].T
        mask_block(r, (r + 1) * BLOCK, ids_column, ids_row, bias)

    def heads_of(r, first, some):
        rows = pl.ds(r * BLOCK, BLOCK)
        count = (r + 1) * BLOCK

        def head(h, carry):
            column = pl.ds(pl.multiple_of(h * HEAD_SIZE, HEAD_SIZE), HEAD_SIZE)
            scores = dot_last(key_rot[:count], query_rot[rows, column]) * scale + bias[:count]
            shifted = jnp.exp(scores - jnp.max(scores, 0, keepdims=True))
            weights = shifted * (1.0 / jnp.sum(shifted, 0, keepdims=True))
            out = dot(value_t[:, :count], weights.astype(jnp.bfloat16))
            mixed[rows, column] = out.T.astype(jnp.bfloat16)
            return carry

        lax.fori_loop(first, first + some, head, 0, unroll=2)

    steps = []
    for r in range(length // BLOCK):
        steps.append(functools.partial(prepare, r))
        some = heads if r == 0 else heads // 2
        for first in range(0, heads, some):
            steps.append(functools.partial(heads_of, r, first, some))
    return steps


def load(pairs, sems):
    copies = [pltpu.make_async_copy(a, b, sems.at[i]) for i, (a, b) in enumerate(pairs)]
    for copy in copies:
        copy.start()
    return copies


def attention(tokens, w_qkv, gain_one, gain_q, gain_k, cosine, sine, ids_column, ids_row, heads):
    length, width = tokens.shape
    wide = w_qkv.shape[1]
    span = heads * HEAD_SIZE
    low, f32 = jnp.bfloat16, jnp.float32
    space, vmem = pl.BlockSpec(memory_space=pl.ANY), pl.BlockSpec(memory_space=pltpu.VMEM)
    shapes = [
        ((length, width), low),
        ((length, wide), f32),
        ((length, span), low),
        ((length, HEAD_SIZE), low),
        ((length, HEAD_SIZE), low),
        ((length, span), low),
    ]

    def steps(*refs):
        ins, outs, scratch = split(refs, (9, 6, 12))
        tok, weight, in_sems, out_sems, bias, value_t = scratch[:6]
        results = scratch[6:]
        copies = load([(ins[0], tok), (ins[1], weight)], in_sems)

        def begin():
            for copy in copies:
                copy.wait()

        saved = []

        def save(picks):
            for i in picks:
                copy = pltpu.make_async_copy(results[i], outs[i], out_sems.at[i])
                copy.start()
                saved.append(copy)

        def end():
            save((5,))
            for copy in saved:
                copy.wait()

        return (
            [begin]
            + project_steps(tok, weight, *ins[2:7], *results[:5])
            + [functools.partial(save, range(5))]
            + attend_steps(*results[2:5], *ins[7:9], results[5], bias, value_t)
            + [end]
        )

    return Extra(
        (tokens, w_qkv, gain_one, gain_q, gain_k, cosine, sine, ids_column, ids_row),
        [space, space] + [vmem] * 7,
        [jax.ShapeDtypeStruct(*shape) for shape in shapes],
        [space] * 6,
        [
            pltpu.VMEM(tokens.shape, low),
            pltpu.VMEM(w_qkv.shape, low),
            pltpu.SemaphoreType.DMA((2,)),
            pltpu.SemaphoreType.DMA((6,)),
            pltpu.VMEM((length, BLOCK), f32),
            pltpu.VMEM((HEAD_SIZE, length), low),
        ]
        + [pltpu.VMEM(*shape) for shape in shapes],
        steps,
    )


def attend_back_steps(
    query_rot, key_rot, value, raw, grad_mixed, ids_column, ids_row, gain_q, gain_k, cosine, sine,
    grad_raw, grad_gains, bias, key_t, grad_key, grad_value, sums,
):
    length = key_rot.shape[0]
    heads = query_rot.shape[1] // HEAD_SIZE
    scale = HEAD_SIZE ** (-0.5)
    low = jnp.bfloat16

    def back(grad, rows, column, gain, index):
        unit = grad * cosine[rows] - turn(grad * sine[rows])
        v = raw[rows, column]
        inverse = inverse_rms(v)
        sums[index] += jnp.sum((unit * v * inverse).reshape(-1, 8, HEAD_SIZE), 0)
        grad_raw[rows, column] = norm_backward(unit, v, inverse, gain).astype(low)

    def prepare(r):
        if r == 0:
            key_t[...] = key_rot[...].T
            grad_key[...] = jnp.zeros_like(grad_key)
            grad_value[...] = jnp.zeros_like(grad_value)
            sums[...] = jnp.zeros_like(sums)
        mask_block(r, (r + 1) * BLOCK, ids_column, ids_row, bias)

    def heads_of(r, first, some):
        rows = pl.ds(r * BLOCK, BLOCK)
        count = (r + 1) * BLOCK

        def head(h, carry):
            column = pl.ds(pl.multiple_of(h * HEAD_SIZE, HEAD_SIZE), HEAD_SIZE)
            query = query_rot[rows, column]
            grad_out = grad_mixed[rows, column]
            scores = dot_last(key_rot[:count], query) * scale + bias[:count]
            shifted = jnp.exp(scores - jnp.max(scores, 0, keepdims=True))
            weights = shifted * (1.0 / jnp.sum(shifted, 0, keepdims=True))
            grad_value[:count] += dot(weights.astype(low), grad_out)
            grad_weights = dot_last(value[:count], grad_out)
            spread = jnp.sum(weights * grad_weights, 0, keepdims=True)
            grad_scores = (weights * (grad_weights - spread)).astype(low)
            grad_key[:count] += dot(grad_scores, query)
            grad_query = dot(key_t[:, :count], grad_scores).T * scale
            back(grad_query, rows, column, gain_q[...], 0)
            return carry

        lax.fori_loop(first, first + some, head, 0, unroll=2)

    def last():
        column = pl.ds(heads * HEAD_SIZE, HEAD_SIZE)
        for r in range(length // BLOCK):
            rows = pl.ds(r * BLOCK, BLOCK)
            back(grad_key[rows] * scale, rows, column, gain_k[...], 1)
            grad_raw[rows, pl.ds((heads + 1) * HEAD_SIZE, HEAD_SIZE)] = grad_value[rows].astype(low)
        grad_gains[...] = jnp.sum(sums[...], 1)

    steps = []
    for r in range(length // BLOCK):
        steps.append(functools.partial(prepare, r))
        some = heads if r == 0 else (heads // 2 if r == 1 else heads // 4)
        for first in range(0, heads, some):
            steps.append(functools.partial(heads_of, r, first, some))
    return steps + [last]


def attention_back(
    query_rot, key_rot, value, raw, grad_mixed, ids_column, ids_row, gain_q, gain_k, cosine, sine
):
    length = key_rot.shape[0]
    low, f32 = jnp.bfloat16, jnp.float32
    space, vmem = pl.BlockSpec(memory_space=pl.ANY), pl.BlockSpec(memory_space=pltpu.VMEM)
    operands = (
        query_rot, key_rot, value, raw, grad_mixed, ids_column, ids_row, gain_q, gain_k, cosine, sine,
    )

    def steps(*refs):
        ins, outs, scratch = split(refs, (11, 2, 13))
        held, (in_sems, out_sems, result), work = split(scratch, (5, 3, 5))
        copies = load(list(zip(ins[:5], held)), in_sems)

        def begin():
            for copy in copies:
                copy.wait()

        def end():
            copy = pltpu.make_async_copy(result, outs[0], out_sems.at[0])
            copy.start()
            copy.wait()

        return [begin] + attend_back_steps(*held, *ins[5:], result, outs[1], *work) + [end]

    return Extra(
        operands,
        [space] * 5 + [vmem] * 6,
        [jax.ShapeDtypeStruct(raw.shape, low), jax.ShapeDtypeStruct((2, HEAD_SIZE), f32)],
        [space, vmem],
        [pltpu.VMEM(a.shape, a.dtype) for a in operands[:5]]
        + [
            pltpu.SemaphoreType.DMA((5,)),
            pltpu.SemaphoreType.DMA((1,)),
            pltpu.VMEM(raw.shape, low),
            pltpu.VMEM((length, BLOCK), f32),
            pltpu.VMEM((HEAD_SIZE, length), low),
            pltpu.VMEM((length, HEAD_SIZE), f32),
            pltpu.VMEM((length, HEAD_SIZE), f32),
            pltpu.VMEM((2, 8, HEAD_SIZE), f32),
        ],
        steps,
    )


def weight_grads(rows, grad_result, inner, grad_a, grad_b):
    count, width = rows.shape
    inside = inner.shape[1]
    low, f32 = jnp.bfloat16, jnp.float32
    space = pl.BlockSpec(memory_space=pl.ANY)
    tiles = width // BLOCK

    def dot_first(a, b):
        return lax.dot_general(a, b, (((0,), (0,)), ((), ())), preferred_element_type=f32)

    def steps(*refs):
        ins, outs, scratch = split(refs, (5, 3, 9))
        a_held, b_held, inner_held, tile, wide, tall, in_sems, tile_sems, out_sems = scratch
        copies = load([(ins[3], a_held), (ins[4], b_held), (ins[2], inner_held)], in_sems)

        def fetch(i):
            source = ins[0] if i < tiles else ins[1]
            columns = pl.ds((i % tiles) * BLOCK, BLOCK)
            return pltpu.make_async_copy(source.at[:, columns], tile.at[i % 2], tile_sems.at[i % 2])

        def store(i, k):
            at = pl.ds((i % tiles) * BLOCK, BLOCK)
            if i < tiles:
                return pltpu.make_async_copy(wide.at[k, i % 2], outs[k].at[at], out_sems.at[k, i % 2])
            return pltpu.make_async_copy(tall.at[i % 2], outs[2].at[:, at], out_sems.at[2, i % 2])

        def begin():
            fetch(0).start()
            for copy in copies:
                copy.wait()

        def prepare(i):
            fetch(i).wait()
            if i + 1 < 2 * tiles:
                fetch(i + 1).start()

        def first(i, k):
            if k == 0:
                prepare(i)
            if i >= 2:
                store(i - 2, k).wait()
            wide[k, i % 2] = dot_first(tile[i % 2], (a_held, b_held)[k][...])
            store(i, k).start()

        def second(i):
            prepare(i)
            if i >= tiles + 2:
                store(i - 2, 2).wait()
            tall[i % 2] = dot_first(inner_held[...], tile[i % 2])
            store(i, 2).start()

        def end():
            for i in (tiles - 2, tiles - 1):
                store(i, 0).wait()
                store(i, 1).wait()
            for i in (2 * tiles - 2, 2 * tiles - 1):
                store(i, 2).wait()

        found = [begin]
        for i in range(tiles):
            found += [functools.partial(first, i, 0), functools.partial(first, i, 1)]
        for i in range(tiles, 2 * tiles):
            found.append(functools.partial(second, i))
        return found + [end]

    return Extra(
        (rows, grad_result, inner, grad_a, grad_b),
        [space] * 5,
        [
            jax.ShapeDtypeStruct((width, inside), f32),
            jax.ShapeDtypeStruct((width, inside), f32),
            jax.ShapeDtypeStruct((inside, width), f32),
        ],
        [space] * 3,
        [
            pltpu.VMEM((count, inside), low),
            pltpu.VMEM((count, inside), low),
            pltpu.VMEM((count, inside), low),
            pltpu.VMEM((2, count, BLOCK), low),
            pltpu.VMEM((2, 2, BLOCK, inside), f32),
            pltpu.VMEM((2, inside, BLOCK), f32),
            pltpu.SemaphoreType.DMA((3,)),
            pltpu.SemaphoreType.DMA((2,)),
            pltpu.SemaphoreType.DMA((3, 2)),
        ],
        steps,
    )


WIDE = 512


def dispatch_expert_kernel(
    dims, tok, sel, small, grads, picks, ids, w_gate, w_up, w_down,
    small_all, rows_out, weighted, grad_result, inner, grad_a, grad_b, grad_rows, gate_grad,
    held, stage, picked, arrive, leave, pick_out, pick_in, local, small_out, small_in,
    gates, weights_in, gate_held, up_held, down_held, g_held, g_in,
    weighted_s, result_s, inner_s, a_s, b_s, rows_s, a_wide, b_wide, store_sems, keep_sems,
):
    experts, shards = dims
    low, f32 = jnp.bfloat16, jnp.float32
    place = Place()
    width = tok.shape[1]
    near, far = place.line()
    mine = (place.x, place.y)
    me = place.e * shards + place.f
    greet_all(place, *dims)
    end_small = exchange_small(
        place, dims, lambda i: small, small_all, small_out, small_in, local.at[1]
    )
    keep = pltpu.make_async_copy(tok, held.at[place.z], local.at[0])
    keep.start()
    loads = load([(w_gate.at[0], gate_held), (w_up.at[0], up_held), (w_down.at[0], down_held)], weights_in)
    pending = []
    targets = (place.device("c"), place.at(far, place.c), place.at(far, 1 - place.c))
    half = tok.shape[0] // HALVES

    def pick(ar, zs):
        block = ar * 4 + zs
        number = block_number(mine, place.c, ar, zs)

        def tile(i, carry):
            columns = pl.ds(pl.multiple_of(i * WIDE, WIDE), WIDE)
            chosen = dot(sel[block], held[block, :, columns]).astype(low)
            picked[number, :, columns] = chosen[:SLOTS]
            stage[block, :, columns] = chosen[SLOTS:]
            return carry

        lax.fori_loop(0, width // WIDE, tile, 0)
        for k in (2, 1, 0):
            away = remote(
                stage.at[block, pl.ds(k * SLOTS, SLOTS)], picked.at[number],
                pick_out.at[block, k], pick_in.at[number], targets[k],
            )
            away.start()
            pending.append((None, away))

    def wait_rows(i):
        xs, cs, ys = i // 16, i // 8 % 2, i % 2
        inside = (cs == place.c) & jnp.where(place.c == 0, ys == place.y, xs == place.x)

        @pl.when(~inside)
        def _():
            window = picked.at[i]
            remote(window, window, pick_out.at[0, 0], pick_in.at[i], place.device("c")).wait_recv()

    def sources(n):
        first = n % 2 * 16 + place.ranked(n // 2) * 2
        return first, first + 8

    def grads_of(n):
        return [
            pltpu.make_async_copy(
                grads.at[pl.ds(first, 2)], g_held.at[n % 2, pl.ds(2 * k, 2)], g_in.at[n % 2, k]
            )
            for k, first in enumerate(sources(n))
        ]

    kept = []
    for copy in grads_of(0):
        copy.start()

    def stores(n):
        pairs = (
            (weighted_s, weighted), (result_s, grad_result), (inner_s, inner), (a_s, grad_a),
            (b_s, grad_b), (rows_s, grad_rows),
        )
        return [
            pltpu.make_async_copy(
                source.at[pl.ds(2 * k, 2)], target.at[pl.ds(first, 2)], store_sems.at[i, k]
            )
            for i, (source, target) in enumerate(pairs)
            for k, first in enumerate(sources(n))
        ]

    def compute(n):
        first, second = sources(n)
        from_devices = (first, first + 1, second, second + 1)
        if n == 0:
            end_small()
            copy = pltpu.make_async_copy(small_all, gates, local.at[2])
            copy.start()
            for done in loads:
                done.wait()
            copy.wait()
        if n + 1 < 8:
            for copy in grads_of(n + 1):
                copy.start()
        for i in from_devices:
            wait_rows(i)
        for k, start in enumerate((first, second)):
            copy = pltpu.make_async_copy(
                picked.at[pl.ds(start, 2)], rows_out.at[pl.ds(start, 2)], keep_sems.at[n, k]
            )
            copy.start()
            kept.append(copy)
        here = []
        for i in from_devices:
            value = jnp.sum(jnp.where(ids[i] == me, gates[i], 0.0), 0, keepdims=True)
            here.append(jnp.sum(picks[i].astype(f32) * value, -1, keepdims=True))
        here = jnp.concatenate(here, 0)
        count = 4 * SLOTS
        x = jnp.concatenate([picked[i] for i in from_devices], 0)
        a_wide[...] = dot(x, gate_held[...])
        b_wide[...] = dot(x, up_held[...])
        for copy in grads_of(n):
            copy.wait()
        if n:
            for copy in stores(n - 1):
                copy.wait()
        inner_low = (jax.nn.silu(a_wide[...]) * b_wide[...]).astype(low)
        inner_s[...] = inner_low.reshape(inner_s.shape)

        def forward(t, found):
            columns = pl.ds(pl.multiple_of(t * WIDE, WIDE), WIDE)
            result = dot(inner_s[...].reshape(count, -1), down_held[:, columns])
            g = g_held[n % 2, :, :, columns].reshape(count, WIDE).astype(f32)
            weighted_s[:, :, columns] = (result * here).astype(low).reshape(4, SLOTS, WIDE)
            result_s[:, :, columns] = (g * here).astype(low).reshape(4, SLOTS, WIDE)
            return found + jnp.sum(result * g, -1, keepdims=True)

        found = lax.fori_loop(0, width // WIDE, forward, jnp.zeros((count, 1), f32))
        for k, i in enumerate(from_devices):
            part = picks[i].astype(f32) * found[k * SLOTS : (k + 1) * SLOTS]
            gate_grad[i] = jnp.broadcast_to(jnp.sum(part, 0, keepdims=True), gate_grad.shape[1:])
        grad_inner = dot_last(result_s[...].reshape(count, width), down_held[...])
        a, b = a_wide[...], b_wide[...]
        sigmoid = jax.nn.sigmoid(a)
        slope = sigmoid * (1.0 + a * (1.0 - sigmoid))
        a_s[...] = (grad_inner * b * slope).astype(low).reshape(a_s.shape)
        b_s[...] = (grad_inner * (a * sigmoid)).astype(low).reshape(b_s.shape)

        def backward(t, carry):
            columns = pl.ds(pl.multiple_of(t * WIDE, WIDE), WIDE)
            total = dot_last(a_s[...].reshape(count, -1), gate_held[columns])
            total += dot_last(b_s[...].reshape(count, -1), up_held[columns])
            rows_s[:, :, columns] = total.astype(low).reshape(4, SLOTS, WIDE)
            return carry

        lax.fori_loop(0, width // WIDE, backward, 0)
        for copy in stores(n):
            copy.start()

    work = {3: (0,), 5: (1,), 6: (2,), 7: (3, 4, 5, 6, 7)}
    for event, (ar, j) in enumerate(FAR_FIRST[::-1]):
        zs = place.ranked(j)
        block = ar * 4 + zs
        for h in range(HALVES):
            part = pl.ds(h * half, half)
            window = held.at[block, part]
            if ar or j:
                remote(
                    window, window, leave.at[zs, 0, h], arrive.at[block, h], place.device("c")
                ).wait_recv()
            if ar:
                continue
            source = tok.at[part] if j == 0 else window
            onward = (
                (UP, zs, 0, (zs <= place.z) & (place.z < 3)),
                (DOWN, zs, 1, (zs >= place.z) & (place.z > 0)),
                ("near", 4 + zs, 2, None),
            )
            for axis, there, k, condition in onward:
                device = place.at(near, place.c) if axis == "near" else place.device(axis)
                copy = remote(
                    source, held.at[there, part], leave.at[zs, k, h], arrive.at[there, h], device
                )
                run(condition, copy.start)
                pending.append((condition, copy))
        if not ar and j == 0:
            keep.wait()
        pick(ar, zs)
        for n in work.get(event, ()):
            compute(n)
    for copy in stores(7):
        copy.wait()
    for copy in kept:
        copy.wait()
    for condition, copy in pending:
        run(condition, copy.wait_send)


def dispatch_expert(experts, shards, number, tok, sel, small, grads, picks, ids, w_gate, w_up, w_down):
    rows, width = tok.shape
    devices = experts * shards
    inside = w_gate.shape[2]
    space = pl.BlockSpec(memory_space=pl.ANY)
    vmem = pl.BlockSpec(memory_space=pltpu.VMEM)
    dma = pltpu.SemaphoreType.DMA
    low, f32 = jnp.bfloat16, jnp.float32

    def lots(columns):
        return jax.ShapeDtypeStruct((devices, SLOTS, columns), low)

    def some(columns):
        return pltpu.VMEM((4, SLOTS, columns), low)

    return pl.pallas_call(
        functools.partial(dispatch_expert_kernel, (experts, shards)),
        out_shape=[
            jax.ShapeDtypeStruct((devices,) + small.shape, f32),
            lots(width), lots(width), lots(width), lots(inside), lots(inside), lots(inside), lots(width),
            jax.ShapeDtypeStruct((devices, 8, rows), f32),
        ],
        in_specs=[space, vmem, space, space, vmem, vmem, space, space, space],
        out_specs=[space] * 8 + [vmem],
        scratch_shapes=[
            pltpu.VMEM((8, rows, width), low),
            pltpu.VMEM((8, 3 * SLOTS, width), low),
            pltpu.VMEM((devices, SLOTS, width), low),
            dma((8, HALVES)),
            dma((4, 3, HALVES)),
            dma((8, 3)),
            dma((devices,)),
            dma((3,)),
            dma((devices,)),
            dma((devices,)),
            pltpu.VMEM((devices,) + small.shape, f32),
            dma((3,)),
            pltpu.VMEM(w_gate.shape[1:], low),
            pltpu.VMEM(w_up.shape[1:], low),
            pltpu.VMEM(w_down.shape[1:], low),
            pltpu.VMEM((2, 4, SLOTS, width), low),
            dma((2, 2)),
            some(width), some(width), some(inside), some(inside), some(inside), some(width),
            pltpu.VMEM((4 * SLOTS, inside), f32),
            pltpu.VMEM((4 * SLOTS, inside), f32),
            dma((6, 2)),
            dma((8, 2)),
        ],
        compiler_params=pltpu.CompilerParams(
            collective_id=number, has_side_effects=True, vmem_limit_bytes=62 * 2**20
        ),
        name="dispatch_expert",
    )(tok, sel, small, grads, picks, ids, w_gate, w_up, w_down)


def local(
    layer_input,
    doc_ids,
    expert_ids,
    w_query,
    w_key,
    w_value,
    w_out,
    w_router,
    gain_attn,
    gain_ffn,
    gain_query,
    gain_key,
    w_gate,
    w_up,
    w_down,
    grad_output,
):
    single_float = jnp.float32
    brain_float_half = jnp.bfloat16
    row_count = layer_input.shape[1]
    width = layer_input.shape[2]
    length_total = doc_ids.shape[1]
    query_groups = QUERY_HEADS // KEY_VALUE_HEADS
    scale = HEAD_SIZE ** (-0.5)
    experts = w_router.shape[1]
    capacity = max(2, 6 * row_count * TOP // (5 * experts))
    pairs = row_count * TOP
    (
        full_query,
        gathered_key,
        full_value,
        full_out,
        full_router,
        gain_one,
        gain_two,
        gain_q,
        key_gain_vector,
    ) = (
        lax.all_gather(w_query, FSDP, axis=0, tiled=True),
        lax.all_gather(w_key, FSDP, axis=0, tiled=True),
        lax.all_gather(w_value, FSDP, axis=0, tiled=True),
        lax.all_gather(w_out, FSDP, axis=0, tiled=True),
        lax.all_gather(w_router, FSDP, axis=0, tiled=True),
        lax.all_gather(gain_attn, FSDP, axis=0, tiled=True),
        lax.all_gather(gain_ffn, FSDP, axis=0, tiled=True),
        lax.all_gather(gain_query, FSDP, axis=0, tiled=True),
        lax.all_gather(gain_key, FSDP, axis=0, tiled=True),
    )
    gain_one = gain_one.astype(single_float)
    gain_two = gain_two.astype(single_float)
    gain_q = gain_q.astype(single_float)
    key_gain_vector = key_gain_vector.astype(single_float)
    inputs = layer_input[0].astype(single_float)
    offset = lax.axis_index(EXPERT) * row_count
    own_pos = offset + jnp.arange(row_count, dtype=jnp.int32)
    all_pos = jnp.arange(length_total, dtype=jnp.int32)
    seq_ids = doc_ids[0]
    own_ids = lax.dynamic_slice_in_dim(seq_ids, offset, row_count)
    allowed = (own_ids[:, None] == seq_ids[None, :]) & (own_pos[:, None] >= all_pos[None, :])
    cosine_table, sine_table = angles(own_pos)
    cosine_table = cosine_table[:, None, :]
    sine_table = sine_table[:, None, :]
    scale_one = inverse_rms(inputs)
    normalized_input = (inputs * scale_one * gain_one).astype(brain_float_half)
    query_raw = jnp.dot(normalized_input, full_query, preferred_element_type=single_float).reshape(
        row_count, QUERY_HEADS, HEAD_SIZE
    )
    key_unnormalized = jnp.dot(
        normalized_input, gathered_key, preferred_element_type=single_float
    ).reshape(row_count, KEY_VALUE_HEADS, HEAD_SIZE)
    value_low = jnp.dot(normalized_input, full_value, preferred_element_type=single_float).astype(
        brain_float_half
    )
    query_scale = inverse_rms(query_raw)
    key_norm_scale = inverse_rms(key_unnormalized)
    query_rot = (
        apply_rotary(query_raw * query_scale * gain_q, cosine_table, sine_table)
        .astype(brain_float_half)
        .reshape(row_count, KEY_VALUE_HEADS, query_groups, HEAD_SIZE)
    )
    key_rotated = apply_rotary(
        key_unnormalized * key_norm_scale * key_gain_vector, cosine_table, sine_table
    ).astype(brain_float_half)
    key_gathered_rows, value_gathered_rows = (
        lax.all_gather(
            key_rotated.reshape(row_count, KEY_VALUE_HEADS * HEAD_SIZE),
            EXPERT,
            axis=0,
            tiled=True,
        ),
        lax.all_gather(value_low, EXPERT, axis=0, tiled=True),
    )
    key_gathered_rows = key_gathered_rows.reshape(length_total, KEY_VALUE_HEADS, HEAD_SIZE)
    value_gathered_rows = value_gathered_rows.reshape(length_total, KEY_VALUE_HEADS, HEAD_SIZE)

    def masked_scores():
        raw = (
            jnp.einsum(
                "tkgd,skd->kgts", query_rot, key_gathered_rows, preferred_element_type=single_float
            )
            * scale
        )
        return jnp.where(allowed, raw, -1e30)

    scores = masked_scores()
    peak = jnp.max(scores, -1, keepdims=True)
    shifted = jnp.exp(scores - peak)
    totals = jnp.sum(shifted, -1, keepdims=True)
    weights_low = (shifted / totals).astype(brain_float_half)
    log_total = peak + jnp.log(totals)
    mixed = (
        jnp.einsum(
            "kgts,skd->tkgd", weights_low, value_gathered_rows, preferred_element_type=single_float
        )
        .reshape(row_count, QUERY_HEADS * HEAD_SIZE)
        .astype(brain_float_half)
    )
    hidden = inputs + jnp.dot(mixed, full_out, preferred_element_type=single_float)
    scale_two = inverse_rms(hidden)
    normed_two = (hidden * scale_two * gain_two).astype(brain_float_half)
    logits = jnp.dot(normed_two, full_router, preferred_element_type=single_float)
    selector = (expert_ids[0][:, :, None] == jnp.arange(experts, dtype=jnp.int32)).astype(
        single_float
    )
    chosen = jnp.einsum("tke,te->tk", selector, logits, precision=HIGHEST)
    gates = jax.nn.softmax(chosen, -1)
    flat_routes = expert_ids[0].reshape(pairs)
    hits = (flat_routes[:, None] == jnp.arange(experts, dtype=jnp.int32)).astype(jnp.int32)
    before = jnp.cumsum(hits, 0) - hits
    ranks = jnp.sum(before * hits, 1)
    slot_index = flat_routes * capacity + ranks
    owner_rows = jnp.arange(pairs, dtype=jnp.int32) // TOP
    outgoing = (
        jnp.zeros((experts * capacity, width), brain_float_half)
        .at[slot_index]
        .set(normed_two[owner_rows])
    )
    arrived = lax.all_to_all(
        outgoing.reshape(experts, capacity, width),
        (EXPERT, FSDP),
        split_axis=0,
        concat_axis=0,
        tiled=True,
    ).reshape(experts * capacity, width)
    gate_pre = jnp.dot(arrived, w_gate[0], preferred_element_type=single_float)
    up_pre = jnp.dot(arrived, w_up[0], preferred_element_type=single_float)
    activated = jax.nn.silu(gate_pre)
    inner = (activated * up_pre).astype(brain_float_half)
    result = jnp.dot(inner, w_down[0], preferred_element_type=single_float).astype(brain_float_half)
    returned = lax.all_to_all(
        result.reshape(experts, capacity, width),
        (EXPERT, FSDP),
        split_axis=0,
        concat_axis=0,
        tiled=True,
    ).reshape(experts * capacity, width)
    expert_rows = returned[slot_index].astype(single_float).reshape(row_count, TOP, width)
    output = hidden + jnp.einsum("tk,tkd->td", gates, expert_rows, precision=HIGHEST)
    grad_top = grad_output[0]
    grad_gates = jnp.einsum("tkd,td->tk", expert_rows, grad_top, precision=HIGHEST)
    grad_pairs = (
        (gates[:, :, None] * grad_top[:, None, :]).astype(brain_float_half).reshape(pairs, width)
    )
    grad_send = (
        jnp.zeros((experts * capacity, width), brain_float_half).at[slot_index].set(grad_pairs)
    )
    grad_arrived = lax.all_to_all(
        grad_send.reshape(experts, capacity, width),
        (EXPERT, FSDP),
        split_axis=0,
        concat_axis=0,
        tiled=True,
    ).reshape(experts * capacity, width)
    grad_down = jnp.einsum("rf,rd->fd", inner, grad_arrived, preferred_element_type=single_float)
    grad_inner = jnp.einsum(
        "rd,fd->rf", grad_arrived, w_down[0], preferred_element_type=single_float
    )
    sigmoid_gate = jax.nn.sigmoid(gate_pre)
    slope = sigmoid_gate * (1.0 + gate_pre * (1.0 - sigmoid_gate))
    grad_gate_pre = (grad_inner * up_pre * slope).astype(brain_float_half)
    grad_up_pre = (grad_inner * activated).astype(brain_float_half)
    grad_gate_w = jnp.einsum(
        "rd,rf->df", arrived, grad_gate_pre, preferred_element_type=single_float
    )
    grad_up_w = jnp.einsum("rd,rf->df", arrived, grad_up_pre, preferred_element_type=single_float)
    grad_rows = (
        jnp.einsum("rf,df->rd", grad_gate_pre, w_gate[0], preferred_element_type=single_float)
        + jnp.einsum("rf,df->rd", grad_up_pre, w_up[0], preferred_element_type=single_float)
    ).astype(brain_float_half)
    grad_back = lax.all_to_all(
        grad_rows.reshape(experts, capacity, width),
        (EXPERT, FSDP),
        split_axis=0,
        concat_axis=0,
        tiled=True,
    ).reshape(experts * capacity, width)
    grad_normed_two = jnp.sum(
        grad_back[slot_index].astype(single_float).reshape(row_count, TOP, width), 1
    )
    grad_chosen = gates * (grad_gates - jnp.sum(gates * grad_gates, -1, keepdims=True))
    grad_logits = jnp.einsum("tke,tk->te", selector, grad_chosen, precision=HIGHEST).astype(
        brain_float_half
    )
    grad_normed_two = grad_normed_two + jnp.einsum(
        "te,de->td", grad_logits, full_router, preferred_element_type=single_float
    )
    grad_router = jnp.einsum(
        "td,te->de", normed_two, grad_logits, preferred_element_type=single_float
    )
    grad_gain_two = jnp.sum(grad_normed_two * hidden * scale_two, 0)
    grad_hidden = grad_top + norm_backward(grad_normed_two, hidden, scale_two, gain_two)
    grad_branch = grad_hidden.astype(brain_float_half)
    grad_out_w = jnp.einsum("tq,td->qd", mixed, grad_branch, preferred_element_type=single_float)
    grad_mixed = (
        jnp.einsum("td,qd->tq", grad_branch, full_out, preferred_element_type=single_float)
        .astype(brain_float_half)
        .reshape(row_count, KEY_VALUE_HEADS, query_groups, HEAD_SIZE)
    )
    again = masked_scores()
    weights = jnp.exp(again - log_total)
    weights_again = weights.astype(brain_float_half)
    grad_weights = jnp.einsum(
        "tkgd,skd->kgts", grad_mixed, value_gathered_rows, preferred_element_type=single_float
    )
    spread = jnp.sum(weights * grad_weights, -1, keepdims=True)
    grad_scores = (weights * (grad_weights - spread)).astype(brain_float_half)
    grad_query_rot = (
        jnp.einsum(
            "kgts,skd->tkgd", grad_scores, key_gathered_rows, preferred_element_type=single_float
        )
        * scale
    ).reshape(row_count, QUERY_HEADS, HEAD_SIZE)
    grad_key_all = (
        jnp.einsum("kgts,tkgd->skd", grad_scores, query_rot, preferred_element_type=single_float)
        * scale
    ).reshape(length_total, KEY_VALUE_HEADS * HEAD_SIZE)
    grad_value_all = jnp.einsum(
        "kgts,tkgd->skd", weights_again, grad_mixed, preferred_element_type=single_float
    ).reshape(length_total, KEY_VALUE_HEADS * HEAD_SIZE)
    gradient_key_rotated, grad_value = (
        lax.psum_scatter(
            grad_key_all.astype(jnp.bfloat16), EXPERT, scatter_dimension=0, tiled=True
        ).astype(jnp.float32),
        lax.psum_scatter(
            grad_value_all.astype(jnp.bfloat16), EXPERT, scatter_dimension=0, tiled=True
        ).astype(jnp.float32),
    )
    gradient_key_rotated = gradient_key_rotated.reshape(row_count, KEY_VALUE_HEADS, HEAD_SIZE)
    grad_query_unit = unrotate(grad_query_rot, cosine_table, sine_table)
    gradient_key_normalized = unrotate(gradient_key_rotated, cosine_table, sine_table)
    grad_gain_q = jnp.sum(grad_query_unit * query_raw * query_scale, (0, 1))
    grad_gain_k = jnp.sum(gradient_key_normalized * key_unnormalized * key_norm_scale, (0, 1))
    grad_query = (
        norm_backward(grad_query_unit, query_raw, query_scale, gain_q)
        .reshape(row_count, QUERY_HEADS * HEAD_SIZE)
        .astype(brain_float_half)
    )
    grad_key = (
        norm_backward(gradient_key_normalized, key_unnormalized, key_norm_scale, key_gain_vector)
        .reshape(row_count, KEY_VALUE_HEADS * HEAD_SIZE)
        .astype(brain_float_half)
    )
    grad_value_low = grad_value.astype(brain_float_half)
    grad_query_w = jnp.einsum(
        "td,tq->dq", normalized_input, grad_query, preferred_element_type=single_float
    )
    grad_key_w = jnp.einsum(
        "td,tq->dq", normalized_input, grad_key, preferred_element_type=single_float
    )
    grad_value_w = jnp.einsum(
        "td,tq->dq", normalized_input, grad_value_low, preferred_element_type=single_float
    )
    grad_normed = (
        jnp.einsum("tq,dq->td", grad_query, full_query, preferred_element_type=single_float)
        + jnp.einsum("tq,dq->td", grad_key, gathered_key, preferred_element_type=single_float)
        + jnp.einsum("tq,dq->td", grad_value_low, full_value, preferred_element_type=single_float)
    )
    grad_gain_one = jnp.sum(grad_normed * inputs * scale_one, 0)
    grad_inputs = grad_hidden + norm_backward(grad_normed, inputs, scale_one, gain_one)
    local_grads = (
        grad_query_w,
        grad_key_w,
        grad_value_w,
        grad_out_w,
        grad_router,
        grad_gain_one,
        grad_gain_two,
        grad_gain_q,
        grad_gain_k,
    )
    shards = (
        lax.psum_scatter(
            local_grads[0].astype(jnp.bfloat16), FSDP, scatter_dimension=0, tiled=True
        ).astype(jnp.float32),
        lax.psum_scatter(
            local_grads[1].astype(jnp.bfloat16), FSDP, scatter_dimension=0, tiled=True
        ).astype(jnp.float32),
        lax.psum_scatter(
            local_grads[2].astype(jnp.bfloat16), FSDP, scatter_dimension=0, tiled=True
        ).astype(jnp.float32),
        lax.psum_scatter(
            local_grads[3].astype(jnp.bfloat16), FSDP, scatter_dimension=0, tiled=True
        ).astype(jnp.float32),
        lax.psum_scatter(
            local_grads[4].astype(jnp.bfloat16), FSDP, scatter_dimension=0, tiled=True
        ).astype(jnp.float32),
        lax.psum_scatter(
            local_grads[5].astype(jnp.bfloat16), FSDP, scatter_dimension=0, tiled=True
        ).astype(jnp.float32),
        lax.psum_scatter(
            local_grads[6].astype(jnp.bfloat16), FSDP, scatter_dimension=0, tiled=True
        ).astype(jnp.float32),
        lax.psum_scatter(
            local_grads[7].astype(jnp.bfloat16), FSDP, scatter_dimension=0, tiled=True
        ).astype(jnp.float32),
        lax.psum_scatter(
            local_grads[8].astype(jnp.bfloat16), FSDP, scatter_dimension=0, tiled=True
        ).astype(jnp.float32),
    )
    shards = (
        lax.psum(shards[0].astype(jnp.bfloat16), EXPERT).astype(jnp.float32),
        lax.psum(shards[1].astype(jnp.bfloat16), EXPERT).astype(jnp.float32),
        lax.psum(shards[2].astype(jnp.bfloat16), EXPERT).astype(jnp.float32),
        lax.psum(shards[3].astype(jnp.bfloat16), EXPERT).astype(jnp.float32),
        lax.psum(shards[4].astype(jnp.bfloat16), EXPERT).astype(jnp.float32),
        lax.psum(shards[5].astype(jnp.bfloat16), EXPERT).astype(jnp.float32),
        lax.psum(shards[6].astype(jnp.bfloat16), EXPERT).astype(jnp.float32),
        lax.psum(shards[7].astype(jnp.bfloat16), EXPERT).astype(jnp.float32),
        lax.psum(shards[8].astype(jnp.bfloat16), EXPERT).astype(jnp.float32),
    )
    return (
        output[None],
        grad_inputs[None],
        shards[0],
        shards[1],
        shards[2],
        shards[3],
        shards[4],
        shards[5],
        shards[6],
        shards[7],
        shards[8],
        grad_gate_w[None],
        grad_up_w[None],
        grad_down[None],
    )


def angle_tables(length):
    power = -(np.arange(HEAD_SIZE // 2, dtype=np.float32) * np.float32(2.0)) / np.float32(HEAD_SIZE)
    freq = np.power(np.float32(THETA), power).astype(np.float32)
    turns = np.arange(length, dtype=np.float32)[:, None] * freq[None, :]
    turns = np.concatenate([turns, turns], -1)
    return jnp.asarray(np.cos(turns)), jnp.asarray(np.sin(turns))


def one_hots(ids, numbers):
    rows = ids.shape[2]
    hit = jnp.any(ids[:, None] == numbers[None, :, None, None], 2)
    earlier = (jnp.arange(rows)[:, None] < jnp.arange(rows)[None, :]).astype(jnp.bfloat16)
    rank = jnp.dot(hit.astype(jnp.bfloat16), earlier, preferred_element_type=jnp.float32)
    places = jnp.arange(SLOTS, dtype=jnp.int32)[:, None]
    taken = hit[:, :, None, :] & (rank.astype(jnp.int32)[:, :, None, :] == places)
    return taken.astype(jnp.bfloat16)


def routes(ids):
    place = Place()
    _, far = place.line()
    mine = (place.x, place.y)
    me = place.e * lax.axis_size(FSDP) + place.f
    numbers = []
    for chip, core in ((mine, place.c), (mine, 1 - place.c), (far, place.c), (far, 1 - place.c)):
        expert_at, shard_at = place.at(chip, core)
        numbers.append(expert_at * lax.axis_size(FSDP) + shard_at)
    blocks = [block_number(mine, place.c, ar, zs) for ar in range(2) for zs in range(4)]
    near = jnp.stack([lax.dynamic_index_in_dim(ids, i, 0, keepdims=False) for i in blocks])
    pick = one_hots(near, jnp.stack(numbers)).reshape(8, 4 * SLOTS, -1)
    return me, one_hots(ids, me[None])[:, 0], pick, pick.swapaxes(1, 2)


def packed(pieces, lead, rows):
    flat = jnp.concatenate([piece.reshape(lead, -1) for piece in pieces], 1)
    flat = jnp.pad(flat, ((0, 0), (0, rows * 128 - flat.shape[1])))
    return flat.reshape(lead, rows, 128)


def local_staged(
    layer_input,
    doc_ids,
    expert_ids,
    w_query,
    w_key,
    w_value,
    w_out,
    w_router,
    gain_attn,
    gain_ffn,
    gain_query,
    gain_key,
    w_gate,
    w_up,
    w_down,
    grad_output,
):
    f32 = jnp.float32
    low = jnp.bfloat16
    rows, width = layer_input.shape[1:]
    length = doc_ids.shape[1]
    depth = w_router.shape[0]
    groups, shards = lax.axis_size(EXPERT), lax.axis_size(FSDP)
    experts = w_router.shape[1]
    heads = QUERY_HEADS // groups
    span = heads * HEAD_SIZE
    mine = lax.axis_index(EXPERT)

    def columns(weight, count):
        return lax.dynamic_slice_in_dim(weight, mine * count, count, 1)

    flat = jnp.concatenate(
        [columns(w_query, span), columns(w_key, HEAD_SIZE), columns(w_value, HEAD_SIZE)], 1
    )
    pack = packed([w_router, gain_attn, gain_ffn, gain_query, gain_key], 1, 80)[0]
    w_qkv, w_mix, tokens, pack_all, ids_all = gather(
        groups,
        shards,
        5,
        flat,
        w_out,
        layer_input[0],
        pack,
        expert_ids[0].T,
    )
    w_qkv = w_qkv.reshape(width, span + 2 * HEAD_SIZE)
    w_mix = w_mix.reshape(span, width)
    tokens = tokens.reshape(length, width)
    pack_all = pack_all.reshape(shards, -1)
    at = depth * experts
    full_router = pack_all[:, :at].reshape(width, experts)
    gain_one = pack_all[:, at : at + depth].reshape(width).astype(f32)
    gain_two = pack_all[:, at + depth : at + 2 * depth].reshape(width).astype(f32)
    at += 2 * depth
    small = HEAD_SIZE // shards
    gain_q = pack_all[:, at : at + small].reshape(HEAD_SIZE).astype(f32)
    gain_k = pack_all[:, at + small : at + 2 * small].reshape(HEAD_SIZE).astype(f32)
    me, mine_picks, pick, spread = routes(ids_all)
    grad_top = grad_output[0]
    ids_column, ids_row = doc_ids[0][:, None], doc_ids[0][None, :]
    cosine, sine = angle_tables(length)
    gain_q, gain_k = gain_q[None], gain_k[None]
    attend = attention(
        tokens, w_qkv, gain_one[None], gain_q, gain_k, cosine, sine, ids_column, ids_row, heads
    )
    grads_in, normed_one, raw, query_rot, key_rot, value, mixed = dispatch(
        groups, shards, 1, grad_top.astype(low), pick, extra=attend
    )
    branch = jnp.dot(mixed, w_mix, preferred_element_type=f32).astype(low)
    inputs = layer_input[0].astype(f32)
    hidden = inputs + group_scatter(8, branch.reshape(groups, rows, width))
    scale_two = inverse_rms(hidden)
    normed_two = (hidden * scale_two * gain_two).astype(low)
    logits = jnp.dot(normed_two, full_router, preferred_element_type=f32)
    selector = (expert_ids[0][:, :, None] == jnp.arange(experts, dtype=jnp.int32)).astype(f32)
    gates = jax.nn.softmax(jnp.sum(selector * logits[:, None, :], -1), -1)
    _, arrived, weighted, grad_arrived, inner, grad_a, grad_b, grad_rows, gate_grads = dispatch_expert(
        groups, shards, 2, normed_two, pick, gates.T, grads_in, mine_picks, ids_all, w_gate, w_up, w_down
    )

    def flat_rows(blocks):
        return blocks.reshape(-1, blocks.shape[-1])

    grad_normed_two, gates_back, grad_gate_w, grad_up_w, grad_down = combine(
        groups,
        shards,
        3,
        grad_rows,
        spread,
        gate_grads,
        weight_grads(*(flat_rows(a) for a in (arrived, grad_arrived, inner, grad_a, grad_b))),
    )
    grad_gates = jnp.sum(selector * gates_back[:, 0].T[:, None, :], -1)
    grad_chosen = gates * (grad_gates - jnp.sum(gates * grad_gates, -1, keepdims=True))
    grad_logits = jnp.sum(selector * grad_chosen[:, :, None], 1).astype(low)
    grad_normed_two = grad_normed_two + jnp.einsum(
        "te,de->td", grad_logits, full_router, preferred_element_type=f32
    )
    grad_router = jnp.einsum("td,te->de", normed_two, grad_logits, preferred_element_type=f32)
    grad_gain_two = jnp.sum(grad_normed_two * hidden * scale_two, 0)
    grad_hidden = grad_top + norm_backward(grad_normed_two, hidden, scale_two, gain_two)
    grad_branch = group_gather(7, grad_hidden.astype(low)).reshape(length, width)
    grad_mix = jnp.einsum("tq,td->qd", mixed, grad_branch, preferred_element_type=f32).astype(low)
    grad_mixed = jnp.einsum("td,qd->tq", grad_branch, w_mix, preferred_element_type=f32)
    grad_mixed = grad_mixed.astype(low)

    back = attention_back(
        query_rot, key_rot, value, raw, grad_mixed, ids_column, ids_row, gain_q, gain_k, cosine, sine
    )
    combined, grad_raw, gain_grads = combine(
        groups, shards, 4, weighted, spread, extra=back
    )
    output = hidden + combined
    grad_qkv = jnp.einsum("td,tq->dq", normed_one, grad_raw, preferred_element_type=f32).astype(low)
    grad_normed_one = jnp.einsum("tq,dq->td", grad_raw, w_qkv, preferred_element_type=f32)
    wide_tokens = tokens.astype(f32)
    grad_gain_one = jnp.sum(grad_normed_one * wide_tokens * inverse_rms(wide_tokens), 0)
    grad_normed_one = grad_normed_one.astype(low).reshape(groups, rows, width)
    sums = [grad_router, grad_gain_one, grad_gain_two, gain_grads[0], gain_grads[1]]
    sums = packed(sums, shards, 16 * (span + 2 * HEAD_SIZE) // 128)
    sums = sums.reshape(shards, 16, -1).astype(low)
    query_sum, key_sum, value_sum, tall_sum, pack_sum, grad_normed_one = reduce(
        groups,
        shards,
        6,
        grad_qkv.reshape(shards, depth, -1),
        grad_mix.reshape(2, -1, width),
        sums,
        grad_normed_one,
    )
    pack_sum = jnp.sum(pack_sum.astype(f32), 0).reshape(-1)
    scale_own = inverse_rms(inputs)
    grad_inputs = grad_hidden + norm_backward(grad_normed_one, inputs, scale_own, gain_one)
    at = depth * experts
    return (
        output[None],
        grad_inputs[None],
        query_sum.astype(f32),
        key_sum.astype(f32),
        value_sum.astype(f32),
        tall_sum.astype(f32),
        pack_sum[:at].reshape(depth, experts),
        pack_sum[at : at + depth],
        pack_sum[at + depth : at + 2 * depth],
        pack_sum[at + 2 * depth : at + 2 * depth + small],
        pack_sum[at + 2 * depth + small : at + 2 * depth + 2 * small],
        grad_gate_w[None],
        grad_up_w[None],
        grad_down[None],
    )


def solution(mesh):
    in_specs = (
        P(FSDP, EXPERT, None),
        P(FSDP, None),
        P(FSDP, EXPERT, None),
        P(FSDP, None),
        P(FSDP, None),
        P(FSDP, None),
        P(FSDP, None),
        P(FSDP, None),
        P(FSDP),
        P(FSDP),
        P(FSDP),
        P(FSDP),
        P((EXPERT, FSDP), None, None),
        P((EXPERT, FSDP), None, None),
        P((EXPERT, FSDP), None, None),
        P(FSDP, EXPERT, None),
    )
    out_specs = (
        P(FSDP, EXPERT, None),
        P(FSDP, EXPERT, None),
        P(FSDP, None),
        P(FSDP, None),
        P(FSDP, None),
        P(FSDP, None),
        P(FSDP, None),
        P(FSDP),
        P(FSDP),
        P(FSDP),
        P(FSDP),
        P((EXPERT, FSDP), None, None),
        P((EXPERT, FSDP), None, None),
        P((EXPERT, FSDP), None, None),
    )
    staged = mesh.shape[EXPERT] == 4 and mesh.shape[FSDP] == 8
    return jax.shard_map(local_staged if staged else local, mesh=mesh, in_specs=in_specs, out_specs=out_specs, check_vma=False)
```

```python
import functools

import jax
import jax.numpy as jnp
import numpy as np
from jax import lax
from jax.experimental import pallas as pl
from jax.experimental.pallas import tpu as pltpu
from jax.sharding import PartitionSpec as P

EXPERT = "expert"
FSDP = "fsdp"
UP, DOWN, ABOVE, BELOW = "up", "down", "above", "below"
QUERY_HEADS = 32
KEY_VALUE_HEADS = 4
HEAD_SIZE = 128
TOP = 8


EPS = 1e-06
THETA = 1000000.0
HIGHEST = lax.Precision.HIGHEST


def angles(positions):
    freq = THETA ** (-(jnp.arange(HEAD_SIZE // 2, dtype=jnp.float32) * 2.0) / HEAD_SIZE)
    turn = positions.astype(jnp.float32)[:, None] * freq[None, :]
    turn = jnp.concatenate([turn, turn], -1)
    return (jnp.cos(turn), jnp.sin(turn))


def apply_rotary(value_rows_local, cosine_table, sine_table):
    half = value_rows_local.shape[-1] // 2
    turned = jnp.concatenate([-value_rows_local[..., half:], value_rows_local[..., :half]], -1)
    return value_rows_local * cosine_table + turned * sine_table


def unrotate(grads, cosine_table, sine_table):
    half = grads.shape[-1] // 2
    scaled = grads * sine_table
    turned = jnp.concatenate([-scaled[..., half:], scaled[..., :half]], -1)
    return grads * cosine_table - turned


def inverse_rms(value_rows_local):
    return lax.rsqrt(jnp.mean(value_rows_local * value_rows_local, -1, keepdims=True) + EPS)


def norm_backward(grad, value_rows_local, inverse, gain):
    scaled = grad * gain
    return inverse * scaled - inverse * inverse * inverse * value_rows_local * jnp.mean(
        scaled * value_rows_local, -1, keepdims=True
    )


MESH = pl.DeviceIdType.MESH
SLOTS = 80
FAR_FIRST = ((1, 3), (1, 2), (0, 3), (1, 1), (0, 2), (0, 1), (1, 0), (0, 0))
BACK = FAR_FIRST
AHEAD = 2
HALVES = 2


class Place:
    def __init__(self):
        self.e = lax.axis_index(EXPERT)
        self.f = lax.axis_index(FSDP)
        self.x, self.c = self.e // 2, self.e % 2
        self.z, self.y = self.f // 2, self.f % 2

    def device(self, axis):
        if axis == "c":
            return (self.x * 2 + 1 - self.c, self.f)
        if axis == "x":
            return ((1 - self.x) * 2 + self.c, self.f)
        if axis == "y":
            return (self.e, self.z * 2 + 1 - self.y)
        if axis == UP:
            return (self.e, jnp.minimum(self.z + 1, 3) * 2 + self.y)
        return (self.e, jnp.maximum(self.z - 1, 0) * 2 + self.y)

    def ranked(self, j):
        inner = (1, 0, 2, 3)[j]
        end = (self.z == 0) | (self.z == 3)
        low = jnp.where(end, j, inner)
        return jnp.where(self.z < 2, low, 3 - low)

    def line(self):
        x, y, even = self.x, self.y, self.c == 0
        near = (jnp.where(even, 1 - x, x), jnp.where(even, y, 1 - y))
        far = (jnp.where(even, x, 1 - x), jnp.where(even, 1 - y, y))
        return near, far

    def at(self, chip, core):
        return (chip[0] * 2 + core, self.z * 2 + chip[1])


def block_number(chip, core, ar, zs):
    x, y = chip
    xs = jnp.where(core == 0, 1 - x, x) if ar else x
    ys = jnp.where(core == 0, y, 1 - y) if ar else y
    return (xs * 2 + core) * 8 + zs * 2 + ys


def greet(place):
    barrier = pltpu.get_barrier_semaphore()
    beside = [place.device("c")]
    for chip in ((1 - place.x, place.y), (place.x, 1 - place.y)):
        beside += [place.at(chip, 0), place.at(chip, 1)]
    for device in beside:
        pl.semaphore_signal(barrier, 1, device_id=device, device_id_type=MESH)

    @pl.when(place.z < 3)
    def _():
        pl.semaphore_signal(barrier, 1, device_id=place.device(UP), device_id_type=MESH)

    @pl.when(place.z > 0)
    def _():
        pl.semaphore_signal(barrier, 1, device_id=place.device(DOWN), device_id_type=MESH)

    inner = (place.z > 0) & (place.z < 3)
    pl.semaphore_wait(barrier, len(beside) + jnp.where(inner, 2, 1))


def greet_all(place, experts, shards):
    barrier = pltpu.get_barrier_semaphore()
    count = experts * shards

    def one(i, carry):
        target = lax.rem(place.e * shards + place.f + i, count)
        pl.semaphore_signal(
            barrier, 1, device_id=(target // shards, lax.rem(target, shards)), device_id_type=MESH
        )
        return carry

    lax.fori_loop(1, count, one, 0)
    pl.semaphore_wait(barrier, count - 1)


def onward(path, j, xr, yr):
    differs = {"z": j > 0, "x": xr > 0, "y": yr > 0}
    last = -1
    for i, axis in enumerate(path):
        if differs[axis]:
            last = i
    out = []
    if last >= 0 and path[last] == "z":
        out.append("z+")
    for axis in path[last + 1 :]:
        out.append("z*" if axis == "z" else axis)
    return out


def links(place, path, j, xr, yr, zs):
    out = []
    for axis in onward(path, j, xr, yr):
        if axis == "z+":
            out.append((UP, (zs < place.z) & (place.z < 3)))
            out.append((DOWN, (zs > place.z) & (place.z > 0)))
        elif axis == "z*":
            out.append((UP, place.z < 3))
            out.append((DOWN, place.z > 0))
        else:
            out.append((axis, None))
    return out


def run(condition, action):
    if condition is None:
        action()
    else:
        pl.when(condition)(action)


LINK = {"x": 0, "y": 1, UP: 2, DOWN: 3}


def remote(src, dst, send_sem, recv_sem, device):
    return pltpu.make_async_remote_copy(
        src_ref=src,
        dst_ref=dst,
        send_sem=send_sem,
        recv_sem=recv_sem,
        device_id=device,
        device_id_type=MESH,
    )


class Side:
    def __init__(self, steps, events):
        self.steps, self.events = list(steps), events
        self.total, self.seen = len(self.steps), 0

    def event(self):
        self.seen += 1
        left = self.total - self.total * min(self.seen, self.events) // self.events
        while len(self.steps) > left:
            self.steps.pop(0)()


class Extra:
    def __init__(self, operands=(), in_specs=(), outs=(), out_specs=(), scratch=(), steps=None):
        self.operands, self.in_specs = list(operands), list(in_specs)
        self.outs, self.out_specs, self.scratch = list(outs), list(out_specs), list(scratch)
        self.steps = steps if steps is not None else lambda *refs: []


def split(refs, counts):
    out = []
    for count in counts:
        out.append(refs[:count])
        refs = refs[count:]
    return out


def exchange_small(place, dims, src_of, dst, sems_out, sems_in, sem):
    experts, shards = dims
    count = experts * shards
    me = place.e * shards + place.f
    keep = pltpu.make_async_copy(src_of(me), dst.at[me], sem)
    keep.start()

    def copy(i, sending):
        other = lax.rem(me + i, count)
        source = me if sending else other
        device = (other // shards, lax.rem(other, shards))
        return remote(src_of(other), dst.at[source], sems_out.at[i], sems_in.at[source], device)

    def start(i, carry):
        copy(i, True).start()
        return carry

    def finish(i, carry):
        done = copy(i, False)
        done.wait_send()
        done.wait_recv()
        return carry

    lax.fori_loop(1, count, start, 0)

    def end():
        keep.wait()
        lax.fori_loop(1, count, finish, 0)

    return end


def dispatch_kernel(dims, has_small, extra, *refs):
    counts = (
        2 + has_small, len(extra.operands), 1 + has_small, len(extra.outs), 7 + 3 * has_small,
        len(extra.scratch),
    )
    ins, more_in, outs, more_out, scratch, more_scratch = split(refs, counts)
    tok, sel = ins[:2]
    picked = outs[0]
    held, stage, arrive, leave, pick_out, pick_in, local = scratch[:7]
    place = Place()
    width = tok.shape[1]
    near, far = place.line()
    mine = (place.x, place.y)
    if has_small:
        greet_all(place, *dims)
        end_small = exchange_small(
            place, dims, lambda i: ins[2], outs[1], scratch[7], scratch[8], scratch[9].at[0]
        )
    else:
        greet(place)
    side = Side(extra.steps(*more_in, *more_out, *more_scratch), 8)
    keep = pltpu.make_async_copy(tok, held.at[place.z], local.at[8])
    keep.start()
    pending = []
    finish = []
    targets = (place.device("c"), place.at(far, place.c), place.at(far, 1 - place.c))

    def pick(ar, zs):
        block = ar * 4 + zs
        number = block_number(mine, place.c, ar, zs)

        def tile(i, carry):
            columns = pl.ds(pl.multiple_of(i * 512, 512), 512)
            stage[block, :, columns] = jnp.dot(
                sel[block], held[block, :, columns], preferred_element_type=jnp.float32
            ).astype(jnp.bfloat16)
            return carry

        lax.fori_loop(0, width // 512, tile, 0)
        for k in (2, 1, 0):
            away = remote(
                stage.at[block, pl.ds((k + 1) * SLOTS, SLOTS)], picked.at[number],
                pick_out.at[block, k], pick_in.at[number], targets[k],
            )
            away.start()
            finish.append(away)
        stay = pltpu.make_async_copy(
            stage.at[block, pl.ds(0, SLOTS)], picked.at[number], local.at[block]
        )
        stay.start()
        finish.append(stay)

    half = tok.shape[0] // HALVES
    for ar, j in FAR_FIRST[::-1]:
        zs = place.ranked(j)
        block = ar * 4 + zs
        for h in range(HALVES):
            part = pl.ds(h * half, half)
            window = held.at[block, part]
            if ar or j:
                remote(
                    window, window, leave.at[zs, 0, h], arrive.at[block, h], place.device("c")
                ).wait_recv()
            if ar:
                continue
            source = tok.at[part] if j == 0 else window
            onward = (
                (UP, zs, 0, (zs <= place.z) & (place.z < 3)),
                (DOWN, zs, 1, (zs >= place.z) & (place.z > 0)),
                ("near", 4 + zs, 2, None),
            )
            for axis, there, k, condition in onward:
                device = place.at(near, place.c) if axis == "near" else place.device(axis)
                copy = remote(
                    source, held.at[there, part], leave.at[zs, k, h], arrive.at[there, h], device
                )
                run(condition, copy.start)
                pending.append((condition, copy))
        if not ar and j == 0:
            keep.wait()
        pick(ar, zs)
        side.event()
    for condition, copy in pending:
        run(condition, copy.wait_send)

    def arrived(i, carry):
        xs, cs, ys = i // 16, i // 8 % 2, i % 2
        inside = (cs == place.c) & jnp.where(place.c == 0, ys == place.y, xs == place.x)

        @pl.when(~inside)
        def _():
            window = picked.at[i]
            remote(window, window, pick_out.at[0, 0], pick_in.at[i], place.device("c")).wait_recv()

        return carry

    lax.fori_loop(0, 32, arrived, 0)
    for k, copy in enumerate(finish):
        if k % 4 == 3:
            copy.wait()
        else:
            copy.wait_send()
    if has_small:
        end_small()


def dispatch(experts, shards, number, tok, sel, small=None, extra=None):
    rows, width = tok.shape
    devices = experts * shards
    extra = extra or Extra()
    space = pl.BlockSpec(memory_space=pl.ANY)
    vmem = pl.BlockSpec(memory_space=pltpu.VMEM)
    dma = pltpu.SemaphoreType.DMA
    has_small = int(small is not None)
    operands, in_specs = [tok, sel], [space, vmem]
    out_shape = [jax.ShapeDtypeStruct((devices, SLOTS, width), jnp.bfloat16)]
    scratch = [
        pltpu.VMEM((8, rows, width), jnp.bfloat16),
        pltpu.VMEM((8, 4 * SLOTS, width), jnp.bfloat16),
        dma((8, HALVES)),
        dma((4, 3, HALVES)),
        dma((8, 3)),
        dma((devices,)),
        dma((9,)),
    ]
    if has_small:
        operands.append(small)
        in_specs.append(space)
        out_shape.append(jax.ShapeDtypeStruct((devices,) + small.shape, small.dtype))
        scratch += [dma((devices,)), dma((devices,)), dma((1,))]
    return pl.pallas_call(
        functools.partial(dispatch_kernel, (experts, shards), has_small, extra),
        out_shape=out_shape + extra.outs,
        in_specs=in_specs + extra.in_specs,
        out_specs=[space] * len(out_shape) + extra.out_specs,
        scratch_shapes=scratch + extra.scratch,
        compiler_params=pltpu.CompilerParams(
            collective_id=number, has_side_effects=True, vmem_limit_bytes=60 * 2**20
        ),
        name="dispatch",
    )(*operands, *extra.operands)


def combine_kernel(dims, has_small, extra, *refs):
    counts = (
        2 + has_small, len(extra.operands), 1 + has_small, len(extra.outs), 10 + 3 * has_small,
        len(extra.scratch),
    )
    ins, more_in, outs, more_out, scratch, more_scratch = split(refs, counts)
    weighted, sel = ins[:2]
    total = outs[0]
    rows4, acc, beside, chain, rows_in, rows_out, beside_in, beside_out, chain_in, chain_out = scratch[:10]
    place = Place()
    width = total.shape[1]
    near, far = place.line()
    mine = (place.x, place.y)
    if has_small:
        greet_all(place, *dims)
        end_small = exchange_small(
            place, dims, lambda i: ins[2].at[i], outs[1], scratch[10], scratch[11], scratch[12].at[0]
        )
    else:
        greet(place)
    side = Side(extra.steps(*more_in, *more_out, *more_scratch), 8 * HALVES)
    other = 1 - place.c
    homes = ((mine, place.c), (mine, other), (far, place.c), (near, other))

    def row_copy(ar, zs, k):
        chip, core = homes[k]
        source = weighted.at[block_number(chip, core, ar, zs)]
        block = ar * 4 + zs
        window = rows4.at[block, pl.ds(k * SLOTS, SLOTS)]
        if k == 0:
            return pltpu.make_async_copy(source, window, rows_in.at[block, 0])
        return remote(
            source, window, rows_out.at[block, k - 1], rows_in.at[block, k], place.at(chip, core)
        )

    def send_rows(i):
        ar, j = BACK[i]
        for k in (2, 3, 1, 0):
            row_copy(ar, place.ranked(j), k).start()

    for i in range(AHEAD):
        send_rows(i)
    pending = []
    half = total.shape[0] // HALVES
    for i, (ar, j) in enumerate(BACK):
        zs = place.ranked(j)
        block = ar * 4 + zs
        for k in range(4):
            copy = row_copy(ar, zs, k)
            if k == 0:
                copy.wait()
            else:
                copy.wait_recv()
                copy.wait_send()
        if i + AHEAD < 8:
            send_rows(i + AHEAD)
        last = not ar and j == 0
        above = (zs <= place.z) & (place.z < 3)
        below = (zs >= place.z) & (place.z > 0)
        below_slot = jnp.where(zs == place.z, 4, zs)
        for h in range(HALVES):
            part = pl.ds(h * half, half)
            if not ar:
                window = beside.at[zs, part]
                remote(
                    window, window, beside_out.at[zs, h], beside_in.at[zs, h], place.device("c")
                ).wait_recv()
                for condition, slot in ((above, zs), (below, below_slot)):
                    window = chain.at[slot, part]
                    got = remote(
                        window, window, chain_out.at[0, h], chain_in.at[slot, h], place.device("c")
                    )
                    run(condition, got.wait_recv)

            def tile(t, carry):
                columns = pl.ds(pl.multiple_of(t * 512, 512), 512)
                dense = jnp.dot(
                    sel[block, part], rows4[block, :, columns], preferred_element_type=jnp.float32
                )
                if not ar:
                    dense = dense + beside[zs, part, columns].astype(jnp.float32)
                if last:
                    total[part, columns] = dense
                else:
                    acc[block, part, columns] = dense.astype(jnp.bfloat16)
                return carry

            lax.fori_loop(0, width // 512, tile, 0)
            if not ar:

                def add(slot):
                    def step(t, carry):
                        here = pl.ds(pl.multiple_of(h * half + t * 16, 16), 16)
                        more = chain[slot, here].astype(jnp.float32)
                        if last:
                            total[here] += more
                        else:
                            acc[block, here] = (acc[block, here].astype(jnp.float32) + more).astype(
                                jnp.bfloat16
                            )
                        return carry

                    lax.fori_loop(0, half // 16, step, 0)

                run(above, functools.partial(add, zs))
                run(below, functools.partial(add, below_slot))
            if ar:
                copy = remote(
                    acc.at[block, part], beside.at[zs, part], beside_out.at[zs, h],
                    beside_in.at[zs, h], place.at(near, place.c),
                )
                copy.start()
                pending.append((None, copy))
            elif not last:
                there = jnp.where(zs == place.z + 1, 4, zs)
                for condition, axis, slot in (
                    (zs < place.z, DOWN, zs),
                    (zs > place.z, UP, there),
                ):
                    copy = remote(
                        acc.at[block, part], chain.at[slot, part], chain_out.at[zs, h],
                        chain_in.at[slot, h], place.device(axis),
                    )
                    run(condition, copy.start)
                    pending.append((condition, copy))
            side.event()
    for condition, copy in pending:
        run(condition, copy.wait_send)
    if has_small:
        end_small()


def combine(experts, shards, number, weighted, sel, small=None, extra=None):
    rows = sel.shape[1]
    width = weighted.shape[-1]
    devices = experts * shards
    extra = extra or Extra()
    space = pl.BlockSpec(memory_space=pl.ANY)
    vmem = pl.BlockSpec(memory_space=pltpu.VMEM)
    dma = pltpu.SemaphoreType.DMA
    low = jnp.bfloat16
    has_small = int(small is not None)
    operands, in_specs = [weighted, sel], [space, vmem]
    out_shape, out_specs = [jax.ShapeDtypeStruct((rows, width), jnp.float32)], [vmem]
    scratch = [
        pltpu.VMEM((8, 4 * SLOTS, width), low),
        pltpu.VMEM((8, rows, width), low),
        pltpu.VMEM((4, rows, width), low),
        pltpu.VMEM((5, rows, width), low),
        dma((8, 4)),
        dma((8, 3)),
        dma((4, HALVES)),
        dma((4, HALVES)),
        dma((5, HALVES)),
        dma((4, HALVES)),
    ]
    if has_small:
        operands.append(small)
        in_specs.append(space)
        out_shape.append(jax.ShapeDtypeStruct(small.shape, small.dtype))
        out_specs.append(space)
        scratch += [dma((devices,)), dma((devices,)), dma((1,))]
    return pl.pallas_call(
        functools.partial(combine_kernel, (experts, shards), has_small, extra),
        out_shape=out_shape + extra.outs,
        in_specs=in_specs + extra.in_specs,
        out_specs=out_specs + extra.out_specs,
        scratch_shapes=scratch + extra.scratch,
        compiler_params=pltpu.CompilerParams(
            collective_id=number, has_side_effects=True, vmem_limit_bytes=63 * 2**20
        ),
        name="combine",
    )(*operands, *extra.operands)


FLAT = ("zy", "yz")
CHUNKS = 4


def flat_parts(rows):
    return (0, rows * 3 // 4), (rows * 3 // 4, rows - rows * 3 // 4)


def send_around(place, experts, shards, src_of, dst, out_sems, in_sems, across):
    count = experts * shards if across else shards
    me = place.e * shards + place.f if across else place.f

    def copy(i, sending):
        other = lax.rem(me + i, count)
        if across:
            device = (other // shards, lax.rem(other, shards))
        else:
            device = (place.e, other)
        source = me if sending else other
        return remote(src_of(other), dst.at[source], out_sems.at[i], in_sems.at[source], device)

    def start(i, carry):
        copy(i, True).start()
        return carry

    def finish(i, carry):
        done = copy(i, False)
        done.wait_send()
        done.wait_recv()
        return carry

    lax.fori_loop(1, count, start, 0)
    return lambda: lax.fori_loop(1, count, finish, 0)


def gather_kernel(
    dims, flat, tall, tok, pack, ids, flat_all, tall_all, tok_all, pack_all, ids_all,
    picks, pick, spread,
    flat_in, flat_out, tall_in, tall_out, tok_in, tok_out, pack_in, pack_out, ids_in, ids_out, local,
    ids_held, hits, ranks,
):
    experts, shards = dims
    place = Place()
    greet_all(place, experts, shards)
    me = place.e * shards + place.f
    starts, sizes = flat_parts(flat.shape[0])
    chunk = tall.shape[0] // CHUNKS
    pending = []
    keeps = [
        pltpu.make_async_copy(flat, flat_all.at[place.f], local.at[0]),
        pltpu.make_async_copy(tok, tok_all.at[place.e], local.at[1]),
        pltpu.make_async_copy(pack, pack_all.at[place.f], local.at[2]),
        pltpu.make_async_copy(ids, ids_all.at[me], local.at[3]),
    ]

    def go(condition, copy):
        run(condition, copy.start)
        pending.append((condition, copy))

    def both(a, b):
        return b if a is None else (a if b is None else a & b)

    def flat_item(p, j, yr):
        zs = place.ranked(j)
        source = zs * 2 + (1 - place.y if yr else place.y)
        first = j == 0 and yr == 0
        window = flat_all.at[source, pl.ds(starts[p], sizes[p])]
        src = flat.at[pl.ds(starts[p], sizes[p])] if first else window
        if not first:
            remote(
                window, window, flat_out.at[p, source, 0], flat_in.at[p, source], place.device("c")
            ).wait_recv()
        for axis, condition in links(place, FLAT[p], j, 0, yr, zs):
            go(
                condition,
                remote(
                    src,
                    window,
                    flat_out.at[p, source, LINK[axis]],
                    flat_in.at[p, source],
                    place.device(axis),
                ),
            )

    owner = place.z == place.e

    distance = jnp.abs(place.z - place.e)

    def tall_round(r):
        k = r - distance
        live = (k >= 0) & (k < CHUNKS)
        k = jnp.clip(k, 0, CHUNKS - 1)
        piece = pl.ds(pl.multiple_of(k * chunk, chunk), chunk)
        window = tall_all.at[place.y, piece]

        @pl.when(live & ~owner)
        def _():
            remote(window, window, tall_out.at[k, 0], tall_in.at[0, k], place.device("c")).wait_recv()

        for mine in (True, False):
            src = tall.at[piece] if mine else window
            role = live & (owner if mine else ~owner)
            for axis, condition in (
                (UP, (place.z >= place.e) & (place.z < 3)),
                (DOWN, (place.z <= place.e) & (place.z > 0)),
                ("y", None),
            ):
                go(
                    both(role, condition),
                    remote(
                        src,
                        window,
                        tall_out.at[k, LINK[axis]],
                        tall_in.at[1 if axis == "y" else 0, k],
                        place.device(axis),
                    ),
                )

    def rank_rows():
        end_ids()
        keeps[3].wait()
        copy = pltpu.make_async_copy(ids_all, ids_held, local.at[5])
        copy.start()
        copy.wait()
        hits[...] = jnp.zeros_like(hits)

        def hit(i, number):
            found = jnp.where(ids_held[i] == number, 1.0, 0.0)
            return jnp.max(found, 0, keepdims=True)

        def own(i, carry):
            hits[pl.ds(i, 1)] = hit(i, me)
            return carry

        lax.fori_loop(0, experts * shards, own, 0)
        mine, far = (place.x, place.y), place.line()[1]
        for k, (chip, core) in enumerate(
            ((mine, place.c), (mine, 1 - place.c), (far, place.c), (far, 1 - place.c))
        ):
            expert_at, shard_at = place.at(chip, core)
            for ar in range(2):
                for zs in range(4):
                    row = experts * shards + (ar * 4 + zs) * 4 + k
                    at = block_number(mine, place.c, ar, zs)
                    hits[row : row + 1] = hit(at, expert_at * shards + shard_at)
        count = hits.shape[1]
        before = lax.broadcasted_iota(jnp.int32, (count, count), 0)
        after = lax.broadcasted_iota(jnp.int32, (count, count), 1)
        earlier = jnp.where(before < after, 1.0, 0.0).astype(jnp.bfloat16)
        found = jnp.dot(hits[...].astype(jnp.bfloat16), earlier, preferred_element_type=jnp.float32)
        ranks[...] = jnp.where(hits[...] > 0.5, found, -1.0)

    def one_hot_rows():
        shape = (SLOTS, ranks.shape[1])
        slot = lax.broadcasted_iota(jnp.int32, shape, 0).astype(jnp.float32)

        def rows_of(i):
            return jnp.where(ranks[pl.ds(i, 1)] == slot, 1.0, 0.0).astype(jnp.bfloat16)

        def own(i, carry):
            picks[i] = rows_of(i)
            return carry

        def near(i, carry):
            for k in range(4):
                pick[i, k * SLOTS : (k + 1) * SLOTS] = rows_of(experts * shards + i * 4 + k)
            return carry

        lax.fori_loop(0, experts * shards, own, 0)
        lax.fori_loop(0, 8, near, 0)

    def one_hot_columns():
        turned = ranks[...].T
        shape = (turned.shape[0], 4 * SLOTS)
        lane = lax.broadcasted_iota(jnp.int32, shape, 1)
        slot = lax.rem(lane, SLOTS).astype(jnp.float32)
        for i in range(8):
            column = experts * shards + i * 4
            rank = turned[:, column : column + 1]
            for k in range(1, 4):
                rank = jnp.where(lane < k * SLOTS, rank, turned[:, column + k : column + k + 1])
            spread[i] = jnp.where(rank == slot, 1.0, 0.0).astype(jnp.bfloat16)

    flat_item(0, 0, 0)
    flat_item(1, 0, 0)
    go(None, remote(tok, tok_all.at[place.e], tok_out.at[0], tok_in.at[place.e], place.device("x")))
    go(None, remote(tok, tok_all.at[place.e], tok_out.at[1], tok_in.at[place.e], place.device("c")))
    end_pack = send_around(
        place, experts, shards, lambda i: pack, pack_all, pack_out, pack_in, False
    )
    end_ids = send_around(place, experts, shards, lambda i: ids, ids_all, ids_out, ids_in, True)
    for keep in keeps:
        keep.start()
    keep_tall = pltpu.make_async_copy(tall, tall_all.at[place.y], local.at[4])
    run(owner, keep_tall.start)
    across = (1 - place.x) * 2 + place.c
    window = tok_all.at[across]
    relay = remote(window, window, tok_out.at[2], tok_in.at[across], place.device("c"))
    tall_round(0)
    flat_item(1, 0, 1)
    flat_item(0, 1, 0)
    tall_round(1)
    rank_rows()
    flat_item(0, 2, 0)
    one_hot_rows()
    tall_round(2)
    one_hot_columns()
    flat_item(1, 1, 0)
    flat_item(1, 1, 1)
    relay.wait_recv()
    go(None, relay)
    flat_item(0, 3, 0)
    tall_round(3)
    flat_item(1, 2, 0)
    flat_item(1, 2, 1)
    tall_round(4)
    flat_item(1, 3, 0)
    flat_item(1, 3, 1)
    tall_round(5)
    tall_round(6)
    for j in range(4):
        flat_item(0, j, 1)
    for k in range(CHUNKS):
        window = tall_all.at[1 - place.y, pl.ds(k * chunk, chunk)]
        remote(window, window, tall_out.at[k, 0], tall_in.at[1, k], place.device("c")).wait_recv()
    for source in (place.x * 2 + 1 - place.c, (1 - place.x) * 2 + 1 - place.c):
        window = tok_all.at[source]
        remote(window, window, tok_out.at[2], tok_in.at[source], place.device("c")).wait_recv()
    for condition, copy in pending:
        run(condition, copy.wait_send)
    end_pack()
    for keep in keeps[:3]:
        keep.wait()
    run(owner, keep_tall.wait)


def gather(experts, shards, number, flat, tall, tok, pack, ids):
    space = pl.BlockSpec(memory_space=pl.ANY)
    dma = pltpu.SemaphoreType.DMA
    devices = experts * shards

    def shape(lead, a):
        return jax.ShapeDtypeStruct((lead,) + a.shape, a.dtype)

    return pl.pallas_call(
        functools.partial(gather_kernel, (experts, shards)),
        out_shape=[
            shape(shards, flat),
            shape(2, tall),
            shape(experts, tok),
            shape(shards, pack),
            shape(devices, ids),
            jax.ShapeDtypeStruct((devices, SLOTS, ids.shape[1]), jnp.bfloat16),
            jax.ShapeDtypeStruct((8, 4 * SLOTS, ids.shape[1]), jnp.bfloat16),
            jax.ShapeDtypeStruct((8, ids.shape[1], 4 * SLOTS), jnp.bfloat16),
        ],
        in_specs=[space] * 5,
        out_specs=[space] * 5 + [pl.BlockSpec(memory_space=pltpu.VMEM)] * 3,
        scratch_shapes=[
            dma((2, shards)),
            dma((2, shards, 4)),
            dma((2, CHUNKS)),
            dma((CHUNKS, 4)),
            dma((experts,)),
            dma((3,)),
            dma((shards,)),
            dma((shards,)),
            dma((devices,)),
            dma((devices,)),
            dma((6,)),
            pltpu.VMEM((devices,) + ids.shape, ids.dtype),
            pltpu.VMEM((128, ids.shape[1]), jnp.float32),
            pltpu.VMEM((128, ids.shape[1]), jnp.float32),
        ],
        compiler_params=pltpu.CompilerParams(
            collective_id=number, has_side_effects=True, vmem_limit_bytes=16 * 2**20
        ),
        name="gather",
    )(flat, tall, tok, pack, ids)


def add_rows(acc, first, window, rows, step=16):
    def add(i, carry):
        here = pl.ds(pl.multiple_of(i * step, step), step)
        at = pl.ds(pl.multiple_of(first + i * step, step), step)
        acc[at] = (acc[at].astype(jnp.float32) + window[here].astype(jnp.float32)).astype(acc.dtype)
        return carry

    lax.fori_loop(0, rows // step, add, 0)


def reduce_kernel(
    dims, flat, tall, pack, partial, out_q, out_k, out_v, tall_out, pack_all, total,
    acc, tacc, yslot, zslot, yone, zall, ty, tz,
    load, yin, zin, yone_in, zall_in, ty_in, tz_in, flat_send, tall_send, spread_in, spread_out,
    tall_in, keep_tall, local,
    group_acc, group_near, group_cross, group_load, group_out, group_in, cross_out, cross_in,
):
    experts, shards = dims
    place = Place()
    greet_all(place, experts, shards)
    me = place.e * shards + place.f
    tall_keeps = []
    owner = place.z == place.e
    home = place.x == place.z // 2
    same = place.c == place.z % 2
    starts, sizes = flat_parts(flat.shape[1])
    sizes = (sizes[0], sizes[1] + pack.shape[1])
    height = tall.shape[1]
    chunk = height // CHUNKS
    part = partial.shape[1] // CHUNKS
    pending = []

    def go(condition, copy):
        run(condition, copy.start)
        pending.append((condition, copy))

    def both(a, b):
        return a if b is None else a & b

    load_tall = pltpu.make_async_copy(tall, tacc, load.at[0])
    load_flat = pltpu.make_async_copy(flat, acc.at[:, pl.ds(0, flat.shape[1])], load.at[1])
    load_pack = pltpu.make_async_copy(
        pack, acc.at[:, pl.ds(flat.shape[1], pack.shape[1])], load.at[2]
    )
    across_y = []
    order = (3, 2, 1, 0)

    def add_tall(k):
        piece = pl.ds(k * chunk, chunk)
        across_y.append(
            remote(
                tall.at[1 - place.y, piece], ty.at[piece], tall_send.at[0, k], ty_in.at[k],
                place.device("y"),
            )
        )

    def add_flat(j):
        target = place.ranked(j) * 2 + 1 - place.y
        across_y.append(
            remote(
                flat.at[target, pl.ds(starts[0], sizes[0])],
                yslot.at[place.ranked(j)],
                flat_send.at[0, target],
                yin.at[place.ranked(j)],
                place.device("y"),
            )
        )

    add_tall(0)
    add_tall(1)
    add_flat(3)
    add_tall(2)
    add_flat(2)
    add_tall(3)
    add_flat(1)
    add_flat(0)
    started = [0]

    def feed(count):
        while started[0] < min(count + 2, len(across_y)):
            if started[0] >= 2:
                across_y[started[0] - 2].wait_send()
            across_y[started[0]].start()
            started[0] += 1

    feed(0)
    load_tall.start()
    load_flat.start()
    load_pack.start()
    group_sends = []
    group_loads = []
    for half in (1 - place.x, place.x):
        for i in range(CHUNKS):
            piece = pl.ds(i * part, part)
            copy = remote(
                partial.at[half * 2 + 1 - place.c, piece], group_near.at[half, piece],
                group_out.at[half, i], group_in.at[half, i], place.device("c"),
            )
            copy.start()
            group_sends.append(copy)
            copy = pltpu.make_async_copy(
                partial.at[half * 2 + place.c, piece], group_acc.at[half, piece],
                group_load.at[half, i],
            )
            copy.start()
            group_loads.append(copy)

    def group_half(index, half):
        for i in range(CHUNKS):
            piece = pl.ds(i * part, part)
            window = group_near.at[half, piece]
            group_loads[index * CHUNKS + i].wait()
            remote(
                window, window, group_out.at[half, i], group_in.at[half, i], place.device("c")
            ).wait_recv()
            add_rows(group_acc.at[half], i * part, window, part)
            if index == 0:
                copy = remote(
                    group_acc.at[half, piece], group_cross.at[piece], cross_out.at[i],
                    cross_in.at[i], place.device("x"),
                )
                copy.start()
                group_sends.append(copy)

    def group_end():
        for i in range(CHUNKS):
            window = group_cross.at[pl.ds(i * part, part)]
            remote(window, window, cross_out.at[i], cross_in.at[i], place.device("c")).wait_recv()

            def add(t, carry):
                here = pl.ds(pl.multiple_of(i * part + t * 16, 16), 16)
                own = group_acc[place.x, here].astype(jnp.float32)
                total[here] = own + group_cross[here].astype(jnp.float32)
                return carry

            lax.fori_loop(0, part // 16, add, 0)

    load_tall.wait()
    load_flat.wait()
    load_pack.wait()

    def into(slots, sems, zd, side):
        index = jnp.where(zd == place.z, 4, zd) if side == BELOW else zd
        return slots.at[index], sems.at[index]

    def out_to(slots, sems, zd, side):
        there = place.z - 1 if side == ABOVE else place.z + 1
        index = jnp.where(zd == there, 4, zd) if side == BELOW else zd
        return slots.at[index], sems.at[index]

    def line(j, p, first, slots, sems, send_sem, target):
        zd = place.ranked(j)
        rows = sizes[p]
        for side, condition in (
            (ABOVE, (zd <= place.z) & (place.z < 3)),
            (BELOW, (zd >= place.z) & (place.z > 0)),
        ):
            window, sem = into(slots, sems, zd, side)

            def take(window=window, sem=sem):
                remote(window, window, send_sem, sem, place.device("c")).wait_recv()
                add_rows(acc.at[target], first, window, rows)

            if j == 0:
                condition = place.z < 3 if side == ABOVE else place.z > 0
            run(condition, take)
        if j == 0:
            return
        for side, axis, condition in ((ABOVE, DOWN, zd < place.z), (BELOW, UP, zd > place.z)):
            window, sem = out_to(slots, sems, zd, side)
            go(
                condition,
                remote(acc.at[target, pl.ds(first, rows)], window, send_sem, sem, place.device(axis)),
            )

    above_e, below_e = place.z > place.e, place.z < place.e
    hops = jnp.where(above_e, 3 - place.z, jnp.where(below_e, place.z, jnp.maximum(place.e, 3 - place.e)))

    def tall_round(r):
        k = r - hops
        live = (k >= 0) & (k < CHUNKS)
        k = jnp.clip(k, 0, CHUNKS - 1)
        first = pl.multiple_of(k * chunk, chunk)
        piece = pl.ds(first, chunk)

        @pl.when(live)
        def _():
            remote(
                ty.at[piece], ty.at[piece], tall_send.at[0, k], ty_in.at[k], place.device("c")
            ).wait_recv()
            add_rows(tacc.at[place.y], first, ty.at[piece], chunk)

        for index, condition in (
            (0, (place.z >= place.e) & (place.z < 3)),
            (1, (place.z <= place.e) & (place.z > 0)),
        ):
            window = tz.at[index, piece]

            def take(window=window, index=index):
                remote(
                    window, window, tall_send.at[1, k], tz_in.at[index, k], place.device("c")
                ).wait_recv()
                add_rows(tacc.at[place.y], first, window, chunk)

            run(live & condition, take)
        for index, axis, condition in ((0, DOWN, above_e), (1, UP, below_e)):
            go(
                live & condition,
                remote(
                    tacc.at[place.y, piece], tz.at[index, piece], tall_send.at[1, k],
                    tz_in.at[index, k], place.device(axis),
                ),
            )
        piece_out = tall_out.at[piece]
        keep = pltpu.make_async_copy(tacc.at[place.y, piece], piece_out, keep_tall.at[k])
        run(live & owner, keep.start)
        tall_keeps.append((live & owner, keep))
        for row, axis in ((2, "x"), (3, "c")):
            go(
                live & owner,
                remote(
                    tacc.at[place.y, piece], piece_out, tall_send.at[row, k], tall_in.at[k],
                    place.device(axis),
                ),
            )

    def flat_first(j):
        zd = place.ranked(j)
        target = zd * 2 + place.y
        window = yslot.at[zd]
        remote(window, window, flat_send.at[0, target], yin.at[zd], place.device("c")).wait_recv()
        add_rows(acc.at[target], starts[0], window, sizes[0])
        line(j, 0, starts[0], zslot, zin, flat_send.at[0, target], target)

    def flat_second(j, yr):
        zd = place.ranked(j)
        target = zd * 2 + (1 - place.y if yr else place.y)
        line(j, 1, starts[1], zall.at[yr], zall_in.at[yr], flat_send.at[1, target], target)

    flat_second(3, 1)
    flat_second(3, 0)
    tall_round(0)
    feed(1)
    tall_round(1)
    feed(2)
    flat_second(2, 1)
    flat_second(2, 0)
    flat_first(3)
    feed(3)
    group_half(0, 1 - place.x)
    tall_round(2)
    feed(4)
    flat_second(1, 1)
    flat_second(1, 0)
    flat_first(2)
    feed(5)
    tall_round(3)
    feed(6)
    flat_first(1)
    group_half(1, place.x)
    flat_second(0, 1)
    other = place.z * 2 + 1 - place.y
    go(
        None,
        remote(
            acc.at[other, pl.ds(starts[1], sizes[1])], yone, flat_send.at[1, other], yone_in.at[0],
            place.device("y"),
        ),
    )
    flat_second(0, 0)
    flat_first(0)
    remote(yone, yone, flat_send.at[1, other], yone_in.at[0], place.device("c")).wait_recv()
    add_rows(acc.at[place.f], starts[1], yone, sizes[1])
    cuts = []
    first = 0
    for out in (out_q, out_k, out_v):
        wide = out.shape[1] // experts
        cuts.append((out, pl.ds(0, flat.shape[1]), pl.ds(first, wide)))
        first += wide
    cuts.append((pack_all, pl.ds(flat.shape[1], pack.shape[1]), pl.ds(0, first)))

    def window_of(i, source):
        out = cuts[i][0]
        if i == 3:
            return out.at[source]
        wide = out.shape[1] // experts
        return out.at[:, pl.ds(pl.multiple_of(source * wide, 128), wide)]

    flat_keeps = []
    for i, (out, high, wide) in enumerate(cuts):
        done = acc.at[place.f, high, wide]
        keep = pltpu.make_async_copy(done, window_of(i, place.e), local.at[1 + i])
        keep.start()
        flat_keeps.append(keep)
        for row, axis in enumerate(("x", "c")):
            go(
                None,
                remote(
                    done, window_of(i, place.e), spread_out.at[row, i], spread_in.at[place.e, i],
                    place.device(axis),
                ),
            )
    tall_round(4)
    tall_round(5)
    tall_round(6)
    group_end()
    across = (1 - place.x) * 2 + place.c
    for i in range(4):
        window = window_of(i, across)
        relay = remote(window, window, spread_out.at[2, i], spread_in.at[across, i], place.device("c"))
        relay.wait_recv()
        go(None, relay)
    for k in range(CHUNKS):
        window = tall_out.at[pl.ds(k * chunk, chunk)]
        tall_relay = remote(window, window, tall_send.at[4, k], tall_in.at[k], place.device("c"))
        run(~owner, tall_relay.wait_recv)
        go(~home & same, tall_relay)
    for source in (place.x * 2 + 1 - place.c, (1 - place.x) * 2 + 1 - place.c):
        for i in range(4):
            window = window_of(i, source)
            remote(
                window, window, spread_out.at[2, i], spread_in.at[source, i], place.device("c")
            ).wait_recv()
    for copy in across_y[-2:]:
        copy.wait_send()
    for condition, copy in pending:
        run(condition, copy.wait_send)
    for keep in flat_keeps:
        keep.wait()
    for condition, keep in tall_keeps:
        run(condition, keep.wait)
    for copy in group_sends:
        copy.wait_send()


def reduce(experts, shards, number, flat, tall, pack, partial):
    space = pl.BlockSpec(memory_space=pl.ANY)
    dma = pltpu.SemaphoreType.DMA
    _, sizes = flat_parts(flat.shape[1])
    more = sizes[1] + pack.shape[1]
    width, wide = flat.shape[2], tall.shape[2]
    low = jnp.bfloat16
    return pl.pallas_call(
        functools.partial(reduce_kernel, (experts, shards)),
        out_shape=[
            jax.ShapeDtypeStruct((flat.shape[1], experts * (width - 2 * HEAD_SIZE)), low),
            jax.ShapeDtypeStruct((flat.shape[1], experts * HEAD_SIZE), low),
            jax.ShapeDtypeStruct((flat.shape[1], experts * HEAD_SIZE), low),
            jax.ShapeDtypeStruct(tall.shape[1:], low),
            jax.ShapeDtypeStruct((experts,) + pack.shape[1:], low),
            jax.ShapeDtypeStruct(partial.shape[1:], jnp.float32),
        ],
        in_specs=[space] * 4,
        out_specs=[space] * 5 + [pl.BlockSpec(memory_space=pltpu.VMEM)],
        scratch_shapes=[
            pltpu.VMEM((shards, flat.shape[1] + pack.shape[1], width), low),
            pltpu.VMEM(tall.shape, low),
            pltpu.VMEM((4, sizes[0], width), low),
            pltpu.VMEM((5, sizes[0], width), low),
            pltpu.VMEM((more, width), low),
            pltpu.VMEM((2, 5, more, width), low),
            pltpu.VMEM(tall.shape[1:], low),
            pltpu.VMEM((2,) + tall.shape[1:], low),
            dma((3,)),
            dma((4,)),
            dma((5,)),
            dma((1,)),
            dma((2, 5)),
            dma((CHUNKS,)),
            dma((2, CHUNKS)),
            dma((2, shards)),
            dma((5, CHUNKS)),
            dma((experts, 4)),
            dma((3, 4)),
            dma((CHUNKS,)),
            dma((CHUNKS,)),
            dma((5,)),
            pltpu.VMEM((2,) + partial.shape[1:], low),
            pltpu.VMEM((2,) + partial.shape[1:], low),
            pltpu.VMEM(partial.shape[1:], low),
            dma((2, CHUNKS)),
            dma((2, CHUNKS)),
            dma((2, CHUNKS)),
            dma((CHUNKS,)),
            dma((CHUNKS,)),
        ],
        compiler_params=pltpu.CompilerParams(
            collective_id=number, has_side_effects=True, vmem_limit_bytes=48 * 2**20
        ),
        name="reduce",
    )(flat, tall, pack, partial)


def group_gather_kernel(tok, out, x_out, x_in, c_out, c_in, relay_out, relay_in, local):
    place = Place()
    greet(place)
    across = (1 - place.x) * 2 + place.c
    chunk = tok.shape[0] // CHUNKS
    keep = pltpu.make_async_copy(tok, out.at[place.e], local.at[0])
    near = remote(tok, out.at[place.e], c_out.at[0], c_in.at[0], place.device("c"))
    copies = []
    for k in range(CHUNKS):
        piece = pl.ds(k * chunk, chunk)
        copies.append(
            remote(tok.at[piece], out.at[place.e, piece], x_out.at[k], x_in.at[k], place.device("x"))
        )
        copies[-1].start()
    near.start()
    keep.start()
    for k in range(CHUNKS):
        window = out.at[across, pl.ds(k * chunk, chunk)]
        remote(window, window, x_out.at[k], x_in.at[k], place.device("c")).wait_recv()
        relay = remote(window, window, relay_out.at[k], relay_in.at[k], place.device("c"))
        relay.start()
        copies.append(relay)
    for k in range(CHUNKS):
        window = out.at[(1 - place.x) * 2 + 1 - place.c, pl.ds(k * chunk, chunk)]
        remote(window, window, relay_out.at[k], relay_in.at[k], place.device("c")).wait_recv()
    near.wait()
    keep.wait()
    for copy in copies:
        copy.wait_send()


def group_gather(number, tok):
    space = pl.BlockSpec(memory_space=pl.ANY)
    dma = pltpu.SemaphoreType.DMA
    return pl.pallas_call(
        group_gather_kernel,
        out_shape=jax.ShapeDtypeStruct((4,) + tok.shape, tok.dtype),
        in_specs=[space],
        out_specs=space,
        scratch_shapes=[
            dma((CHUNKS,)), dma((CHUNKS,)), dma((1,)), dma((1,)), dma((CHUNKS,)), dma((CHUNKS,)), dma((1,)),
        ],
        compiler_params=pltpu.CompilerParams(
            collective_id=number, has_side_effects=True, vmem_limit_bytes=16 * 2**20
        ),
        name="group_gather",
    )(tok)


def group_scatter_kernel(
    partial, total, acc, near, cross, load_in, near_out, near_in, x_out, x_in
):
    place = Place()
    greet(place)
    rows = partial.shape[1]
    chunk = rows // CHUNKS
    sends = []
    loads = []
    for half in (1 - place.x, place.x):
        for k in range(CHUNKS):
            piece = pl.ds(k * chunk, chunk)
            copy = remote(
                partial.at[half * 2 + 1 - place.c, piece], near.at[half, piece], near_out.at[half, k],
                near_in.at[half, k], place.device("c"),
            )
            copy.start()
            sends.append(copy)
            load = pltpu.make_async_copy(
                partial.at[half * 2 + place.c, piece], acc.at[half, piece], load_in.at[half, k]
            )
            load.start()
            loads.append(load)
    for index, half in enumerate((1 - place.x, place.x)):
        for k in range(CHUNKS):
            piece = pl.ds(k * chunk, chunk)
            window = near.at[half, piece]
            loads[index * CHUNKS + k].wait()
            remote(window, window, near_out.at[half, k], near_in.at[half, k], place.device("c")).wait_recv()
            add_rows(acc.at[half], k * chunk, window, chunk)
            if index == 0:
                copy = remote(
                    acc.at[half, piece], cross.at[piece], x_out.at[k], x_in.at[k], place.device("x")
                )
                copy.start()
                sends.append(copy)
    for k in range(CHUNKS):
        window = cross.at[pl.ds(k * chunk, chunk)]
        remote(window, window, x_out.at[k], x_in.at[k], place.device("c")).wait_recv()

        def add(i, carry):
            here = pl.ds(pl.multiple_of(k * chunk + i * 16, 16), 16)
            total[here] = acc[place.x, here].astype(jnp.float32) + cross[here].astype(jnp.float32)
            return carry

        lax.fori_loop(0, chunk // 16, add, 0)
    for copy in sends:
        copy.wait_send()


def group_scatter(number, partial):
    dma = pltpu.SemaphoreType.DMA
    rows, width = partial.shape[1:]
    low = jnp.bfloat16
    return pl.pallas_call(
        group_scatter_kernel,
        out_shape=jax.ShapeDtypeStruct((rows, width), jnp.float32),
        in_specs=[pl.BlockSpec(memory_space=pl.ANY)],
        out_specs=pl.BlockSpec(memory_space=pltpu.VMEM),
        scratch_shapes=[
            pltpu.VMEM((2, rows, width), low),
            pltpu.VMEM((2, rows, width), low),
            pltpu.VMEM((rows, width), low),
            dma((2, CHUNKS)),
            dma((2, CHUNKS)),
            dma((2, CHUNKS)),
            dma((CHUNKS,)),
            dma((CHUNKS,)),
        ],
        compiler_params=pltpu.CompilerParams(
            collective_id=number, has_side_effects=True, vmem_limit_bytes=16 * 2**20
        ),
        name="group_scatter",
    )(partial)


BLOCK = 256


def dot_last(a, b):
    return lax.dot_general(a, b, (((1,), (1,)), ((), ())), preferred_element_type=jnp.float32)


def dot(a, b):
    return jnp.dot(a, b, preferred_element_type=jnp.float32)


def turn(rows):
    lane = lax.broadcasted_iota(jnp.int32, rows.shape, 1)
    half = HEAD_SIZE // 2
    return pltpu.roll(rows, half, 1) * jnp.where(lane < half, -1.0, 1.0)


def mask_block(r, count, ids_column, ids_row, bias):
    queries = pl.ds(r * BLOCK, BLOCK)

    def part(i, carry):
        keys = pl.ds(pl.multiple_of(i * BLOCK, BLOCK), BLOCK)
        key_at = lax.broadcasted_iota(jnp.int32, (BLOCK, BLOCK), 0) + i * BLOCK
        query_at = lax.broadcasted_iota(jnp.int32, (BLOCK, BLOCK), 1) + r * BLOCK
        allowed = (ids_column[keys] == ids_row[:, queries]) & (key_at <= query_at)
        bias[keys] = jnp.where(allowed, 0.0, -1e30)
        return carry

    lax.fori_loop(0, count // BLOCK, part, 0)


def project_steps(
    tok, w_qkv, gain_one, gain_q, gain_k, cosine, sine, normed, raw, query_rot, key_rot, value, inverses
):
    heads = query_rot.shape[1] // HEAD_SIZE
    low = jnp.bfloat16

    def rotated(v, rows, gain):
        u = v * inverse_rms(v) * gain
        return (u * cosine[rows] + turn(u) * sine[rows]).astype(low)

    def norm(r):
        def part(i, carry):
            here = pl.ds(pl.multiple_of(r * BLOCK + i * 16, 16), 16)
            x = tok[here].astype(jnp.float32)
            inverse = inverse_rms(x)
            inverses[here] = inverse
            normed[here] = (x * inverse * gain_one[...]).astype(low)
            return carry

        lax.fori_loop(0, BLOCK // 16, part, 0, unroll=2)

    def multiply(r):
        rows = pl.ds(r * BLOCK, BLOCK)

        def pair(i, carry):
            column = pl.ds(pl.multiple_of(i * 2 * HEAD_SIZE, 2 * HEAD_SIZE), 2 * HEAD_SIZE)
            both = dot(normed[rows], w_qkv[:, column])
            raw[rows, column] = both
            for k in range(2):
                at = pl.ds(pl.multiple_of((2 * i + k) * HEAD_SIZE, HEAD_SIZE), HEAD_SIZE)
                one = both[:, k * HEAD_SIZE : (k + 1) * HEAD_SIZE]
                query_rot[rows, at] = rotated(one, rows, gain_q[...])
            return carry

        lax.fori_loop(0, heads // 2, pair, 0)
        last = pl.ds(heads * HEAD_SIZE, 2 * HEAD_SIZE)
        both = dot(normed[rows], w_qkv[:, last])
        raw[rows, last] = both
        key_rot[rows] = rotated(both[:, :HEAD_SIZE], rows, gain_k[...])
        value[rows] = both[:, HEAD_SIZE:].astype(low)

    steps = []
    for r in range(tok.shape[0] // BLOCK):
        steps.append(functools.partial(norm, r))
        steps.append(functools.partial(multiply, r))
    return steps


def attend_steps(query_rot, key_rot, value, ids_column, ids_row, mixed, bias, value_t):
    length = key_rot.shape[0]
    heads = query_rot.shape[1] // HEAD_SIZE
    scale = HEAD_SIZE ** (-0.5)

    def prepare(r):
        if r == 0:
            value_t[...] = value[...].T
        mask_block(r, (r + 1) * BLOCK, ids_column, ids_row, bias)

    def heads_of(r, first, some):
        rows = pl.ds(r * BLOCK, BLOCK)
        count = (r + 1) * BLOCK

        def head(h, carry):
            column = pl.ds(pl.multiple_of(h * HEAD_SIZE, HEAD_SIZE), HEAD_SIZE)
            scores = dot_last(key_rot[:count], query_rot[rows, column]) * scale + bias[:count]
            shifted = jnp.exp(scores - jnp.max(scores, 0, keepdims=True))
            weights = shifted * (1.0 / jnp.sum(shifted, 0, keepdims=True))
            out = dot(value_t[:, :count], weights.astype(jnp.bfloat16))
            mixed[rows, column] = out.T.astype(jnp.bfloat16)
            return carry

        lax.fori_loop(first, first + some, head, 0, unroll=2)

    steps = []
    for r in range(length // BLOCK):
        steps.append(functools.partial(prepare, r))
        some = heads if r == 0 else heads // 2
        for first in range(0, heads, some):
            steps.append(functools.partial(heads_of, r, first, some))
    return steps


def load(pairs, sems):
    copies = [pltpu.make_async_copy(a, b, sems.at[i]) for i, (a, b) in enumerate(pairs)]
    for copy in copies:
        copy.start()
    return copies


def attention(tokens, w_qkv, gain_one, gain_q, gain_k, cosine, sine, ids_column, ids_row, heads):
    length, width = tokens.shape
    wide = w_qkv.shape[1]
    span = heads * HEAD_SIZE
    low, f32 = jnp.bfloat16, jnp.float32
    space, vmem = pl.BlockSpec(memory_space=pl.ANY), pl.BlockSpec(memory_space=pltpu.VMEM)
    shapes = [
        ((length, width), low),
        ((length, wide), f32),
        ((length, span), low),
        ((length, HEAD_SIZE), low),
        ((length, HEAD_SIZE), low),
        ((length, span), low),
        ((length, 1), f32),
    ]

    def steps(*refs):
        ins, outs, scratch = split(refs, (9, 7, 15))
        tok, weight, cos_held, sin_held, in_sems, out_sems, bias, value_t = scratch[:8]
        results = scratch[8:]
        copies = load(
            [(ins[0], tok), (ins[1], weight), (ins[5], cos_held), (ins[6], sin_held)], in_sems
        )

        def begin():
            for copy in copies:
                copy.wait()

        saved = []

        def save(picks):
            for i in picks:
                copy = pltpu.make_async_copy(results[i], outs[i], out_sems.at[i])
                copy.start()
                saved.append(copy)

        def end():
            save((5, 6))
            for copy in saved:
                copy.wait()

        return (
            [begin]
            + project_steps(tok, weight, *ins[2:5], cos_held, sin_held, *results[:5], results[6])
            + [functools.partial(save, range(5))]
            + attend_steps(*results[2:5], *ins[7:9], results[5], bias, value_t)
            + [end]
        )

    return Extra(
        (tokens, w_qkv, gain_one, gain_q, gain_k, cosine, sine, ids_column, ids_row),
        [space] * 2 + [vmem] * 3 + [space] * 2 + [vmem] * 2,
        [jax.ShapeDtypeStruct(*shape) for shape in shapes],
        [space] * 7,
        [
            pltpu.VMEM(tokens.shape, low),
            pltpu.VMEM(w_qkv.shape, low),
            pltpu.VMEM(cosine.shape, f32),
            pltpu.VMEM(sine.shape, f32),
            pltpu.SemaphoreType.DMA((4,)),
            pltpu.SemaphoreType.DMA((7,)),
            pltpu.VMEM((length, BLOCK), f32),
            pltpu.VMEM((HEAD_SIZE, length), low),
        ]
        + [pltpu.VMEM(*shape) for shape in shapes],
        steps,
    )


def attend_back_steps(
    query_rot, key_rot, value, raw, grad_mixed, ids_column, ids_row, gain_q, gain_k, cosine, sine,
    grad_raw, grad_gains, bias, key_t, grad_key, grad_value, sums,
):
    length = key_rot.shape[0]
    heads = query_rot.shape[1] // HEAD_SIZE
    scale = HEAD_SIZE ** (-0.5)
    low = jnp.bfloat16

    def back(grad, rows, column, gain, index):
        unit = grad * cosine[rows] - turn(grad * sine[rows])
        v = raw[rows, column]
        inverse = inverse_rms(v)
        sums[index] += jnp.sum((unit * v * inverse).reshape(-1, 8, HEAD_SIZE), 0)
        grad_raw[rows, column] = norm_backward(unit, v, inverse, gain).astype(low)

    def prepare(r):
        if r == 0:
            key_t[...] = key_rot[...].T
            grad_key[...] = jnp.zeros_like(grad_key)
            grad_value[...] = jnp.zeros_like(grad_value)
            sums[...] = jnp.zeros_like(sums)
        mask_block(r, (r + 1) * BLOCK, ids_column, ids_row, bias)

    def heads_of(r, first, some):
        rows = pl.ds(r * BLOCK, BLOCK)
        count = (r + 1) * BLOCK

        def head(h, carry):
            column = pl.ds(pl.multiple_of(h * HEAD_SIZE, HEAD_SIZE), HEAD_SIZE)
            query = query_rot[rows, column]
            grad_out = grad_mixed[rows, column]
            scores = dot_last(key_rot[:count], query) * scale + bias[:count]
            shifted = jnp.exp(scores - jnp.max(scores, 0, keepdims=True))
            weights = shifted * (1.0 / jnp.sum(shifted, 0, keepdims=True))
            grad_value[:count] += dot(weights.astype(low), grad_out)
            grad_weights = dot_last(value[:count], grad_out)
            spread = jnp.sum(weights * grad_weights, 0, keepdims=True)
            grad_scores = (weights * (grad_weights - spread)).astype(low)
            grad_key[:count] += dot(grad_scores, query)
            grad_query = dot(key_t[:, :count], grad_scores).T * scale
            back(grad_query, rows, column, gain_q[...], 0)
            return carry

        lax.fori_loop(first, first + some, head, 0, unroll=2)

    def last():
        column = pl.ds(heads * HEAD_SIZE, HEAD_SIZE)
        for r in range(length // BLOCK):
            rows = pl.ds(r * BLOCK, BLOCK)
            back(grad_key[rows] * scale, rows, column, gain_k[...], 1)
            grad_raw[rows, pl.ds((heads + 1) * HEAD_SIZE, HEAD_SIZE)] = grad_value[rows].astype(low)
        grad_gains[...] = jnp.sum(sums[...], 1)

    steps = []
    for r in range(length // BLOCK):
        steps.append(functools.partial(prepare, r))
        some = heads if r == 0 else (heads // 2 if r == 1 else heads // 4)
        for first in range(0, heads, some):
            steps.append(functools.partial(heads_of, r, first, some))
    return steps + [last]


def attention_back(
    query_rot, key_rot, value, raw, mixed, grad_low, w_mix, normed_one, tokens, w_qkv, inverses,
    ids_column, ids_row, gain_q, gain_k, cosine, sine,
):
    length, width = tokens.shape
    span, wide = mixed.shape[1], raw.shape[1]
    tiles = width // BLOCK
    low, f32 = jnp.bfloat16, jnp.float32
    space, vmem = pl.BlockSpec(memory_space=pl.ANY), pl.BlockSpec(memory_space=pltpu.VMEM)
    whole = (query_rot, key_rot, value, raw, mixed, cosine, sine, inverses)
    streamed = (grad_low, w_mix, normed_one, tokens, w_qkv)
    own_rows = grad_low.shape[0]
    piece = own_rows // CHUNKS
    small = (ids_column, ids_row, gain_q, gain_k)

    def dot_first(a, b):
        return lax.dot_general(a, b, (((0,), (0,)), ((), ())), preferred_element_type=f32)

    def steps(*refs):
        ins, outs, scratch = split(refs, (17, 5, 27))
        held, (in_sems, grad_raw), work, tile_refs, group = split(scratch, (8, 2, 5, 4, 8))
        tall_in, tall_out, wide_out, sems = tile_refs
        mine, mix, normed, tok, weight = ins[8:13]
        inverse = held[7]
        branch, grad_mixed, mix_in, mix_sems, x_out, x_in, c_out, c_in = group
        place = Place()
        beside, other = place.at((1 - place.x, place.y), place.c), place.device("c")
        across = (1 - place.x) * 2 + place.c
        gains, grad_mix, grad_qkv, grad_normed, grad_gain = outs
        copies = load(list(zip(ins[:8], held)), in_sems)

        def rows_from(source, k):
            return branch.at[pl.ds(pl.multiple_of(source * own_rows + k * piece, piece), piece)]

        def own(k):
            return mine.at[pl.ds(k * piece, piece)]

        sends = []
        keeps = []
        for k in range(CHUNKS):
            sends.append(remote(own(k), rows_from(place.e, k), x_out.at[k], x_in.at[k], beside))
            sends.append(remote(own(k), rows_from(place.e, k), c_out.at[0, k], c_in.at[0, k], other))
            keeps.append(pltpu.make_async_copy(own(k), rows_from(place.e, k), mix_sems.at[2 + k]))
        for copy in sends + keeps:
            copy.start()

        def relay(k):
            window = rows_from(across, k)
            copy = remote(window, window, c_out.at[1, k], c_in.at[1, k], other)
            remote(window, window, x_out.at[k], x_in.at[k], other).wait_recv()
            copy.start()
            sends.append(copy)

        def mix_tile(t):
            return pltpu.make_async_copy(mix.at[at(t)], mix_in.at[t % 2], mix_sems.at[t % 2])

        def arrived():
            mix_tile(0).start()
            for copy in keeps:
                copy.wait()
            for k in range(CHUNKS):
                window = rows_from(place.x * 2 + 1 - place.c, k)
                remote(window, window, c_out.at[0, k], c_in.at[0, k], other).wait_recv()
                window = rows_from((1 - place.x) * 2 + 1 - place.c, k)
                remote(window, window, c_out.at[1, k], c_in.at[1, k], other).wait_recv()
            for copy in sends:
                copy.wait_send()

        def mixed_grad(t):
            mix_tile(t).wait()
            if t + 1 < span // BLOCK:
                mix_tile(t + 1).start()
            grad_mixed[:, at(t)] = dot_last(branch[...], mix_in[t % 2]).astype(low)

        def at(t):
            return pl.ds(t * BLOCK, BLOCK)

        def fetch(i):
            kind, t, slot = i // tiles, i % tiles, i % 2
            if kind == 0:
                return []
            source = (None, normed, tok)[kind]
            found = [
                pltpu.make_async_copy(source.at[:, at(t)], tall_in.at[slot], sems.at[0, slot])
            ]
            if kind == 2:
                found.append(
                    pltpu.make_async_copy(
                        weight.at[at(t)], mix_in.at[slot, :, pl.ds(0, wide)], sems.at[1, slot]
                    )
                )
            return found

        def store(i):
            kind, t, slot = i // tiles, i % tiles, i % 2
            if kind == 1:
                return pltpu.make_async_copy(
                    wide_out.at[slot], grad_qkv.at[at(t)], sems.at[2, slot]
                )
            target = grad_normed if kind else grad_mix
            return pltpu.make_async_copy(tall_out.at[slot], target.at[:, at(t)], sems.at[2, slot])

        def begin():
            for copy in copies:
                copy.wait()

        def tile(i):
            kind, t, slot = i // tiles, i % tiles, i % 2
            for copy in fetch(i):
                copy.wait()
            if i + 1 < 3 * tiles:
                for copy in fetch(i + 1):
                    copy.start()
            if i >= 2:
                store(i - 2).wait()
            if kind == 0:
                tall_out[slot] = dot_first(held[4][...], branch[:, at(t)]).astype(low)
            elif kind == 1:
                wide_out[slot] = dot_first(tall_in[slot], grad_raw[...]).astype(low)
            else:
                found = dot_last(grad_raw[...], mix_in[slot, :, :wide])
                scaled = tall_in[slot].astype(f32) * inverse[...]
                grad_gain[:, at(t)] = jnp.sum(found * scaled, 0, keepdims=True)
                tall_out[slot] = found.astype(low)
            store(i).start()

        def end():
            for i in (3 * tiles - 2, 3 * tiles - 1):
                store(i).wait()

        jobs = [functools.partial(tile, i) for i in range(3 * tiles)]
        back = attend_back_steps(
            *held[:4], grad_mixed, *ins[13:], *held[5:7], grad_raw, gains, *work
        )
        start = [functools.partial(relay, k) for k in range(CHUNKS)] + [arrived]
        start += [functools.partial(mixed_grad, t) for t in range(span // BLOCK)]
        return [begin] + start + back + jobs + [end]

    return Extra(
        whole + streamed + small,
        [space] * 13 + [vmem] * 4,
        [
            jax.ShapeDtypeStruct((2, HEAD_SIZE), f32),
            jax.ShapeDtypeStruct((span, width), low),
            jax.ShapeDtypeStruct((width, wide), low),
            jax.ShapeDtypeStruct((length, width), low),
            jax.ShapeDtypeStruct((1, width), f32),
        ],
        [vmem, space, space, space, vmem],
        [pltpu.VMEM(a.shape, a.dtype) for a in whole]
        + [
            pltpu.SemaphoreType.DMA((8,)),
            pltpu.VMEM(raw.shape, low),
            pltpu.VMEM((length, BLOCK), f32),
            pltpu.VMEM((HEAD_SIZE, length), low),
            pltpu.VMEM((length, HEAD_SIZE), f32),
            pltpu.VMEM((length, HEAD_SIZE), f32),
            pltpu.VMEM((2, 8, HEAD_SIZE), f32),
            pltpu.VMEM((2, length, BLOCK), low),
            pltpu.VMEM((2, length, BLOCK), low),
            pltpu.VMEM((2, BLOCK, wide), low),
            pltpu.SemaphoreType.DMA((3, 2)),
            pltpu.VMEM((length, width), low),
            pltpu.VMEM((length, span), low),
            pltpu.VMEM((2, BLOCK, width), low),
            pltpu.SemaphoreType.DMA((2 + CHUNKS,)),
            pltpu.SemaphoreType.DMA((CHUNKS,)),
            pltpu.SemaphoreType.DMA((CHUNKS,)),
            pltpu.SemaphoreType.DMA((2, CHUNKS)),
            pltpu.SemaphoreType.DMA((2, CHUNKS)),
        ],
        steps,
    )


def weight_grads(rows, grad_result, inner, grad_a, grad_b):
    count, width = rows.shape
    inside = inner.shape[1]
    low, f32 = jnp.bfloat16, jnp.float32
    space = pl.BlockSpec(memory_space=pl.ANY)
    tiles = width // BLOCK

    def dot_first(a, b):
        return lax.dot_general(a, b, (((0,), (0,)), ((), ())), preferred_element_type=f32)

    def steps(*refs):
        ins, outs, scratch = split(refs, (5, 3, 9))
        a_held, b_held, inner_held, tile, wide, tall, in_sems, tile_sems, out_sems = scratch
        copies = load([(ins[3], a_held), (ins[4], b_held), (ins[2], inner_held)], in_sems)

        def fetch(i):
            source = ins[0] if i < tiles else ins[1]
            columns = pl.ds((i % tiles) * BLOCK, BLOCK)
            return pltpu.make_async_copy(source.at[:, columns], tile.at[i % 2], tile_sems.at[i % 2])

        def store(i, k):
            at = pl.ds((i % tiles) * BLOCK, BLOCK)
            if i < tiles:
                return pltpu.make_async_copy(wide.at[k, i % 2], outs[k].at[at], out_sems.at[k, i % 2])
            return pltpu.make_async_copy(tall.at[i % 2], outs[2].at[:, at], out_sems.at[2, i % 2])

        def begin():
            fetch(0).start()
            for copy in copies:
                copy.wait()

        def prepare(i):
            fetch(i).wait()
            if i + 1 < 2 * tiles:
                fetch(i + 1).start()

        def first(i, k):
            if k == 0:
                prepare(i)
            if i >= 2:
                store(i - 2, k).wait()
            wide[k, i % 2] = dot_first(tile[i % 2], (a_held, b_held)[k][...])
            store(i, k).start()

        def second(i):
            prepare(i)
            if i >= tiles + 2:
                store(i - 2, 2).wait()
            tall[i % 2] = dot_first(inner_held[...], tile[i % 2])
            store(i, 2).start()

        def end():
            for i in (tiles - 2, tiles - 1):
                store(i, 0).wait()
                store(i, 1).wait()
            for i in (2 * tiles - 2, 2 * tiles - 1):
                store(i, 2).wait()

        found = [begin]
        for i in range(tiles):
            found += [functools.partial(first, i, 0), functools.partial(first, i, 1)]
        for i in range(tiles, 2 * tiles):
            found.append(functools.partial(second, i))
        return found + [end]

    return Extra(
        (rows, grad_result, inner, grad_a, grad_b),
        [space] * 5,
        [
            jax.ShapeDtypeStruct((width, inside), f32),
            jax.ShapeDtypeStruct((width, inside), f32),
            jax.ShapeDtypeStruct((inside, width), f32),
        ],
        [space] * 3,
        [
            pltpu.VMEM((count, inside), low),
            pltpu.VMEM((count, inside), low),
            pltpu.VMEM((count, inside), low),
            pltpu.VMEM((2, count, BLOCK), low),
            pltpu.VMEM((2, 2, BLOCK, inside), f32),
            pltpu.VMEM((2, inside, BLOCK), f32),
            pltpu.SemaphoreType.DMA((3,)),
            pltpu.SemaphoreType.DMA((2,)),
            pltpu.SemaphoreType.DMA((3, 2)),
        ],
        steps,
    )


WIDE = 512


def dispatch_expert_kernel(
    dims, tok, sel, small, grads, picks, ids, w_gate, w_up, w_down,
    small_all, rows_out, weighted, grad_result, inner, grad_a, grad_b, grad_rows, gate_grad,
    held, stage, picked, arrive, leave, pick_out, pick_in, local, small_out, small_in,
    gates, weights_in, gate_held, up_held, down_held, g_held, g_in,
    weighted_s, result_s, inner_s, a_s, b_s, rows_s, a_wide, b_wide, store_sems, keep_sems,
):
    experts, shards = dims
    low, f32 = jnp.bfloat16, jnp.float32
    place = Place()
    width = tok.shape[1]
    near, far = place.line()
    mine = (place.x, place.y)
    me = place.e * shards + place.f
    greet_all(place, *dims)
    end_small = exchange_small(
        place, dims, lambda i: small, small_all, small_out, small_in, local.at[1]
    )
    keep = pltpu.make_async_copy(tok, held.at[place.z], local.at[0])
    keep.start()
    loads = load([(w_gate.at[0], gate_held), (w_up.at[0], up_held), (w_down.at[0], down_held)], weights_in)
    pending = []
    targets = (place.device("c"), place.at(far, place.c), place.at(far, 1 - place.c))
    half = tok.shape[0] // HALVES

    def pick(ar, zs):
        block = ar * 4 + zs
        number = block_number(mine, place.c, ar, zs)

        def tile(i, carry):
            columns = pl.ds(pl.multiple_of(i * WIDE, WIDE), WIDE)
            chosen = dot(sel[block], held[block, :, columns]).astype(low)
            picked[number, :, columns] = chosen[:SLOTS]
            stage[block, :, columns] = chosen[SLOTS:]
            return carry

        lax.fori_loop(0, width // WIDE, tile, 0)
        for k in (2, 1, 0):
            away = remote(
                stage.at[block, pl.ds(k * SLOTS, SLOTS)], picked.at[number],
                pick_out.at[block, k], pick_in.at[number], targets[k],
            )
            away.start()
            pending.append((None, away))

    def wait_rows(i):
        xs, cs, ys = i // 16, i // 8 % 2, i % 2
        inside = (cs == place.c) & jnp.where(place.c == 0, ys == place.y, xs == place.x)

        @pl.when(~inside)
        def _():
            window = picked.at[i]
            remote(window, window, pick_out.at[0, 0], pick_in.at[i], place.device("c")).wait_recv()

    def sources(n):
        first = n % 2 * 16 + place.ranked(n // 2) * 2
        return first, first + 8

    def grads_of(n):
        return [
            pltpu.make_async_copy(
                grads.at[pl.ds(first, 2)], g_held.at[n % 2, pl.ds(2 * k, 2)], g_in.at[n % 2, k]
            )
            for k, first in enumerate(sources(n))
        ]

    kept = []
    for copy in grads_of(0):
        copy.start()

    def stores(n):
        pairs = (
            (weighted_s, weighted), (result_s, grad_result), (inner_s, inner), (a_s, grad_a),
            (b_s, grad_b), (rows_s, grad_rows),
        )
        return [
            pltpu.make_async_copy(
                source.at[pl.ds(2 * k, 2)], target.at[pl.ds(first, 2)], store_sems.at[i, k]
            )
            for i, (source, target) in enumerate(pairs)
            for k, first in enumerate(sources(n))
        ]

    def compute(n):
        first, second = sources(n)
        from_devices = (first, first + 1, second, second + 1)
        if n == 0:
            end_small()
            copy = pltpu.make_async_copy(small_all, gates, local.at[2])
            copy.start()
            for done in loads:
                done.wait()
            copy.wait()
        if n + 1 < 8:
            for copy in grads_of(n + 1):
                copy.start()
        for i in from_devices:
            wait_rows(i)
        for k, start in enumerate((first, second)):
            copy = pltpu.make_async_copy(
                picked.at[pl.ds(start, 2)], rows_out.at[pl.ds(start, 2)], keep_sems.at[n, k]
            )
            copy.start()
            kept.append(copy)
        here = []
        for i in from_devices:
            value = jnp.sum(jnp.where(ids[i] == me, gates[i], 0.0), 0, keepdims=True)
            here.append(jnp.sum(picks[i].astype(f32) * value, -1, keepdims=True))
        here = jnp.concatenate(here, 0)
        count = 4 * SLOTS
        x = jnp.concatenate([picked[i] for i in from_devices], 0)
        a_wide[...] = dot(x, gate_held[...])
        b_wide[...] = dot(x, up_held[...])
        for copy in grads_of(n):
            copy.wait()
        if n:
            for copy in stores(n - 1):
                copy.wait()
        inner_low = (jax.nn.silu(a_wide[...]) * b_wide[...]).astype(low)
        inner_s[...] = inner_low.reshape(inner_s.shape)

        def forward(t, found):
            columns = pl.ds(pl.multiple_of(t * WIDE, WIDE), WIDE)
            result = dot(inner_s[...].reshape(count, -1), down_held[:, columns])
            g = g_held[n % 2, :, :, columns].reshape(count, WIDE).astype(f32)
            weighted_s[:, :, columns] = (result * here).astype(low).reshape(4, SLOTS, WIDE)
            result_s[:, :, columns] = (g * here).astype(low).reshape(4, SLOTS, WIDE)
            return found + jnp.sum(result * g, -1, keepdims=True)

        found = lax.fori_loop(0, width // WIDE, forward, jnp.zeros((count, 1), f32))
        for k, i in enumerate(from_devices):
            part = picks[i].astype(f32) * found[k * SLOTS : (k + 1) * SLOTS]
            gate_grad[i] = jnp.broadcast_to(jnp.sum(part, 0, keepdims=True), gate_grad.shape[1:])
        grad_inner = dot_last(result_s[...].reshape(count, width), down_held[...])
        a, b = a_wide[...], b_wide[...]
        sigmoid = jax.nn.sigmoid(a)
        slope = sigmoid * (1.0 + a * (1.0 - sigmoid))
        a_s[...] = (grad_inner * b * slope).astype(low).reshape(a_s.shape)
        b_s[...] = (grad_inner * (a * sigmoid)).astype(low).reshape(b_s.shape)

        def backward(t, carry):
            columns = pl.ds(pl.multiple_of(t * WIDE, WIDE), WIDE)
            total = dot_last(a_s[...].reshape(count, -1), gate_held[columns])
            total += dot_last(b_s[...].reshape(count, -1), up_held[columns])
            rows_s[:, :, columns] = total.astype(low).reshape(4, SLOTS, WIDE)
            return carry

        lax.fori_loop(0, width // WIDE, backward, 0)
        for copy in stores(n):
            copy.start()

    work = {3: (0,), 5: (1,), 6: (2,), 7: (3, 4, 5, 6, 7)}
    for event, (ar, j) in enumerate(FAR_FIRST[::-1]):
        zs = place.ranked(j)
        block = ar * 4 + zs
        for h in range(HALVES):
            part = pl.ds(h * half, half)
            window = held.at[block, part]
            if ar or j:
                remote(
                    window, window, leave.at[zs, 0, h], arrive.at[block, h], place.device("c")
                ).wait_recv()
            if ar:
                continue
            source = tok.at[part] if j == 0 else window
            onward = (
                (UP, zs, 0, (zs <= place.z) & (place.z < 3)),
                (DOWN, zs, 1, (zs >= place.z) & (place.z > 0)),
                ("near", 4 + zs, 2, None),
            )
            for axis, there, k, condition in onward:
                device = place.at(near, place.c) if axis == "near" else place.device(axis)
                copy = remote(
                    source, held.at[there, part], leave.at[zs, k, h], arrive.at[there, h], device
                )
                run(condition, copy.start)
                pending.append((condition, copy))
        if not ar and j == 0:
            keep.wait()
        pick(ar, zs)
        for n in work.get(event, ()):
            compute(n)
    for copy in stores(7):
        copy.wait()
    for copy in kept:
        copy.wait()
    for condition, copy in pending:
        run(condition, copy.wait_send)


def dispatch_expert(experts, shards, number, tok, sel, small, grads, picks, ids, w_gate, w_up, w_down):
    rows, width = tok.shape
    devices = experts * shards
    inside = w_gate.shape[2]
    space = pl.BlockSpec(memory_space=pl.ANY)
    vmem = pl.BlockSpec(memory_space=pltpu.VMEM)
    dma = pltpu.SemaphoreType.DMA
    low, f32 = jnp.bfloat16, jnp.float32

    def lots(columns):
        return jax.ShapeDtypeStruct((devices, SLOTS, columns), low)

    def some(columns):
        return pltpu.VMEM((4, SLOTS, columns), low)

    return pl.pallas_call(
        functools.partial(dispatch_expert_kernel, (experts, shards)),
        out_shape=[
            jax.ShapeDtypeStruct((devices,) + small.shape, f32),
            lots(width), lots(width), lots(width), lots(inside), lots(inside), lots(inside), lots(width),
            jax.ShapeDtypeStruct((devices, 8, rows), f32),
        ],
        in_specs=[space, vmem, space, space, vmem, vmem, space, space, space],
        out_specs=[space] * 8 + [vmem],
        scratch_shapes=[
            pltpu.VMEM((8, rows, width), low),
            pltpu.VMEM((8, 3 * SLOTS, width), low),
            pltpu.VMEM((devices, SLOTS, width), low),
            dma((8, HALVES)),
            dma((4, 3, HALVES)),
            dma((8, 3)),
            dma((devices,)),
            dma((3,)),
            dma((devices,)),
            dma((devices,)),
            pltpu.VMEM((devices,) + small.shape, f32),
            dma((3,)),
            pltpu.VMEM(w_gate.shape[1:], low),
            pltpu.VMEM(w_up.shape[1:], low),
            pltpu.VMEM(w_down.shape[1:], low),
            pltpu.VMEM((2, 4, SLOTS, width), low),
            dma((2, 2)),
            some(width), some(width), some(inside), some(inside), some(inside), some(width),
            pltpu.VMEM((4 * SLOTS, inside), f32),
            pltpu.VMEM((4 * SLOTS, inside), f32),
            dma((6, 2)),
            dma((8, 2)),
        ],
        compiler_params=pltpu.CompilerParams(
            collective_id=number, has_side_effects=True, vmem_limit_bytes=62 * 2**20
        ),
        name="dispatch_expert",
    )(tok, sel, small, grads, picks, ids, w_gate, w_up, w_down)


def local(
    layer_input,
    doc_ids,
    expert_ids,
    w_query,
    w_key,
    w_value,
    w_out,
    w_router,
    gain_attn,
    gain_ffn,
    gain_query,
    gain_key,
    w_gate,
    w_up,
    w_down,
    grad_output,
):
    single_float = jnp.float32
    brain_float_half = jnp.bfloat16
    row_count = layer_input.shape[1]
    width = layer_input.shape[2]
    length_total = doc_ids.shape[1]
    query_groups = QUERY_HEADS // KEY_VALUE_HEADS
    scale = HEAD_SIZE ** (-0.5)
    experts = w_router.shape[1]
    capacity = max(2, 6 * row_count * TOP // (5 * experts))
    pairs = row_count * TOP
    (
        full_query,
        gathered_key,
        full_value,
        full_out,
        full_router,
        gain_one,
        gain_two,
        gain_q,
        key_gain_vector,
    ) = (
        lax.all_gather(w_query, FSDP, axis=0, tiled=True),
        lax.all_gather(w_key, FSDP, axis=0, tiled=True),
        lax.all_gather(w_value, FSDP, axis=0, tiled=True),
        lax.all_gather(w_out, FSDP, axis=0, tiled=True),
        lax.all_gather(w_router, FSDP, axis=0, tiled=True),
        lax.all_gather(gain_attn, FSDP, axis=0, tiled=True),
        lax.all_gather(gain_ffn, FSDP, axis=0, tiled=True),
        lax.all_gather(gain_query, FSDP, axis=0, tiled=True),
        lax.all_gather(gain_key, FSDP, axis=0, tiled=True),
    )
    gain_one = gain_one.astype(single_float)
    gain_two = gain_two.astype(single_float)
    gain_q = gain_q.astype(single_float)
    key_gain_vector = key_gain_vector.astype(single_float)
    inputs = layer_input[0].astype(single_float)
    offset = lax.axis_index(EXPERT) * row_count
    own_pos = offset + jnp.arange(row_count, dtype=jnp.int32)
    all_pos = jnp.arange(length_total, dtype=jnp.int32)
    seq_ids = doc_ids[0]
    own_ids = lax.dynamic_slice_in_dim(seq_ids, offset, row_count)
    allowed = (own_ids[:, None] == seq_ids[None, :]) & (own_pos[:, None] >= all_pos[None, :])
    cosine_table, sine_table = angles(own_pos)
    cosine_table = cosine_table[:, None, :]
    sine_table = sine_table[:, None, :]
    scale_one = inverse_rms(inputs)
    normalized_input = (inputs * scale_one * gain_one).astype(brain_float_half)
    query_raw = jnp.dot(normalized_input, full_query, preferred_element_type=single_float).reshape(
        row_count, QUERY_HEADS, HEAD_SIZE
    )
    key_unnormalized = jnp.dot(
        normalized_input, gathered_key, preferred_element_type=single_float
    ).reshape(row_count, KEY_VALUE_HEADS, HEAD_SIZE)
    value_low = jnp.dot(normalized_input, full_value, preferred_element_type=single_float).astype(
        brain_float_half
    )
    query_scale = inverse_rms(query_raw)
    key_norm_scale = inverse_rms(key_unnormalized)
    query_rot = (
        apply_rotary(query_raw * query_scale * gain_q, cosine_table, sine_table)
        .astype(brain_float_half)
        .reshape(row_count, KEY_VALUE_HEADS, query_groups, HEAD_SIZE)
    )
    key_rotated = apply_rotary(
        key_unnormalized * key_norm_scale * key_gain_vector, cosine_table, sine_table
    ).astype(brain_float_half)
    key_gathered_rows, value_gathered_rows = (
        lax.all_gather(
            key_rotated.reshape(row_count, KEY_VALUE_HEADS * HEAD_SIZE),
            EXPERT,
            axis=0,
            tiled=True,
        ),
        lax.all_gather(value_low, EXPERT, axis=0, tiled=True),
    )
    key_gathered_rows = key_gathered_rows.reshape(length_total, KEY_VALUE_HEADS, HEAD_SIZE)
    value_gathered_rows = value_gathered_rows.reshape(length_total, KEY_VALUE_HEADS, HEAD_SIZE)

    def masked_scores():
        raw = (
            jnp.einsum(
                "tkgd,skd->kgts", query_rot, key_gathered_rows, preferred_element_type=single_float
            )
            * scale
        )
        return jnp.where(allowed, raw, -1e30)

    scores = masked_scores()
    peak = jnp.max(scores, -1, keepdims=True)
    shifted = jnp.exp(scores - peak)
    totals = jnp.sum(shifted, -1, keepdims=True)
    weights_low = (shifted / totals).astype(brain_float_half)
    log_total = peak + jnp.log(totals)
    mixed = (
        jnp.einsum(
            "kgts,skd->tkgd", weights_low, value_gathered_rows, preferred_element_type=single_float
        )
        .reshape(row_count, QUERY_HEADS * HEAD_SIZE)
        .astype(brain_float_half)
    )
    hidden = inputs + jnp.dot(mixed, full_out, preferred_element_type=single_float)
    scale_two = inverse_rms(hidden)
    normed_two = (hidden * scale_two * gain_two).astype(brain_float_half)
    logits = jnp.dot(normed_two, full_router, preferred_element_type=single_float)
    selector = (expert_ids[0][:, :, None] == jnp.arange(experts, dtype=jnp.int32)).astype(
        single_float
    )
    chosen = jnp.einsum("tke,te->tk", selector, logits, precision=HIGHEST)
    gates = jax.nn.softmax(chosen, -1)
    flat_routes = expert_ids[0].reshape(pairs)
    hits = (flat_routes[:, None] == jnp.arange(experts, dtype=jnp.int32)).astype(jnp.int32)
    before = jnp.cumsum(hits, 0) - hits
    ranks = jnp.sum(before * hits, 1)
    slot_index = flat_routes * capacity + ranks
    owner_rows = jnp.arange(pairs, dtype=jnp.int32) // TOP
    outgoing = (
        jnp.zeros((experts * capacity, width), brain_float_half)
        .at[slot_index]
        .set(normed_two[owner_rows])
    )
    arrived = lax.all_to_all(
        outgoing.reshape(experts, capacity, width),
        (EXPERT, FSDP),
        split_axis=0,
        concat_axis=0,
        tiled=True,
    ).reshape(experts * capacity, width)
    gate_pre = jnp.dot(arrived, w_gate[0], preferred_element_type=single_float)
    up_pre = jnp.dot(arrived, w_up[0], preferred_element_type=single_float)
    activated = jax.nn.silu(gate_pre)
    inner = (activated * up_pre).astype(brain_float_half)
    result = jnp.dot(inner, w_down[0], preferred_element_type=single_float).astype(brain_float_half)
    returned = lax.all_to_all(
        result.reshape(experts, capacity, width),
        (EXPERT, FSDP),
        split_axis=0,
        concat_axis=0,
        tiled=True,
    ).reshape(experts * capacity, width)
    expert_rows = returned[slot_index].astype(single_float).reshape(row_count, TOP, width)
    output = hidden + jnp.einsum("tk,tkd->td", gates, expert_rows, precision=HIGHEST)
    grad_top = grad_output[0]
    grad_gates = jnp.einsum("tkd,td->tk", expert_rows, grad_top, precision=HIGHEST)
    grad_pairs = (
        (gates[:, :, None] * grad_top[:, None, :]).astype(brain_float_half).reshape(pairs, width)
    )
    grad_send = (
        jnp.zeros((experts * capacity, width), brain_float_half).at[slot_index].set(grad_pairs)
    )
    grad_arrived = lax.all_to_all(
        grad_send.reshape(experts, capacity, width),
        (EXPERT, FSDP),
        split_axis=0,
        concat_axis=0,
        tiled=True,
    ).reshape(experts * capacity, width)
    grad_down = jnp.einsum("rf,rd->fd", inner, grad_arrived, preferred_element_type=single_float)
    grad_inner = jnp.einsum(
        "rd,fd->rf", grad_arrived, w_down[0], preferred_element_type=single_float
    )
    sigmoid_gate = jax.nn.sigmoid(gate_pre)
    slope = sigmoid_gate * (1.0 + gate_pre * (1.0 - sigmoid_gate))
    grad_gate_pre = (grad_inner * up_pre * slope).astype(brain_float_half)
    grad_up_pre = (grad_inner * activated).astype(brain_float_half)
    grad_gate_w = jnp.einsum(
        "rd,rf->df", arrived, grad_gate_pre, preferred_element_type=single_float
    )
    grad_up_w = jnp.einsum("rd,rf->df", arrived, grad_up_pre, preferred_element_type=single_float)
    grad_rows = (
        jnp.einsum("rf,df->rd", grad_gate_pre, w_gate[0], preferred_element_type=single_float)
        + jnp.einsum("rf,df->rd", grad_up_pre, w_up[0], preferred_element_type=single_float)
    ).astype(brain_float_half)
    grad_back = lax.all_to_all(
        grad_rows.reshape(experts, capacity, width),
        (EXPERT, FSDP),
        split_axis=0,
        concat_axis=0,
        tiled=True,
    ).reshape(experts * capacity, width)
    grad_normed_two = jnp.sum(
        grad_back[slot_index].astype(single_float).reshape(row_count, TOP, width), 1
    )
    grad_chosen = gates * (grad_gates - jnp.sum(gates * grad_gates, -1, keepdims=True))
    grad_logits = jnp.einsum("tke,tk->te", selector, grad_chosen, precision=HIGHEST).astype(
        brain_float_half
    )
    grad_normed_two = grad_normed_two + jnp.einsum(
        "te,de->td", grad_logits, full_router, preferred_element_type=single_float
    )
    grad_router = jnp.einsum(
        "td,te->de", normed_two, grad_logits, preferred_element_type=single_float
    )
    grad_gain_two = jnp.sum(grad_normed_two * hidden * scale_two, 0)
    grad_hidden = grad_top + norm_backward(grad_normed_two, hidden, scale_two, gain_two)
    grad_branch = grad_hidden.astype(brain_float_half)
    grad_out_w = jnp.einsum("tq,td->qd", mixed, grad_branch, preferred_element_type=single_float)
    grad_mixed = (
        jnp.einsum("td,qd->tq", grad_branch, full_out, preferred_element_type=single_float)
        .astype(brain_float_half)
        .reshape(row_count, KEY_VALUE_HEADS, query_groups, HEAD_SIZE)
    )
    again = masked_scores()
    weights = jnp.exp(again - log_total)
    weights_again = weights.astype(brain_float_half)
    grad_weights = jnp.einsum(
        "tkgd,skd->kgts", grad_mixed, value_gathered_rows, preferred_element_type=single_float
    )
    spread = jnp.sum(weights * grad_weights, -1, keepdims=True)
    grad_scores = (weights * (grad_weights - spread)).astype(brain_float_half)
    grad_query_rot = (
        jnp.einsum(
            "kgts,skd->tkgd", grad_scores, key_gathered_rows, preferred_element_type=single_float
        )
        * scale
    ).reshape(row_count, QUERY_HEADS, HEAD_SIZE)
    grad_key_all = (
        jnp.einsum("kgts,tkgd->skd", grad_scores, query_rot, preferred_element_type=single_float)
        * scale
    ).reshape(length_total, KEY_VALUE_HEADS * HEAD_SIZE)
    grad_value_all = jnp.einsum(
        "kgts,tkgd->skd", weights_again, grad_mixed, preferred_element_type=single_float
    ).reshape(length_total, KEY_VALUE_HEADS * HEAD_SIZE)
    gradient_key_rotated, grad_value = (
        lax.psum_scatter(
            grad_key_all.astype(jnp.bfloat16), EXPERT, scatter_dimension=0, tiled=True
        ).astype(jnp.float32),
        lax.psum_scatter(
            grad_value_all.astype(jnp.bfloat16), EXPERT, scatter_dimension=0, tiled=True
        ).astype(jnp.float32),
    )
    gradient_key_rotated = gradient_key_rotated.reshape(row_count, KEY_VALUE_HEADS, HEAD_SIZE)
    grad_query_unit = unrotate(grad_query_rot, cosine_table, sine_table)
    gradient_key_normalized = unrotate(gradient_key_rotated, cosine_table, sine_table)
    grad_gain_q = jnp.sum(grad_query_unit * query_raw * query_scale, (0, 1))
    grad_gain_k = jnp.sum(gradient_key_normalized * key_unnormalized * key_norm_scale, (0, 1))
    grad_query = (
        norm_backward(grad_query_unit, query_raw, query_scale, gain_q)
        .reshape(row_count, QUERY_HEADS * HEAD_SIZE)
        .astype(brain_float_half)
    )
    grad_key = (
        norm_backward(gradient_key_normalized, key_unnormalized, key_norm_scale, key_gain_vector)
        .reshape(row_count, KEY_VALUE_HEADS * HEAD_SIZE)
        .astype(brain_float_half)
    )
    grad_value_low = grad_value.astype(brain_float_half)
    grad_query_w = jnp.einsum(
        "td,tq->dq", normalized_input, grad_query, preferred_element_type=single_float
    )
    grad_key_w = jnp.einsum(
        "td,tq->dq", normalized_input, grad_key, preferred_element_type=single_float
    )
    grad_value_w = jnp.einsum(
        "td,tq->dq", normalized_input, grad_value_low, preferred_element_type=single_float
    )
    grad_normed = (
        jnp.einsum("tq,dq->td", grad_query, full_query, preferred_element_type=single_float)
        + jnp.einsum("tq,dq->td", grad_key, gathered_key, preferred_element_type=single_float)
        + jnp.einsum("tq,dq->td", grad_value_low, full_value, preferred_element_type=single_float)
    )
    grad_gain_one = jnp.sum(grad_normed * inputs * scale_one, 0)
    grad_inputs = grad_hidden + norm_backward(grad_normed, inputs, scale_one, gain_one)
    local_grads = (
        grad_query_w,
        grad_key_w,
        grad_value_w,
        grad_out_w,
        grad_router,
        grad_gain_one,
        grad_gain_two,
        grad_gain_q,
        grad_gain_k,
    )
    shards = (
        lax.psum_scatter(
            local_grads[0].astype(jnp.bfloat16), FSDP, scatter_dimension=0, tiled=True
        ).astype(jnp.float32),
        lax.psum_scatter(
            local_grads[1].astype(jnp.bfloat16), FSDP, scatter_dimension=0, tiled=True
        ).astype(jnp.float32),
        lax.psum_scatter(
            local_grads[2].astype(jnp.bfloat16), FSDP, scatter_dimension=0, tiled=True
        ).astype(jnp.float32),
        lax.psum_scatter(
            local_grads[3].astype(jnp.bfloat16), FSDP, scatter_dimension=0, tiled=True
        ).astype(jnp.float32),
        lax.psum_scatter(
            local_grads[4].astype(jnp.bfloat16), FSDP, scatter_dimension=0, tiled=True
        ).astype(jnp.float32),
        lax.psum_scatter(
            local_grads[5].astype(jnp.bfloat16), FSDP, scatter_dimension=0, tiled=True
        ).astype(jnp.float32),
        lax.psum_scatter(
            local_grads[6].astype(jnp.bfloat16), FSDP, scatter_dimension=0, tiled=True
        ).astype(jnp.float32),
        lax.psum_scatter(
            local_grads[7].astype(jnp.bfloat16), FSDP, scatter_dimension=0, tiled=True
        ).astype(jnp.float32),
        lax.psum_scatter(
            local_grads[8].astype(jnp.bfloat16), FSDP, scatter_dimension=0, tiled=True
        ).astype(jnp.float32),
    )
    shards = (
        lax.psum(shards[0].astype(jnp.bfloat16), EXPERT).astype(jnp.float32),
        lax.psum(shards[1].astype(jnp.bfloat16), EXPERT).astype(jnp.float32),
        lax.psum(shards[2].astype(jnp.bfloat16), EXPERT).astype(jnp.float32),
        lax.psum(shards[3].astype(jnp.bfloat16), EXPERT).astype(jnp.float32),
        lax.psum(shards[4].astype(jnp.bfloat16), EXPERT).astype(jnp.float32),
        lax.psum(shards[5].astype(jnp.bfloat16), EXPERT).astype(jnp.float32),
        lax.psum(shards[6].astype(jnp.bfloat16), EXPERT).astype(jnp.float32),
        lax.psum(shards[7].astype(jnp.bfloat16), EXPERT).astype(jnp.float32),
        lax.psum(shards[8].astype(jnp.bfloat16), EXPERT).astype(jnp.float32),
    )
    return (
        output[None],
        grad_inputs[None],
        shards[0],
        shards[1],
        shards[2],
        shards[3],
        shards[4],
        shards[5],
        shards[6],
        shards[7],
        shards[8],
        grad_gate_w[None],
        grad_up_w[None],
        grad_down[None],
    )


def angle_tables(length):
    power = -(np.arange(HEAD_SIZE // 2, dtype=np.float32) * np.float32(2.0)) / np.float32(HEAD_SIZE)
    freq = np.power(np.float32(THETA), power).astype(np.float32)
    turns = np.arange(length, dtype=np.float32)[:, None] * freq[None, :]
    turns = np.concatenate([turns, turns], -1)
    return jnp.asarray(np.cos(turns)), jnp.asarray(np.sin(turns))


def packed(pieces, lead, rows):
    flat = jnp.concatenate([piece.reshape(lead, -1) for piece in pieces], 1)
    flat = jnp.pad(flat, ((0, 0), (0, rows * 128 - flat.shape[1])))
    return flat.reshape(lead, rows, 128)


def local_staged(
    layer_input,
    doc_ids,
    expert_ids,
    w_query,
    w_key,
    w_value,
    w_out,
    w_router,
    gain_attn,
    gain_ffn,
    gain_query,
    gain_key,
    w_gate,
    w_up,
    w_down,
    grad_output,
):
    f32 = jnp.float32
    low = jnp.bfloat16
    rows, width = layer_input.shape[1:]
    length = doc_ids.shape[1]
    depth = w_router.shape[0]
    groups, shards = lax.axis_size(EXPERT), lax.axis_size(FSDP)
    experts = w_router.shape[1]
    heads = QUERY_HEADS // groups
    span = heads * HEAD_SIZE
    mine = lax.axis_index(EXPERT)

    def columns(weight, count):
        return lax.dynamic_slice_in_dim(weight, mine * count, count, 1)

    flat = jnp.concatenate(
        [columns(w_query, span), columns(w_key, HEAD_SIZE), columns(w_value, HEAD_SIZE)], 1
    )
    pack = packed([w_router, gain_attn, gain_ffn, gain_query, gain_key], 1, 80)[0]
    w_qkv, w_mix, tokens, pack_all, ids_all, mine_picks, pick, spread = gather(
        groups,
        shards,
        5,
        flat,
        w_out,
        layer_input[0],
        pack,
        expert_ids[0].T,
    )
    w_qkv = w_qkv.reshape(width, span + 2 * HEAD_SIZE)
    w_mix = w_mix.reshape(span, width)
    tokens = tokens.reshape(length, width)
    pack_all = pack_all.reshape(shards, -1)
    at = depth * experts
    full_router = pack_all[:, :at].reshape(width, experts)
    gain_one = pack_all[:, at : at + depth].reshape(width).astype(f32)
    gain_two = pack_all[:, at + depth : at + 2 * depth].reshape(width).astype(f32)
    at += 2 * depth
    small = HEAD_SIZE // shards
    gain_q = pack_all[:, at : at + small].reshape(HEAD_SIZE).astype(f32)
    gain_k = pack_all[:, at + small : at + 2 * small].reshape(HEAD_SIZE).astype(f32)
    grad_top = grad_output[0]
    ids_column, ids_row = doc_ids[0][:, None], doc_ids[0][None, :]
    cosine, sine = angle_tables(length)
    gain_q, gain_k = gain_q[None], gain_k[None]
    attend = attention(
        tokens, w_qkv, gain_one[None], gain_q, gain_k, cosine, sine, ids_column, ids_row, heads
    )
    grads_in, normed_one, raw, query_rot, key_rot, value, mixed, inverses = dispatch(
        groups, shards, 1, grad_top.astype(low), pick, extra=attend
    )
    branch = jnp.dot(mixed, w_mix, preferred_element_type=f32).astype(low)
    inputs = layer_input[0].astype(f32)
    hidden = inputs + group_scatter(8, branch.reshape(groups, rows, width))
    scale_two = inverse_rms(hidden)
    normed_two = (hidden * scale_two * gain_two).astype(low)
    logits = jnp.dot(normed_two, full_router, preferred_element_type=f32)
    selector = (expert_ids[0][:, :, None] == jnp.arange(experts, dtype=jnp.int32)).astype(f32)
    gates = jax.nn.softmax(jnp.sum(selector * logits[:, None, :], -1), -1)
    _, arrived, weighted, grad_arrived, inner, grad_a, grad_b, grad_rows, gate_grads = dispatch_expert(
        groups, shards, 2, normed_two, pick, gates.T, grads_in, mine_picks, ids_all, w_gate, w_up, w_down
    )

    def flat_rows(blocks):
        return blocks.reshape(-1, blocks.shape[-1])

    grad_normed_two, gates_back, grad_gate_w, grad_up_w, grad_down = combine(
        groups,
        shards,
        3,
        grad_rows,
        spread,
        gate_grads,
        weight_grads(*(flat_rows(a) for a in (arrived, grad_arrived, inner, grad_a, grad_b))),
    )
    grad_gates = jnp.sum(selector * gates_back[:, 0].T[:, None, :], -1)
    grad_chosen = gates * (grad_gates - jnp.sum(gates * grad_gates, -1, keepdims=True))
    grad_logits = jnp.sum(selector * grad_chosen[:, :, None], 1).astype(low)
    grad_normed_two = grad_normed_two + jnp.einsum(
        "te,de->td", grad_logits, full_router, preferred_element_type=f32
    )
    grad_router = jnp.einsum("td,te->de", normed_two, grad_logits, preferred_element_type=f32)
    grad_gain_two = jnp.sum(grad_normed_two * hidden * scale_two, 0)
    grad_hidden = grad_top + norm_backward(grad_normed_two, hidden, scale_two, gain_two)
    back = attention_back(
        query_rot, key_rot, value, raw, mixed, grad_hidden.astype(low), w_mix, normed_one, tokens, w_qkv,
        inverses, ids_column, ids_row, gain_q, gain_k, cosine, sine,
    )
    combined, gain_grads, grad_mix, grad_qkv, grad_normed_one, grad_gain_one = combine(
        groups, shards, 4, weighted, spread, extra=back
    )
    output = hidden + combined
    sums = [grad_router, grad_gain_one, grad_gain_two, gain_grads[0], gain_grads[1]]
    sums = packed(sums, shards, 16 * (span + 2 * HEAD_SIZE) // 128)
    sums = sums.reshape(shards, 16, -1).astype(low)
    query_sum, key_sum, value_sum, tall_sum, pack_sum, grad_normed_one = reduce(
        groups,
        shards,
        6,
        grad_qkv.reshape(shards, depth, -1),
        grad_mix.reshape(2, -1, width),
        sums,
        grad_normed_one.reshape(groups, rows, width),
    )
    pack_sum = jnp.sum(pack_sum.astype(f32), 0).reshape(-1)
    scale_own = inverse_rms(inputs)
    grad_inputs = grad_hidden + norm_backward(grad_normed_one, inputs, scale_own, gain_one)
    at = depth * experts
    return (
        output[None],
        grad_inputs[None],
        query_sum.astype(f32),
        key_sum.astype(f32),
        value_sum.astype(f32),
        tall_sum.astype(f32),
        pack_sum[:at].reshape(depth, experts),
        pack_sum[at : at + depth],
        pack_sum[at + depth : at + 2 * depth],
        pack_sum[at + 2 * depth : at + 2 * depth + small],
        pack_sum[at + 2 * depth + small : at + 2 * depth + 2 * small],
        grad_gate_w[None],
        grad_up_w[None],
        grad_down[None],
    )


def solution(mesh):
    in_specs = (
        P(FSDP, EXPERT, None),
        P(FSDP, None),
        P(FSDP, EXPERT, None),
        P(FSDP, None),
        P(FSDP, None),
        P(FSDP, None),
        P(FSDP, None),
        P(FSDP, None),
        P(FSDP),
        P(FSDP),
        P(FSDP),
        P(FSDP),
        P((EXPERT, FSDP), None, None),
        P((EXPERT, FSDP), None, None),
        P((EXPERT, FSDP), None, None),
        P(FSDP, EXPERT, None),
    )
    out_specs = (
        P(FSDP, EXPERT, None),
        P(FSDP, EXPERT, None),
        P(FSDP, None),
        P(FSDP, None),
        P(FSDP, None),
        P(FSDP, None),
        P(FSDP, None),
        P(FSDP),
        P(FSDP),
        P(FSDP),
        P(FSDP),
        P((EXPERT, FSDP), None, None),
        P((EXPERT, FSDP), None, None),
        P((EXPERT, FSDP), None, None),
    )
    staged = mesh.shape[EXPERT] == 4 and mesh.shape[FSDP] == 8
    return jax.shard_map(local_staged if staged else local, mesh=mesh, in_specs=in_specs, out_specs=out_specs, check_vma=False)
```

```python
import functools

import jax
import jax.numpy as jnp
import numpy as np
from jax import lax
from jax.experimental import pallas as pl
from jax.experimental.pallas import tpu as pltpu
from jax.sharding import PartitionSpec as P

EXPERT = "expert"
FSDP = "fsdp"
UP, DOWN, ABOVE, BELOW = "up", "down", "above", "below"
QUERY_HEADS = 32
KEY_VALUE_HEADS = 4
HEAD_SIZE = 128
TOP = 8


EPS = 1e-06
THETA = 1000000.0
HIGHEST = lax.Precision.HIGHEST


def angles(positions):
    freq = THETA ** (-(jnp.arange(HEAD_SIZE // 2, dtype=jnp.float32) * 2.0) / HEAD_SIZE)
    turn = positions.astype(jnp.float32)[:, None] * freq[None, :]
    turn = jnp.concatenate([turn, turn], -1)
    return (jnp.cos(turn), jnp.sin(turn))


def apply_rotary(value_rows_local, cosine_table, sine_table):
    half = value_rows_local.shape[-1] // 2
    turned = jnp.concatenate([-value_rows_local[..., half:], value_rows_local[..., :half]], -1)
    return value_rows_local * cosine_table + turned * sine_table


def unrotate(grads, cosine_table, sine_table):
    half = grads.shape[-1] // 2
    scaled = grads * sine_table
    turned = jnp.concatenate([-scaled[..., half:], scaled[..., :half]], -1)
    return grads * cosine_table - turned


def inverse_rms(value_rows_local):
    return lax.rsqrt(jnp.mean(value_rows_local * value_rows_local, -1, keepdims=True) + EPS)


def norm_backward(grad, value_rows_local, inverse, gain):
    scaled = grad * gain
    return inverse * scaled - inverse * inverse * inverse * value_rows_local * jnp.mean(
        scaled * value_rows_local, -1, keepdims=True
    )


MESH = pl.DeviceIdType.MESH
SLOTS = 80
FAR_FIRST = ((1, 3), (1, 2), (0, 3), (1, 1), (0, 2), (0, 1), (1, 0), (0, 0))
BACK = FAR_FIRST
AHEAD = 2
HALVES = 2


class Place:
    def __init__(self):
        self.e = lax.axis_index(EXPERT)
        self.f = lax.axis_index(FSDP)
        self.x, self.c = self.e // 2, self.e % 2
        self.z, self.y = self.f // 2, self.f % 2

    def device(self, axis):
        if axis == "c":
            return (self.x * 2 + 1 - self.c, self.f)
        if axis == "x":
            return ((1 - self.x) * 2 + self.c, self.f)
        if axis == "y":
            return (self.e, self.z * 2 + 1 - self.y)
        if axis == UP:
            return (self.e, jnp.minimum(self.z + 1, 3) * 2 + self.y)
        return (self.e, jnp.maximum(self.z - 1, 0) * 2 + self.y)

    def ranked(self, j):
        inner = (1, 0, 2, 3)[j]
        end = (self.z == 0) | (self.z == 3)
        low = jnp.where(end, j, inner)
        return jnp.where(self.z < 2, low, 3 - low)

    def line(self):
        x, y, even = self.x, self.y, self.c == 0
        near = (jnp.where(even, 1 - x, x), jnp.where(even, y, 1 - y))
        far = (jnp.where(even, x, 1 - x), jnp.where(even, 1 - y, y))
        return near, far

    def at(self, chip, core):
        return (chip[0] * 2 + core, self.z * 2 + chip[1])


def block_number(chip, core, ar, zs):
    x, y = chip
    xs = jnp.where(core == 0, 1 - x, x) if ar else x
    ys = jnp.where(core == 0, y, 1 - y) if ar else y
    return (xs * 2 + core) * 8 + zs * 2 + ys


def greet(place):
    barrier = pltpu.get_barrier_semaphore()
    beside = [place.device("c")]
    for chip in ((1 - place.x, place.y), (place.x, 1 - place.y)):
        beside += [place.at(chip, 0), place.at(chip, 1)]
    for device in beside:
        pl.semaphore_signal(barrier, 1, device_id=device, device_id_type=MESH)

    @pl.when(place.z < 3)
    def _():
        pl.semaphore_signal(barrier, 1, device_id=place.device(UP), device_id_type=MESH)

    @pl.when(place.z > 0)
    def _():
        pl.semaphore_signal(barrier, 1, device_id=place.device(DOWN), device_id_type=MESH)

    inner = (place.z > 0) & (place.z < 3)
    pl.semaphore_wait(barrier, len(beside) + jnp.where(inner, 2, 1))


def greet_all(place, experts, shards):
    barrier = pltpu.get_barrier_semaphore()
    count = experts * shards

    def one(i, carry):
        target = lax.rem(place.e * shards + place.f + i, count)
        pl.semaphore_signal(
            barrier, 1, device_id=(target // shards, lax.rem(target, shards)), device_id_type=MESH
        )
        return carry

    lax.fori_loop(1, count, one, 0)
    pl.semaphore_wait(barrier, count - 1)


def onward(path, j, xr, yr):
    differs = {"z": j > 0, "x": xr > 0, "y": yr > 0}
    last = -1
    for i, axis in enumerate(path):
        if differs[axis]:
            last = i
    out = []
    if last >= 0 and path[last] == "z":
        out.append("z+")
    for axis in path[last + 1 :]:
        out.append("z*" if axis == "z" else axis)
    return out


def links(place, path, j, xr, yr, zs):
    out = []
    for axis in onward(path, j, xr, yr):
        if axis == "z+":
            out.append((UP, (zs < place.z) & (place.z < 3)))
            out.append((DOWN, (zs > place.z) & (place.z > 0)))
        elif axis == "z*":
            out.append((UP, place.z < 3))
            out.append((DOWN, place.z > 0))
        else:
            out.append((axis, None))
    return out


def run(condition, action):
    if condition is None:
        action()
    else:
        pl.when(condition)(action)


LINK = {"x": 0, "y": 1, UP: 2, DOWN: 3}


def remote(src, dst, send_sem, recv_sem, device):
    return pltpu.make_async_remote_copy(
        src_ref=src,
        dst_ref=dst,
        send_sem=send_sem,
        recv_sem=recv_sem,
        device_id=device,
        device_id_type=MESH,
    )


class Side:
    def __init__(self, steps, events):
        self.steps, self.events = list(steps), events
        self.total, self.seen = len(self.steps), 0

    def event(self):
        self.seen += 1
        left = self.total - self.total * min(self.seen, self.events) // self.events
        while len(self.steps) > left:
            self.steps.pop(0)()


class Extra:
    def __init__(self, operands=(), in_specs=(), outs=(), out_specs=(), scratch=(), steps=None):
        self.operands, self.in_specs = list(operands), list(in_specs)
        self.outs, self.out_specs, self.scratch = list(outs), list(out_specs), list(scratch)
        self.steps = steps if steps is not None else lambda *refs: []


def split(refs, counts):
    out = []
    for count in counts:
        out.append(refs[:count])
        refs = refs[count:]
    return out


def exchange_small(place, dims, src_of, dst, sems_out, sems_in, sem):
    experts, shards = dims
    count = experts * shards
    me = place.e * shards + place.f
    keep = pltpu.make_async_copy(src_of(me), dst.at[me], sem)
    keep.start()

    def copy(i, sending):
        other = lax.rem(me + i, count)
        source = me if sending else other
        device = (other // shards, lax.rem(other, shards))
        return remote(src_of(other), dst.at[source], sems_out.at[i], sems_in.at[source], device)

    def start(i, carry):
        copy(i, True).start()
        return carry

    def finish(i, carry):
        done = copy(i, False)
        done.wait_send()
        done.wait_recv()
        return carry

    lax.fori_loop(1, count, start, 0)

    def end():
        keep.wait()
        lax.fori_loop(1, count, finish, 0)

    return end


def dispatch_kernel(dims, has_small, extra, *refs):
    counts = (
        2 + has_small, len(extra.operands), 1 + has_small, len(extra.outs), 7 + 3 * has_small,
        len(extra.scratch),
    )
    ins, more_in, outs, more_out, scratch, more_scratch = split(refs, counts)
    tok, sel = ins[:2]
    picked = outs[0]
    held, stage, arrive, leave, pick_out, pick_in, local = scratch[:7]
    place = Place()
    width = tok.shape[1]
    near, far = place.line()
    mine = (place.x, place.y)
    if has_small:
        greet_all(place, *dims)
        end_small = exchange_small(
            place, dims, lambda i: ins[2], outs[1], scratch[7], scratch[8], scratch[9].at[0]
        )
    else:
        greet(place)
    side = Side(extra.steps(*more_in, *more_out, *more_scratch), 8)
    keep = pltpu.make_async_copy(tok, held.at[place.z], local.at[8])
    keep.start()
    pending = []
    finish = []
    targets = (place.device("c"), place.at(far, place.c), place.at(far, 1 - place.c))

    def pick(ar, zs):
        block = ar * 4 + zs
        number = block_number(mine, place.c, ar, zs)

        def tile(i, carry):
            columns = pl.ds(pl.multiple_of(i * 512, 512), 512)
            stage[block, :, columns] = jnp.dot(
                sel[block], held[block, :, columns], preferred_element_type=jnp.float32
            ).astype(jnp.bfloat16)
            return carry

        lax.fori_loop(0, width // 512, tile, 0)
        for k in (2, 1, 0):
            away = remote(
                stage.at[block, pl.ds((k + 1) * SLOTS, SLOTS)], picked.at[number],
                pick_out.at[block, k], pick_in.at[number], targets[k],
            )
            away.start()
            finish.append(away)
        stay = pltpu.make_async_copy(
            stage.at[block, pl.ds(0, SLOTS)], picked.at[number], local.at[block]
        )
        stay.start()
        finish.append(stay)

    half = tok.shape[0] // HALVES
    for ar, j in FAR_FIRST[::-1]:
        zs = place.ranked(j)
        block = ar * 4 + zs
        for h in range(HALVES):
            part = pl.ds(h * half, half)
            window = held.at[block, part]
            if ar or j:
                remote(
                    window, window, leave.at[zs, 0, h], arrive.at[block, h], place.device("c")
                ).wait_recv()
            if ar:
                continue
            source = tok.at[part] if j == 0 else window
            onward = (
                (UP, zs, 0, (zs <= place.z) & (place.z < 3)),
                (DOWN, zs, 1, (zs >= place.z) & (place.z > 0)),
                ("near", 4 + zs, 2, None),
            )
            for axis, there, k, condition in onward:
                device = place.at(near, place.c) if axis == "near" else place.device(axis)
                copy = remote(
                    source, held.at[there, part], leave.at[zs, k, h], arrive.at[there, h], device
                )
                run(condition, copy.start)
                pending.append((condition, copy))
        if not ar and j == 0:
            keep.wait()
        pick(ar, zs)
        side.event()
    for condition, copy in pending:
        run(condition, copy.wait_send)

    def arrived(i, carry):
        xs, cs, ys = i // 16, i // 8 % 2, i % 2
        inside = (cs == place.c) & jnp.where(place.c == 0, ys == place.y, xs == place.x)

        @pl.when(~inside)
        def _():
            window = picked.at[i]
            remote(window, window, pick_out.at[0, 0], pick_in.at[i], place.device("c")).wait_recv()

        return carry

    lax.fori_loop(0, 32, arrived, 0)
    for k, copy in enumerate(finish):
        if k % 4 == 3:
            copy.wait()
        else:
            copy.wait_send()
    if has_small:
        end_small()


def dispatch(experts, shards, number, tok, sel, small=None, extra=None):
    rows, width = tok.shape
    devices = experts * shards
    extra = extra or Extra()
    space = pl.BlockSpec(memory_space=pl.ANY)
    vmem = pl.BlockSpec(memory_space=pltpu.VMEM)
    dma = pltpu.SemaphoreType.DMA
    has_small = int(small is not None)
    operands, in_specs = [tok, sel], [space, vmem]
    out_shape = [jax.ShapeDtypeStruct((devices, SLOTS, width), jnp.bfloat16)]
    scratch = [
        pltpu.VMEM((8, rows, width), jnp.bfloat16),
        pltpu.VMEM((8, 4 * SLOTS, width), jnp.bfloat16),
        dma((8, HALVES)),
        dma((4, 3, HALVES)),
        dma((8, 3)),
        dma((devices,)),
        dma((9,)),
    ]
    if has_small:
        operands.append(small)
        in_specs.append(space)
        out_shape.append(jax.ShapeDtypeStruct((devices,) + small.shape, small.dtype))
        scratch += [dma((devices,)), dma((devices,)), dma((1,))]
    return pl.pallas_call(
        functools.partial(dispatch_kernel, (experts, shards), has_small, extra),
        out_shape=out_shape + extra.outs,
        in_specs=in_specs + extra.in_specs,
        out_specs=[space] * len(out_shape) + extra.out_specs,
        scratch_shapes=scratch + extra.scratch,
        compiler_params=pltpu.CompilerParams(
            collective_id=number, has_side_effects=True, vmem_limit_bytes=60 * 2**20
        ),
        name="dispatch",
    )(*operands, *extra.operands)


def combine_kernel(dims, has_small, extra, *refs):
    counts = (
        2 + has_small, len(extra.operands), 1 + has_small, len(extra.outs), 10 + 3 * has_small,
        len(extra.scratch),
    )
    ins, more_in, outs, more_out, scratch, more_scratch = split(refs, counts)
    weighted, sel = ins[:2]
    total = outs[0]
    rows4, acc, beside, chain, rows_in, rows_out, beside_in, beside_out, chain_in, chain_out = scratch[:10]
    place = Place()
    width = total.shape[1]
    near, far = place.line()
    mine = (place.x, place.y)
    if has_small:
        greet_all(place, *dims)
        end_small = exchange_small(
            place, dims, lambda i: ins[2].at[i], outs[1], scratch[10], scratch[11], scratch[12].at[0]
        )
    else:
        greet(place)
    side = Side(extra.steps(*more_in, *more_out, *more_scratch), 8 * HALVES)
    other = 1 - place.c
    homes = ((mine, place.c), (mine, other), (far, place.c), (near, other))

    def row_copy(ar, zs, k):
        chip, core = homes[k]
        source = weighted.at[block_number(chip, core, ar, zs)]
        block = ar * 4 + zs
        window = rows4.at[block, pl.ds(k * SLOTS, SLOTS)]
        if k == 0:
            return pltpu.make_async_copy(source, window, rows_in.at[block, 0])
        return remote(
            source, window, rows_out.at[block, k - 1], rows_in.at[block, k], place.at(chip, core)
        )

    def send_rows(i):
        ar, j = BACK[i]
        for k in (2, 3, 1, 0):
            row_copy(ar, place.ranked(j), k).start()

    for i in range(AHEAD):
        send_rows(i)
    pending = []
    half = total.shape[0] // HALVES
    for i, (ar, j) in enumerate(BACK):
        zs = place.ranked(j)
        block = ar * 4 + zs
        for k in range(4):
            copy = row_copy(ar, zs, k)
            if k == 0:
                copy.wait()
            else:
                copy.wait_recv()
                copy.wait_send()
        if i + AHEAD < 8:
            send_rows(i + AHEAD)
        last = not ar and j == 0
        above = (zs <= place.z) & (place.z < 3)
        below = (zs >= place.z) & (place.z > 0)
        below_slot = jnp.where(zs == place.z, 4, zs)
        for h in range(HALVES):
            part = pl.ds(h * half, half)
            if not ar:
                window = beside.at[zs, part]
                remote(
                    window, window, beside_out.at[zs, h], beside_in.at[zs, h], place.device("c")
                ).wait_recv()
                for condition, slot in ((above, zs), (below, below_slot)):
                    window = chain.at[slot, part]
                    got = remote(
                        window, window, chain_out.at[0, h], chain_in.at[slot, h], place.device("c")
                    )
                    run(condition, got.wait_recv)

            def tile(t, carry):
                columns = pl.ds(pl.multiple_of(t * 512, 512), 512)
                dense = jnp.dot(
                    sel[block, part], rows4[block, :, columns], preferred_element_type=jnp.float32
                )
                if not ar:
                    dense = dense + beside[zs, part, columns].astype(jnp.float32)
                if last:
                    total[part, columns] = dense
                else:
                    acc[block, part, columns] = dense.astype(jnp.bfloat16)
                return carry

            lax.fori_loop(0, width // 512, tile, 0)
            if not ar:

                def add(slot):
                    def step(t, carry):
                        here = pl.ds(pl.multiple_of(h * half + t * 16, 16), 16)
                        more = chain[slot, here].astype(jnp.float32)
                        if last:
                            total[here] += more
                        else:
                            acc[block, here] = (acc[block, here].astype(jnp.float32) + more).astype(
                                jnp.bfloat16
                            )
                        return carry

                    lax.fori_loop(0, half // 16, step, 0)

                run(above, functools.partial(add, zs))
                run(below, functools.partial(add, below_slot))
            if ar:
                copy = remote(
                    acc.at[block, part], beside.at[zs, part], beside_out.at[zs, h],
                    beside_in.at[zs, h], place.at(near, place.c),
                )
                copy.start()
                pending.append((None, copy))
            elif not last:
                there = jnp.where(zs == place.z + 1, 4, zs)
                for condition, axis, slot in (
                    (zs < place.z, DOWN, zs),
                    (zs > place.z, UP, there),
                ):
                    copy = remote(
                        acc.at[block, part], chain.at[slot, part], chain_out.at[zs, h],
                        chain_in.at[slot, h], place.device(axis),
                    )
                    run(condition, copy.start)
                    pending.append((condition, copy))
            side.event()
    for condition, copy in pending:
        run(condition, copy.wait_send)
    if has_small:
        end_small()


def combine(experts, shards, number, weighted, sel, small=None, extra=None):
    rows = sel.shape[1]
    width = weighted.shape[-1]
    devices = experts * shards
    extra = extra or Extra()
    space = pl.BlockSpec(memory_space=pl.ANY)
    vmem = pl.BlockSpec(memory_space=pltpu.VMEM)
    dma = pltpu.SemaphoreType.DMA
    low = jnp.bfloat16
    has_small = int(small is not None)
    operands, in_specs = [weighted, sel], [space, vmem]
    out_shape, out_specs = [jax.ShapeDtypeStruct((rows, width), jnp.float32)], [vmem]
    scratch = [
        pltpu.VMEM((8, 4 * SLOTS, width), low),
        pltpu.VMEM((8, rows, width), low),
        pltpu.VMEM((4, rows, width), low),
        pltpu.VMEM((5, rows, width), low),
        dma((8, 4)),
        dma((8, 3)),
        dma((4, HALVES)),
        dma((4, HALVES)),
        dma((5, HALVES)),
        dma((4, HALVES)),
    ]
    if has_small:
        operands.append(small)
        in_specs.append(space)
        out_shape.append(jax.ShapeDtypeStruct(small.shape, small.dtype))
        out_specs.append(space)
        scratch += [dma((devices,)), dma((devices,)), dma((1,))]
    return pl.pallas_call(
        functools.partial(combine_kernel, (experts, shards), has_small, extra),
        out_shape=out_shape + extra.outs,
        in_specs=in_specs + extra.in_specs,
        out_specs=out_specs + extra.out_specs,
        scratch_shapes=scratch + extra.scratch,
        compiler_params=pltpu.CompilerParams(
            collective_id=number, has_side_effects=True, vmem_limit_bytes=63 * 2**20
        ),
        name="combine",
    )(*operands, *extra.operands)


FLAT = ("zy", "yz")
CHUNKS = 4
PIECES = 8


def flat_parts(rows):
    return (0, rows * 3 // 4), (rows * 3 // 4, rows - rows * 3 // 4)


def send_around(place, experts, shards, src_of, dst, out_sems, in_sems, across):
    count = experts * shards if across else shards
    me = place.e * shards + place.f if across else place.f

    def copy(i, sending):
        other = lax.rem(me + i, count)
        if across:
            device = (other // shards, lax.rem(other, shards))
        else:
            device = (place.e, other)
        source = me if sending else other
        return remote(src_of(other), dst.at[source], out_sems.at[i], in_sems.at[source], device)

    def start(i, carry):
        copy(i, True).start()
        return carry

    def finish(i, carry):
        done = copy(i, False)
        done.wait_send()
        done.wait_recv()
        return carry

    lax.fori_loop(1, count, start, 0)
    return lambda: lax.fori_loop(1, count, finish, 0)


def gather_kernel(
    dims, flat, tall, tok, pack, ids, wide, flat_out_all, tall_out_all, tok_out_all, pack_all, ids_all,
    picks, pick, spread, narrow, wide_held, flat_all, tall_all, tok_all, put_sems,
    flat_in, flat_out, tall_in, tall_out, tok_in, tok_out, pack_in, pack_out, ids_in, ids_out, local,
    ids_held, hits, ranks,
):
    experts, shards = dims
    place = Place()
    greet_all(place, experts, shards)
    me = place.e * shards + place.f
    starts, sizes = flat_parts(flat.shape[0])
    chunk = tall.shape[0] // PIECES
    pending = []
    keeps = [
        pltpu.make_async_copy(flat, flat_all.at[place.f], local.at[0]),
        pltpu.make_async_copy(tok, tok_all.at[place.e], local.at[1]),
        pltpu.make_async_copy(pack, pack_all.at[place.f], local.at[2]),
        pltpu.make_async_copy(ids, ids_all.at[me], local.at[3]),
    ]

    def go(condition, copy):
        run(condition, copy.start)
        pending.append((condition, copy))

    def both(a, b):
        return b if a is None else (a if b is None else a & b)

    puts = []

    def put(src, dst, condition=None):
        copy = pltpu.make_async_copy(src, dst, put_sems.at[len(puts)])
        run(condition, copy.start)
        puts.append((condition, copy))

    def flat_item(p, j, yr):
        zs = place.ranked(j)
        source = zs * 2 + (1 - place.y if yr else place.y)
        first = j == 0 and yr == 0
        window = flat_all.at[source, pl.ds(starts[p], sizes[p])]
        src = window
        if not first:
            remote(
                window, window, flat_out.at[p, source, 0], flat_in.at[p, source], place.device("c")
            ).wait_recv()
        put(window, flat_out_all.at[source, pl.ds(starts[p], sizes[p])])
        for axis, condition in links(place, FLAT[p], j, 0, yr, zs):
            go(
                condition,
                remote(
                    src,
                    window,
                    flat_out.at[p, source, LINK[axis]],
                    flat_in.at[p, source],
                    place.device(axis),
                ),
            )

    owner = place.z == place.e

    distance = jnp.abs(place.z - place.e)

    def tall_round(r):
        k = r - distance
        live = (k >= 0) & (k < PIECES)
        k = jnp.clip(k, 0, PIECES - 1)
        piece = pl.ds(pl.multiple_of(k * chunk, chunk), chunk)
        window = tall_all.at[place.y, piece]

        @pl.when(live & ~owner)
        def _():
            remote(window, window, tall_out.at[k, 0], tall_in.at[0, k], place.device("c")).wait_recv()

        for axis, condition in (
            (UP, (place.z >= place.e) & (place.z < 3)),
            (DOWN, (place.z <= place.e) & (place.z > 0)),
            ("y", None),
        ):
            go(
                both(live, condition),
                remote(
                    window,
                    window,
                    tall_out.at[k, LINK[axis]],
                    tall_in.at[1 if axis == "y" else 0, k],
                    place.device(axis),
                ),
            )
        put(window, tall_out_all.at[place.y, piece], live)

    def rank_rows():
        end_ids()
        keeps[3].wait()
        copy = pltpu.make_async_copy(ids_all, ids_held, local.at[5])
        copy.start()
        copy.wait()
        hits[...] = jnp.zeros_like(hits)

        def hit(i, number):
            found = jnp.where(ids_held[i] == number, 1.0, 0.0)
            return jnp.max(found, 0, keepdims=True)

        def own(i, carry):
            hits[pl.ds(i, 1)] = hit(i, me)
            return carry

        lax.fori_loop(0, experts * shards, own, 0)
        mine, far = (place.x, place.y), place.line()[1]
        for k, (chip, core) in enumerate(
            ((mine, place.c), (mine, 1 - place.c), (far, place.c), (far, 1 - place.c))
        ):
            expert_at, shard_at = place.at(chip, core)
            for ar in range(2):
                for zs in range(4):
                    row = experts * shards + (ar * 4 + zs) * 4 + k
                    at = block_number(mine, place.c, ar, zs)
                    hits[row : row + 1] = hit(at, expert_at * shards + shard_at)
        count = hits.shape[1]
        before = lax.broadcasted_iota(jnp.int32, (count, count), 0)
        after = lax.broadcasted_iota(jnp.int32, (count, count), 1)
        earlier = jnp.where(before < after, 1.0, 0.0).astype(jnp.bfloat16)
        found = jnp.dot(hits[...].astype(jnp.bfloat16), earlier, preferred_element_type=jnp.float32)
        ranks[...] = jnp.where(hits[...] > 0.5, found, -1.0)

    def one_hot_rows():
        shape = (SLOTS, ranks.shape[1])
        slot = lax.broadcasted_iota(jnp.int32, shape, 0).astype(jnp.float32)

        def rows_of(i):
            return jnp.where(ranks[pl.ds(i, 1)] == slot, 1.0, 0.0).astype(jnp.bfloat16)

        def own(i, carry):
            picks[i] = rows_of(i)
            return carry

        def near(i, carry):
            for k in range(4):
                pick[i, k * SLOTS : (k + 1) * SLOTS] = rows_of(experts * shards + i * 4 + k)
            return carry

        lax.fori_loop(0, experts * shards, own, 0)
        lax.fori_loop(0, 8, near, 0)

    def one_hot_columns():
        turned = ranks[...].T
        shape = (turned.shape[0], 4 * SLOTS)
        lane = lax.broadcasted_iota(jnp.int32, shape, 1)
        slot = lax.rem(lane, SLOTS).astype(jnp.float32)
        for i in range(8):
            column = experts * shards + i * 4
            rank = turned[:, column : column + 1]
            for k in range(1, 4):
                rank = jnp.where(lane < k * SLOTS, rank, turned[:, column + k : column + k + 1])
            spread[i] = jnp.where(rank == slot, 1.0, 0.0).astype(jnp.bfloat16)

    for keep in keeps:
        keep.start()
    keep_tall = pltpu.make_async_copy(tall, tall_all.at[place.y], local.at[4])
    run(owner, keep_tall.start)
    keeps[0].wait()
    def narrow_rows():
        fetch.wait()

        def part(i, carry):
            here = pl.ds(pl.multiple_of(i * 16, 16), 16)
            narrow[here] = wide_held[here].astype(narrow.dtype)
            return carry

        lax.fori_loop(0, wide.shape[0] // 16, part, 0)

    fetch = pltpu.make_async_copy(wide, wide_held, local.at[6])
    flat_item(0, 0, 0)
    flat_item(1, 0, 0)
    go(None, remote(tok, tok_all.at[place.e], tok_out.at[0], tok_in.at[place.e], place.device("x")))
    go(None, remote(tok, tok_all.at[place.e], tok_out.at[1], tok_in.at[place.e], place.device("c")))
    end_pack = send_around(
        place, experts, shards, lambda i: pack, pack_all, pack_out, pack_in, False
    )
    end_ids = send_around(place, experts, shards, lambda i: ids, ids_all, ids_out, ids_in, True)
    run(owner, keep_tall.wait)
    keeps[1].wait()
    put(tok_all.at[place.e], tok_out_all.at[place.e])
    fetch.start()
    across = (1 - place.x) * 2 + place.c
    window = tok_all.at[across]
    relay = remote(window, window, tok_out.at[2], tok_in.at[across], place.device("c"))
    tall_round(0)
    flat_item(1, 0, 1)
    flat_item(0, 1, 0)
    tall_round(1)
    rank_rows()
    flat_item(0, 2, 0)
    one_hot_rows()
    tall_round(2)
    one_hot_columns()
    narrow_rows()
    flat_item(1, 1, 0)
    flat_item(1, 1, 1)
    relay.wait_recv()
    go(None, relay)
    put(window, tok_out_all.at[across])
    flat_item(0, 3, 0)
    tall_round(3)
    flat_item(1, 2, 0)
    flat_item(1, 2, 1)
    tall_round(4)
    flat_item(1, 3, 0)
    flat_item(1, 3, 1)
    for r in range(5, PIECES + 3):
        tall_round(r)
    for j in range(4):
        flat_item(0, j, 1)
    for k in range(PIECES):
        window = tall_all.at[1 - place.y, pl.ds(k * chunk, chunk)]
        remote(window, window, tall_out.at[k, 0], tall_in.at[1, k], place.device("c")).wait_recv()
        put(window, tall_out_all.at[1 - place.y, pl.ds(k * chunk, chunk)])
    for source in (place.x * 2 + 1 - place.c, (1 - place.x) * 2 + 1 - place.c):
        window = tok_all.at[source]
        remote(window, window, tok_out.at[2], tok_in.at[source], place.device("c")).wait_recv()
        put(window, tok_out_all.at[source])
    for condition, copy in puts:
        run(condition, copy.wait)
    for condition, copy in pending:
        run(condition, copy.wait_send)
    end_pack()
    keeps[2].wait()


def gather(experts, shards, number, flat, tall, tok, pack, ids, wide):
    space = pl.BlockSpec(memory_space=pl.ANY)
    dma = pltpu.SemaphoreType.DMA
    devices = experts * shards

    def shape(lead, a):
        return jax.ShapeDtypeStruct((lead,) + a.shape, a.dtype)

    return pl.pallas_call(
        functools.partial(gather_kernel, (experts, shards)),
        out_shape=[
            shape(shards, flat),
            shape(2, tall),
            shape(experts, tok),
            shape(shards, pack),
            shape(devices, ids),
            jax.ShapeDtypeStruct((devices, SLOTS, ids.shape[1]), jnp.bfloat16),
            jax.ShapeDtypeStruct((8, 4 * SLOTS, ids.shape[1]), jnp.bfloat16),
            jax.ShapeDtypeStruct((8, ids.shape[1], 4 * SLOTS), jnp.bfloat16),
            jax.ShapeDtypeStruct(wide.shape, jnp.bfloat16),
        ],
        in_specs=[space] * 6,
        out_specs=[space] * 5 + [pl.BlockSpec(memory_space=pltpu.VMEM)] * 4,
        scratch_shapes=[
            pltpu.VMEM(wide.shape, wide.dtype),
            pltpu.VMEM((shards,) + flat.shape, flat.dtype),
            pltpu.VMEM((2,) + tall.shape, tall.dtype),
            pltpu.VMEM((experts,) + tok.shape, tok.dtype),
            dma((64,)),
            dma((2, shards)),
            dma((2, shards, 4)),
            dma((2, PIECES)),
            dma((PIECES, 4)),
            dma((experts,)),
            dma((3,)),
            dma((shards,)),
            dma((shards,)),
            dma((devices,)),
            dma((devices,)),
            dma((7,)),
            pltpu.VMEM((devices,) + ids.shape, ids.dtype),
            pltpu.VMEM((128, ids.shape[1]), jnp.float32),
            pltpu.VMEM((128, ids.shape[1]), jnp.float32),
        ],
        compiler_params=pltpu.CompilerParams(
            collective_id=number, has_side_effects=True, vmem_limit_bytes=60 * 2**20
        ),
        name="gather",
    )(flat, tall, tok, pack, ids, wide)


def add_rows(acc, first, window, rows, step=16):
    def add(i, carry):
        here = pl.ds(pl.multiple_of(i * step, step), step)
        at = pl.ds(pl.multiple_of(first + i * step, step), step)
        acc[at] = (acc[at].astype(jnp.float32) + window[here].astype(jnp.float32)).astype(acc.dtype)
        return carry

    lax.fori_loop(0, rows // step, add, 0)


def reduce_kernel(
    dims, flat, tall, pack, partial, out_q, out_k, out_v, tall_out, pack_all, total,
    acc, tacc, yslot, zslot, yone, zall, ty, tz,
    load, yin, zin, yone_in, zall_in, ty_in, tz_in, flat_send, tall_send, spread_in, spread_out,
    tall_in, keep_tall, local,
    group_acc, group_near, group_cross, group_load, group_out, group_in, cross_out, cross_in,
):
    experts, shards = dims
    place = Place()
    greet(place)
    tall_keeps = []
    owner = place.z == place.e
    home = place.x == place.z // 2
    same = place.c == place.z % 2
    starts, sizes = flat_parts(flat.shape[1])
    sizes = (sizes[0], sizes[1] + pack.shape[1])
    height = tall.shape[1]
    chunk = height // CHUNKS
    part = partial.shape[1] // CHUNKS
    pending = []

    def go(condition, copy):
        run(condition, copy.start)
        pending.append((condition, copy))

    def both(a, b):
        return a if b is None else a & b

    load_tall = pltpu.make_async_copy(tall, tacc, load.at[0])
    load_flat = pltpu.make_async_copy(flat, acc.at[:, pl.ds(0, flat.shape[1])], load.at[1])
    load_pack = pltpu.make_async_copy(
        pack, acc.at[:, pl.ds(flat.shape[1], pack.shape[1])], load.at[2]
    )
    across_y = []
    order = (3, 2, 1, 0)

    def add_tall(k):
        piece = pl.ds(k * chunk, chunk)
        across_y.append(
            remote(
                tall.at[1 - place.y, piece], ty.at[piece], tall_send.at[0, k], ty_in.at[k],
                place.device("y"),
            )
        )

    def add_flat(j):
        target = place.ranked(j) * 2 + 1 - place.y
        across_y.append(
            remote(
                flat.at[target, pl.ds(starts[0], sizes[0])],
                yslot.at[place.ranked(j)],
                flat_send.at[0, target],
                yin.at[place.ranked(j)],
                place.device("y"),
            )
        )

    add_tall(0)
    add_tall(1)
    add_flat(3)
    add_tall(2)
    add_flat(2)
    add_tall(3)
    add_flat(1)
    add_flat(0)
    started = [0]

    def feed(count):
        while started[0] < min(count + 2, len(across_y)):
            if started[0] >= 2:
                across_y[started[0] - 2].wait_send()
            across_y[started[0]].start()
            started[0] += 1

    feed(0)
    load_tall.start()
    load_flat.start()
    load_pack.start()
    group_sends = []
    group_loads = []
    for half in (1 - place.x, place.x):
        for i in range(CHUNKS):
            piece = pl.ds(i * part, part)
            copy = remote(
                partial.at[half * 2 + 1 - place.c, piece], group_near.at[half, piece],
                group_out.at[half, i], group_in.at[half, i], place.device("c"),
            )
            copy.start()
            group_sends.append(copy)
            copy = pltpu.make_async_copy(
                partial.at[half * 2 + place.c, piece], group_acc.at[half, piece],
                group_load.at[half, i],
            )
            copy.start()
            group_loads.append(copy)

    def group_half(index, half):
        for i in range(CHUNKS):
            piece = pl.ds(i * part, part)
            window = group_near.at[half, piece]
            group_loads[index * CHUNKS + i].wait()
            remote(
                window, window, group_out.at[half, i], group_in.at[half, i], place.device("c")
            ).wait_recv()
            add_rows(group_acc.at[half], i * part, window, part)
            if index == 0:
                copy = remote(
                    group_acc.at[half, piece], group_cross.at[piece], cross_out.at[i],
                    cross_in.at[i], place.device("x"),
                )
                copy.start()
                group_sends.append(copy)

    def group_end():
        for i in range(CHUNKS):
            window = group_cross.at[pl.ds(i * part, part)]
            remote(window, window, cross_out.at[i], cross_in.at[i], place.device("c")).wait_recv()

            def add(t, carry):
                here = pl.ds(pl.multiple_of(i * part + t * 16, 16), 16)
                own = group_acc[place.x, here].astype(jnp.float32)
                total[here] = own + group_cross[here].astype(jnp.float32)
                return carry

            lax.fori_loop(0, part // 16, add, 0)

    load_tall.wait()
    load_flat.wait()
    load_pack.wait()

    def into(slots, sems, zd, side):
        index = jnp.where(zd == place.z, 4, zd) if side == BELOW else zd
        return slots.at[index], sems.at[index]

    def out_to(slots, sems, zd, side):
        there = place.z - 1 if side == ABOVE else place.z + 1
        index = jnp.where(zd == there, 4, zd) if side == BELOW else zd
        return slots.at[index], sems.at[index]

    def line(j, p, first, slots, sems, send_sem, target):
        zd = place.ranked(j)
        rows = sizes[p]
        for side, condition in (
            (ABOVE, (zd <= place.z) & (place.z < 3)),
            (BELOW, (zd >= place.z) & (place.z > 0)),
        ):
            window, sem = into(slots, sems, zd, side)

            def take(window=window, sem=sem):
                remote(window, window, send_sem, sem, place.device("c")).wait_recv()
                add_rows(acc.at[target], first, window, rows)

            if j == 0:
                condition = place.z < 3 if side == ABOVE else place.z > 0
            run(condition, take)
        if j == 0:
            return
        for side, axis, condition in ((ABOVE, DOWN, zd < place.z), (BELOW, UP, zd > place.z)):
            window, sem = out_to(slots, sems, zd, side)
            go(
                condition,
                remote(acc.at[target, pl.ds(first, rows)], window, send_sem, sem, place.device(axis)),
            )

    above_e, below_e = place.z > place.e, place.z < place.e
    hops = jnp.where(above_e, 3 - place.z, jnp.where(below_e, place.z, jnp.maximum(place.e, 3 - place.e)))

    def tall_round(r):
        k = r - hops
        live = (k >= 0) & (k < CHUNKS)
        k = jnp.clip(k, 0, CHUNKS - 1)
        first = pl.multiple_of(k * chunk, chunk)
        piece = pl.ds(first, chunk)

        @pl.when(live)
        def _():
            remote(
                ty.at[piece], ty.at[piece], tall_send.at[0, k], ty_in.at[k], place.device("c")
            ).wait_recv()
            add_rows(tacc.at[place.y], first, ty.at[piece], chunk)

        for index, condition in (
            (0, (place.z >= place.e) & (place.z < 3)),
            (1, (place.z <= place.e) & (place.z > 0)),
        ):
            window = tz.at[index, piece]

            def take(window=window, index=index):
                remote(
                    window, window, tall_send.at[1, k], tz_in.at[index, k], place.device("c")
                ).wait_recv()
                add_rows(tacc.at[place.y], first, window, chunk)

            run(live & condition, take)
        for index, axis, condition in ((0, DOWN, above_e), (1, UP, below_e)):
            go(
                live & condition,
                remote(
                    tacc.at[place.y, piece], tz.at[index, piece], tall_send.at[1, k],
                    tz_in.at[index, k], place.device(axis),
                ),
            )
        piece_out = tall_out.at[piece]
        keep = pltpu.make_async_copy(tacc.at[place.y, piece], piece_out, keep_tall.at[k])
        run(live & owner, keep.start)
        tall_keeps.append((live & owner, keep))
        for row, axis in ((2, "x"), (3, "c")):
            go(
                live & owner,
                remote(
                    tacc.at[place.y, piece], piece_out, tall_send.at[row, k], tall_in.at[k],
                    place.device(axis),
                ),
            )

    def flat_first(j):
        zd = place.ranked(j)
        target = zd * 2 + place.y
        window = yslot.at[zd]
        remote(window, window, flat_send.at[0, target], yin.at[zd], place.device("c")).wait_recv()
        add_rows(acc.at[target], starts[0], window, sizes[0])
        line(j, 0, starts[0], zslot, zin, flat_send.at[0, target], target)

    def flat_second(j, yr):
        zd = place.ranked(j)
        target = zd * 2 + (1 - place.y if yr else place.y)
        line(j, 1, starts[1], zall.at[yr], zall_in.at[yr], flat_send.at[1, target], target)

    flat_second(3, 1)
    flat_second(3, 0)
    tall_round(0)
    feed(1)
    tall_round(1)
    feed(2)
    flat_second(2, 1)
    flat_second(2, 0)
    flat_first(3)
    feed(3)
    group_half(0, 1 - place.x)
    tall_round(2)
    feed(4)
    flat_second(1, 1)
    flat_second(1, 0)
    flat_first(2)
    feed(5)
    tall_round(3)
    feed(6)
    flat_first(1)
    group_half(1, place.x)
    flat_second(0, 1)
    other = place.z * 2 + 1 - place.y
    go(
        None,
        remote(
            acc.at[other, pl.ds(starts[1], sizes[1])], yone, flat_send.at[1, other], yone_in.at[0],
            place.device("y"),
        ),
    )
    flat_second(0, 0)
    flat_first(0)
    remote(yone, yone, flat_send.at[1, other], yone_in.at[0], place.device("c")).wait_recv()
    add_rows(acc.at[place.f], starts[1], yone, sizes[1])
    cuts = []
    first = 0
    for out in (out_q, out_k, out_v):
        wide = out.shape[1] // experts
        cuts.append((out, pl.ds(0, flat.shape[1]), pl.ds(first, wide)))
        first += wide
    cuts.append((pack_all, pl.ds(flat.shape[1], pack.shape[1]), pl.ds(0, first)))

    def window_of(i, source):
        out = cuts[i][0]
        if i == 3:
            return out.at[source]
        wide = out.shape[1] // experts
        return out.at[:, pl.ds(pl.multiple_of(source * wide, 128), wide)]

    flat_keeps = []
    for i, (out, high, wide) in enumerate(cuts):
        done = acc.at[place.f, high, wide]
        keep = pltpu.make_async_copy(done, window_of(i, place.e), local.at[1 + i])
        keep.start()
        flat_keeps.append(keep)
        for row, axis in enumerate(("x", "c")):
            go(
                None,
                remote(
                    done, window_of(i, place.e), spread_out.at[row, i], spread_in.at[place.e, i],
                    place.device(axis),
                ),
            )
    tall_round(4)
    tall_round(5)
    tall_round(6)
    group_end()
    across = (1 - place.x) * 2 + place.c
    for i in range(4):
        window = window_of(i, across)
        relay = remote(window, window, spread_out.at[2, i], spread_in.at[across, i], place.device("c"))
        relay.wait_recv()
        go(None, relay)
    for k in range(CHUNKS):
        window = tall_out.at[pl.ds(k * chunk, chunk)]
        tall_relay = remote(window, window, tall_send.at[4, k], tall_in.at[k], place.device("c"))
        run(~owner, tall_relay.wait_recv)
        go(~home & same, tall_relay)
    for source in (place.x * 2 + 1 - place.c, (1 - place.x) * 2 + 1 - place.c):
        for i in range(4):
            window = window_of(i, source)
            remote(
                window, window, spread_out.at[2, i], spread_in.at[source, i], place.device("c")
            ).wait_recv()
    for copy in across_y[-2:]:
        copy.wait_send()
    for condition, copy in pending:
        run(condition, copy.wait_send)
    for keep in flat_keeps:
        keep.wait()
    for condition, keep in tall_keeps:
        run(condition, keep.wait)
    for copy in group_sends:
        copy.wait_send()


def reduce(experts, shards, number, flat, tall, pack, partial):
    space = pl.BlockSpec(memory_space=pl.ANY)
    dma = pltpu.SemaphoreType.DMA
    _, sizes = flat_parts(flat.shape[1])
    more = sizes[1] + pack.shape[1]
    width, wide = flat.shape[2], tall.shape[2]
    low = jnp.bfloat16
    return pl.pallas_call(
        functools.partial(reduce_kernel, (experts, shards)),
        out_shape=[
            jax.ShapeDtypeStruct((flat.shape[1], experts * (width - 2 * HEAD_SIZE)), low),
            jax.ShapeDtypeStruct((flat.shape[1], experts * HEAD_SIZE), low),
            jax.ShapeDtypeStruct((flat.shape[1], experts * HEAD_SIZE), low),
            jax.ShapeDtypeStruct(tall.shape[1:], low),
            jax.ShapeDtypeStruct((experts,) + pack.shape[1:], low),
            jax.ShapeDtypeStruct(partial.shape[1:], jnp.float32),
        ],
        in_specs=[space] * 4,
        out_specs=[space] * 5 + [pl.BlockSpec(memory_space=pltpu.VMEM)],
        scratch_shapes=[
            pltpu.VMEM((shards, flat.shape[1] + pack.shape[1], width), low),
            pltpu.VMEM(tall.shape, low),
            pltpu.VMEM((4, sizes[0], width), low),
            pltpu.VMEM((5, sizes[0], width), low),
            pltpu.VMEM((more, width), low),
            pltpu.VMEM((2, 5, more, width), low),
            pltpu.VMEM(tall.shape[1:], low),
            pltpu.VMEM((2,) + tall.shape[1:], low),
            dma((3,)),
            dma((4,)),
            dma((5,)),
            dma((1,)),
            dma((2, 5)),
            dma((CHUNKS,)),
            dma((2, CHUNKS)),
            dma((2, shards)),
            dma((5, CHUNKS)),
            dma((experts, 4)),
            dma((3, 4)),
            dma((CHUNKS,)),
            dma((CHUNKS,)),
            dma((5,)),
            pltpu.VMEM((2,) + partial.shape[1:], low),
            pltpu.VMEM((2,) + partial.shape[1:], low),
            pltpu.VMEM(partial.shape[1:], low),
            dma((2, CHUNKS)),
            dma((2, CHUNKS)),
            dma((2, CHUNKS)),
            dma((CHUNKS,)),
            dma((CHUNKS,)),
        ],
        compiler_params=pltpu.CompilerParams(
            collective_id=number, has_side_effects=True, vmem_limit_bytes=48 * 2**20
        ),
        name="reduce",
    )(flat, tall, pack, partial)


def branch_scatter_kernel(
    mixed, weight, total, blocks, near, cross, near_out, near_in, x_out, x_in
):
    place = Place()
    greet(place)
    rows, width = total.shape
    chunk = rows // CHUNKS
    sends = []
    for index, half in enumerate((1 - place.x, place.x)):
        for core in (1 - place.c, place.c):
            block = half * 2 + core
            here = pl.ds(pl.multiple_of(block * rows, rows), rows)

            def tile(t, carry):
                columns = pl.ds(pl.multiple_of(t * 512, 512), 512)
                blocks[block, :, columns] = jnp.dot(
                    mixed[here], weight[:, columns], preferred_element_type=jnp.float32
                ).astype(jnp.bfloat16)
                return carry

            lax.fori_loop(0, width // 512, tile, 0)
        for k in range(CHUNKS):
            piece = pl.ds(k * chunk, chunk)
            copy = remote(
                blocks.at[half * 2 + 1 - place.c, piece], near.at[half, piece], near_out.at[half, k],
                near_in.at[half, k], place.device("c"),
            )
            copy.start()
            sends.append(copy)
        for k in range(CHUNKS):
            piece = pl.ds(k * chunk, chunk)
            window = near.at[half, piece]
            remote(window, window, near_out.at[half, k], near_in.at[half, k], place.device("c")).wait_recv()
            add_rows(blocks.at[half * 2 + place.c], k * chunk, window, chunk)
            if index == 0:
                copy = remote(
                    blocks.at[half * 2 + place.c, piece], cross.at[piece], x_out.at[k], x_in.at[k],
                    place.device("x"),
                )
                copy.start()
                sends.append(copy)
    for k in range(CHUNKS):
        window = cross.at[pl.ds(k * chunk, chunk)]
        remote(window, window, x_out.at[k], x_in.at[k], place.device("c")).wait_recv()

        def add(i, carry):
            here = pl.ds(pl.multiple_of(k * chunk + i * 16, 16), 16)
            own = blocks[place.e, here].astype(jnp.float32)
            total[here] = own + cross[here].astype(jnp.float32)
            return carry

        lax.fori_loop(0, chunk // 16, add, 0)
    for copy in sends:
        copy.wait_send()


def branch_scatter(number, mixed, weight):
    dma = pltpu.SemaphoreType.DMA
    rows, width = mixed.shape[0] // 4, weight.shape[1]
    low = jnp.bfloat16
    vmem = pl.BlockSpec(memory_space=pltpu.VMEM)
    return pl.pallas_call(
        branch_scatter_kernel,
        out_shape=jax.ShapeDtypeStruct((rows, width), jnp.float32),
        in_specs=[vmem, vmem],
        out_specs=vmem,
        scratch_shapes=[
            pltpu.VMEM((4, rows, width), low),
            pltpu.VMEM((2, rows, width), low),
            pltpu.VMEM((rows, width), low),
            dma((2, CHUNKS)),
            dma((2, CHUNKS)),
            dma((CHUNKS,)),
            dma((CHUNKS,)),
        ],
        compiler_params=pltpu.CompilerParams(
            collective_id=number, has_side_effects=True, vmem_limit_bytes=32 * 2**20
        ),
        name="branch_scatter",
    )(mixed, weight)


BLOCK = 256


def dot_last(a, b):
    return lax.dot_general(a, b, (((1,), (1,)), ((), ())), preferred_element_type=jnp.float32)


def dot(a, b):
    return jnp.dot(a, b, preferred_element_type=jnp.float32)


def turn(rows):
    lane = lax.broadcasted_iota(jnp.int32, rows.shape, 1)
    half = HEAD_SIZE // 2
    return pltpu.roll(rows, half, 1) * jnp.where(lane < half, -1.0, 1.0)


def mask_block(r, count, ids_column, ids_row, bias):
    queries = pl.ds(r * BLOCK, BLOCK)

    def part(i, carry):
        keys = pl.ds(pl.multiple_of(i * BLOCK, BLOCK), BLOCK)
        key_at = lax.broadcasted_iota(jnp.int32, (BLOCK, BLOCK), 0) + i * BLOCK
        query_at = lax.broadcasted_iota(jnp.int32, (BLOCK, BLOCK), 1) + r * BLOCK
        allowed = (ids_column[keys] == ids_row[:, queries]) & (key_at <= query_at)
        bias[keys] = jnp.where(allowed, 0.0, -1e30)
        return carry

    lax.fori_loop(0, count // BLOCK, part, 0)


def project_steps(
    tok, w_qkv, gain_one, gain_q, gain_k, cosine, sine, normed, raw, query_rot, key_rot, value, inverses
):
    heads = query_rot.shape[1] // HEAD_SIZE
    low = jnp.bfloat16

    def rotated(v, rows, gain):
        u = v * inverse_rms(v) * gain
        return (u * cosine[rows] + turn(u) * sine[rows]).astype(low)

    def norm(r):
        def part(i, carry):
            here = pl.ds(pl.multiple_of(r * BLOCK + i * 16, 16), 16)
            x = tok[here].astype(jnp.float32)
            inverse = inverse_rms(x)
            inverses[here] = inverse
            normed[here] = (x * inverse * gain_one[...]).astype(low)
            return carry

        lax.fori_loop(0, BLOCK // 16, part, 0, unroll=2)

    def multiply(r):
        rows = pl.ds(r * BLOCK, BLOCK)

        def pair(i, carry):
            column = pl.ds(pl.multiple_of(i * 2 * HEAD_SIZE, 2 * HEAD_SIZE), 2 * HEAD_SIZE)
            both = dot(normed[rows], w_qkv[:, column])
            raw[rows, column] = both
            for k in range(2):
                at = pl.ds(pl.multiple_of((2 * i + k) * HEAD_SIZE, HEAD_SIZE), HEAD_SIZE)
                one = both[:, k * HEAD_SIZE : (k + 1) * HEAD_SIZE]
                query_rot[rows, at] = rotated(one, rows, gain_q[...])
            return carry

        lax.fori_loop(0, heads // 2, pair, 0)
        last = pl.ds(heads * HEAD_SIZE, 2 * HEAD_SIZE)
        both = dot(normed[rows], w_qkv[:, last])
        raw[rows, last] = both
        key_rot[rows] = rotated(both[:, :HEAD_SIZE], rows, gain_k[...])
        value[rows] = both[:, HEAD_SIZE:].astype(low)

    steps = []
    for r in range(tok.shape[0] // BLOCK):
        steps.append(functools.partial(norm, r))
        steps.append(functools.partial(multiply, r))
    return steps


def attend_steps(query_rot, key_rot, value, ids_column, ids_row, mixed, bias, value_t):
    length = key_rot.shape[0]
    heads = query_rot.shape[1] // HEAD_SIZE
    scale = HEAD_SIZE ** (-0.5)

    def prepare(r):
        if r == 0:
            value_t[...] = value[...].T
        mask_block(r, (r + 1) * BLOCK, ids_column, ids_row, bias)

    def heads_of(r, first, some):
        rows = pl.ds(r * BLOCK, BLOCK)
        count = (r + 1) * BLOCK

        def head(h, carry):
            column = pl.ds(pl.multiple_of(h * HEAD_SIZE, HEAD_SIZE), HEAD_SIZE)
            scores = dot_last(key_rot[:count], query_rot[rows, column]) * scale + bias[:count]
            shifted = jnp.exp(scores - jnp.max(scores, 0, keepdims=True))
            weights = shifted * (1.0 / jnp.sum(shifted, 0, keepdims=True))
            out = dot(value_t[:, :count], weights.astype(jnp.bfloat16))
            mixed[rows, column] = out.T.astype(jnp.bfloat16)
            return carry

        lax.fori_loop(first, first + some, head, 0, unroll=2)

    steps = []
    for r in range(length // BLOCK):
        steps.append(functools.partial(prepare, r))
        some = heads if r == 0 else heads // 2
        for first in range(0, heads, some):
            steps.append(functools.partial(heads_of, r, first, some))
    return steps


def load(pairs, sems):
    copies = [pltpu.make_async_copy(a, b, sems.at[i]) for i, (a, b) in enumerate(pairs)]
    for copy in copies:
        copy.start()
    return copies


def attention(tokens, w_qkv, gain_one, gain_q, gain_k, cosine, sine, ids_column, ids_row, heads):
    length, width = tokens.shape
    wide = w_qkv.shape[1]
    span = heads * HEAD_SIZE
    low, f32 = jnp.bfloat16, jnp.float32
    space, vmem = pl.BlockSpec(memory_space=pl.ANY), pl.BlockSpec(memory_space=pltpu.VMEM)
    shapes = [
        ((length, width), low),
        ((length, wide), f32),
        ((length, span), low),
        ((length, HEAD_SIZE), low),
        ((length, HEAD_SIZE), low),
        ((length, span), low),
        ((length, 1), f32),
    ]

    def steps(*refs):
        ins, outs, scratch = split(refs, (9, 7, 15))
        tok, weight, cos_held, sin_held, in_sems, out_sems, bias, value_t = scratch[:8]
        results = scratch[8:]
        copies = load(
            [(ins[0], tok), (ins[1], weight), (ins[5], cos_held), (ins[6], sin_held)], in_sems
        )

        def begin():
            for copy in copies:
                copy.wait()

        saved = []

        def save(picks):
            for i in picks:
                copy = pltpu.make_async_copy(results[i], outs[i], out_sems.at[i])
                copy.start()
                saved.append(copy)

        def end():
            save((5, 6))
            for copy in saved:
                copy.wait()

        return (
            [begin]
            + project_steps(tok, weight, *ins[2:5], cos_held, sin_held, *results[:5], results[6])
            + [functools.partial(save, range(5))]
            + attend_steps(*results[2:5], *ins[7:9], results[5], bias, value_t)
            + [end]
        )

    return Extra(
        (tokens, w_qkv, gain_one, gain_q, gain_k, cosine, sine, ids_column, ids_row),
        [space] * 2 + [vmem] * 3 + [space] * 2 + [vmem] * 2,
        [jax.ShapeDtypeStruct(*shape) for shape in shapes],
        [space] * 7,
        [
            pltpu.VMEM(tokens.shape, low),
            pltpu.VMEM(w_qkv.shape, low),
            pltpu.VMEM(cosine.shape, f32),
            pltpu.VMEM(sine.shape, f32),
            pltpu.SemaphoreType.DMA((4,)),
            pltpu.SemaphoreType.DMA((7,)),
            pltpu.VMEM((length, BLOCK), f32),
            pltpu.VMEM((HEAD_SIZE, length), low),
        ]
        + [pltpu.VMEM(*shape) for shape in shapes],
        steps,
    )


def attend_back_steps(
    query_rot, key_rot, value, raw, grad_mixed, ids_column, ids_row, gain_q, gain_k, cosine, sine,
    grad_raw, grad_gains, bias, key_t, grad_key, grad_value, sums,
):
    length = key_rot.shape[0]
    heads = query_rot.shape[1] // HEAD_SIZE
    scale = HEAD_SIZE ** (-0.5)
    low = jnp.bfloat16

    def back(grad, rows, column, gain, index):
        unit = grad * cosine[rows] - turn(grad * sine[rows])
        v = raw[rows, column]
        inverse = inverse_rms(v)
        sums[index] += jnp.sum((unit * v * inverse).reshape(-1, 8, HEAD_SIZE), 0)
        grad_raw[rows, column] = norm_backward(unit, v, inverse, gain).astype(low)

    def prepare(r):
        if r == 0:
            key_t[...] = key_rot[...].T
            grad_key[...] = jnp.zeros_like(grad_key)
            grad_value[...] = jnp.zeros_like(grad_value)
            sums[...] = jnp.zeros_like(sums)
        mask_block(r, (r + 1) * BLOCK, ids_column, ids_row, bias)

    def heads_of(r, first, some):
        rows = pl.ds(r * BLOCK, BLOCK)
        count = (r + 1) * BLOCK

        def head(h, carry):
            column = pl.ds(pl.multiple_of(h * HEAD_SIZE, HEAD_SIZE), HEAD_SIZE)
            query = query_rot[rows, column]
            grad_out = grad_mixed[rows, column]
            scores = dot_last(key_rot[:count], query) * scale + bias[:count]
            shifted = jnp.exp(scores - jnp.max(scores, 0, keepdims=True))
            weights = shifted * (1.0 / jnp.sum(shifted, 0, keepdims=True))
            grad_value[:count] += dot(weights.astype(low), grad_out)
            grad_weights = dot_last(value[:count], grad_out)
            spread = jnp.sum(weights * grad_weights, 0, keepdims=True)
            grad_scores = (weights * (grad_weights - spread)).astype(low)
            grad_key[:count] += dot(grad_scores, query)
            grad_query = dot(key_t[:, :count], grad_scores).T * scale
            back(grad_query, rows, column, gain_q[...], 0)
            return carry

        lax.fori_loop(first, first + some, head, 0, unroll=2)

    def last():
        column = pl.ds(heads * HEAD_SIZE, HEAD_SIZE)
        for r in range(length // BLOCK):
            rows = pl.ds(r * BLOCK, BLOCK)
            back(grad_key[rows] * scale, rows, column, gain_k[...], 1)
            grad_raw[rows, pl.ds((heads + 1) * HEAD_SIZE, HEAD_SIZE)] = grad_value[rows].astype(low)
        grad_gains[...] = jnp.sum(sums[...], 1)

    steps = []
    for r in range(length // BLOCK):
        steps.append(functools.partial(prepare, r))
        some = heads if r == 0 else (heads // 2 if r == 1 else heads // 4)
        for first in range(0, heads, some):
            steps.append(functools.partial(heads_of, r, first, some))
    return steps + [last]


def attention_back(
    query_rot, key_rot, value, raw, mixed, grad_low, w_mix, normed_one, tokens, w_qkv, inverses,
    ids_column, ids_row, gain_q, gain_k, cosine, sine,
):
    length, width = tokens.shape
    span, wide = mixed.shape[1], raw.shape[1]
    tiles = width // BLOCK
    low, f32 = jnp.bfloat16, jnp.float32
    space, vmem = pl.BlockSpec(memory_space=pl.ANY), pl.BlockSpec(memory_space=pltpu.VMEM)
    whole = (query_rot, key_rot, value, raw, mixed, cosine, sine, inverses)
    streamed = (grad_low, w_mix, normed_one, tokens, w_qkv)
    own_rows = grad_low.shape[0]
    piece = own_rows // CHUNKS
    small = (ids_column, ids_row, gain_q, gain_k)

    def dot_first(a, b):
        return lax.dot_general(a, b, (((0,), (0,)), ((), ())), preferred_element_type=f32)

    def steps(*refs):
        ins, outs, scratch = split(refs, (17, 5, 27))
        held, (in_sems, grad_raw), work, tile_refs, group = split(scratch, (8, 2, 5, 4, 8))
        tall_in, tall_out, wide_out, sems = tile_refs
        mine, mix, normed, tok, weight = ins[8:13]
        inverse = held[7]
        branch, grad_mixed, mix_in, mix_sems, x_out, x_in, c_out, c_in = group
        place = Place()
        beside, other = place.at((1 - place.x, place.y), place.c), place.device("c")
        across = (1 - place.x) * 2 + place.c
        gains, grad_mix, grad_qkv, grad_normed, grad_gain = outs
        copies = load(list(zip(ins[:8], held)), in_sems)

        def rows_from(source, k):
            return branch.at[pl.ds(pl.multiple_of(source * own_rows + k * piece, piece), piece)]

        def own(k):
            return mine.at[pl.ds(k * piece, piece)]

        sends = []
        keeps = []
        for k in range(CHUNKS):
            sends.append(remote(own(k), rows_from(place.e, k), x_out.at[k], x_in.at[k], beside))
            sends.append(remote(own(k), rows_from(place.e, k), c_out.at[0, k], c_in.at[0, k], other))
            keeps.append(pltpu.make_async_copy(own(k), rows_from(place.e, k), mix_sems.at[2 + k]))
        for copy in sends + keeps:
            copy.start()

        def relay(k):
            window = rows_from(across, k)
            copy = remote(window, window, c_out.at[1, k], c_in.at[1, k], other)
            remote(window, window, x_out.at[k], x_in.at[k], other).wait_recv()
            copy.start()
            sends.append(copy)

        def mix_tile(t):
            return pltpu.make_async_copy(mix.at[at(t)], mix_in.at[t % 2], mix_sems.at[t % 2])

        def arrived():
            mix_tile(0).start()
            for copy in keeps:
                copy.wait()
            for k in range(CHUNKS):
                window = rows_from(place.x * 2 + 1 - place.c, k)
                remote(window, window, c_out.at[0, k], c_in.at[0, k], other).wait_recv()
                window = rows_from((1 - place.x) * 2 + 1 - place.c, k)
                remote(window, window, c_out.at[1, k], c_in.at[1, k], other).wait_recv()
            for copy in sends:
                copy.wait_send()

        def mixed_grad(t):
            mix_tile(t).wait()
            if t + 1 < span // BLOCK:
                mix_tile(t + 1).start()
            grad_mixed[:, at(t)] = dot_last(branch[...], mix_in[t % 2]).astype(low)

        def at(t):
            return pl.ds(t * BLOCK, BLOCK)

        def fetch(i):
            kind, t, slot = i // tiles, i % tiles, i % 2
            if kind == 0:
                return []
            source = (None, normed, tok)[kind]
            found = [
                pltpu.make_async_copy(source.at[:, at(t)], tall_in.at[slot], sems.at[0, slot])
            ]
            if kind == 2:
                found.append(
                    pltpu.make_async_copy(
                        weight.at[at(t)], mix_in.at[slot, :, pl.ds(0, wide)], sems.at[1, slot]
                    )
                )
            return found

        def store(i):
            kind, t, slot = i // tiles, i % tiles, i % 2
            if kind == 1:
                return pltpu.make_async_copy(
                    wide_out.at[slot], grad_qkv.at[at(t)], sems.at[2, slot]
                )
            target = grad_normed if kind else grad_mix
            return pltpu.make_async_copy(tall_out.at[slot], target.at[:, at(t)], sems.at[2, slot])

        def begin():
            for copy in copies:
                copy.wait()

        def tile(i):
            kind, t, slot = i // tiles, i % tiles, i % 2
            for copy in fetch(i):
                copy.wait()
            if i + 1 < 3 * tiles:
                for copy in fetch(i + 1):
                    copy.start()
            if i >= 2:
                store(i - 2).wait()
            if kind == 0:
                tall_out[slot] = dot_first(held[4][...], branch[:, at(t)]).astype(low)
            elif kind == 1:
                wide_out[slot] = dot_first(tall_in[slot], grad_raw[...]).astype(low)
            else:
                found = dot_last(grad_raw[...], mix_in[slot, :, :wide])
                scaled = tall_in[slot].astype(f32) * inverse[...]
                grad_gain[:, at(t)] = jnp.sum(found * scaled, 0, keepdims=True)
                tall_out[slot] = found.astype(low)
            store(i).start()

        def end():
            for i in (3 * tiles - 2, 3 * tiles - 1):
                store(i).wait()

        jobs = [functools.partial(tile, i) for i in range(3 * tiles)]
        back = attend_back_steps(
            *held[:4], grad_mixed, *ins[13:], *held[5:7], grad_raw, gains, *work
        )
        start = [functools.partial(relay, k) for k in range(CHUNKS)] + [arrived]
        start += [functools.partial(mixed_grad, t) for t in range(span // BLOCK)]
        return [begin] + start + back + jobs + [end]

    return Extra(
        whole + streamed + small,
        [space] * 13 + [vmem] * 4,
        [
            jax.ShapeDtypeStruct((2, HEAD_SIZE), f32),
            jax.ShapeDtypeStruct((span, width), low),
            jax.ShapeDtypeStruct((width, wide), low),
            jax.ShapeDtypeStruct((length, width), low),
            jax.ShapeDtypeStruct((1, width), f32),
        ],
        [vmem, space, space, space, vmem],
        [pltpu.VMEM(a.shape, a.dtype) for a in whole]
        + [
            pltpu.SemaphoreType.DMA((8,)),
            pltpu.VMEM(raw.shape, low),
            pltpu.VMEM((length, BLOCK), f32),
            pltpu.VMEM((HEAD_SIZE, length), low),
            pltpu.VMEM((length, HEAD_SIZE), f32),
            pltpu.VMEM((length, HEAD_SIZE), f32),
            pltpu.VMEM((2, 8, HEAD_SIZE), f32),
            pltpu.VMEM((2, length, BLOCK), low),
            pltpu.VMEM((2, length, BLOCK), low),
            pltpu.VMEM((2, BLOCK, wide), low),
            pltpu.SemaphoreType.DMA((3, 2)),
            pltpu.VMEM((length, width), low),
            pltpu.VMEM((length, span), low),
            pltpu.VMEM((2, BLOCK, width), low),
            pltpu.SemaphoreType.DMA((2 + CHUNKS,)),
            pltpu.SemaphoreType.DMA((CHUNKS,)),
            pltpu.SemaphoreType.DMA((CHUNKS,)),
            pltpu.SemaphoreType.DMA((2, CHUNKS)),
            pltpu.SemaphoreType.DMA((2, CHUNKS)),
        ],
        steps,
    )


def weight_grads(rows, grad_result, inner, grad_a, grad_b):
    count, width = rows.shape
    inside = inner.shape[1]
    low, f32 = jnp.bfloat16, jnp.float32
    space = pl.BlockSpec(memory_space=pl.ANY)
    tiles = width // BLOCK

    def dot_first(a, b):
        return lax.dot_general(a, b, (((0,), (0,)), ((), ())), preferred_element_type=f32)

    def steps(*refs):
        ins, outs, scratch = split(refs, (5, 3, 9))
        a_held, b_held, inner_held, tile, wide, tall, in_sems, tile_sems, out_sems = scratch
        copies = load([(ins[3], a_held), (ins[4], b_held), (ins[2], inner_held)], in_sems)

        def fetch(i):
            source = ins[0] if i < tiles else ins[1]
            columns = pl.ds((i % tiles) * BLOCK, BLOCK)
            return pltpu.make_async_copy(source.at[:, columns], tile.at[i % 2], tile_sems.at[i % 2])

        def store(i, k):
            at = pl.ds((i % tiles) * BLOCK, BLOCK)
            if i < tiles:
                return pltpu.make_async_copy(wide.at[k, i % 2], outs[k].at[at], out_sems.at[k, i % 2])
            return pltpu.make_async_copy(tall.at[i % 2], outs[2].at[:, at], out_sems.at[2, i % 2])

        def begin():
            fetch(0).start()
            for copy in copies:
                copy.wait()

        def prepare(i):
            fetch(i).wait()
            if i + 1 < 2 * tiles:
                fetch(i + 1).start()

        def first(i, k):
            if k == 0:
                prepare(i)
            if i >= 2:
                store(i - 2, k).wait()
            wide[k, i % 2] = dot_first(tile[i % 2], (a_held, b_held)[k][...])
            store(i, k).start()

        def second(i):
            prepare(i)
            if i >= tiles + 2:
                store(i - 2, 2).wait()
            tall[i % 2] = dot_first(inner_held[...], tile[i % 2])
            store(i, 2).start()

        def end():
            for i in (tiles - 2, tiles - 1):
                store(i, 0).wait()
                store(i, 1).wait()
            for i in (2 * tiles - 2, 2 * tiles - 1):
                store(i, 2).wait()

        found = [begin]
        for i in range(tiles):
            found += [functools.partial(first, i, 0), functools.partial(first, i, 1)]
        for i in range(tiles, 2 * tiles):
            found.append(functools.partial(second, i))
        return found + [end]

    return Extra(
        (rows, grad_result, inner, grad_a, grad_b),
        [space] * 5,
        [
            jax.ShapeDtypeStruct((width, inside), f32),
            jax.ShapeDtypeStruct((width, inside), f32),
            jax.ShapeDtypeStruct((inside, width), f32),
        ],
        [space] * 3,
        [
            pltpu.VMEM((count, inside), low),
            pltpu.VMEM((count, inside), low),
            pltpu.VMEM((count, inside), low),
            pltpu.VMEM((2, count, BLOCK), low),
            pltpu.VMEM((2, 2, BLOCK, inside), f32),
            pltpu.VMEM((2, inside, BLOCK), f32),
            pltpu.SemaphoreType.DMA((3,)),
            pltpu.SemaphoreType.DMA((2,)),
            pltpu.SemaphoreType.DMA((3, 2)),
        ],
        steps,
    )


WIDE = 512


def dispatch_expert_kernel(
    dims, tok, sel, small, grads, picks, ids, w_gate, w_up, w_down,
    small_all, rows_out, weighted, grad_result, inner, grad_a, grad_b, grad_rows, gate_grad,
    held, stage, picked, arrive, leave, pick_out, pick_in, local, small_out, small_in,
    gates, weights_in, gate_held, up_held, down_held, g_held, g_in,
    weighted_s, result_s, inner_s, a_s, b_s, rows_s, a_wide, b_wide, store_sems, keep_sems,
):
    experts, shards = dims
    low, f32 = jnp.bfloat16, jnp.float32
    place = Place()
    width = tok.shape[1]
    near, far = place.line()
    mine = (place.x, place.y)
    me = place.e * shards + place.f
    greet_all(place, *dims)
    end_small = exchange_small(
        place, dims, lambda i: small, small_all, small_out, small_in, local.at[1]
    )
    keep = pltpu.make_async_copy(tok, held.at[place.z], local.at[0])
    keep.start()
    loads = load([(w_gate.at[0], gate_held), (w_up.at[0], up_held), (w_down.at[0], down_held)], weights_in)
    pending = []
    targets = (place.device("c"), place.at(far, place.c), place.at(far, 1 - place.c))
    half = tok.shape[0] // HALVES

    def pick(ar, zs):
        block = ar * 4 + zs
        number = block_number(mine, place.c, ar, zs)

        def tile(i, carry):
            columns = pl.ds(pl.multiple_of(i * WIDE, WIDE), WIDE)
            chosen = dot(sel[block], held[block, :, columns]).astype(low)
            picked[number, :, columns] = chosen[:SLOTS]
            stage[block, :, columns] = chosen[SLOTS:]
            return carry

        lax.fori_loop(0, width // WIDE, tile, 0)
        for k in (2, 1, 0):
            away = remote(
                stage.at[block, pl.ds(k * SLOTS, SLOTS)], picked.at[number],
                pick_out.at[block, k], pick_in.at[number], targets[k],
            )
            away.start()
            pending.append((None, away))

    def wait_rows(i):
        xs, cs, ys = i // 16, i // 8 % 2, i % 2
        inside = (cs == place.c) & jnp.where(place.c == 0, ys == place.y, xs == place.x)

        @pl.when(~inside)
        def _():
            window = picked.at[i]
            remote(window, window, pick_out.at[0, 0], pick_in.at[i], place.device("c")).wait_recv()

    def sources(n):
        first = n % 2 * 16 + place.ranked(n // 2) * 2
        return first, first + 8

    def grads_of(n):
        return [
            pltpu.make_async_copy(
                grads.at[pl.ds(first, 2)], g_held.at[n % 2, pl.ds(2 * k, 2)], g_in.at[n % 2, k]
            )
            for k, first in enumerate(sources(n))
        ]

    kept = []
    for copy in grads_of(0):
        copy.start()

    def stores(n):
        pairs = (
            (weighted_s, weighted), (result_s, grad_result), (inner_s, inner), (a_s, grad_a),
            (b_s, grad_b), (rows_s, grad_rows),
        )
        return [
            pltpu.make_async_copy(
                source.at[pl.ds(2 * k, 2)], target.at[pl.ds(first, 2)], store_sems.at[i, k]
            )
            for i, (source, target) in enumerate(pairs)
            for k, first in enumerate(sources(n))
        ]

    def compute(n):
        first, second = sources(n)
        from_devices = (first, first + 1, second, second + 1)
        if n == 0:
            end_small()
            copy = pltpu.make_async_copy(small_all, gates, local.at[2])
            copy.start()
            for done in loads:
                done.wait()
            copy.wait()
        if n + 1 < 8:
            for copy in grads_of(n + 1):
                copy.start()
        for i in from_devices:
            wait_rows(i)
        for k, start in enumerate((first, second)):
            copy = pltpu.make_async_copy(
                picked.at[pl.ds(start, 2)], rows_out.at[pl.ds(start, 2)], keep_sems.at[n, k]
            )
            copy.start()
            kept.append(copy)
        here = []
        for i in from_devices:
            value = jnp.sum(jnp.where(ids[i] == me, gates[i], 0.0), 0, keepdims=True)
            here.append(jnp.sum(picks[i].astype(f32) * value, -1, keepdims=True))
        here = jnp.concatenate(here, 0)
        count = 4 * SLOTS
        x = jnp.concatenate([picked[i] for i in from_devices], 0)
        a = dot(x, gate_held[...])
        b = dot(x, up_held[...])
        for copy in grads_of(n):
            copy.wait()
        if n:
            for copy in stores(n - 1):
                copy.wait()
        sigmoid = jax.nn.sigmoid(a)
        active = a * sigmoid
        inner_s[...] = (active * b).astype(low).reshape(inner_s.shape)
        a_wide[...] = b * (sigmoid * (1.0 + a * (1.0 - sigmoid)))
        b_wide[...] = active

        def forward(t, found):
            columns = pl.ds(pl.multiple_of(t * WIDE, WIDE), WIDE)
            result = dot(inner_s[...].reshape(count, -1), down_held[:, columns])
            g = g_held[n % 2, :, :, columns].reshape(count, WIDE).astype(f32)
            weighted_s[:, :, columns] = (result * here).astype(low).reshape(4, SLOTS, WIDE)
            result_s[:, :, columns] = (g * here).astype(low).reshape(4, SLOTS, WIDE)
            return found + jnp.sum(result * g, -1, keepdims=True)

        found = lax.fori_loop(0, width // WIDE, forward, jnp.zeros((count, 1), f32))
        for k, i in enumerate(from_devices):
            part = picks[i].astype(f32) * found[k * SLOTS : (k + 1) * SLOTS]
            gate_grad[i] = jnp.broadcast_to(jnp.sum(part, 0, keepdims=True), gate_grad.shape[1:])
        grad_inner = dot_last(result_s[...].reshape(count, width), down_held[...])
        a_s[...] = (grad_inner * a_wide[...]).astype(low).reshape(a_s.shape)
        b_s[...] = (grad_inner * b_wide[...]).astype(low).reshape(b_s.shape)

        def backward(t, carry):
            columns = pl.ds(pl.multiple_of(t * WIDE, WIDE), WIDE)
            total = dot_last(a_s[...].reshape(count, -1), gate_held[columns])
            total += dot_last(b_s[...].reshape(count, -1), up_held[columns])
            rows_s[:, :, columns] = total.astype(low).reshape(4, SLOTS, WIDE)
            return carry

        lax.fori_loop(0, width // WIDE, backward, 0)
        for copy in stores(n):
            copy.start()

    work = {3: (0,), 4: (1,), 5: (2,), 6: (3,), 7: (4, 5, 6, 7)}
    for event, (ar, j) in enumerate(FAR_FIRST[::-1]):
        zs = place.ranked(j)
        block = ar * 4 + zs
        for h in range(HALVES):
            part = pl.ds(h * half, half)
            window = held.at[block, part]
            if ar or j:
                remote(
                    window, window, leave.at[zs, 0, h], arrive.at[block, h], place.device("c")
                ).wait_recv()
            if ar:
                continue
            source = tok.at[part] if j == 0 else window
            onward = (
                (UP, zs, 0, (zs <= place.z) & (place.z < 3)),
                (DOWN, zs, 1, (zs >= place.z) & (place.z > 0)),
                ("near", 4 + zs, 2, None),
            )
            for axis, there, k, condition in onward:
                device = place.at(near, place.c) if axis == "near" else place.device(axis)
                copy = remote(
                    source, held.at[there, part], leave.at[zs, k, h], arrive.at[there, h], device
                )
                run(condition, copy.start)
                pending.append((condition, copy))
        if not ar and j == 0:
            keep.wait()
        pick(ar, zs)
        for n in work.get(event, ()):
            compute(n)
    for copy in stores(7):
        copy.wait()
    for copy in kept:
        copy.wait()
    for condition, copy in pending:
        run(condition, copy.wait_send)


def dispatch_expert(experts, shards, number, tok, sel, small, grads, picks, ids, w_gate, w_up, w_down):
    rows, width = tok.shape
    devices = experts * shards
    inside = w_gate.shape[2]
    space = pl.BlockSpec(memory_space=pl.ANY)
    vmem = pl.BlockSpec(memory_space=pltpu.VMEM)
    dma = pltpu.SemaphoreType.DMA
    low, f32 = jnp.bfloat16, jnp.float32

    def lots(columns):
        return jax.ShapeDtypeStruct((devices, SLOTS, columns), low)

    def some(columns):
        return pltpu.VMEM((4, SLOTS, columns), low)

    return pl.pallas_call(
        functools.partial(dispatch_expert_kernel, (experts, shards)),
        out_shape=[
            jax.ShapeDtypeStruct((devices,) + small.shape, f32),
            lots(width), lots(width), lots(width), lots(inside), lots(inside), lots(inside), lots(width),
            jax.ShapeDtypeStruct((devices, 8, rows), f32),
        ],
        in_specs=[space, vmem, space, space, vmem, vmem, space, space, space],
        out_specs=[space] * 8 + [vmem],
        scratch_shapes=[
            pltpu.VMEM((8, rows, width), low),
            pltpu.VMEM((8, 3 * SLOTS, width), low),
            pltpu.VMEM((devices, SLOTS, width), low),
            dma((8, HALVES)),
            dma((4, 3, HALVES)),
            dma((8, 3)),
            dma((devices,)),
            dma((3,)),
            dma((devices,)),
            dma((devices,)),
            pltpu.VMEM((devices,) + small.shape, f32),
            dma((3,)),
            pltpu.VMEM(w_gate.shape[1:], low),
            pltpu.VMEM(w_up.shape[1:], low),
            pltpu.VMEM(w_down.shape[1:], low),
            pltpu.VMEM((2, 4, SLOTS, width), low),
            dma((2, 2)),
            some(width), some(width), some(inside), some(inside), some(inside), some(width),
            pltpu.VMEM((4 * SLOTS, inside), f32),
            pltpu.VMEM((4 * SLOTS, inside), f32),
            dma((6, 2)),
            dma((8, 2)),
        ],
        compiler_params=pltpu.CompilerParams(
            collective_id=number, has_side_effects=True, vmem_limit_bytes=62 * 2**20
        ),
        name="dispatch_expert",
    )(tok, sel, small, grads, picks, ids, w_gate, w_up, w_down)


def local(
    layer_input,
    doc_ids,
    expert_ids,
    w_query,
    w_key,
    w_value,
    w_out,
    w_router,
    gain_attn,
    gain_ffn,
    gain_query,
    gain_key,
    w_gate,
    w_up,
    w_down,
    grad_output,
):
    single_float = jnp.float32
    brain_float_half = jnp.bfloat16
    row_count = layer_input.shape[1]
    width = layer_input.shape[2]
    length_total = doc_ids.shape[1]
    query_groups = QUERY_HEADS // KEY_VALUE_HEADS
    scale = HEAD_SIZE ** (-0.5)
    experts = w_router.shape[1]
    capacity = max(2, 6 * row_count * TOP // (5 * experts))
    pairs = row_count * TOP
    (
        full_query,
        gathered_key,
        full_value,
        full_out,
        full_router,
        gain_one,
        gain_two,
        gain_q,
        key_gain_vector,
    ) = (
        lax.all_gather(w_query, FSDP, axis=0, tiled=True),
        lax.all_gather(w_key, FSDP, axis=0, tiled=True),
        lax.all_gather(w_value, FSDP, axis=0, tiled=True),
        lax.all_gather(w_out, FSDP, axis=0, tiled=True),
        lax.all_gather(w_router, FSDP, axis=0, tiled=True),
        lax.all_gather(gain_attn, FSDP, axis=0, tiled=True),
        lax.all_gather(gain_ffn, FSDP, axis=0, tiled=True),
        lax.all_gather(gain_query, FSDP, axis=0, tiled=True),
        lax.all_gather(gain_key, FSDP, axis=0, tiled=True),
    )
    gain_one = gain_one.astype(single_float)
    gain_two = gain_two.astype(single_float)
    gain_q = gain_q.astype(single_float)
    key_gain_vector = key_gain_vector.astype(single_float)
    inputs = layer_input[0].astype(single_float)
    offset = lax.axis_index(EXPERT) * row_count
    own_pos = offset + jnp.arange(row_count, dtype=jnp.int32)
    all_pos = jnp.arange(length_total, dtype=jnp.int32)
    seq_ids = doc_ids[0]
    own_ids = lax.dynamic_slice_in_dim(seq_ids, offset, row_count)
    allowed = (own_ids[:, None] == seq_ids[None, :]) & (own_pos[:, None] >= all_pos[None, :])
    cosine_table, sine_table = angles(own_pos)
    cosine_table = cosine_table[:, None, :]
    sine_table = sine_table[:, None, :]
    scale_one = inverse_rms(inputs)
    normalized_input = (inputs * scale_one * gain_one).astype(brain_float_half)
    query_raw = jnp.dot(normalized_input, full_query, preferred_element_type=single_float).reshape(
        row_count, QUERY_HEADS, HEAD_SIZE
    )
    key_unnormalized = jnp.dot(
        normalized_input, gathered_key, preferred_element_type=single_float
    ).reshape(row_count, KEY_VALUE_HEADS, HEAD_SIZE)
    value_low = jnp.dot(normalized_input, full_value, preferred_element_type=single_float).astype(
        brain_float_half
    )
    query_scale = inverse_rms(query_raw)
    key_norm_scale = inverse_rms(key_unnormalized)
    query_rot = (
        apply_rotary(query_raw * query_scale * gain_q, cosine_table, sine_table)
        .astype(brain_float_half)
        .reshape(row_count, KEY_VALUE_HEADS, query_groups, HEAD_SIZE)
    )
    key_rotated = apply_rotary(
        key_unnormalized * key_norm_scale * key_gain_vector, cosine_table, sine_table
    ).astype(brain_float_half)
    key_gathered_rows, value_gathered_rows = (
        lax.all_gather(
            key_rotated.reshape(row_count, KEY_VALUE_HEADS * HEAD_SIZE),
            EXPERT,
            axis=0,
            tiled=True,
        ),
        lax.all_gather(value_low, EXPERT, axis=0, tiled=True),
    )
    key_gathered_rows = key_gathered_rows.reshape(length_total, KEY_VALUE_HEADS, HEAD_SIZE)
    value_gathered_rows = value_gathered_rows.reshape(length_total, KEY_VALUE_HEADS, HEAD_SIZE)

    def masked_scores():
        raw = (
            jnp.einsum(
                "tkgd,skd->kgts", query_rot, key_gathered_rows, preferred_element_type=single_float
            )
            * scale
        )
        return jnp.where(allowed, raw, -1e30)

    scores = masked_scores()
    peak = jnp.max(scores, -1, keepdims=True)
    shifted = jnp.exp(scores - peak)
    totals = jnp.sum(shifted, -1, keepdims=True)
    weights_low = (shifted / totals).astype(brain_float_half)
    log_total = peak + jnp.log(totals)
    mixed = (
        jnp.einsum(
            "kgts,skd->tkgd", weights_low, value_gathered_rows, preferred_element_type=single_float
        )
        .reshape(row_count, QUERY_HEADS * HEAD_SIZE)
        .astype(brain_float_half)
    )
    hidden = inputs + jnp.dot(mixed, full_out, preferred_element_type=single_float)
    scale_two = inverse_rms(hidden)
    normed_two = (hidden * scale_two * gain_two).astype(brain_float_half)
    logits = jnp.dot(normed_two, full_router, preferred_element_type=single_float)
    selector = (expert_ids[0][:, :, None] == jnp.arange(experts, dtype=jnp.int32)).astype(
        single_float
    )
    chosen = jnp.einsum("tke,te->tk", selector, logits, precision=HIGHEST)
    gates = jax.nn.softmax(chosen, -1)
    flat_routes = expert_ids[0].reshape(pairs)
    hits = (flat_routes[:, None] == jnp.arange(experts, dtype=jnp.int32)).astype(jnp.int32)
    before = jnp.cumsum(hits, 0) - hits
    ranks = jnp.sum(before * hits, 1)
    slot_index = flat_routes * capacity + ranks
    owner_rows = jnp.arange(pairs, dtype=jnp.int32) // TOP
    outgoing = (
        jnp.zeros((experts * capacity, width), brain_float_half)
        .at[slot_index]
        .set(normed_two[owner_rows])
    )
    arrived = lax.all_to_all(
        outgoing.reshape(experts, capacity, width),
        (EXPERT, FSDP),
        split_axis=0,
        concat_axis=0,
        tiled=True,
    ).reshape(experts * capacity, width)
    gate_pre = jnp.dot(arrived, w_gate[0], preferred_element_type=single_float)
    up_pre = jnp.dot(arrived, w_up[0], preferred_element_type=single_float)
    activated = jax.nn.silu(gate_pre)
    inner = (activated * up_pre).astype(brain_float_half)
    result = jnp.dot(inner, w_down[0], preferred_element_type=single_float).astype(brain_float_half)
    returned = lax.all_to_all(
        result.reshape(experts, capacity, width),
        (EXPERT, FSDP),
        split_axis=0,
        concat_axis=0,
        tiled=True,
    ).reshape(experts * capacity, width)
    expert_rows = returned[slot_index].astype(single_float).reshape(row_count, TOP, width)
    output = hidden + jnp.einsum("tk,tkd->td", gates, expert_rows, precision=HIGHEST)
    grad_top = grad_output[0]
    grad_gates = jnp.einsum("tkd,td->tk", expert_rows, grad_top, precision=HIGHEST)
    grad_pairs = (
        (gates[:, :, None] * grad_top[:, None, :]).astype(brain_float_half).reshape(pairs, width)
    )
    grad_send = (
        jnp.zeros((experts * capacity, width), brain_float_half).at[slot_index].set(grad_pairs)
    )
    grad_arrived = lax.all_to_all(
        grad_send.reshape(experts, capacity, width),
        (EXPERT, FSDP),
        split_axis=0,
        concat_axis=0,
        tiled=True,
    ).reshape(experts * capacity, width)
    grad_down = jnp.einsum("rf,rd->fd", inner, grad_arrived, preferred_element_type=single_float)
    grad_inner = jnp.einsum(
        "rd,fd->rf", grad_arrived, w_down[0], preferred_element_type=single_float
    )
    sigmoid_gate = jax.nn.sigmoid(gate_pre)
    slope = sigmoid_gate * (1.0 + gate_pre * (1.0 - sigmoid_gate))
    grad_gate_pre = (grad_inner * up_pre * slope).astype(brain_float_half)
    grad_up_pre = (grad_inner * activated).astype(brain_float_half)
    grad_gate_w = jnp.einsum(
        "rd,rf->df", arrived, grad_gate_pre, preferred_element_type=single_float
    )
    grad_up_w = jnp.einsum("rd,rf->df", arrived, grad_up_pre, preferred_element_type=single_float)
    grad_rows = (
        jnp.einsum("rf,df->rd", grad_gate_pre, w_gate[0], preferred_element_type=single_float)
        + jnp.einsum("rf,df->rd", grad_up_pre, w_up[0], preferred_element_type=single_float)
    ).astype(brain_float_half)
    grad_back = lax.all_to_all(
        grad_rows.reshape(experts, capacity, width),
        (EXPERT, FSDP),
        split_axis=0,
        concat_axis=0,
        tiled=True,
    ).reshape(experts * capacity, width)
    grad_normed_two = jnp.sum(
        grad_back[slot_index].astype(single_float).reshape(row_count, TOP, width), 1
    )
    grad_chosen = gates * (grad_gates - jnp.sum(gates * grad_gates, -1, keepdims=True))
    grad_logits = jnp.einsum("tke,tk->te", selector, grad_chosen, precision=HIGHEST).astype(
        brain_float_half
    )
    grad_normed_two = grad_normed_two + jnp.einsum(
        "te,de->td", grad_logits, full_router, preferred_element_type=single_float
    )
    grad_router = jnp.einsum(
        "td,te->de", normed_two, grad_logits, preferred_element_type=single_float
    )
    grad_gain_two = jnp.sum(grad_normed_two * hidden * scale_two, 0)
    grad_hidden = grad_top + norm_backward(grad_normed_two, hidden, scale_two, gain_two)
    grad_branch = grad_hidden.astype(brain_float_half)
    grad_out_w = jnp.einsum("tq,td->qd", mixed, grad_branch, preferred_element_type=single_float)
    grad_mixed = (
        jnp.einsum("td,qd->tq", grad_branch, full_out, preferred_element_type=single_float)
        .astype(brain_float_half)
        .reshape(row_count, KEY_VALUE_HEADS, query_groups, HEAD_SIZE)
    )
    again = masked_scores()
    weights = jnp.exp(again - log_total)
    weights_again = weights.astype(brain_float_half)
    grad_weights = jnp.einsum(
        "tkgd,skd->kgts", grad_mixed, value_gathered_rows, preferred_element_type=single_float
    )
    spread = jnp.sum(weights * grad_weights, -1, keepdims=True)
    grad_scores = (weights * (grad_weights - spread)).astype(brain_float_half)
    grad_query_rot = (
        jnp.einsum(
            "kgts,skd->tkgd", grad_scores, key_gathered_rows, preferred_element_type=single_float
        )
        * scale
    ).reshape(row_count, QUERY_HEADS, HEAD_SIZE)
    grad_key_all = (
        jnp.einsum("kgts,tkgd->skd", grad_scores, query_rot, preferred_element_type=single_float)
        * scale
    ).reshape(length_total, KEY_VALUE_HEADS * HEAD_SIZE)
    grad_value_all = jnp.einsum(
        "kgts,tkgd->skd", weights_again, grad_mixed, preferred_element_type=single_float
    ).reshape(length_total, KEY_VALUE_HEADS * HEAD_SIZE)
    gradient_key_rotated, grad_value = (
        lax.psum_scatter(
            grad_key_all.astype(jnp.bfloat16), EXPERT, scatter_dimension=0, tiled=True
        ).astype(jnp.float32),
        lax.psum_scatter(
            grad_value_all.astype(jnp.bfloat16), EXPERT, scatter_dimension=0, tiled=True
        ).astype(jnp.float32),
    )
    gradient_key_rotated = gradient_key_rotated.reshape(row_count, KEY_VALUE_HEADS, HEAD_SIZE)
    grad_query_unit = unrotate(grad_query_rot, cosine_table, sine_table)
    gradient_key_normalized = unrotate(gradient_key_rotated, cosine_table, sine_table)
    grad_gain_q = jnp.sum(grad_query_unit * query_raw * query_scale, (0, 1))
    grad_gain_k = jnp.sum(gradient_key_normalized * key_unnormalized * key_norm_scale, (0, 1))
    grad_query = (
        norm_backward(grad_query_unit, query_raw, query_scale, gain_q)
        .reshape(row_count, QUERY_HEADS * HEAD_SIZE)
        .astype(brain_float_half)
    )
    grad_key = (
        norm_backward(gradient_key_normalized, key_unnormalized, key_norm_scale, key_gain_vector)
        .reshape(row_count, KEY_VALUE_HEADS * HEAD_SIZE)
        .astype(brain_float_half)
    )
    grad_value_low = grad_value.astype(brain_float_half)
    grad_query_w = jnp.einsum(
        "td,tq->dq", normalized_input, grad_query, preferred_element_type=single_float
    )
    grad_key_w = jnp.einsum(
        "td,tq->dq", normalized_input, grad_key, preferred_element_type=single_float
    )
    grad_value_w = jnp.einsum(
        "td,tq->dq", normalized_input, grad_value_low, preferred_element_type=single_float
    )
    grad_normed = (
        jnp.einsum("tq,dq->td", grad_query, full_query, preferred_element_type=single_float)
        + jnp.einsum("tq,dq->td", grad_key, gathered_key, preferred_element_type=single_float)
        + jnp.einsum("tq,dq->td", grad_value_low, full_value, preferred_element_type=single_float)
    )
    grad_gain_one = jnp.sum(grad_normed * inputs * scale_one, 0)
    grad_inputs = grad_hidden + norm_backward(grad_normed, inputs, scale_one, gain_one)
    local_grads = (
        grad_query_w,
        grad_key_w,
        grad_value_w,
        grad_out_w,
        grad_router,
        grad_gain_one,
        grad_gain_two,
        grad_gain_q,
        grad_gain_k,
    )
    shards = (
        lax.psum_scatter(
            local_grads[0].astype(jnp.bfloat16), FSDP, scatter_dimension=0, tiled=True
        ).astype(jnp.float32),
        lax.psum_scatter(
            local_grads[1].astype(jnp.bfloat16), FSDP, scatter_dimension=0, tiled=True
        ).astype(jnp.float32),
        lax.psum_scatter(
            local_grads[2].astype(jnp.bfloat16), FSDP, scatter_dimension=0, tiled=True
        ).astype(jnp.float32),
        lax.psum_scatter(
            local_grads[3].astype(jnp.bfloat16), FSDP, scatter_dimension=0, tiled=True
        ).astype(jnp.float32),
        lax.psum_scatter(
            local_grads[4].astype(jnp.bfloat16), FSDP, scatter_dimension=0, tiled=True
        ).astype(jnp.float32),
        lax.psum_scatter(
            local_grads[5].astype(jnp.bfloat16), FSDP, scatter_dimension=0, tiled=True
        ).astype(jnp.float32),
        lax.psum_scatter(
            local_grads[6].astype(jnp.bfloat16), FSDP, scatter_dimension=0, tiled=True
        ).astype(jnp.float32),
        lax.psum_scatter(
            local_grads[7].astype(jnp.bfloat16), FSDP, scatter_dimension=0, tiled=True
        ).astype(jnp.float32),
        lax.psum_scatter(
            local_grads[8].astype(jnp.bfloat16), FSDP, scatter_dimension=0, tiled=True
        ).astype(jnp.float32),
    )
    shards = (
        lax.psum(shards[0].astype(jnp.bfloat16), EXPERT).astype(jnp.float32),
        lax.psum(shards[1].astype(jnp.bfloat16), EXPERT).astype(jnp.float32),
        lax.psum(shards[2].astype(jnp.bfloat16), EXPERT).astype(jnp.float32),
        lax.psum(shards[3].astype(jnp.bfloat16), EXPERT).astype(jnp.float32),
        lax.psum(shards[4].astype(jnp.bfloat16), EXPERT).astype(jnp.float32),
        lax.psum(shards[5].astype(jnp.bfloat16), EXPERT).astype(jnp.float32),
        lax.psum(shards[6].astype(jnp.bfloat16), EXPERT).astype(jnp.float32),
        lax.psum(shards[7].astype(jnp.bfloat16), EXPERT).astype(jnp.float32),
        lax.psum(shards[8].astype(jnp.bfloat16), EXPERT).astype(jnp.float32),
    )
    return (
        output[None],
        grad_inputs[None],
        shards[0],
        shards[1],
        shards[2],
        shards[3],
        shards[4],
        shards[5],
        shards[6],
        shards[7],
        shards[8],
        grad_gate_w[None],
        grad_up_w[None],
        grad_down[None],
    )


def angle_tables(length):
    power = -(np.arange(HEAD_SIZE // 2, dtype=np.float32) * np.float32(2.0)) / np.float32(HEAD_SIZE)
    freq = np.power(np.float32(THETA), power).astype(np.float32)
    turns = np.arange(length, dtype=np.float32)[:, None] * freq[None, :]
    turns = np.concatenate([turns, turns], -1)
    return jnp.asarray(np.cos(turns)), jnp.asarray(np.sin(turns))


def packed(pieces, lead, rows):
    flat = jnp.concatenate([piece.reshape(lead, -1) for piece in pieces], 1)
    flat = jnp.pad(flat, ((0, 0), (0, rows * 128 - flat.shape[1])))
    return flat.reshape(lead, rows, 128)


def local_staged(
    layer_input,
    doc_ids,
    expert_ids,
    w_query,
    w_key,
    w_value,
    w_out,
    w_router,
    gain_attn,
    gain_ffn,
    gain_query,
    gain_key,
    w_gate,
    w_up,
    w_down,
    grad_output,
):
    f32 = jnp.float32
    low = jnp.bfloat16
    rows, width = layer_input.shape[1:]
    length = doc_ids.shape[1]
    depth = w_router.shape[0]
    groups, shards = lax.axis_size(EXPERT), lax.axis_size(FSDP)
    experts = w_router.shape[1]
    heads = QUERY_HEADS // groups
    span = heads * HEAD_SIZE
    mine = lax.axis_index(EXPERT)

    def columns(weight, count):
        return lax.dynamic_slice_in_dim(weight, mine * count, count, 1)

    flat = jnp.concatenate(
        [columns(w_query, span), columns(w_key, HEAD_SIZE), columns(w_value, HEAD_SIZE)], 1
    )
    pack = packed([w_router, gain_attn, gain_ffn, gain_query, gain_key], 1, 80)[0]
    w_qkv, w_mix, tokens, pack_all, ids_all, mine_picks, pick, spread, grad_top_low = gather(
        groups,
        shards,
        5,
        flat,
        w_out,
        layer_input[0],
        pack,
        expert_ids[0].T,
        grad_output[0],
    )
    w_qkv = w_qkv.reshape(width, span + 2 * HEAD_SIZE)
    w_mix = w_mix.reshape(span, width)
    tokens = tokens.reshape(length, width)
    pack_all = pack_all.reshape(shards, -1)
    at = depth * experts
    full_router = pack_all[:, :at].reshape(width, experts)
    gain_one = pack_all[:, at : at + depth].reshape(width).astype(f32)
    gain_two = pack_all[:, at + depth : at + 2 * depth].reshape(width).astype(f32)
    at += 2 * depth
    small = HEAD_SIZE // shards
    gain_q = pack_all[:, at : at + small].reshape(HEAD_SIZE).astype(f32)
    gain_k = pack_all[:, at + small : at + 2 * small].reshape(HEAD_SIZE).astype(f32)
    grad_top = grad_output[0]
    ids_column, ids_row = doc_ids[0][:, None], doc_ids[0][None, :]
    cosine, sine = angle_tables(length)
    gain_q, gain_k = gain_q[None], gain_k[None]
    attend = attention(
        tokens, w_qkv, gain_one[None], gain_q, gain_k, cosine, sine, ids_column, ids_row, heads
    )
    grads_in, normed_one, raw, query_rot, key_rot, value, mixed, inverses = dispatch(
        groups, shards, 1, grad_top_low, pick, extra=attend
    )
    inputs = layer_input[0].astype(f32)
    hidden = inputs + branch_scatter(8, mixed, w_mix)
    scale_two = inverse_rms(hidden)
    normed_two = (hidden * scale_two * gain_two).astype(low)
    logits = jnp.dot(normed_two, full_router, preferred_element_type=f32)
    selector = (expert_ids[0][:, :, None] == jnp.arange(experts, dtype=jnp.int32)).astype(f32)
    gates = jax.nn.softmax(jnp.sum(selector * logits[:, None, :], -1), -1)
    _, arrived, weighted, grad_arrived, inner, grad_a, grad_b, grad_rows, gate_grads = dispatch_expert(
        groups, shards, 2, normed_two, pick, gates.T, grads_in, mine_picks, ids_all, w_gate, w_up, w_down
    )

    def flat_rows(blocks):
        return blocks.reshape(-1, blocks.shape[-1])

    grad_normed_two, gates_back, grad_gate_w, grad_up_w, grad_down = combine(
        groups,
        shards,
        3,
        grad_rows,
        spread,
        gate_grads,
        weight_grads(*(flat_rows(a) for a in (arrived, grad_arrived, inner, grad_a, grad_b))),
    )
    grad_gates = jnp.sum(selector * gates_back[:, 0].T[:, None, :], -1)
    grad_chosen = gates * (grad_gates - jnp.sum(gates * grad_gates, -1, keepdims=True))
    grad_logits = jnp.sum(selector * grad_chosen[:, :, None], 1).astype(low)
    grad_normed_two = grad_normed_two + jnp.einsum(
        "te,de->td", grad_logits, full_router, preferred_element_type=f32
    )
    grad_router = jnp.einsum("td,te->de", normed_two, grad_logits, preferred_element_type=f32)
    grad_gain_two = jnp.sum(grad_normed_two * hidden * scale_two, 0)
    grad_hidden = grad_top + norm_backward(grad_normed_two, hidden, scale_two, gain_two)
    back = attention_back(
        query_rot, key_rot, value, raw, mixed, grad_hidden.astype(low), w_mix, normed_one, tokens, w_qkv,
        inverses, ids_column, ids_row, gain_q, gain_k, cosine, sine,
    )
    combined, gain_grads, grad_mix, grad_qkv, grad_normed_one, grad_gain_one = combine(
        groups, shards, 4, weighted, spread, extra=back
    )
    output = hidden + combined
    sums = [grad_router, grad_gain_one, grad_gain_two, gain_grads[0], gain_grads[1]]
    sums = packed(sums, shards, 16 * (span + 2 * HEAD_SIZE) // 128)
    sums = sums.reshape(shards, 16, -1).astype(low)
    query_sum, key_sum, value_sum, tall_sum, pack_sum, grad_normed_one = reduce(
        groups,
        shards,
        6,
        grad_qkv.reshape(shards, depth, -1),
        grad_mix.reshape(2, -1, width),
        sums,
        grad_normed_one.reshape(groups, rows, width),
    )
    pack_sum = jnp.sum(pack_sum.astype(f32), 0).reshape(-1)
    scale_own = inverse_rms(inputs)
    grad_inputs = grad_hidden + norm_backward(grad_normed_one, inputs, scale_own, gain_one)
    at = depth * experts
    return (
        output[None],
        grad_inputs[None],
        query_sum.astype(f32),
        key_sum.astype(f32),
        value_sum.astype(f32),
        tall_sum.astype(f32),
        pack_sum[:at].reshape(depth, experts),
        pack_sum[at : at + depth],
        pack_sum[at + depth : at + 2 * depth],
        pack_sum[at + 2 * depth : at + 2 * depth + small],
        pack_sum[at + 2 * depth + small : at + 2 * depth + 2 * small],
        grad_gate_w[None],
        grad_up_w[None],
        grad_down[None],
    )


def solution(mesh):
    in_specs = (
        P(FSDP, EXPERT, None),
        P(FSDP, None),
        P(FSDP, EXPERT, None),
        P(FSDP, None),
        P(FSDP, None),
        P(FSDP, None),
        P(FSDP, None),
        P(FSDP, None),
        P(FSDP),
        P(FSDP),
        P(FSDP),
        P(FSDP),
        P((EXPERT, FSDP), None, None),
        P((EXPERT, FSDP), None, None),
        P((EXPERT, FSDP), None, None),
        P(FSDP, EXPERT, None),
    )
    out_specs = (
        P(FSDP, EXPERT, None),
        P(FSDP, EXPERT, None),
        P(FSDP, None),
        P(FSDP, None),
        P(FSDP, None),
        P(FSDP, None),
        P(FSDP, None),
        P(FSDP),
        P(FSDP),
        P(FSDP),
        P(FSDP),
        P((EXPERT, FSDP), None, None),
        P((EXPERT, FSDP), None, None),
        P((EXPERT, FSDP), None, None),
    )
    staged = mesh.shape[EXPERT] == 4 and mesh.shape[FSDP] == 8
    return jax.shard_map(local_staged if staged else local, mesh=mesh, in_specs=in_specs, out_specs=out_specs, check_vma=False)
```

```python
import functools

import jax
import jax.numpy as jnp
import numpy as np
from jax import lax
from jax.experimental import pallas as pl
from jax.experimental.pallas import tpu as pltpu
from jax.sharding import PartitionSpec as P

EXPERT = "expert"
FSDP = "fsdp"
UP, DOWN, ABOVE, BELOW = "up", "down", "above", "below"
QUERY_HEADS = 32
KEY_VALUE_HEADS = 4
HEAD_SIZE = 128
TOP = 8


EPS = 1e-06
THETA = 1000000.0
HIGHEST = lax.Precision.HIGHEST


def angles(positions):
    freq = THETA ** (-(jnp.arange(HEAD_SIZE // 2, dtype=jnp.float32) * 2.0) / HEAD_SIZE)
    turn = positions.astype(jnp.float32)[:, None] * freq[None, :]
    turn = jnp.concatenate([turn, turn], -1)
    return (jnp.cos(turn), jnp.sin(turn))


def apply_rotary(value_rows_local, cosine_table, sine_table):
    half = value_rows_local.shape[-1] // 2
    turned = jnp.concatenate([-value_rows_local[..., half:], value_rows_local[..., :half]], -1)
    return value_rows_local * cosine_table + turned * sine_table


def unrotate(grads, cosine_table, sine_table):
    half = grads.shape[-1] // 2
    scaled = grads * sine_table
    turned = jnp.concatenate([-scaled[..., half:], scaled[..., :half]], -1)
    return grads * cosine_table - turned


def inverse_rms(value_rows_local):
    return lax.rsqrt(jnp.mean(value_rows_local * value_rows_local, -1, keepdims=True) + EPS)


def norm_backward(grad, value_rows_local, inverse, gain):
    scaled = grad * gain
    return inverse * scaled - inverse * inverse * inverse * value_rows_local * jnp.mean(
        scaled * value_rows_local, -1, keepdims=True
    )


MESH = pl.DeviceIdType.MESH
SLOTS = 80
TILE = 512
FAR_FIRST = ((1, 3), (1, 2), (0, 3), (1, 1), (0, 2), (0, 1), (1, 0), (0, 0))
BACK = FAR_FIRST
AHEAD = 2
HALVES = 2


class Place:
    def __init__(self):
        self.e = lax.axis_index(EXPERT)
        self.f = lax.axis_index(FSDP)
        self.x, self.c = self.e // 2, self.e % 2
        self.z, self.y = self.f // 2, self.f % 2

    def device(self, axis):
        if axis == "c":
            return (self.x * 2 + 1 - self.c, self.f)
        if axis == "x":
            return ((1 - self.x) * 2 + self.c, self.f)
        if axis == "y":
            return (self.e, self.z * 2 + 1 - self.y)
        if axis == UP:
            return (self.e, jnp.minimum(self.z + 1, 3) * 2 + self.y)
        return (self.e, jnp.maximum(self.z - 1, 0) * 2 + self.y)

    def ranked(self, j):
        inner = (1, 0, 2, 3)[j]
        end = (self.z == 0) | (self.z == 3)
        low = jnp.where(end, j, inner)
        return jnp.where(self.z < 2, low, 3 - low)

    def line(self):
        x, y, even = self.x, self.y, self.c == 0
        near = (jnp.where(even, 1 - x, x), jnp.where(even, y, 1 - y))
        far = (jnp.where(even, x, 1 - x), jnp.where(even, 1 - y, y))
        return near, far

    def at(self, chip, core):
        return (chip[0] * 2 + core, self.z * 2 + chip[1])


def block_number(chip, core, ar, zs):
    x, y = chip
    xs = jnp.where(core == 0, 1 - x, x) if ar else x
    ys = jnp.where(core == 0, y, 1 - y) if ar else y
    return (xs * 2 + core) * 8 + zs * 2 + ys


def greet(place):
    barrier = pltpu.get_barrier_semaphore()
    beside = [place.device("c")]
    for chip in ((1 - place.x, place.y), (place.x, 1 - place.y)):
        beside += [place.at(chip, 0), place.at(chip, 1)]
    for device in beside:
        pl.semaphore_signal(barrier, 1, device_id=device, device_id_type=MESH)

    @pl.when(place.z < 3)
    def _():
        pl.semaphore_signal(barrier, 1, device_id=place.device(UP), device_id_type=MESH)

    @pl.when(place.z > 0)
    def _():
        pl.semaphore_signal(barrier, 1, device_id=place.device(DOWN), device_id_type=MESH)

    inner = (place.z > 0) & (place.z < 3)
    pl.semaphore_wait(barrier, len(beside) + jnp.where(inner, 2, 1))


def greet_all(place, experts, shards):
    barrier = pltpu.get_barrier_semaphore()
    count = experts * shards

    def one(i, carry):
        target = lax.rem(place.e * shards + place.f + i, count)
        pl.semaphore_signal(
            barrier, 1, device_id=(target // shards, lax.rem(target, shards)), device_id_type=MESH
        )
        return carry

    lax.fori_loop(1, count, one, 0)
    pl.semaphore_wait(barrier, count - 1)


def onward(path, j, xr, yr):
    differs = {"z": j > 0, "x": xr > 0, "y": yr > 0}
    last = -1
    for i, axis in enumerate(path):
        if differs[axis]:
            last = i
    out = []
    if last >= 0 and path[last] == "z":
        out.append("z+")
    for axis in path[last + 1 :]:
        out.append("z*" if axis == "z" else axis)
    return out


def links(place, path, j, xr, yr, zs):
    out = []
    for axis in onward(path, j, xr, yr):
        if axis == "z+":
            out.append((UP, (zs < place.z) & (place.z < 3)))
            out.append((DOWN, (zs > place.z) & (place.z > 0)))
        elif axis == "z*":
            out.append((UP, place.z < 3))
            out.append((DOWN, place.z > 0))
        else:
            out.append((axis, None))
    return out


def run(condition, action):
    if condition is None:
        action()
    else:
        pl.when(condition)(action)


LINK = {"x": 0, "y": 1, UP: 2, DOWN: 3}


def remote(src, dst, send_sem, recv_sem, device):
    return pltpu.make_async_remote_copy(
        src_ref=src,
        dst_ref=dst,
        send_sem=send_sem,
        recv_sem=recv_sem,
        device_id=device,
        device_id_type=MESH,
    )


class Side:
    def __init__(self, steps, events):
        self.steps, self.events = list(steps), events
        self.total, self.seen = len(self.steps), 0

    def event(self):
        self.seen += 1
        left = self.total - self.total * min(self.seen, self.events) // self.events
        while len(self.steps) > left:
            self.steps.pop(0)()


class Extra:
    def __init__(self, operands=(), in_specs=(), outs=(), out_specs=(), scratch=(), steps=None):
        self.operands, self.in_specs = list(operands), list(in_specs)
        self.outs, self.out_specs, self.scratch = list(outs), list(out_specs), list(scratch)
        self.steps = steps if steps is not None else lambda *refs: []


def split(refs, counts):
    out = []
    for count in counts:
        out.append(refs[:count])
        refs = refs[count:]
    return out


def exchange_small(place, dims, src_of, dst, sems_out, sems_in, sem):
    experts, shards = dims
    count = experts * shards
    me = place.e * shards + place.f
    keep = pltpu.make_async_copy(src_of(me), dst.at[me], sem)
    keep.start()

    def copy(i, sending):
        other = lax.rem(me + i, count)
        source = me if sending else other
        device = (other // shards, lax.rem(other, shards))
        return remote(src_of(other), dst.at[source], sems_out.at[i], sems_in.at[source], device)

    def start(i, carry):
        copy(i, True).start()
        return carry

    def finish(i, carry):
        done = copy(i, False)
        done.wait_send()
        done.wait_recv()
        return carry

    lax.fori_loop(1, count, start, 0)

    def end():
        keep.wait()
        lax.fori_loop(1, count, finish, 0)

    return end


def dispatch_kernel(dims, has_small, extra, *refs):
    counts = (
        2 + has_small, len(extra.operands), 1 + has_small, len(extra.outs), 7 + 3 * has_small,
        len(extra.scratch),
    )
    ins, more_in, outs, more_out, scratch, more_scratch = split(refs, counts)
    tok, sel = ins[:2]
    picked = outs[0]
    held, stage, arrive, leave, pick_out, pick_in, local = scratch[:7]
    place = Place()
    width = tok.shape[1]
    near, far = place.line()
    mine = (place.x, place.y)
    if has_small:
        greet_all(place, *dims)
        end_small = exchange_small(
            place, dims, lambda i: ins[2], outs[1], scratch[7], scratch[8], scratch[9].at[0]
        )
    else:
        greet(place)
    side = Side(extra.steps(*more_in, *more_out, *more_scratch), 8)
    keep = pltpu.make_async_copy(tok, held.at[place.z], local.at[8])
    keep.start()
    pending = []
    finish = []
    targets = (place.device("c"), place.at(far, place.c), place.at(far, 1 - place.c))

    def pick(ar, zs):
        block = ar * 4 + zs
        number = block_number(mine, place.c, ar, zs)

        def tile(i, carry):
            columns = pl.ds(pl.multiple_of(i * 512, 512), 512)
            stage[block, :, columns] = jnp.dot(
                sel[block], held[block, :, columns], preferred_element_type=jnp.float32
            ).astype(jnp.bfloat16)
            return carry

        lax.fori_loop(0, width // 512, tile, 0)
        for k in (2, 1, 0):
            away = remote(
                stage.at[block, pl.ds((k + 1) * SLOTS, SLOTS)], picked.at[number],
                pick_out.at[block, k], pick_in.at[number], targets[k],
            )
            away.start()
            finish.append(away)
        stay = pltpu.make_async_copy(
            stage.at[block, pl.ds(0, SLOTS)], picked.at[number], local.at[block]
        )
        stay.start()
        finish.append(stay)

    half = tok.shape[0] // HALVES
    for ar, j in FAR_FIRST[::-1]:
        zs = place.ranked(j)
        block = ar * 4 + zs
        for h in range(HALVES):
            part = pl.ds(h * half, half)
            window = held.at[block, part]
            if ar or j:
                remote(
                    window, window, leave.at[zs, 0, h], arrive.at[block, h], place.device("c")
                ).wait_recv()
            if ar:
                continue
            source = tok.at[part] if j == 0 else window
            onward = (
                (UP, zs, 0, (zs <= place.z) & (place.z < 3)),
                (DOWN, zs, 1, (zs >= place.z) & (place.z > 0)),
                ("near", 4 + zs, 2, None),
            )
            for axis, there, k, condition in onward:
                device = place.at(near, place.c) if axis == "near" else place.device(axis)
                copy = remote(
                    source, held.at[there, part], leave.at[zs, k, h], arrive.at[there, h], device
                )
                run(condition, copy.start)
                pending.append((condition, copy))
        if not ar and j == 0:
            keep.wait()
        pick(ar, zs)
        side.event()
    for condition, copy in pending:
        run(condition, copy.wait_send)

    def arrived(i, carry):
        xs, cs, ys = i // 16, i // 8 % 2, i % 2
        inside = (cs == place.c) & jnp.where(place.c == 0, ys == place.y, xs == place.x)

        @pl.when(~inside)
        def _():
            window = picked.at[i]
            remote(window, window, pick_out.at[0, 0], pick_in.at[i], place.device("c")).wait_recv()

        return carry

    lax.fori_loop(0, 32, arrived, 0)
    for k, copy in enumerate(finish):
        if k % 4 == 3:
            copy.wait()
        else:
            copy.wait_send()
    if has_small:
        end_small()


def dispatch(experts, shards, number, tok, sel, small=None, extra=None):
    rows, width = tok.shape
    devices = experts * shards
    extra = extra or Extra()
    space = pl.BlockSpec(memory_space=pl.ANY)
    vmem = pl.BlockSpec(memory_space=pltpu.VMEM)
    dma = pltpu.SemaphoreType.DMA
    has_small = int(small is not None)
    operands, in_specs = [tok, sel], [space, vmem]
    out_shape = [jax.ShapeDtypeStruct((devices, SLOTS, width), jnp.bfloat16)]
    scratch = [
        pltpu.VMEM((8, rows, width), jnp.bfloat16),
        pltpu.VMEM((8, 4 * SLOTS, width), jnp.bfloat16),
        dma((8, HALVES)),
        dma((4, 3, HALVES)),
        dma((8, 3)),
        dma((devices,)),
        dma((9,)),
    ]
    if has_small:
        operands.append(small)
        in_specs.append(space)
        out_shape.append(jax.ShapeDtypeStruct((devices,) + small.shape, small.dtype))
        scratch += [dma((devices,)), dma((devices,)), dma((1,))]
    return pl.pallas_call(
        functools.partial(dispatch_kernel, (experts, shards), has_small, extra),
        out_shape=out_shape + extra.outs,
        in_specs=in_specs + extra.in_specs,
        out_specs=[space] * len(out_shape) + extra.out_specs,
        scratch_shapes=scratch + extra.scratch,
        compiler_params=pltpu.CompilerParams(
            collective_id=number, has_side_effects=True, vmem_limit_bytes=60 * 2**20
        ),
        name="dispatch",
    )(*operands, *extra.operands)


def combine_kernel(dims, has_small, extra, *refs):
    counts = (
        2 + has_small, len(extra.operands), 1 + has_small, len(extra.outs), 10 + 3 * has_small,
        len(extra.scratch),
    )
    ins, more_in, outs, more_out, scratch, more_scratch = split(refs, counts)
    weighted, sel = ins[:2]
    total = outs[0]
    rows4, acc, beside, chain, rows_in, rows_out, beside_in, beside_out, chain_in, chain_out = scratch[:10]
    place = Place()
    width = total.shape[1]
    near, far = place.line()
    mine = (place.x, place.y)
    if has_small:
        greet_all(place, *dims)
        end_small = exchange_small(
            place, dims, lambda i: ins[2].at[i], outs[1], scratch[10], scratch[11], scratch[12].at[0]
        )
    else:
        greet(place)
    side = Side(extra.steps(*more_in, *more_out, *more_scratch), 8 * HALVES)
    other = 1 - place.c
    homes = ((mine, place.c), (mine, other), (far, place.c), (near, other))

    def row_copy(ar, zs, k):
        chip, core = homes[k]
        source = weighted.at[block_number(chip, core, ar, zs)]
        block = ar * 4 + zs
        window = rows4.at[block, pl.ds(k * SLOTS, SLOTS)]
        if k == 0:
            return pltpu.make_async_copy(source, window, rows_in.at[block, 0])
        return remote(
            source, window, rows_out.at[block, k - 1], rows_in.at[block, k], place.at(chip, core)
        )

    def send_rows(i):
        ar, j = BACK[i]
        for k in (2, 3, 1, 0):
            row_copy(ar, place.ranked(j), k).start()

    for i in range(AHEAD):
        send_rows(i)
    pending = []
    half = total.shape[0] // HALVES
    for i, (ar, j) in enumerate(BACK):
        zs = place.ranked(j)
        block = ar * 4 + zs
        for k in range(4):
            copy = row_copy(ar, zs, k)
            if k == 0:
                copy.wait()
            else:
                copy.wait_recv()
                copy.wait_send()
        if i + AHEAD < 8:
            send_rows(i + AHEAD)
        last = not ar and j == 0
        above = (zs <= place.z) & (place.z < 3)
        below = (zs >= place.z) & (place.z > 0)
        below_slot = jnp.where(zs == place.z, 4, zs)
        for h in range(HALVES):
            part = pl.ds(h * half, half)
            if not ar:
                window = beside.at[zs, part]
                remote(
                    window, window, beside_out.at[zs, h], beside_in.at[zs, h], place.device("c")
                ).wait_recv()
                for condition, slot in ((above, zs), (below, below_slot)):
                    window = chain.at[slot, part]
                    got = remote(
                        window, window, chain_out.at[0, h], chain_in.at[slot, h], place.device("c")
                    )
                    run(condition, got.wait_recv)

            def tile(t, carry):
                columns = pl.ds(pl.multiple_of(t * 512, 512), 512)
                dense = jnp.dot(
                    sel[block, part], rows4[block, :, columns], preferred_element_type=jnp.float32
                )
                if not ar:
                    dense = dense + beside[zs, part, columns].astype(jnp.float32)
                if last:
                    total[part, columns] = dense
                else:
                    acc[block, part, columns] = dense.astype(jnp.bfloat16)
                return carry

            lax.fori_loop(0, width // 512, tile, 0)
            if not ar:

                def add(slot):
                    def step(t, carry):
                        here = pl.ds(pl.multiple_of(h * half + t * 16, 16), 16)
                        more = chain[slot, here].astype(jnp.float32)
                        if last:
                            total[here] += more
                        else:
                            acc[block, here] = (acc[block, here].astype(jnp.float32) + more).astype(
                                jnp.bfloat16
                            )
                        return carry

                    lax.fori_loop(0, half // 16, step, 0)

                run(above, functools.partial(add, zs))
                run(below, functools.partial(add, below_slot))
            if ar:
                copy = remote(
                    acc.at[block, part], beside.at[zs, part], beside_out.at[zs, h],
                    beside_in.at[zs, h], place.at(near, place.c),
                )
                copy.start()
                pending.append((None, copy))
            elif not last:
                there = jnp.where(zs == place.z + 1, 4, zs)
                for condition, axis, slot in (
                    (zs < place.z, DOWN, zs),
                    (zs > place.z, UP, there),
                ):
                    copy = remote(
                        acc.at[block, part], chain.at[slot, part], chain_out.at[zs, h],
                        chain_in.at[slot, h], place.device(axis),
                    )
                    run(condition, copy.start)
                    pending.append((condition, copy))
            side.event()
    for condition, copy in pending:
        run(condition, copy.wait_send)
    if has_small:
        end_small()


def combine(experts, shards, number, weighted, sel, small=None, extra=None):
    rows = sel.shape[1]
    width = weighted.shape[-1]
    devices = experts * shards
    extra = extra or Extra()
    space = pl.BlockSpec(memory_space=pl.ANY)
    vmem = pl.BlockSpec(memory_space=pltpu.VMEM)
    dma = pltpu.SemaphoreType.DMA
    low = jnp.bfloat16
    has_small = int(small is not None)
    operands, in_specs = [weighted, sel], [space, vmem]
    out_shape, out_specs = [jax.ShapeDtypeStruct((rows, width), jnp.float32)], [vmem]
    scratch = [
        pltpu.VMEM((8, 4 * SLOTS, width), low),
        pltpu.VMEM((8, rows, width), low),
        pltpu.VMEM((4, rows, width), low),
        pltpu.VMEM((5, rows, width), low),
        dma((8, 4)),
        dma((8, 3)),
        dma((4, HALVES)),
        dma((4, HALVES)),
        dma((5, HALVES)),
        dma((4, HALVES)),
    ]
    if has_small:
        operands.append(small)
        in_specs.append(space)
        out_shape.append(jax.ShapeDtypeStruct(small.shape, small.dtype))
        out_specs.append(space)
        scratch += [dma((devices,)), dma((devices,)), dma((1,))]
    return pl.pallas_call(
        functools.partial(combine_kernel, (experts, shards), has_small, extra),
        out_shape=out_shape + extra.outs,
        in_specs=in_specs + extra.in_specs,
        out_specs=out_specs + extra.out_specs,
        scratch_shapes=scratch + extra.scratch,
        compiler_params=pltpu.CompilerParams(
            collective_id=number, has_side_effects=True, vmem_limit_bytes=63 * 2**20
        ),
        name="combine",
    )(*operands, *extra.operands)


FLAT = ("zy", "yz")
CHUNKS = 4
PIECES = 8


def flat_parts(rows):
    return (0, rows * 3 // 4), (rows * 3 // 4, rows - rows * 3 // 4)


def send_around(place, experts, shards, src_of, dst, out_sems, in_sems, across):
    count = experts * shards if across else shards
    me = place.e * shards + place.f if across else place.f

    def copy(i, sending):
        other = lax.rem(me + i, count)
        if across:
            device = (other // shards, lax.rem(other, shards))
        else:
            device = (place.e, other)
        source = me if sending else other
        return remote(src_of(other), dst.at[source], out_sems.at[i], in_sems.at[source], device)

    def start(i, carry):
        copy(i, True).start()
        return carry

    def finish(i, carry):
        done = copy(i, False)
        done.wait_send()
        done.wait_recv()
        return carry

    lax.fori_loop(1, count, start, 0)
    return lambda: lax.fori_loop(1, count, finish, 0)


def gather_kernel(
    dims, flat, tall, tok, pack, ids, wide, flat_out_all, tall_out_all, tok_out_all, pack_all, ids_all,
    picks, pick, spread, narrow, wide_held, flat_all, tall_all, tok_all, put_sems,
    flat_in, flat_out, tall_in, tall_out, tok_in, tok_out, pack_in, pack_out, ids_in, ids_out, local,
    ids_held, hits, ranks,
):
    experts, shards = dims
    place = Place()
    greet_all(place, experts, shards)
    me = place.e * shards + place.f
    starts, sizes = flat_parts(flat.shape[0])
    chunk = tall.shape[0] // PIECES
    pending = []
    keeps = [
        pltpu.make_async_copy(flat, flat_all.at[place.f], local.at[0]),
        pltpu.make_async_copy(tok, tok_all.at[place.e], local.at[1]),
        pltpu.make_async_copy(pack, pack_all.at[place.f], local.at[2]),
        pltpu.make_async_copy(ids, ids_all.at[me], local.at[3]),
    ]

    def go(condition, copy):
        run(condition, copy.start)
        pending.append((condition, copy))

    def both(a, b):
        return b if a is None else (a if b is None else a & b)

    puts = []

    def put(src, dst, condition=None):
        copy = pltpu.make_async_copy(src, dst, put_sems.at[len(puts)])
        run(condition, copy.start)
        puts.append((condition, copy))

    def flat_item(p, j, yr):
        zs = place.ranked(j)
        source = zs * 2 + (1 - place.y if yr else place.y)
        first = j == 0 and yr == 0
        window = flat_all.at[source, pl.ds(starts[p], sizes[p])]
        src = window
        if not first:
            remote(
                window, window, flat_out.at[p, source, 0], flat_in.at[p, source], place.device("c")
            ).wait_recv()
        put(window, flat_out_all.at[source, pl.ds(starts[p], sizes[p])])
        for axis, condition in links(place, FLAT[p], j, 0, yr, zs):
            go(
                condition,
                remote(
                    src,
                    window,
                    flat_out.at[p, source, LINK[axis]],
                    flat_in.at[p, source],
                    place.device(axis),
                ),
            )

    owner = place.z == place.e

    distance = jnp.abs(place.z - place.e)

    def tall_round(r):
        k = r - distance
        live = (k >= 0) & (k < PIECES)
        k = jnp.clip(k, 0, PIECES - 1)
        piece = pl.ds(pl.multiple_of(k * chunk, chunk), chunk)
        window = tall_all.at[place.y, piece]

        @pl.when(live & ~owner)
        def _():
            remote(window, window, tall_out.at[k, 0], tall_in.at[0, k], place.device("c")).wait_recv()

        for axis, condition in (
            (UP, (place.z >= place.e) & (place.z < 3)),
            (DOWN, (place.z <= place.e) & (place.z > 0)),
            ("y", None),
        ):
            go(
                both(live, condition),
                remote(
                    window,
                    window,
                    tall_out.at[k, LINK[axis]],
                    tall_in.at[1 if axis == "y" else 0, k],
                    place.device(axis),
                ),
            )
        put(window, tall_out_all.at[place.y, piece], live)

    def rank_rows():
        end_ids()
        keeps[3].wait()
        copy = pltpu.make_async_copy(ids_all, ids_held, local.at[5])
        copy.start()
        copy.wait()
        hits[...] = jnp.zeros_like(hits)

        def hit(i, number):
            found = jnp.where(ids_held[i] == number, 1.0, 0.0)
            return jnp.max(found, 0, keepdims=True)

        def own(i, carry):
            hits[pl.ds(i, 1)] = hit(i, me)
            return carry

        lax.fori_loop(0, experts * shards, own, 0)
        mine, far = (place.x, place.y), place.line()[1]
        for k, (chip, core) in enumerate(
            ((mine, place.c), (mine, 1 - place.c), (far, place.c), (far, 1 - place.c))
        ):
            expert_at, shard_at = place.at(chip, core)
            for ar in range(2):
                for zs in range(4):
                    row = experts * shards + (ar * 4 + zs) * 4 + k
                    at = block_number(mine, place.c, ar, zs)
                    hits[row : row + 1] = hit(at, expert_at * shards + shard_at)
        count = hits.shape[1]
        before = lax.broadcasted_iota(jnp.int32, (count, count), 0)
        after = lax.broadcasted_iota(jnp.int32, (count, count), 1)
        earlier = jnp.where(before < after, 1.0, 0.0).astype(jnp.bfloat16)
        found = jnp.dot(hits[...].astype(jnp.bfloat16), earlier, preferred_element_type=jnp.float32)
        ranks[...] = jnp.where(hits[...] > 0.5, found, -1.0)

    def one_hot_rows():
        shape = (SLOTS, ranks.shape[1])
        slot = lax.broadcasted_iota(jnp.int32, shape, 0).astype(jnp.float32)

        def rows_of(i):
            return jnp.where(ranks[pl.ds(i, 1)] == slot, 1.0, 0.0).astype(jnp.bfloat16)

        def own(i, carry):
            picks[i] = rows_of(i)
            return carry

        def near(i, carry):
            for k in range(4):
                pick[i, k * SLOTS : (k + 1) * SLOTS] = rows_of(experts * shards + i * 4 + k)
            return carry

        lax.fori_loop(0, experts * shards, own, 0)
        lax.fori_loop(0, 8, near, 0)

    def one_hot_columns():
        turned = ranks[...].T
        shape = (turned.shape[0], 4 * SLOTS)
        lane = lax.broadcasted_iota(jnp.int32, shape, 1)
        slot = lax.rem(lane, SLOTS).astype(jnp.float32)
        for i in range(8):
            column = experts * shards + i * 4
            rank = turned[:, column : column + 1]
            for k in range(1, 4):
                rank = jnp.where(lane < k * SLOTS, rank, turned[:, column + k : column + k + 1])
            spread[i] = jnp.where(rank == slot, 1.0, 0.0).astype(jnp.bfloat16)

    for keep in keeps:
        keep.start()
    keep_tall = pltpu.make_async_copy(tall, tall_all.at[place.y], local.at[4])
    run(owner, keep_tall.start)
    keeps[0].wait()
    def narrow_rows():
        fetch.wait()

        def part(i, carry):
            here = pl.ds(pl.multiple_of(i * 16, 16), 16)
            narrow[here] = wide_held[here].astype(narrow.dtype)
            return carry

        lax.fori_loop(0, wide.shape[0] // 16, part, 0)

    fetch = pltpu.make_async_copy(wide, wide_held, local.at[6])
    flat_item(0, 0, 0)
    flat_item(1, 0, 0)
    go(None, remote(tok, tok_all.at[place.e], tok_out.at[0], tok_in.at[place.e], place.device("x")))
    go(None, remote(tok, tok_all.at[place.e], tok_out.at[1], tok_in.at[place.e], place.device("c")))
    end_pack = send_around(
        place, experts, shards, lambda i: pack, pack_all, pack_out, pack_in, False
    )
    end_ids = send_around(place, experts, shards, lambda i: ids, ids_all, ids_out, ids_in, True)
    run(owner, keep_tall.wait)
    keeps[1].wait()
    put(tok_all.at[place.e], tok_out_all.at[place.e])
    fetch.start()
    across = (1 - place.x) * 2 + place.c
    window = tok_all.at[across]
    relay = remote(window, window, tok_out.at[2], tok_in.at[across], place.device("c"))
    tall_round(0)
    flat_item(1, 0, 1)
    flat_item(0, 1, 0)
    tall_round(1)
    rank_rows()
    flat_item(0, 2, 0)
    one_hot_rows()
    tall_round(2)
    one_hot_columns()
    narrow_rows()
    flat_item(1, 1, 0)
    flat_item(1, 1, 1)
    relay.wait_recv()
    go(None, relay)
    put(window, tok_out_all.at[across])
    flat_item(0, 3, 0)
    tall_round(3)
    flat_item(1, 2, 0)
    flat_item(1, 2, 1)
    tall_round(4)
    flat_item(1, 3, 0)
    flat_item(1, 3, 1)
    for r in range(5, PIECES + 3):
        tall_round(r)
    for j in range(4):
        flat_item(0, j, 1)
    for k in range(PIECES):
        window = tall_all.at[1 - place.y, pl.ds(k * chunk, chunk)]
        remote(window, window, tall_out.at[k, 0], tall_in.at[1, k], place.device("c")).wait_recv()
        put(window, tall_out_all.at[1 - place.y, pl.ds(k * chunk, chunk)])
    for source in (place.x * 2 + 1 - place.c, (1 - place.x) * 2 + 1 - place.c):
        window = tok_all.at[source]
        remote(window, window, tok_out.at[2], tok_in.at[source], place.device("c")).wait_recv()
        put(window, tok_out_all.at[source])
    for condition, copy in puts:
        run(condition, copy.wait)
    for condition, copy in pending:
        run(condition, copy.wait_send)
    end_pack()
    keeps[2].wait()


def gather(experts, shards, number, flat, tall, tok, pack, ids, wide):
    space = pl.BlockSpec(memory_space=pl.ANY)
    dma = pltpu.SemaphoreType.DMA
    devices = experts * shards

    def shape(lead, a):
        return jax.ShapeDtypeStruct((lead,) + a.shape, a.dtype)

    return pl.pallas_call(
        functools.partial(gather_kernel, (experts, shards)),
        out_shape=[
            shape(shards, flat),
            shape(2, tall),
            shape(experts, tok),
            shape(shards, pack),
            shape(devices, ids),
            jax.ShapeDtypeStruct((devices, SLOTS, ids.shape[1]), jnp.bfloat16),
            jax.ShapeDtypeStruct((8, 4 * SLOTS, ids.shape[1]), jnp.bfloat16),
            jax.ShapeDtypeStruct((8, ids.shape[1], 4 * SLOTS), jnp.bfloat16),
            jax.ShapeDtypeStruct(wide.shape, jnp.bfloat16),
        ],
        in_specs=[space] * 6,
        out_specs=[space] * 5 + [pl.BlockSpec(memory_space=pltpu.VMEM)] * 4,
        scratch_shapes=[
            pltpu.VMEM(wide.shape, wide.dtype),
            pltpu.VMEM((shards,) + flat.shape, flat.dtype),
            pltpu.VMEM((2,) + tall.shape, tall.dtype),
            pltpu.VMEM((experts,) + tok.shape, tok.dtype),
            dma((64,)),
            dma((2, shards)),
            dma((2, shards, 4)),
            dma((2, PIECES)),
            dma((PIECES, 4)),
            dma((experts,)),
            dma((3,)),
            dma((shards,)),
            dma((shards,)),
            dma((devices,)),
            dma((devices,)),
            dma((7,)),
            pltpu.VMEM((devices,) + ids.shape, ids.dtype),
            pltpu.VMEM((128, ids.shape[1]), jnp.float32),
            pltpu.VMEM((128, ids.shape[1]), jnp.float32),
        ],
        compiler_params=pltpu.CompilerParams(
            collective_id=number, has_side_effects=True, vmem_limit_bytes=60 * 2**20
        ),
        name="gather",
    )(flat, tall, tok, pack, ids, wide)


def add_rows(acc, first, window, rows, step=16):
    def add(i, carry):
        here = pl.ds(pl.multiple_of(i * step, step), step)
        at = pl.ds(pl.multiple_of(first + i * step, step), step)
        acc[at] = (acc[at].astype(jnp.float32) + window[here].astype(jnp.float32)).astype(acc.dtype)
        return carry

    lax.fori_loop(0, rows // step, add, 0)


def reduce_body(
    dims, side, flat, tall, pack, partial, out_q, out_k, out_v, tall_out, pack_all, total,
    acc, tacc, yslot, zslot, yone, zall, ty, tz,
    load, yin, zin, yone_in, zall_in, ty_in, tz_in, flat_send, tall_send, spread_in, spread_out,
    tall_in, keep_tall, local,
    group_acc, group_near, group_cross, group_load, group_out, group_in, cross_out, cross_in,
):
    experts, shards = dims
    place = Place()
    greet(place)
    tall_keeps = []
    owner = place.z == place.e
    home = place.x == place.z // 2
    same = place.c == place.z % 2
    starts, sizes = flat_parts(flat.shape[1])
    sizes = (sizes[0], sizes[1] + pack.shape[1])
    height = tall.shape[1]
    chunk = height // CHUNKS
    part = partial.shape[1] // CHUNKS
    pending = []

    def go(condition, copy):
        run(condition, copy.start)
        pending.append((condition, copy))

    def both(a, b):
        return a if b is None else a & b

    load_tall = pltpu.make_async_copy(tall, tacc, load.at[0])
    load_flat = pltpu.make_async_copy(flat, acc.at[:, pl.ds(0, flat.shape[1])], load.at[1])
    load_pack = pltpu.make_async_copy(
        pack, acc.at[:, pl.ds(flat.shape[1], pack.shape[1])], load.at[2]
    )
    across_y = []
    order = (3, 2, 1, 0)

    def add_tall(k):
        piece = pl.ds(k * chunk, chunk)
        across_y.append(
            remote(
                tall.at[1 - place.y, piece], ty.at[piece], tall_send.at[0, k], ty_in.at[k],
                place.device("y"),
            )
        )

    def add_flat(j):
        target = place.ranked(j) * 2 + 1 - place.y
        across_y.append(
            remote(
                flat.at[target, pl.ds(starts[0], sizes[0])],
                yslot.at[place.ranked(j)],
                flat_send.at[0, target],
                yin.at[place.ranked(j)],
                place.device("y"),
            )
        )

    add_tall(0)
    add_tall(1)
    add_flat(3)
    add_tall(2)
    add_flat(2)
    add_tall(3)
    add_flat(1)
    add_flat(0)
    started = [0]

    def feed(count):
        while started[0] < min(count + 2, len(across_y)):
            if started[0] >= 2:
                across_y[started[0] - 2].wait_send()
            across_y[started[0]].start()
            started[0] += 1

    feed(0)
    load_tall.start()
    load_flat.start()
    load_pack.start()
    group_sends = []
    group_loads = []
    for half in (1 - place.x, place.x):
        for i in range(CHUNKS):
            piece = pl.ds(i * part, part)
            copy = remote(
                partial.at[half * 2 + 1 - place.c, piece], group_near.at[half, piece],
                group_out.at[half, i], group_in.at[half, i], place.device("c"),
            )
            copy.start()
            group_sends.append(copy)
            copy = pltpu.make_async_copy(
                partial.at[half * 2 + place.c, piece], group_acc.at[half, piece],
                group_load.at[half, i],
            )
            copy.start()
            group_loads.append(copy)

    def group_half(index, half):
        for i in range(CHUNKS):
            piece = pl.ds(i * part, part)
            window = group_near.at[half, piece]
            group_loads[index * CHUNKS + i].wait()
            remote(
                window, window, group_out.at[half, i], group_in.at[half, i], place.device("c")
            ).wait_recv()
            add_rows(group_acc.at[half], i * part, window, part)
            if index == 0:
                copy = remote(
                    group_acc.at[half, piece], group_cross.at[piece], cross_out.at[i],
                    cross_in.at[i], place.device("x"),
                )
                copy.start()
                group_sends.append(copy)

    def group_end():
        for i in range(CHUNKS):
            window = group_cross.at[pl.ds(i * part, part)]
            remote(window, window, cross_out.at[i], cross_in.at[i], place.device("c")).wait_recv()

            def add(t, carry):
                here = pl.ds(pl.multiple_of(i * part + t * 16, 16), 16)
                own = group_acc[place.x, here].astype(jnp.float32)
                total[here] = own + group_cross[here].astype(jnp.float32)
                return carry

            lax.fori_loop(0, part // 16, add, 0)

    load_tall.wait()
    load_flat.wait()
    load_pack.wait()

    def into(slots, sems, zd, side):
        index = jnp.where(zd == place.z, 4, zd) if side == BELOW else zd
        return slots.at[index], sems.at[index]

    def out_to(slots, sems, zd, side):
        there = place.z - 1 if side == ABOVE else place.z + 1
        index = jnp.where(zd == there, 4, zd) if side == BELOW else zd
        return slots.at[index], sems.at[index]

    def line(j, p, first, slots, sems, send_sem, target):
        zd = place.ranked(j)
        rows = sizes[p]
        for side, condition in (
            (ABOVE, (zd <= place.z) & (place.z < 3)),
            (BELOW, (zd >= place.z) & (place.z > 0)),
        ):
            window, sem = into(slots, sems, zd, side)

            def take(window=window, sem=sem):
                remote(window, window, send_sem, sem, place.device("c")).wait_recv()
                add_rows(acc.at[target], first, window, rows)

            if j == 0:
                condition = place.z < 3 if side == ABOVE else place.z > 0
            run(condition, take)
        if j == 0:
            return
        for side, axis, condition in ((ABOVE, DOWN, zd < place.z), (BELOW, UP, zd > place.z)):
            window, sem = out_to(slots, sems, zd, side)
            go(
                condition,
                remote(acc.at[target, pl.ds(first, rows)], window, send_sem, sem, place.device(axis)),
            )

    above_e, below_e = place.z > place.e, place.z < place.e
    hops = jnp.where(above_e, 3 - place.z, jnp.where(below_e, place.z, jnp.maximum(place.e, 3 - place.e)))

    def tall_round(r):
        k = r - hops
        live = (k >= 0) & (k < CHUNKS)
        k = jnp.clip(k, 0, CHUNKS - 1)
        first = pl.multiple_of(k * chunk, chunk)
        piece = pl.ds(first, chunk)

        @pl.when(live)
        def _():
            remote(
                ty.at[piece], ty.at[piece], tall_send.at[0, k], ty_in.at[k], place.device("c")
            ).wait_recv()
            add_rows(tacc.at[place.y], first, ty.at[piece], chunk)

        for index, condition in (
            (0, (place.z >= place.e) & (place.z < 3)),
            (1, (place.z <= place.e) & (place.z > 0)),
        ):
            window = tz.at[index, piece]

            def take(window=window, index=index):
                remote(
                    window, window, tall_send.at[1, k], tz_in.at[index, k], place.device("c")
                ).wait_recv()
                add_rows(tacc.at[place.y], first, window, chunk)

            run(live & condition, take)
        for index, axis, condition in ((0, DOWN, above_e), (1, UP, below_e)):
            go(
                live & condition,
                remote(
                    tacc.at[place.y, piece], tz.at[index, piece], tall_send.at[1, k],
                    tz_in.at[index, k], place.device(axis),
                ),
            )
        piece_out = tall_out.at[piece]
        keep = pltpu.make_async_copy(tacc.at[place.y, piece], piece_out, keep_tall.at[k])
        run(live & owner, keep.start)
        tall_keeps.append((live & owner, keep))
        for row, axis in ((2, "x"), (3, "c")):
            go(
                live & owner,
                remote(
                    tacc.at[place.y, piece], piece_out, tall_send.at[row, k], tall_in.at[k],
                    place.device(axis),
                ),
            )

    def flat_first(j):
        zd = place.ranked(j)
        target = zd * 2 + place.y
        window = yslot.at[zd]
        remote(window, window, flat_send.at[0, target], yin.at[zd], place.device("c")).wait_recv()
        add_rows(acc.at[target], starts[0], window, sizes[0])
        line(j, 0, starts[0], zslot, zin, flat_send.at[0, target], target)

    def flat_second(j, yr):
        zd = place.ranked(j)
        target = zd * 2 + (1 - place.y if yr else place.y)
        line(j, 1, starts[1], zall.at[yr], zall_in.at[yr], flat_send.at[1, target], target)

    flat_second(3, 1)
    flat_second(3, 0)
    side.event()
    tall_round(0)
    side.event()
    feed(1)
    tall_round(1)
    side.event()
    feed(2)
    flat_second(2, 1)
    flat_second(2, 0)
    side.event()
    flat_first(3)
    side.event()
    feed(3)
    group_half(0, 1 - place.x)
    tall_round(2)
    side.event()
    feed(4)
    flat_second(1, 1)
    flat_second(1, 0)
    side.event()
    flat_first(2)
    side.event()
    feed(5)
    tall_round(3)
    side.event()
    feed(6)
    flat_first(1)
    side.event()
    group_half(1, place.x)
    flat_second(0, 1)
    other = place.z * 2 + 1 - place.y
    go(
        None,
        remote(
            acc.at[other, pl.ds(starts[1], sizes[1])], yone, flat_send.at[1, other], yone_in.at[0],
            place.device("y"),
        ),
    )
    flat_second(0, 0)
    flat_first(0)
    remote(yone, yone, flat_send.at[1, other], yone_in.at[0], place.device("c")).wait_recv()
    add_rows(acc.at[place.f], starts[1], yone, sizes[1])
    cuts = []
    first = 0
    for out in (out_q, out_k, out_v):
        wide = out.shape[1] // experts
        cuts.append((out, pl.ds(0, flat.shape[1]), pl.ds(first, wide)))
        first += wide
    cuts.append((pack_all, pl.ds(flat.shape[1], pack.shape[1]), pl.ds(0, first)))

    def window_of(i, source):
        out = cuts[i][0]
        if i == 3:
            return out.at[source]
        wide = out.shape[1] // experts
        return out.at[:, pl.ds(pl.multiple_of(source * wide, 128), wide)]

    flat_keeps = []
    for i, (out, high, wide) in enumerate(cuts):
        done = acc.at[place.f, high, wide]
        keep = pltpu.make_async_copy(done, window_of(i, place.e), local.at[1 + i])
        keep.start()
        flat_keeps.append(keep)
        for row, axis in enumerate(("x", "c")):
            go(
                None,
                remote(
                    done, window_of(i, place.e), spread_out.at[row, i], spread_in.at[place.e, i],
                    place.device(axis),
                ),
            )
    tall_round(4)
    side.event()
    tall_round(5)
    side.event()
    tall_round(6)
    side.event()
    group_end()
    across = (1 - place.x) * 2 + place.c
    for i in range(4):
        window = window_of(i, across)
        relay = remote(window, window, spread_out.at[2, i], spread_in.at[across, i], place.device("c"))
        relay.wait_recv()
        go(None, relay)
    for k in range(CHUNKS):
        window = tall_out.at[pl.ds(k * chunk, chunk)]
        tall_relay = remote(window, window, tall_send.at[4, k], tall_in.at[k], place.device("c"))
        run(~owner, tall_relay.wait_recv)
        go(~home & same, tall_relay)
    for source in (place.x * 2 + 1 - place.c, (1 - place.x) * 2 + 1 - place.c):
        for i in range(4):
            window = window_of(i, source)
            remote(
                window, window, spread_out.at[2, i], spread_in.at[source, i], place.device("c")
            ).wait_recv()
    for copy in across_y[-2:]:
        copy.wait_send()
    for condition, copy in pending:
        run(condition, copy.wait_send)
    for keep in flat_keeps:
        keep.wait()
    for condition, keep in tall_keeps:
        run(condition, keep.wait)
    for copy in group_sends:
        copy.wait_send()


def reduce_kernel(dims, extra, *refs):
    more = len(extra.operands), len(extra.outs), len(extra.scratch)
    rest = len(refs) - 10 - sum(more)
    ins, more_in, outs, more_out, scratch, more_scratch = split(
        refs, (4, more[0], 6, more[1], rest, more[2])
    )
    side = Side(extra.steps(*more_in, *more_out, *more_scratch), 13)
    reduce_body(dims, side, *ins, *outs, *scratch)


def reduce(experts, shards, number, flat, tall, pack, partial, extra):
    space = pl.BlockSpec(memory_space=pl.ANY)
    dma = pltpu.SemaphoreType.DMA
    _, sizes = flat_parts(flat.shape[1])
    more = sizes[1] + pack.shape[1]
    width, wide = flat.shape[2], tall.shape[2]
    low = jnp.bfloat16
    return pl.pallas_call(
        functools.partial(reduce_kernel, (experts, shards), extra),
        out_shape=[
            jax.ShapeDtypeStruct((flat.shape[1], experts * (width - 2 * HEAD_SIZE)), low),
            jax.ShapeDtypeStruct((flat.shape[1], experts * HEAD_SIZE), low),
            jax.ShapeDtypeStruct((flat.shape[1], experts * HEAD_SIZE), low),
            jax.ShapeDtypeStruct(tall.shape[1:], low),
            jax.ShapeDtypeStruct((experts,) + pack.shape[1:], low),
            jax.ShapeDtypeStruct(partial.shape[1:], jnp.float32),
        ]
        + extra.outs,
        in_specs=[space] * 4 + extra.in_specs,
        out_specs=[space] * 5 + [pl.BlockSpec(memory_space=pltpu.VMEM)] + extra.out_specs,
        scratch_shapes=[
            pltpu.VMEM((shards, flat.shape[1] + pack.shape[1], width), low),
            pltpu.VMEM(tall.shape, low),
            pltpu.VMEM((4, sizes[0], width), low),
            pltpu.VMEM((5, sizes[0], width), low),
            pltpu.VMEM((more, width), low),
            pltpu.VMEM((2, 5, more, width), low),
            pltpu.VMEM(tall.shape[1:], low),
            pltpu.VMEM((2,) + tall.shape[1:], low),
            dma((3,)),
            dma((4,)),
            dma((5,)),
            dma((1,)),
            dma((2, 5)),
            dma((CHUNKS,)),
            dma((2, CHUNKS)),
            dma((2, shards)),
            dma((5, CHUNKS)),
            dma((experts, 4)),
            dma((3, 4)),
            dma((CHUNKS,)),
            dma((CHUNKS,)),
            dma((5,)),
            pltpu.VMEM((2,) + partial.shape[1:], low),
            pltpu.VMEM((2,) + partial.shape[1:], low),
            pltpu.VMEM(partial.shape[1:], low),
            dma((2, CHUNKS)),
            dma((2, CHUNKS)),
            dma((2, CHUNKS)),
            dma((CHUNKS,)),
            dma((CHUNKS,)),
        ]
        + extra.scratch,
        compiler_params=pltpu.CompilerParams(
            collective_id=number, has_side_effects=True, vmem_limit_bytes=58 * 2**20
        ),
        name="reduce",
    )(flat, tall, pack, partial, *extra.operands)


def branch_scatter_kernel(
    mixed, weight, total, blocks, near, cross, near_out, near_in, x_out, x_in
):
    place = Place()
    greet(place)
    rows, width = total.shape
    chunk = rows // CHUNKS
    sends = []
    for index, half in enumerate((1 - place.x, place.x)):
        for core in (1 - place.c, place.c):
            block = half * 2 + core
            here = pl.ds(pl.multiple_of(block * rows, rows), rows)

            def tile(t, carry):
                columns = pl.ds(pl.multiple_of(t * 512, 512), 512)
                blocks[block, :, columns] = jnp.dot(
                    mixed[here], weight[:, columns], preferred_element_type=jnp.float32
                ).astype(jnp.bfloat16)
                return carry

            lax.fori_loop(0, width // 512, tile, 0)
        for k in range(CHUNKS):
            piece = pl.ds(k * chunk, chunk)
            copy = remote(
                blocks.at[half * 2 + 1 - place.c, piece], near.at[half, piece], near_out.at[half, k],
                near_in.at[half, k], place.device("c"),
            )
            copy.start()
            sends.append(copy)
        for k in range(CHUNKS):
            piece = pl.ds(k * chunk, chunk)
            window = near.at[half, piece]
            remote(window, window, near_out.at[half, k], near_in.at[half, k], place.device("c")).wait_recv()
            add_rows(blocks.at[half * 2 + place.c], k * chunk, window, chunk)
            if index == 0:
                copy = remote(
                    blocks.at[half * 2 + place.c, piece], cross.at[piece], x_out.at[k], x_in.at[k],
                    place.device("x"),
                )
                copy.start()
                sends.append(copy)
    for k in range(CHUNKS):
        window = cross.at[pl.ds(k * chunk, chunk)]
        remote(window, window, x_out.at[k], x_in.at[k], place.device("c")).wait_recv()

        def add(i, carry):
            here = pl.ds(pl.multiple_of(k * chunk + i * 16, 16), 16)
            own = blocks[place.e, here].astype(jnp.float32)
            total[here] = own + cross[here].astype(jnp.float32)
            return carry

        lax.fori_loop(0, chunk // 16, add, 0)
    for copy in sends:
        copy.wait_send()


def branch_scatter(number, mixed, weight):
    dma = pltpu.SemaphoreType.DMA
    rows, width = mixed.shape[0] // 4, weight.shape[1]
    low = jnp.bfloat16
    vmem = pl.BlockSpec(memory_space=pltpu.VMEM)
    return pl.pallas_call(
        branch_scatter_kernel,
        out_shape=jax.ShapeDtypeStruct((rows, width), jnp.float32),
        in_specs=[vmem, vmem],
        out_specs=vmem,
        scratch_shapes=[
            pltpu.VMEM((4, rows, width), low),
            pltpu.VMEM((2, rows, width), low),
            pltpu.VMEM((rows, width), low),
            dma((2, CHUNKS)),
            dma((2, CHUNKS)),
            dma((CHUNKS,)),
            dma((CHUNKS,)),
        ],
        compiler_params=pltpu.CompilerParams(
            collective_id=number, has_side_effects=True, vmem_limit_bytes=32 * 2**20
        ),
        name="branch_scatter",
    )(mixed, weight)


BLOCK = 256


def dot_last(a, b):
    return lax.dot_general(a, b, (((1,), (1,)), ((), ())), preferred_element_type=jnp.float32)


def dot(a, b):
    return jnp.dot(a, b, preferred_element_type=jnp.float32)


def turn(rows):
    lane = lax.broadcasted_iota(jnp.int32, rows.shape, 1)
    half = HEAD_SIZE // 2
    return pltpu.roll(rows, half, 1) * jnp.where(lane < half, -1.0, 1.0)


def mask_block(r, count, ids_column, ids_row, bias):
    queries = pl.ds(r * BLOCK, BLOCK)

    def part(i, carry):
        keys = pl.ds(pl.multiple_of(i * BLOCK, BLOCK), BLOCK)
        key_at = lax.broadcasted_iota(jnp.int32, (BLOCK, BLOCK), 0) + i * BLOCK
        query_at = lax.broadcasted_iota(jnp.int32, (BLOCK, BLOCK), 1) + r * BLOCK
        allowed = (ids_column[keys] == ids_row[:, queries]) & (key_at <= query_at)
        bias[keys] = jnp.where(allowed, 0.0, -1e30)
        return carry

    lax.fori_loop(0, count // BLOCK, part, 0)


def project_steps(
    tok, w_qkv, gain_one, gain_q, gain_k, cosine, sine, normed, raw, query_rot, key_rot, value, inverses
):
    heads = query_rot.shape[1] // HEAD_SIZE
    low = jnp.bfloat16

    def rotated(v, rows, gain):
        u = v * inverse_rms(v) * gain
        return (u * cosine[rows] + turn(u) * sine[rows]).astype(low)

    def norm(r):
        def part(i, carry):
            here = pl.ds(pl.multiple_of(r * BLOCK + i * 16, 16), 16)
            x = tok[here].astype(jnp.float32)
            inverse = inverse_rms(x)
            inverses[here] = inverse
            normed[here] = (x * inverse * gain_one[...]).astype(low)
            return carry

        lax.fori_loop(0, BLOCK // 16, part, 0, unroll=2)

    def multiply(r):
        rows = pl.ds(r * BLOCK, BLOCK)

        def pair(i, carry):
            column = pl.ds(pl.multiple_of(i * 2 * HEAD_SIZE, 2 * HEAD_SIZE), 2 * HEAD_SIZE)
            both = dot(normed[rows], w_qkv[:, column])
            raw[rows, column] = both
            for k in range(2):
                at = pl.ds(pl.multiple_of((2 * i + k) * HEAD_SIZE, HEAD_SIZE), HEAD_SIZE)
                one = both[:, k * HEAD_SIZE : (k + 1) * HEAD_SIZE]
                query_rot[rows, at] = rotated(one, rows, gain_q[...])
            return carry

        lax.fori_loop(0, heads // 2, pair, 0)
        last = pl.ds(heads * HEAD_SIZE, 2 * HEAD_SIZE)
        both = dot(normed[rows], w_qkv[:, last])
        raw[rows, last] = both
        key_rot[rows] = rotated(both[:, :HEAD_SIZE], rows, gain_k[...])
        value[rows] = both[:, HEAD_SIZE:].astype(low)

    steps = []
    for r in range(tok.shape[0] // BLOCK):
        steps.append(functools.partial(norm, r))
        steps.append(functools.partial(multiply, r))
    return steps


def attend_steps(query_rot, key_rot, value, ids_column, ids_row, mixed, bias, value_t):
    length = key_rot.shape[0]
    heads = query_rot.shape[1] // HEAD_SIZE
    scale = HEAD_SIZE ** (-0.5)

    def prepare(r):
        if r == 0:
            value_t[...] = value[...].T
        mask_block(r, (r + 1) * BLOCK, ids_column, ids_row, bias)

    def heads_of(r, first, some):
        rows = pl.ds(r * BLOCK, BLOCK)
        count = (r + 1) * BLOCK

        def head(h, carry):
            column = pl.ds(pl.multiple_of(h * HEAD_SIZE, HEAD_SIZE), HEAD_SIZE)
            scores = dot_last(key_rot[:count], query_rot[rows, column]) * scale + bias[:count]
            shifted = jnp.exp(scores - jnp.max(scores, 0, keepdims=True))
            weights = shifted * (1.0 / jnp.sum(shifted, 0, keepdims=True))
            out = dot(value_t[:, :count], weights.astype(jnp.bfloat16))
            mixed[rows, column] = out.T.astype(jnp.bfloat16)
            return carry

        lax.fori_loop(first, first + some, head, 0, unroll=2)

    steps = []
    for r in range(length // BLOCK):
        steps.append(functools.partial(prepare, r))
        some = heads if r == 0 else heads // 2
        for first in range(0, heads, some):
            steps.append(functools.partial(heads_of, r, first, some))
    return steps


def load(pairs, sems):
    copies = [pltpu.make_async_copy(a, b, sems.at[i]) for i, (a, b) in enumerate(pairs)]
    for copy in copies:
        copy.start()
    return copies


def attention(tokens, w_qkv, gain_one, gain_q, gain_k, cosine, sine, ids_column, ids_row, heads):
    length, width = tokens.shape
    wide = w_qkv.shape[1]
    span = heads * HEAD_SIZE
    low, f32 = jnp.bfloat16, jnp.float32
    space, vmem = pl.BlockSpec(memory_space=pl.ANY), pl.BlockSpec(memory_space=pltpu.VMEM)
    shapes = [
        ((length, width), low),
        ((length, wide), f32),
        ((length, span), low),
        ((length, HEAD_SIZE), low),
        ((length, HEAD_SIZE), low),
        ((length, span), low),
        ((length, 1), f32),
    ]

    def steps(*refs):
        ins, outs, scratch = split(refs, (9, 7, 15))
        tok, weight, cos_held, sin_held, in_sems, out_sems, bias, value_t = scratch[:8]
        results = scratch[8:]
        copies = load(
            [(ins[0], tok), (ins[1], weight), (ins[5], cos_held), (ins[6], sin_held)], in_sems
        )

        def begin():
            for copy in copies:
                copy.wait()

        saved = []

        def save(picks):
            for i in picks:
                copy = pltpu.make_async_copy(results[i], outs[i], out_sems.at[i])
                copy.start()
                saved.append(copy)

        def end():
            save((5, 6))
            for copy in saved:
                copy.wait()

        return (
            [begin]
            + project_steps(tok, weight, *ins[2:5], cos_held, sin_held, *results[:5], results[6])
            + [functools.partial(save, range(5))]
            + attend_steps(*results[2:5], *ins[7:9], results[5], bias, value_t)
            + [end]
        )

    return Extra(
        (tokens, w_qkv, gain_one, gain_q, gain_k, cosine, sine, ids_column, ids_row),
        [space] * 2 + [vmem] * 3 + [space] * 2 + [vmem] * 2,
        [jax.ShapeDtypeStruct(*shape) for shape in shapes],
        [space] * 7,
        [
            pltpu.VMEM(tokens.shape, low),
            pltpu.VMEM(w_qkv.shape, low),
            pltpu.VMEM(cosine.shape, f32),
            pltpu.VMEM(sine.shape, f32),
            pltpu.SemaphoreType.DMA((4,)),
            pltpu.SemaphoreType.DMA((7,)),
            pltpu.VMEM((length, BLOCK), f32),
            pltpu.VMEM((HEAD_SIZE, length), low),
        ]
        + [pltpu.VMEM(*shape) for shape in shapes],
        steps,
    )


def attend_back_steps(
    query_rot, key_rot, value, raw, grad_mixed, ids_column, ids_row, gain_q, gain_k, cosine, sine,
    grad_raw, grad_gains, bias, key_t, grad_key, grad_value, sums,
):
    length = key_rot.shape[0]
    heads = query_rot.shape[1] // HEAD_SIZE
    scale = HEAD_SIZE ** (-0.5)
    low = jnp.bfloat16

    def back(grad, rows, column, gain, index):
        unit = grad * cosine[rows] - turn(grad * sine[rows])
        v = raw[rows, column]
        inverse = inverse_rms(v)
        sums[index] += jnp.sum((unit * v * inverse).reshape(-1, 8, HEAD_SIZE), 0)
        grad_raw[rows, column] = norm_backward(unit, v, inverse, gain).astype(low)

    def prepare(r):
        if r == 0:
            key_t[...] = key_rot[...].T
            grad_key[...] = jnp.zeros_like(grad_key)
            grad_value[...] = jnp.zeros_like(grad_value)
            sums[...] = jnp.zeros_like(sums)
        mask_block(r, (r + 1) * BLOCK, ids_column, ids_row, bias)

    def heads_of(r, first, some):
        rows = pl.ds(r * BLOCK, BLOCK)
        count = (r + 1) * BLOCK

        def head(h, carry):
            column = pl.ds(pl.multiple_of(h * HEAD_SIZE, HEAD_SIZE), HEAD_SIZE)
            query = query_rot[rows, column]
            grad_out = grad_mixed[rows, column]
            scores = dot_last(key_rot[:count], query) * scale + bias[:count]
            shifted = jnp.exp(scores - jnp.max(scores, 0, keepdims=True))
            weights = shifted * (1.0 / jnp.sum(shifted, 0, keepdims=True))
            grad_value[:count] += dot(weights.astype(low), grad_out)
            grad_weights = dot_last(value[:count], grad_out)
            spread = jnp.sum(weights * grad_weights, 0, keepdims=True)
            grad_scores = (weights * (grad_weights - spread)).astype(low)
            grad_key[:count] += dot(grad_scores, query)
            grad_query = dot(key_t[:, :count], grad_scores).T * scale
            back(grad_query, rows, column, gain_q[...], 0)
            return carry

        lax.fori_loop(first, first + some, head, 0, unroll=2)

    def last():
        column = pl.ds(heads * HEAD_SIZE, HEAD_SIZE)
        for r in range(length // BLOCK):
            rows = pl.ds(r * BLOCK, BLOCK)
            back(grad_key[rows] * scale, rows, column, gain_k[...], 1)
            grad_raw[rows, pl.ds((heads + 1) * HEAD_SIZE, HEAD_SIZE)] = grad_value[rows].astype(low)
        grad_gains[...] = jnp.sum(sums[...], 1)

    steps = []
    for r in range(length // BLOCK):
        steps.append(functools.partial(prepare, r))
        some = heads if r == 0 else (heads // 2 if r == 1 else heads // 4)
        for first in range(0, heads, some):
            steps.append(functools.partial(heads_of, r, first, some))
    return steps + [last]


def attention_back(
    query_rot, key_rot, value, raw, mixed, grad_low, w_mix, normed_one, tokens, w_qkv, inverses,
    ids_column, ids_row, gain_q, gain_k, cosine, sine,
):
    length, width = tokens.shape
    span, wide = mixed.shape[1], raw.shape[1]
    tiles = width // BLOCK
    low, f32 = jnp.bfloat16, jnp.float32
    space, vmem = pl.BlockSpec(memory_space=pl.ANY), pl.BlockSpec(memory_space=pltpu.VMEM)
    whole = (query_rot, key_rot, value, raw, mixed, cosine, sine, inverses)
    streamed = (grad_low, w_mix, normed_one, tokens, w_qkv)
    own_rows = grad_low.shape[0]
    piece = own_rows // CHUNKS
    small = (ids_column, ids_row, gain_q, gain_k)

    def dot_first(a, b):
        return lax.dot_general(a, b, (((0,), (0,)), ((), ())), preferred_element_type=f32)

    def steps(*refs):
        ins, outs, scratch = split(refs, (17, 5, 27))
        held, (in_sems, grad_raw), work, tile_refs, group = split(scratch, (8, 2, 5, 4, 8))
        tall_in, tall_out, wide_out, sems = tile_refs
        mine, mix, normed, tok, weight = ins[8:13]
        inverse = held[7]
        branch, grad_mixed, mix_in, mix_sems, x_out, x_in, c_out, c_in = group
        place = Place()
        beside, other = place.at((1 - place.x, place.y), place.c), place.device("c")
        across = (1 - place.x) * 2 + place.c
        gains, grad_mix, grad_qkv, grad_normed, grad_gain = outs
        copies = load(list(zip(ins[:8], held)), in_sems)

        def rows_from(source, k):
            return branch.at[pl.ds(pl.multiple_of(source * own_rows + k * piece, piece), piece)]

        def own(k):
            return mine.at[pl.ds(k * piece, piece)]

        sends = []
        keeps = []
        for k in range(CHUNKS):
            sends.append(remote(own(k), rows_from(place.e, k), x_out.at[k], x_in.at[k], beside))
            sends.append(remote(own(k), rows_from(place.e, k), c_out.at[0, k], c_in.at[0, k], other))
            keeps.append(pltpu.make_async_copy(own(k), rows_from(place.e, k), mix_sems.at[2 + k]))
        for copy in sends + keeps:
            copy.start()

        def relay(k):
            window = rows_from(across, k)
            copy = remote(window, window, c_out.at[1, k], c_in.at[1, k], other)
            remote(window, window, x_out.at[k], x_in.at[k], other).wait_recv()
            copy.start()
            sends.append(copy)

        def mix_tile(t):
            return pltpu.make_async_copy(mix.at[at(t)], mix_in.at[t % 2], mix_sems.at[t % 2])

        def arrived():
            mix_tile(0).start()
            for copy in keeps:
                copy.wait()
            for k in range(CHUNKS):
                window = rows_from(place.x * 2 + 1 - place.c, k)
                remote(window, window, c_out.at[0, k], c_in.at[0, k], other).wait_recv()
                window = rows_from((1 - place.x) * 2 + 1 - place.c, k)
                remote(window, window, c_out.at[1, k], c_in.at[1, k], other).wait_recv()
            for copy in sends:
                copy.wait_send()

        def mixed_grad(t):
            mix_tile(t).wait()
            if t + 1 < span // BLOCK:
                mix_tile(t + 1).start()
            grad_mixed[:, at(t)] = dot_last(branch[...], mix_in[t % 2]).astype(low)

        def at(t):
            return pl.ds(t * BLOCK, BLOCK)

        def fetch(i):
            kind, t, slot = i // tiles, i % tiles, i % 2
            if kind == 0:
                return []
            source = (None, normed, tok)[kind]
            found = [
                pltpu.make_async_copy(source.at[:, at(t)], tall_in.at[slot], sems.at[0, slot])
            ]
            if kind == 2:
                found.append(
                    pltpu.make_async_copy(
                        weight.at[at(t)], mix_in.at[slot, :, pl.ds(0, wide)], sems.at[1, slot]
                    )
                )
            return found

        def store(i):
            kind, t, slot = i // tiles, i % tiles, i % 2
            if kind == 1:
                return pltpu.make_async_copy(
                    wide_out.at[slot], grad_qkv.at[at(t)], sems.at[2, slot]
                )
            target = grad_normed if kind else grad_mix
            return pltpu.make_async_copy(tall_out.at[slot], target.at[:, at(t)], sems.at[2, slot])

        def begin():
            for copy in copies:
                copy.wait()

        def tile(i):
            kind, t, slot = i // tiles, i % tiles, i % 2
            for copy in fetch(i):
                copy.wait()
            if i + 1 < 3 * tiles:
                for copy in fetch(i + 1):
                    copy.start()
            if i >= 2:
                store(i - 2).wait()
            if kind == 0:
                tall_out[slot] = dot_first(held[4][...], branch[:, at(t)]).astype(low)
            elif kind == 1:
                wide_out[slot] = dot_first(tall_in[slot], grad_raw[...]).astype(low)
            else:
                found = dot_last(grad_raw[...], mix_in[slot, :, :wide])
                scaled = tall_in[slot].astype(f32) * inverse[...]
                grad_gain[:, at(t)] = jnp.sum(found * scaled, 0, keepdims=True)
                tall_out[slot] = found.astype(low)
            store(i).start()

        def end():
            for i in (3 * tiles - 2, 3 * tiles - 1):
                store(i).wait()

        jobs = [functools.partial(tile, i) for i in range(3 * tiles)]
        back = attend_back_steps(
            *held[:4], grad_mixed, *ins[13:], *held[5:7], grad_raw, gains, *work
        )
        start = [functools.partial(relay, k) for k in range(CHUNKS)] + [arrived]
        start += [functools.partial(mixed_grad, t) for t in range(span // BLOCK)]
        return [begin] + start + back + jobs + [end]

    return Extra(
        whole + streamed + small,
        [space] * 13 + [vmem] * 4,
        [
            jax.ShapeDtypeStruct((2, HEAD_SIZE), f32),
            jax.ShapeDtypeStruct((span, width), low),
            jax.ShapeDtypeStruct((width, wide), low),
            jax.ShapeDtypeStruct((length, width), low),
            jax.ShapeDtypeStruct((1, width), f32),
        ],
        [vmem, space, space, space, vmem],
        [pltpu.VMEM(a.shape, a.dtype) for a in whole]
        + [
            pltpu.SemaphoreType.DMA((8,)),
            pltpu.VMEM(raw.shape, low),
            pltpu.VMEM((length, BLOCK), f32),
            pltpu.VMEM((HEAD_SIZE, length), low),
            pltpu.VMEM((length, HEAD_SIZE), f32),
            pltpu.VMEM((length, HEAD_SIZE), f32),
            pltpu.VMEM((2, 8, HEAD_SIZE), f32),
            pltpu.VMEM((2, length, BLOCK), low),
            pltpu.VMEM((2, length, BLOCK), low),
            pltpu.VMEM((2, BLOCK, wide), low),
            pltpu.SemaphoreType.DMA((3, 2)),
            pltpu.VMEM((length, width), low),
            pltpu.VMEM((length, span), low),
            pltpu.VMEM((2, BLOCK, width), low),
            pltpu.SemaphoreType.DMA((2 + CHUNKS,)),
            pltpu.SemaphoreType.DMA((CHUNKS,)),
            pltpu.SemaphoreType.DMA((CHUNKS,)),
            pltpu.SemaphoreType.DMA((2, CHUNKS)),
            pltpu.SemaphoreType.DMA((2, CHUNKS)),
        ],
        steps,
    )


def weight_grads(rows, grads, inner, grad_a, grad_b):
    count, width = rows.shape
    inside = inner.shape[1]
    low, f32 = jnp.bfloat16, jnp.float32
    space = pl.BlockSpec(memory_space=pl.ANY)
    tiles = width // BLOCK

    def dot_first(a, b):
        return lax.dot_general(a, b, (((0,), (0,)), ((), ())), preferred_element_type=f32)

    def steps(*refs):
        ins, outs, scratch = split(refs, (5, 3, 9))
        a_held, b_held, inner_held, tile, wide, tall, in_sems, tile_sems, out_sems = scratch
        copies = load([(ins[3], a_held), (ins[4], b_held), (ins[2], inner_held)], in_sems)

        def fetch(i):
            source = ins[0] if i < tiles else ins[1]
            columns = pl.ds((i % tiles) * BLOCK, BLOCK)
            return pltpu.make_async_copy(source.at[:, columns], tile.at[i % 2], tile_sems.at[i % 2])

        def store(i, k):
            at = pl.ds((i % tiles) * BLOCK, BLOCK)
            if i < tiles:
                return pltpu.make_async_copy(wide.at[k, i % 2], outs[k].at[at], out_sems.at[k, i % 2])
            return pltpu.make_async_copy(tall.at[i % 2], outs[2].at[:, at], out_sems.at[2, i % 2])

        def begin():
            fetch(0).start()
            for copy in copies:
                copy.wait()

        def prepare(i):
            fetch(i).wait()
            if i + 1 < 2 * tiles:
                fetch(i + 1).start()

        def first(i, k):
            if k == 0:
                prepare(i)
            if i >= 2:
                store(i - 2, k).wait()
            wide[k, i % 2] = dot_first(tile[i % 2], (a_held, b_held)[k][...])
            store(i, k).start()

        def second(i):
            prepare(i)
            if i >= tiles + 2:
                store(i - 2, 2).wait()
            tall[i % 2] = dot_first(inner_held[...], tile[i % 2])
            store(i, 2).start()

        def end():
            for i in (tiles - 2, tiles - 1):
                store(i, 0).wait()
                store(i, 1).wait()
            for i in (2 * tiles - 2, 2 * tiles - 1):
                store(i, 2).wait()

        found = [begin]
        for i in range(tiles):
            found += [functools.partial(first, i, 0), functools.partial(first, i, 1)]
        for i in range(tiles, 2 * tiles):
            found.append(functools.partial(second, i))
        return found + [end]

    return Extra(
        (rows, grads, inner, grad_a, grad_b),
        [space] * 5,
        [
            jax.ShapeDtypeStruct((width, inside), f32),
            jax.ShapeDtypeStruct((width, inside), f32),
            jax.ShapeDtypeStruct((inside, width), f32),
        ],
        [space] * 3,
        [
            pltpu.VMEM((count, inside), low),
            pltpu.VMEM((count, inside), low),
            pltpu.VMEM((count, inside), low),
            pltpu.VMEM((2, count, BLOCK), low),
            pltpu.VMEM((2, 2, BLOCK, inside), f32),
            pltpu.VMEM((2, inside, BLOCK), f32),
            pltpu.SemaphoreType.DMA((3,)),
            pltpu.SemaphoreType.DMA((2,)),
            pltpu.SemaphoreType.DMA((3, 2)),
        ],
        steps,
    )


def gated_results(inner, w_down):
    count, inside = inner.shape
    width = w_down.shape[1]
    low = jnp.bfloat16
    space = pl.BlockSpec(memory_space=pl.ANY)
    tiles = width // BLOCK

    def steps(*refs):
        ins, outs, scratch = split(refs, (2, 1, 6))
        inner_held, down, result, in_sems, down_sems, result_sems = scratch
        copies = load([(ins[0], inner_held)], in_sems)

        def down_of(i):
            columns = pl.ds(i * BLOCK, BLOCK)
            return pltpu.make_async_copy(ins[1].at[:, columns], down.at[i % 2], down_sems.at[i % 2])

        def result_of(i):
            columns = pl.ds(i * BLOCK, BLOCK)
            return pltpu.make_async_copy(
                result.at[i % 2], outs[0].at[:, columns], result_sems.at[i % 2]
            )

        def third(i):
            if i == 0:
                down_of(0).start()
                copies[0].wait()
            down_of(i).wait()
            if i + 1 < tiles:
                down_of(i + 1).start()
            if i >= 2:
                result_of(i - 2).wait()
            result[i % 2] = dot(inner_held[...], down[i % 2]).astype(low)
            result_of(i).start()

        def end():
            result_of(tiles - 2).wait()
            result_of(tiles - 1).wait()

        return [functools.partial(third, i) for i in range(tiles)] + [end]

    return Extra(
        (inner, w_down),
        [space] * 2,
        [jax.ShapeDtypeStruct((count, width), low)],
        [space],
        [
            pltpu.VMEM(inner.shape, low),
            pltpu.VMEM((2, inside, BLOCK), low),
            pltpu.VMEM((2, count, BLOCK), low),
            pltpu.SemaphoreType.DMA((1,)),
            pltpu.SemaphoreType.DMA((2,)),
            pltpu.SemaphoreType.DMA((2,)),
        ],
        steps,
    )


WIDE = 512


def dispatch_expert_kernel(
    dims, tok, sel, small, grads, picks, ids, w_gate, w_up, w_down,
    small_all, rows_out, inner, grad_a, grad_b, grad_rows, gate_grad,
    held, stage, picked, arrive, leave, pick_out, pick_in, local, small_out, small_in,
    gates, weights_in, gate_held, up_held, down_held, g_held, g_in,
    inner_s, a_s, b_s, rows_s, store_sems, keep_sems,
):
    experts, shards = dims
    low, f32 = jnp.bfloat16, jnp.float32
    place = Place()
    width = tok.shape[1]
    near, far = place.line()
    mine = (place.x, place.y)
    me = place.e * shards + place.f
    greet_all(place, *dims)
    end_small = exchange_small(
        place, dims, lambda i: small, small_all, small_out, small_in, local.at[1]
    )
    keep = pltpu.make_async_copy(tok, held.at[place.z], local.at[0])
    keep.start()
    loads = load([(w_gate.at[0], gate_held), (w_up.at[0], up_held), (w_down.at[0], down_held)], weights_in)
    pending = []
    targets = (place.device("c"), place.at(far, place.c), place.at(far, 1 - place.c))
    half = tok.shape[0] // HALVES

    def pick(ar, zs):
        block = ar * 4 + zs
        number = block_number(mine, place.c, ar, zs)

        def tile(i, carry):
            columns = pl.ds(pl.multiple_of(i * WIDE, WIDE), WIDE)
            chosen = dot(sel[block], held[block, :, columns]).astype(low)
            picked[number, :, columns] = chosen[:SLOTS]
            stage[block, :, columns] = chosen[SLOTS:]
            return carry

        lax.fori_loop(0, width // WIDE, tile, 0)
        for k in (2, 1, 0):
            away = remote(
                stage.at[block, pl.ds(k * SLOTS, SLOTS)], picked.at[number],
                pick_out.at[block, k], pick_in.at[number], targets[k],
            )
            away.start()
            pending.append((None, away))

    def wait_rows(i):
        xs, cs, ys = i // 16, i // 8 % 2, i % 2
        inside = (cs == place.c) & jnp.where(place.c == 0, ys == place.y, xs == place.x)

        @pl.when(~inside)
        def _():
            window = picked.at[i]
            remote(window, window, pick_out.at[0, 0], pick_in.at[i], place.device("c")).wait_recv()

    def sources(n):
        first = n % 2 * 16 + place.ranked(n // 2) * 2
        return first, first + 8

    def grads_of(n):
        return [
            pltpu.make_async_copy(
                grads.at[pl.ds(first, 2)], g_held.at[n % 2, pl.ds(2 * k, 2)], g_in.at[n % 2, k]
            )
            for k, first in enumerate(sources(n))
        ]

    kept = []
    for copy in grads_of(0):
        copy.start()

    def stores(n):
        pairs = ((inner_s, inner), (a_s, grad_a), (b_s, grad_b), (rows_s, grad_rows))
        return [
            pltpu.make_async_copy(
                source.at[pl.ds(2 * k, 2)], target.at[pl.ds(first, 2)], store_sems.at[i, k]
            )
            for i, (source, target) in enumerate(pairs)
            for k, first in enumerate(sources(n))
        ]

    def compute(n):
        first, second = sources(n)
        from_devices = (first, first + 1, second, second + 1)
        if n == 0:
            end_small()
            copy = pltpu.make_async_copy(small_all, gates, local.at[2])
            copy.start()
            for done in loads:
                done.wait()
            copy.wait()
        if n + 1 < 8:
            for copy in grads_of(n + 1):
                copy.start()
        for i in from_devices:
            wait_rows(i)
        for k, start in enumerate((first, second)):
            copy = pltpu.make_async_copy(
                picked.at[pl.ds(start, 2)], rows_out.at[pl.ds(start, 2)], keep_sems.at[n, k]
            )
            copy.start()
            kept.append(copy)
        here = []
        for i in from_devices:
            value = jnp.sum(jnp.where(ids[i] == me, gates[i], 0.0), 0, keepdims=True)
            here.append(jnp.sum(picks[i].astype(f32) * value, -1, keepdims=True))
        here = jnp.concatenate(here, 0)
        count = 4 * SLOTS
        x = jnp.concatenate([picked[i] for i in from_devices], 0)
        a = dot(x, gate_held[...])
        b = dot(x, up_held[...])
        sigmoid = jax.nn.sigmoid(a)
        active = a * sigmoid
        into_a = b * (sigmoid * (1.0 + a * (1.0 - sigmoid)))
        for copy in grads_of(n):
            copy.wait()
        if n:
            for copy in stores(n - 1):
                copy.wait()
        back = dot_last(g_held[n % 2].reshape(count, width), down_held[...])
        product = active * b
        found = jnp.sum(product * back, -1, keepdims=True)
        for k, i in enumerate(from_devices):
            part = picks[i].astype(f32) * found[k * SLOTS : (k + 1) * SLOTS]
            gate_grad[i] = jnp.broadcast_to(jnp.sum(part, 0, keepdims=True), gate_grad.shape[1:])
        inner_s[...] = (product * here).astype(low).reshape(inner_s.shape)
        back = back * here
        a_s[...] = (back * into_a).astype(low).reshape(a_s.shape)
        b_s[...] = (back * active).astype(low).reshape(b_s.shape)

        def backward(t, carry):
            columns = pl.ds(pl.multiple_of(t * WIDE, WIDE), WIDE)
            total = dot_last(a_s[...].reshape(count, -1), gate_held[columns])
            total += dot_last(b_s[...].reshape(count, -1), up_held[columns])
            rows_s[:, :, columns] = total.astype(low).reshape(4, SLOTS, WIDE)
            return carry

        lax.fori_loop(0, width // WIDE, backward, 0)
        for copy in stores(n):
            copy.start()

    work = {3: (0,), 4: (1,), 5: (2,), 6: (3, 4), 7: (5, 6, 7)}
    for event, (ar, j) in enumerate(FAR_FIRST[::-1]):
        zs = place.ranked(j)
        block = ar * 4 + zs
        for h in range(HALVES):
            part = pl.ds(h * half, half)
            window = held.at[block, part]
            if ar or j:
                remote(
                    window, window, leave.at[zs, 0, h], arrive.at[block, h], place.device("c")
                ).wait_recv()
            if ar:
                continue
            source = tok.at[part] if j == 0 else window
            onward = (
                (UP, zs, 0, (zs <= place.z) & (place.z < 3)),
                (DOWN, zs, 1, (zs >= place.z) & (place.z > 0)),
                ("near", 4 + zs, 2, None),
            )
            for axis, there, k, condition in onward:
                device = place.at(near, place.c) if axis == "near" else place.device(axis)
                copy = remote(
                    source, held.at[there, part], leave.at[zs, k, h], arrive.at[there, h], device
                )
                run(condition, copy.start)
                pending.append((condition, copy))
        if not ar and j == 0:
            keep.wait()
        pick(ar, zs)
        for n in work.get(event, ()):
            compute(n)
    for copy in stores(7):
        copy.wait()
    for copy in kept:
        copy.wait()
    for condition, copy in pending:
        run(condition, copy.wait_send)


def dispatch_expert(experts, shards, number, tok, sel, small, grads, picks, ids, w_gate, w_up, w_down):
    rows, width = tok.shape
    devices = experts * shards
    inside = w_gate.shape[2]
    space = pl.BlockSpec(memory_space=pl.ANY)
    vmem = pl.BlockSpec(memory_space=pltpu.VMEM)
    dma = pltpu.SemaphoreType.DMA
    low, f32 = jnp.bfloat16, jnp.float32

    def lots(columns):
        return jax.ShapeDtypeStruct((devices, SLOTS, columns), low)

    def some(columns):
        return pltpu.VMEM((4, SLOTS, columns), low)

    return pl.pallas_call(
        functools.partial(dispatch_expert_kernel, (experts, shards)),
        out_shape=[
            jax.ShapeDtypeStruct((devices,) + small.shape, f32),
            lots(width), lots(inside), lots(inside), lots(inside), lots(width),
            jax.ShapeDtypeStruct((devices, 8, rows), f32),
        ],
        in_specs=[space, vmem, space, space, vmem, vmem, space, space, space],
        out_specs=[space] * 6 + [vmem],
        scratch_shapes=[
            pltpu.VMEM((8, rows, width), low),
            pltpu.VMEM((8, 3 * SLOTS, width), low),
            pltpu.VMEM((devices, SLOTS, width), low),
            dma((8, HALVES)),
            dma((4, 3, HALVES)),
            dma((8, 3)),
            dma((devices,)),
            dma((3,)),
            dma((devices,)),
            dma((devices,)),
            pltpu.VMEM((devices,) + small.shape, f32),
            dma((3,)),
            pltpu.VMEM(w_gate.shape[1:], low),
            pltpu.VMEM(w_up.shape[1:], low),
            pltpu.VMEM(w_down.shape[1:], low),
            pltpu.VMEM((2, 4, SLOTS, width), low),
            dma((2, 2)),
            some(inside), some(inside), some(inside), some(width),
            dma((4, 2)),
            dma((8, 2)),
        ],
        compiler_params=pltpu.CompilerParams(
            collective_id=number, has_side_effects=True, vmem_limit_bytes=62 * 2**20
        ),
        name="dispatch_expert",
    )(tok, sel, small, grads, picks, ids, w_gate, w_up, w_down)


def local(
    layer_input,
    doc_ids,
    expert_ids,
    w_query,
    w_key,
    w_value,
    w_out,
    w_router,
    gain_attn,
    gain_ffn,
    gain_query,
    gain_key,
    w_gate,
    w_up,
    w_down,
    grad_output,
):
    single_float = jnp.float32
    brain_float_half = jnp.bfloat16
    row_count = layer_input.shape[1]
    width = layer_input.shape[2]
    length_total = doc_ids.shape[1]
    query_groups = QUERY_HEADS // KEY_VALUE_HEADS
    scale = HEAD_SIZE ** (-0.5)
    experts = w_router.shape[1]
    capacity = max(2, 6 * row_count * TOP // (5 * experts))
    pairs = row_count * TOP
    (
        full_query,
        gathered_key,
        full_value,
        full_out,
        full_router,
        gain_one,
        gain_two,
        gain_q,
        key_gain_vector,
    ) = (
        lax.all_gather(w_query, FSDP, axis=0, tiled=True),
        lax.all_gather(w_key, FSDP, axis=0, tiled=True),
        lax.all_gather(w_value, FSDP, axis=0, tiled=True),
        lax.all_gather(w_out, FSDP, axis=0, tiled=True),
        lax.all_gather(w_router, FSDP, axis=0, tiled=True),
        lax.all_gather(gain_attn, FSDP, axis=0, tiled=True),
        lax.all_gather(gain_ffn, FSDP, axis=0, tiled=True),
        lax.all_gather(gain_query, FSDP, axis=0, tiled=True),
        lax.all_gather(gain_key, FSDP, axis=0, tiled=True),
    )
    gain_one = gain_one.astype(single_float)
    gain_two = gain_two.astype(single_float)
    gain_q = gain_q.astype(single_float)
    key_gain_vector = key_gain_vector.astype(single_float)
    inputs = layer_input[0].astype(single_float)
    offset = lax.axis_index(EXPERT) * row_count
    own_pos = offset + jnp.arange(row_count, dtype=jnp.int32)
    all_pos = jnp.arange(length_total, dtype=jnp.int32)
    seq_ids = doc_ids[0]
    own_ids = lax.dynamic_slice_in_dim(seq_ids, offset, row_count)
    allowed = (own_ids[:, None] == seq_ids[None, :]) & (own_pos[:, None] >= all_pos[None, :])
    cosine_table, sine_table = angles(own_pos)
    cosine_table = cosine_table[:, None, :]
    sine_table = sine_table[:, None, :]
    scale_one = inverse_rms(inputs)
    normalized_input = (inputs * scale_one * gain_one).astype(brain_float_half)
    query_raw = jnp.dot(normalized_input, full_query, preferred_element_type=single_float).reshape(
        row_count, QUERY_HEADS, HEAD_SIZE
    )
    key_unnormalized = jnp.dot(
        normalized_input, gathered_key, preferred_element_type=single_float
    ).reshape(row_count, KEY_VALUE_HEADS, HEAD_SIZE)
    value_low = jnp.dot(normalized_input, full_value, preferred_element_type=single_float).astype(
        brain_float_half
    )
    query_scale = inverse_rms(query_raw)
    key_norm_scale = inverse_rms(key_unnormalized)
    query_rot = (
        apply_rotary(query_raw * query_scale * gain_q, cosine_table, sine_table)
        .astype(brain_float_half)
        .reshape(row_count, KEY_VALUE_HEADS, query_groups, HEAD_SIZE)
    )
    key_rotated = apply_rotary(
        key_unnormalized * key_norm_scale * key_gain_vector, cosine_table, sine_table
    ).astype(brain_float_half)
    key_gathered_rows, value_gathered_rows = (
        lax.all_gather(
            key_rotated.reshape(row_count, KEY_VALUE_HEADS * HEAD_SIZE),
            EXPERT,
            axis=0,
            tiled=True,
        ),
        lax.all_gather(value_low, EXPERT, axis=0, tiled=True),
    )
    key_gathered_rows = key_gathered_rows.reshape(length_total, KEY_VALUE_HEADS, HEAD_SIZE)
    value_gathered_rows = value_gathered_rows.reshape(length_total, KEY_VALUE_HEADS, HEAD_SIZE)

    def masked_scores():
        raw = (
            jnp.einsum(
                "tkgd,skd->kgts", query_rot, key_gathered_rows, preferred_element_type=single_float
            )
            * scale
        )
        return jnp.where(allowed, raw, -1e30)

    scores = masked_scores()
    peak = jnp.max(scores, -1, keepdims=True)
    shifted = jnp.exp(scores - peak)
    totals = jnp.sum(shifted, -1, keepdims=True)
    weights_low = (shifted / totals).astype(brain_float_half)
    log_total = peak + jnp.log(totals)
    mixed = (
        jnp.einsum(
            "kgts,skd->tkgd", weights_low, value_gathered_rows, preferred_element_type=single_float
        )
        .reshape(row_count, QUERY_HEADS * HEAD_SIZE)
        .astype(brain_float_half)
    )
    hidden = inputs + jnp.dot(mixed, full_out, preferred_element_type=single_float)
    scale_two = inverse_rms(hidden)
    normed_two = (hidden * scale_two * gain_two).astype(brain_float_half)
    logits = jnp.dot(normed_two, full_router, preferred_element_type=single_float)
    selector = (expert_ids[0][:, :, None] == jnp.arange(experts, dtype=jnp.int32)).astype(
        single_float
    )
    chosen = jnp.einsum("tke,te->tk", selector, logits, precision=HIGHEST)
    gates = jax.nn.softmax(chosen, -1)
    flat_routes = expert_ids[0].reshape(pairs)
    hits = (flat_routes[:, None] == jnp.arange(experts, dtype=jnp.int32)).astype(jnp.int32)
    before = jnp.cumsum(hits, 0) - hits
    ranks = jnp.sum(before * hits, 1)
    slot_index = flat_routes * capacity + ranks
    owner_rows = jnp.arange(pairs, dtype=jnp.int32) // TOP
    outgoing = (
        jnp.zeros((experts * capacity, width), brain_float_half)
        .at[slot_index]
        .set(normed_two[owner_rows])
    )
    arrived = lax.all_to_all(
        outgoing.reshape(experts, capacity, width),
        (EXPERT, FSDP),
        split_axis=0,
        concat_axis=0,
        tiled=True,
    ).reshape(experts * capacity, width)
    gate_pre = jnp.dot(arrived, w_gate[0], preferred_element_type=single_float)
    up_pre = jnp.dot(arrived, w_up[0], preferred_element_type=single_float)
    activated = jax.nn.silu(gate_pre)
    inner = (activated * up_pre).astype(brain_float_half)
    result = jnp.dot(inner, w_down[0], preferred_element_type=single_float).astype(brain_float_half)
    returned = lax.all_to_all(
        result.reshape(experts, capacity, width),
        (EXPERT, FSDP),
        split_axis=0,
        concat_axis=0,
        tiled=True,
    ).reshape(experts * capacity, width)
    expert_rows = returned[slot_index].astype(single_float).reshape(row_count, TOP, width)
    output = hidden + jnp.einsum("tk,tkd->td", gates, expert_rows, precision=HIGHEST)
    grad_top = grad_output[0]
    grad_gates = jnp.einsum("tkd,td->tk", expert_rows, grad_top, precision=HIGHEST)
    grad_pairs = (
        (gates[:, :, None] * grad_top[:, None, :]).astype(brain_float_half).reshape(pairs, width)
    )
    grad_send = (
        jnp.zeros((experts * capacity, width), brain_float_half).at[slot_index].set(grad_pairs)
    )
    grad_arrived = lax.all_to_all(
        grad_send.reshape(experts, capacity, width),
        (EXPERT, FSDP),
        split_axis=0,
        concat_axis=0,
        tiled=True,
    ).reshape(experts * capacity, width)
    grad_down = jnp.einsum("rf,rd->fd", inner, grad_arrived, preferred_element_type=single_float)
    grad_inner = jnp.einsum(
        "rd,fd->rf", grad_arrived, w_down[0], preferred_element_type=single_float
    )
    sigmoid_gate = jax.nn.sigmoid(gate_pre)
    slope = sigmoid_gate * (1.0 + gate_pre * (1.0 - sigmoid_gate))
    grad_gate_pre = (grad_inner * up_pre * slope).astype(brain_float_half)
    grad_up_pre = (grad_inner * activated).astype(brain_float_half)
    grad_gate_w = jnp.einsum(
        "rd,rf->df", arrived, grad_gate_pre, preferred_element_type=single_float
    )
    grad_up_w = jnp.einsum("rd,rf->df", arrived, grad_up_pre, preferred_element_type=single_float)
    grad_rows = (
        jnp.einsum("rf,df->rd", grad_gate_pre, w_gate[0], preferred_element_type=single_float)
        + jnp.einsum("rf,df->rd", grad_up_pre, w_up[0], preferred_element_type=single_float)
    ).astype(brain_float_half)
    grad_back = lax.all_to_all(
        grad_rows.reshape(experts, capacity, width),
        (EXPERT, FSDP),
        split_axis=0,
        concat_axis=0,
        tiled=True,
    ).reshape(experts * capacity, width)
    grad_normed_two = jnp.sum(
        grad_back[slot_index].astype(single_float).reshape(row_count, TOP, width), 1
    )
    grad_chosen = gates * (grad_gates - jnp.sum(gates * grad_gates, -1, keepdims=True))
    grad_logits = jnp.einsum("tke,tk->te", selector, grad_chosen, precision=HIGHEST).astype(
        brain_float_half
    )
    grad_normed_two = grad_normed_two + jnp.einsum(
        "te,de->td", grad_logits, full_router, preferred_element_type=single_float
    )
    grad_router = jnp.einsum(
        "td,te->de", normed_two, grad_logits, preferred_element_type=single_float
    )
    grad_gain_two = jnp.sum(grad_normed_two * hidden * scale_two, 0)
    grad_hidden = grad_top + norm_backward(grad_normed_two, hidden, scale_two, gain_two)
    grad_branch = grad_hidden.astype(brain_float_half)
    grad_out_w = jnp.einsum("tq,td->qd", mixed, grad_branch, preferred_element_type=single_float)
    grad_mixed = (
        jnp.einsum("td,qd->tq", grad_branch, full_out, preferred_element_type=single_float)
        .astype(brain_float_half)
        .reshape(row_count, KEY_VALUE_HEADS, query_groups, HEAD_SIZE)
    )
    again = masked_scores()
    weights = jnp.exp(again - log_total)
    weights_again = weights.astype(brain_float_half)
    grad_weights = jnp.einsum(
        "tkgd,skd->kgts", grad_mixed, value_gathered_rows, preferred_element_type=single_float
    )
    spread = jnp.sum(weights * grad_weights, -1, keepdims=True)
    grad_scores = (weights * (grad_weights - spread)).astype(brain_float_half)
    grad_query_rot = (
        jnp.einsum(
            "kgts,skd->tkgd", grad_scores, key_gathered_rows, preferred_element_type=single_float
        )
        * scale
    ).reshape(row_count, QUERY_HEADS, HEAD_SIZE)
    grad_key_all = (
        jnp.einsum("kgts,tkgd->skd", grad_scores, query_rot, preferred_element_type=single_float)
        * scale
    ).reshape(length_total, KEY_VALUE_HEADS * HEAD_SIZE)
    grad_value_all = jnp.einsum(
        "kgts,tkgd->skd", weights_again, grad_mixed, preferred_element_type=single_float
    ).reshape(length_total, KEY_VALUE_HEADS * HEAD_SIZE)
    gradient_key_rotated, grad_value = (
        lax.psum_scatter(
            grad_key_all.astype(jnp.bfloat16), EXPERT, scatter_dimension=0, tiled=True
        ).astype(jnp.float32),
        lax.psum_scatter(
            grad_value_all.astype(jnp.bfloat16), EXPERT, scatter_dimension=0, tiled=True
        ).astype(jnp.float32),
    )
    gradient_key_rotated = gradient_key_rotated.reshape(row_count, KEY_VALUE_HEADS, HEAD_SIZE)
    grad_query_unit = unrotate(grad_query_rot, cosine_table, sine_table)
    gradient_key_normalized = unrotate(gradient_key_rotated, cosine_table, sine_table)
    grad_gain_q = jnp.sum(grad_query_unit * query_raw * query_scale, (0, 1))
    grad_gain_k = jnp.sum(gradient_key_normalized * key_unnormalized * key_norm_scale, (0, 1))
    grad_query = (
        norm_backward(grad_query_unit, query_raw, query_scale, gain_q)
        .reshape(row_count, QUERY_HEADS * HEAD_SIZE)
        .astype(brain_float_half)
    )
    grad_key = (
        norm_backward(gradient_key_normalized, key_unnormalized, key_norm_scale, key_gain_vector)
        .reshape(row_count, KEY_VALUE_HEADS * HEAD_SIZE)
        .astype(brain_float_half)
    )
    grad_value_low = grad_value.astype(brain_float_half)
    grad_query_w = jnp.einsum(
        "td,tq->dq", normalized_input, grad_query, preferred_element_type=single_float
    )
    grad_key_w = jnp.einsum(
        "td,tq->dq", normalized_input, grad_key, preferred_element_type=single_float
    )
    grad_value_w = jnp.einsum(
        "td,tq->dq", normalized_input, grad_value_low, preferred_element_type=single_float
    )
    grad_normed = (
        jnp.einsum("tq,dq->td", grad_query, full_query, preferred_element_type=single_float)
        + jnp.einsum("tq,dq->td", grad_key, gathered_key, preferred_element_type=single_float)
        + jnp.einsum("tq,dq->td", grad_value_low, full_value, preferred_element_type=single_float)
    )
    grad_gain_one = jnp.sum(grad_normed * inputs * scale_one, 0)
    grad_inputs = grad_hidden + norm_backward(grad_normed, inputs, scale_one, gain_one)
    local_grads = (
        grad_query_w,
        grad_key_w,
        grad_value_w,
        grad_out_w,
        grad_router,
        grad_gain_one,
        grad_gain_two,
        grad_gain_q,
        grad_gain_k,
    )
    shards = (
        lax.psum_scatter(
            local_grads[0].astype(jnp.bfloat16), FSDP, scatter_dimension=0, tiled=True
        ).astype(jnp.float32),
        lax.psum_scatter(
            local_grads[1].astype(jnp.bfloat16), FSDP, scatter_dimension=0, tiled=True
        ).astype(jnp.float32),
        lax.psum_scatter(
            local_grads[2].astype(jnp.bfloat16), FSDP, scatter_dimension=0, tiled=True
        ).astype(jnp.float32),
        lax.psum_scatter(
            local_grads[3].astype(jnp.bfloat16), FSDP, scatter_dimension=0, tiled=True
        ).astype(jnp.float32),
        lax.psum_scatter(
            local_grads[4].astype(jnp.bfloat16), FSDP, scatter_dimension=0, tiled=True
        ).astype(jnp.float32),
        lax.psum_scatter(
            local_grads[5].astype(jnp.bfloat16), FSDP, scatter_dimension=0, tiled=True
        ).astype(jnp.float32),
        lax.psum_scatter(
            local_grads[6].astype(jnp.bfloat16), FSDP, scatter_dimension=0, tiled=True
        ).astype(jnp.float32),
        lax.psum_scatter(
            local_grads[7].astype(jnp.bfloat16), FSDP, scatter_dimension=0, tiled=True
        ).astype(jnp.float32),
        lax.psum_scatter(
            local_grads[8].astype(jnp.bfloat16), FSDP, scatter_dimension=0, tiled=True
        ).astype(jnp.float32),
    )
    shards = (
        lax.psum(shards[0].astype(jnp.bfloat16), EXPERT).astype(jnp.float32),
        lax.psum(shards[1].astype(jnp.bfloat16), EXPERT).astype(jnp.float32),
        lax.psum(shards[2].astype(jnp.bfloat16), EXPERT).astype(jnp.float32),
        lax.psum(shards[3].astype(jnp.bfloat16), EXPERT).astype(jnp.float32),
        lax.psum(shards[4].astype(jnp.bfloat16), EXPERT).astype(jnp.float32),
        lax.psum(shards[5].astype(jnp.bfloat16), EXPERT).astype(jnp.float32),
        lax.psum(shards[6].astype(jnp.bfloat16), EXPERT).astype(jnp.float32),
        lax.psum(shards[7].astype(jnp.bfloat16), EXPERT).astype(jnp.float32),
        lax.psum(shards[8].astype(jnp.bfloat16), EXPERT).astype(jnp.float32),
    )
    return (
        output[None],
        grad_inputs[None],
        shards[0],
        shards[1],
        shards[2],
        shards[3],
        shards[4],
        shards[5],
        shards[6],
        shards[7],
        shards[8],
        grad_gate_w[None],
        grad_up_w[None],
        grad_down[None],
    )


def angle_tables(length):
    power = -(np.arange(HEAD_SIZE // 2, dtype=np.float32) * np.float32(2.0)) / np.float32(HEAD_SIZE)
    freq = np.power(np.float32(THETA), power).astype(np.float32)
    turns = np.arange(length, dtype=np.float32)[:, None] * freq[None, :]
    turns = np.concatenate([turns, turns], -1)
    return jnp.asarray(np.cos(turns)), jnp.asarray(np.sin(turns))


def packed(pieces, lead, rows):
    flat = jnp.concatenate([piece.reshape(lead, -1) for piece in pieces], 1)
    flat = jnp.pad(flat, ((0, 0), (0, rows * 128 - flat.shape[1])))
    return flat.reshape(lead, rows, 128)


def local_staged(
    layer_input,
    doc_ids,
    expert_ids,
    w_query,
    w_key,
    w_value,
    w_out,
    w_router,
    gain_attn,
    gain_ffn,
    gain_query,
    gain_key,
    w_gate,
    w_up,
    w_down,
    grad_output,
):
    f32 = jnp.float32
    low = jnp.bfloat16
    rows, width = layer_input.shape[1:]
    length = doc_ids.shape[1]
    depth = w_router.shape[0]
    groups, shards = lax.axis_size(EXPERT), lax.axis_size(FSDP)
    experts = w_router.shape[1]
    heads = QUERY_HEADS // groups
    span = heads * HEAD_SIZE
    mine = lax.axis_index(EXPERT)

    def columns(weight, count):
        return lax.dynamic_slice_in_dim(weight, mine * count, count, 1)

    flat = jnp.concatenate(
        [columns(w_query, span), columns(w_key, HEAD_SIZE), columns(w_value, HEAD_SIZE)], 1
    )
    pack = packed([w_router, gain_attn, gain_ffn, gain_query, gain_key], 1, 80)[0]
    w_qkv, w_mix, tokens, pack_all, ids_all, mine_picks, pick, spread, grad_top_low = gather(
        groups,
        shards,
        5,
        flat,
        w_out,
        layer_input[0],
        pack,
        expert_ids[0].T,
        grad_output[0],
    )
    w_qkv = w_qkv.reshape(width, span + 2 * HEAD_SIZE)
    w_mix = w_mix.reshape(span, width)
    tokens = tokens.reshape(length, width)
    pack_all = pack_all.reshape(shards, -1)
    at = depth * experts
    full_router = pack_all[:, :at].reshape(width, experts)
    gain_one = pack_all[:, at : at + depth].reshape(width).astype(f32)
    gain_two = pack_all[:, at + depth : at + 2 * depth].reshape(width).astype(f32)
    at += 2 * depth
    small = HEAD_SIZE // shards
    gain_q = pack_all[:, at : at + small].reshape(HEAD_SIZE).astype(f32)
    gain_k = pack_all[:, at + small : at + 2 * small].reshape(HEAD_SIZE).astype(f32)
    grad_top = grad_output[0]
    ids_column, ids_row = doc_ids[0][:, None], doc_ids[0][None, :]
    cosine, sine = angle_tables(length)
    gain_q, gain_k = gain_q[None], gain_k[None]
    attend = attention(
        tokens, w_qkv, gain_one[None], gain_q, gain_k, cosine, sine, ids_column, ids_row, heads
    )
    grads_in, normed_one, raw, query_rot, key_rot, value, mixed, inverses = dispatch(
        groups, shards, 1, grad_top_low, pick, extra=attend
    )
    inputs = layer_input[0].astype(f32)
    hidden = inputs + branch_scatter(8, mixed, w_mix)
    scale_two = inverse_rms(hidden)
    normed_two = (hidden * scale_two * gain_two).astype(low)
    logits = jnp.dot(normed_two, full_router, preferred_element_type=f32)
    selector = (expert_ids[0][:, :, None] == jnp.arange(experts, dtype=jnp.int32)).astype(f32)
    gates = jax.nn.softmax(jnp.sum(selector * logits[:, None, :], -1), -1)
    _, arrived, inner, grad_a, grad_b, grad_rows, gate_grads = dispatch_expert(
        groups, shards, 2, normed_two, pick, gates.T, grads_in, mine_picks, ids_all, w_gate, w_up, w_down
    )

    def flat_rows(blocks):
        return blocks.reshape(-1, blocks.shape[-1])

    grad_normed_two, gates_back, weighted = combine(
        groups,
        shards,
        3,
        grad_rows,
        spread,
        gate_grads,
        gated_results(flat_rows(inner), w_down[0]),
    )
    grad_gates = jnp.sum(selector * gates_back[:, 0].T[:, None, :], -1)
    grad_chosen = gates * (grad_gates - jnp.sum(gates * grad_gates, -1, keepdims=True))
    grad_logits = jnp.sum(selector * grad_chosen[:, :, None], 1).astype(low)
    grad_normed_two = grad_normed_two + jnp.einsum(
        "te,de->td", grad_logits, full_router, preferred_element_type=f32
    )
    grad_router = jnp.einsum("td,te->de", normed_two, grad_logits, preferred_element_type=f32)
    grad_gain_two = jnp.sum(grad_normed_two * hidden * scale_two, 0)
    grad_hidden = grad_top + norm_backward(grad_normed_two, hidden, scale_two, gain_two)
    back = attention_back(
        query_rot, key_rot, value, raw, mixed, grad_hidden.astype(low), w_mix, normed_one, tokens, w_qkv,
        inverses, ids_column, ids_row, gain_q, gain_k, cosine, sine,
    )
    combined, gain_grads, grad_mix, grad_qkv, grad_normed_one, grad_gain_one = combine(
        groups, shards, 4, weighted.reshape(experts, SLOTS, width), spread, extra=back
    )
    output = hidden + combined
    sums = [grad_router, grad_gain_one, grad_gain_two, gain_grads[0], gain_grads[1]]
    sums = packed(sums, shards, 16 * (span + 2 * HEAD_SIZE) // 128)
    sums = sums.reshape(shards, 16, -1).astype(low)
    (
        query_sum, key_sum, value_sum, tall_sum, pack_sum, grad_normed_one,
        grad_gate_w, grad_up_w, grad_down,
    ) = reduce(
        groups,
        shards,
        6,
        grad_qkv.reshape(shards, depth, -1),
        grad_mix.reshape(2, -1, width),
        sums,
        grad_normed_one.reshape(groups, rows, width),
        weight_grads(*(flat_rows(a) for a in (arrived, grads_in, inner, grad_a, grad_b))),
    )
    pack_sum = jnp.sum(pack_sum.astype(f32), 0).reshape(-1)
    scale_own = inverse_rms(inputs)
    grad_inputs = grad_hidden + norm_backward(grad_normed_one, inputs, scale_own, gain_one)
    at = depth * experts
    return (
        output[None],
        grad_inputs[None],
        query_sum.astype(f32),
        key_sum.astype(f32),
        value_sum.astype(f32),
        tall_sum.astype(f32),
        pack_sum[:at].reshape(depth, experts),
        pack_sum[at : at + depth],
        pack_sum[at + depth : at + 2 * depth],
        pack_sum[at + 2 * depth : at + 2 * depth + small],
        pack_sum[at + 2 * depth + small : at + 2 * depth + 2 * small],
        grad_gate_w[None],
        grad_up_w[None],
        grad_down[None],
    )


def solution(mesh):
    in_specs = (
        P(FSDP, EXPERT, None),
        P(FSDP, None),
        P(FSDP, EXPERT, None),
        P(FSDP, None),
        P(FSDP, None),
        P(FSDP, None),
        P(FSDP, None),
        P(FSDP, None),
        P(FSDP),
        P(FSDP),
        P(FSDP),
        P(FSDP),
        P((EXPERT, FSDP), None, None),
        P((EXPERT, FSDP), None, None),
        P((EXPERT, FSDP), None, None),
        P(FSDP, EXPERT, None),
    )
    out_specs = (
        P(FSDP, EXPERT, None),
        P(FSDP, EXPERT, None),
        P(FSDP, None),
        P(FSDP, None),
        P(FSDP, None),
        P(FSDP, None),
        P(FSDP, None),
        P(FSDP),
        P(FSDP),
        P(FSDP),
        P(FSDP),
        P((EXPERT, FSDP), None, None),
        P((EXPERT, FSDP), None, None),
        P((EXPERT, FSDP), None, None),
    )
    staged = mesh.shape[EXPERT] == 4 and mesh.shape[FSDP] == 8
    return jax.shard_map(local_staged if staged else local, mesh=mesh, in_specs=in_specs, out_specs=out_specs, check_vma=False)
```

```python
import functools

import jax
import jax.numpy as jnp
import numpy as np
from jax import lax
from jax.experimental import pallas as pl
from jax.experimental.pallas import tpu as pltpu
from jax.sharding import PartitionSpec as P

EXPERT = "expert"
FSDP = "fsdp"
UP, DOWN, ABOVE, BELOW = "up", "down", "above", "below"
QUERY_HEADS = 32
KEY_VALUE_HEADS = 4
HEAD_SIZE = 128
TOP = 8


EPS = 1e-06
THETA = 1000000.0
HIGHEST = lax.Precision.HIGHEST


def angles(positions):
    freq = THETA ** (-(jnp.arange(HEAD_SIZE // 2, dtype=jnp.float32) * 2.0) / HEAD_SIZE)
    turn = positions.astype(jnp.float32)[:, None] * freq[None, :]
    turn = jnp.concatenate([turn, turn], -1)
    return (jnp.cos(turn), jnp.sin(turn))


def apply_rotary(value_rows_local, cosine_table, sine_table):
    half = value_rows_local.shape[-1] // 2
    turned = jnp.concatenate([-value_rows_local[..., half:], value_rows_local[..., :half]], -1)
    return value_rows_local * cosine_table + turned * sine_table


def unrotate(grads, cosine_table, sine_table):
    half = grads.shape[-1] // 2
    scaled = grads * sine_table
    turned = jnp.concatenate([-scaled[..., half:], scaled[..., :half]], -1)
    return grads * cosine_table - turned


def inverse_rms(value_rows_local):
    return lax.rsqrt(jnp.mean(value_rows_local * value_rows_local, -1, keepdims=True) + EPS)


def norm_backward(grad, value_rows_local, inverse, gain):
    scaled = grad * gain
    return inverse * scaled - inverse * inverse * inverse * value_rows_local * jnp.mean(
        scaled * value_rows_local, -1, keepdims=True
    )


MESH = pl.DeviceIdType.MESH
SLOTS = 80
TILE = 512
FAR_FIRST = ((1, 3), (1, 2), (0, 3), (1, 1), (0, 2), (0, 1), (1, 0), (0, 0))
BACK = FAR_FIRST
AHEAD = 2
HALVES = 2
QUARTERS = 4


class Place:
    def __init__(self):
        self.e = lax.axis_index(EXPERT)
        self.f = lax.axis_index(FSDP)
        self.x, self.c = self.e // 2, self.e % 2
        self.z, self.y = self.f // 2, self.f % 2

    def device(self, axis):
        if axis == "c":
            return (self.x * 2 + 1 - self.c, self.f)
        if axis == "x":
            return ((1 - self.x) * 2 + self.c, self.f)
        if axis == "y":
            return (self.e, self.z * 2 + 1 - self.y)
        if axis == UP:
            return (self.e, jnp.minimum(self.z + 1, 3) * 2 + self.y)
        return (self.e, jnp.maximum(self.z - 1, 0) * 2 + self.y)

    def ranked(self, j):
        inner = (1, 0, 2, 3)[j]
        end = (self.z == 0) | (self.z == 3)
        low = jnp.where(end, j, inner)
        return jnp.where(self.z < 2, low, 3 - low)

    def line(self):
        x, y, even = self.x, self.y, self.c == 0
        near = (jnp.where(even, 1 - x, x), jnp.where(even, y, 1 - y))
        far = (jnp.where(even, x, 1 - x), jnp.where(even, 1 - y, y))
        return near, far

    def at(self, chip, core):
        return (chip[0] * 2 + core, self.z * 2 + chip[1])


def block_number(chip, core, ar, zs):
    x, y = chip
    xs = jnp.where(core == 0, 1 - x, x) if ar else x
    ys = jnp.where(core == 0, y, 1 - y) if ar else y
    return (xs * 2 + core) * 8 + zs * 2 + ys


def greet(place):
    barrier = pltpu.get_barrier_semaphore()
    beside = [place.device("c")]
    for chip in ((1 - place.x, place.y), (place.x, 1 - place.y)):
        beside += [place.at(chip, 0), place.at(chip, 1)]
    for device in beside:
        pl.semaphore_signal(barrier, 1, device_id=device, device_id_type=MESH)

    @pl.when(place.z < 3)
    def _():
        pl.semaphore_signal(barrier, 1, device_id=place.device(UP), device_id_type=MESH)

    @pl.when(place.z > 0)
    def _():
        pl.semaphore_signal(barrier, 1, device_id=place.device(DOWN), device_id_type=MESH)

    inner = (place.z > 0) & (place.z < 3)
    pl.semaphore_wait(barrier, len(beside) + jnp.where(inner, 2, 1))


def greet_all(place, experts, shards):
    barrier = pltpu.get_barrier_semaphore()
    count = experts * shards

    def one(i, carry):
        target = lax.rem(place.e * shards + place.f + i, count)
        pl.semaphore_signal(
            barrier, 1, device_id=(target // shards, lax.rem(target, shards)), device_id_type=MESH
        )
        return carry

    lax.fori_loop(1, count, one, 0)
    pl.semaphore_wait(barrier, count - 1)


def onward(path, j, xr, yr):
    differs = {"z": j > 0, "x": xr > 0, "y": yr > 0}
    last = -1
    for i, axis in enumerate(path):
        if differs[axis]:
            last = i
    out = []
    if last >= 0 and path[last] == "z":
        out.append("z+")
    for axis in path[last + 1 :]:
        out.append("z*" if axis == "z" else axis)
    return out


def links(place, path, j, xr, yr, zs):
    out = []
    for axis in onward(path, j, xr, yr):
        if axis == "z+":
            out.append((UP, (zs < place.z) & (place.z < 3)))
            out.append((DOWN, (zs > place.z) & (place.z > 0)))
        elif axis == "z*":
            out.append((UP, place.z < 3))
            out.append((DOWN, place.z > 0))
        else:
            out.append((axis, None))
    return out


def run(condition, action):
    if condition is None:
        action()
    else:
        pl.when(condition)(action)


LINK = {"x": 0, "y": 1, UP: 2, DOWN: 3}


def remote(src, dst, send_sem, recv_sem, device):
    return pltpu.make_async_remote_copy(
        src_ref=src,
        dst_ref=dst,
        send_sem=send_sem,
        recv_sem=recv_sem,
        device_id=device,
        device_id_type=MESH,
    )


class Side:
    def __init__(self, steps, events):
        self.steps, self.events = list(steps), events
        self.total, self.seen = len(self.steps), 0

    def event(self):
        self.seen += 1
        left = self.total - self.total * min(self.seen, self.events) // self.events
        while len(self.steps) > left:
            self.steps.pop(0)()


class Extra:
    def __init__(self, operands=(), in_specs=(), outs=(), out_specs=(), scratch=(), steps=None):
        self.operands, self.in_specs = list(operands), list(in_specs)
        self.outs, self.out_specs, self.scratch = list(outs), list(out_specs), list(scratch)
        self.steps = steps if steps is not None else lambda *refs: []


def split(refs, counts):
    out = []
    for count in counts:
        out.append(refs[:count])
        refs = refs[count:]
    return out


def exchange_small(place, dims, src_of, dst, sems_out, sems_in, sem):
    experts, shards = dims
    count = experts * shards
    me = place.e * shards + place.f
    keep = pltpu.make_async_copy(src_of(me), dst.at[me], sem)
    keep.start()

    def copy(i, sending):
        other = lax.rem(me + i, count)
        source = me if sending else other
        device = (other // shards, lax.rem(other, shards))
        return remote(src_of(other), dst.at[source], sems_out.at[i], sems_in.at[source], device)

    def start(i, carry):
        copy(i, True).start()
        return carry

    def finish(i, carry):
        done = copy(i, False)
        done.wait_send()
        done.wait_recv()
        return carry

    lax.fori_loop(1, count, start, 0)

    def end():
        keep.wait()
        lax.fori_loop(1, count, finish, 0)

    return end


def dispatch_kernel(dims, has_small, extra, *refs):
    counts = (
        2 + has_small, len(extra.operands), 1 + has_small, len(extra.outs), 7 + 3 * has_small,
        len(extra.scratch),
    )
    ins, more_in, outs, more_out, scratch, more_scratch = split(refs, counts)
    tok, sel = ins[:2]
    picked = outs[0]
    held, stage, arrive, leave, pick_out, pick_in, local = scratch[:7]
    place = Place()
    width = tok.shape[1]
    near, far = place.line()
    mine = (place.x, place.y)
    if has_small:
        greet_all(place, *dims)
        end_small = exchange_small(
            place, dims, lambda i: ins[2], outs[1], scratch[7], scratch[8], scratch[9].at[0]
        )
    else:
        greet(place)
    side = Side(extra.steps(*more_in, *more_out, *more_scratch), 8)
    keep = pltpu.make_async_copy(tok, held.at[place.z], local.at[8])
    keep.start()
    pending = []
    finish = []
    targets = (place.device("c"), place.at(far, place.c), place.at(far, 1 - place.c))

    def pick(ar, zs):
        block = ar * 4 + zs
        number = block_number(mine, place.c, ar, zs)

        def tile(i, carry):
            columns = pl.ds(pl.multiple_of(i * 512, 512), 512)
            stage[block, :, columns] = jnp.dot(
                sel[block], held[block, :, columns], preferred_element_type=jnp.float32
            ).astype(jnp.bfloat16)
            return carry

        lax.fori_loop(0, width // 512, tile, 0)
        for k in (2, 1, 0):
            away = remote(
                stage.at[block, pl.ds((k + 1) * SLOTS, SLOTS)], picked.at[number],
                pick_out.at[block, k], pick_in.at[number], targets[k],
            )
            away.start()
            finish.append(away)
        stay = pltpu.make_async_copy(
            stage.at[block, pl.ds(0, SLOTS)], picked.at[number], local.at[block]
        )
        stay.start()
        finish.append(stay)

    half = tok.shape[0] // HALVES
    for ar, j in FAR_FIRST[::-1]:
        zs = place.ranked(j)
        block = ar * 4 + zs
        for h in range(HALVES):
            part = pl.ds(h * half, half)
            window = held.at[block, part]
            if ar or j:
                remote(
                    window, window, leave.at[zs, 0, h], arrive.at[block, h], place.device("c")
                ).wait_recv()
            if ar:
                continue
            source = tok.at[part] if j == 0 else window
            onward = (
                (UP, zs, 0, (zs <= place.z) & (place.z < 3)),
                (DOWN, zs, 1, (zs >= place.z) & (place.z > 0)),
                ("near", 4 + zs, 2, None),
            )
            for axis, there, k, condition in onward:
                device = place.at(near, place.c) if axis == "near" else place.device(axis)
                copy = remote(
                    source, held.at[there, part], leave.at[zs, k, h], arrive.at[there, h], device
                )
                run(condition, copy.start)
                pending.append((condition, copy))
        if not ar and j == 0:
            keep.wait()
        pick(ar, zs)
        side.event()
    for condition, copy in pending:
        run(condition, copy.wait_send)

    def arrived(i, carry):
        xs, cs, ys = i // 16, i // 8 % 2, i % 2
        inside = (cs == place.c) & jnp.where(place.c == 0, ys == place.y, xs == place.x)

        @pl.when(~inside)
        def _():
            window = picked.at[i]
            remote(window, window, pick_out.at[0, 0], pick_in.at[i], place.device("c")).wait_recv()

        return carry

    lax.fori_loop(0, 32, arrived, 0)
    for k, copy in enumerate(finish):
        if k % 4 == 3:
            copy.wait()
        else:
            copy.wait_send()
    if has_small:
        end_small()


def dispatch(experts, shards, number, tok, sel, small=None, extra=None):
    rows, width = tok.shape
    devices = experts * shards
    extra = extra or Extra()
    space = pl.BlockSpec(memory_space=pl.ANY)
    vmem = pl.BlockSpec(memory_space=pltpu.VMEM)
    dma = pltpu.SemaphoreType.DMA
    has_small = int(small is not None)
    operands, in_specs = [tok, sel], [space, vmem]
    out_shape = [jax.ShapeDtypeStruct((devices, SLOTS, width), jnp.bfloat16)]
    scratch = [
        pltpu.VMEM((8, rows, width), jnp.bfloat16),
        pltpu.VMEM((8, 4 * SLOTS, width), jnp.bfloat16),
        dma((8, HALVES)),
        dma((4, 3, HALVES)),
        dma((8, 3)),
        dma((devices,)),
        dma((9,)),
    ]
    if has_small:
        operands.append(small)
        in_specs.append(space)
        out_shape.append(jax.ShapeDtypeStruct((devices,) + small.shape, small.dtype))
        scratch += [dma((devices,)), dma((devices,)), dma((1,))]
    return pl.pallas_call(
        functools.partial(dispatch_kernel, (experts, shards), has_small, extra),
        out_shape=out_shape + extra.outs,
        in_specs=in_specs + extra.in_specs,
        out_specs=[space] * len(out_shape) + extra.out_specs,
        scratch_shapes=scratch + extra.scratch,
        compiler_params=pltpu.CompilerParams(
            collective_id=number, has_side_effects=True, vmem_limit_bytes=60 * 2**20
        ),
        name="dispatch",
    )(*operands, *extra.operands)


def combine_kernel(dims, has_small, extra, *refs):
    counts = (
        2 + has_small, len(extra.operands), 1 + has_small, len(extra.outs), 10 + 3 * has_small,
        len(extra.scratch),
    )
    ins, more_in, outs, more_out, scratch, more_scratch = split(refs, counts)
    weighted, sel = ins[:2]
    total = outs[0]
    rows4, acc, beside, chain, rows_in, rows_out, beside_in, beside_out, chain_in, chain_out = scratch[:10]
    place = Place()
    width = total.shape[1]
    near, far = place.line()
    mine = (place.x, place.y)
    if has_small:
        greet_all(place, *dims)
        end_small = exchange_small(
            place, dims, lambda i: ins[2].at[i], outs[1], scratch[10], scratch[11], scratch[12].at[0]
        )
    else:
        greet(place)
    side = Side(extra.steps(*more_in, *more_out, *more_scratch), 8 * QUARTERS)
    other = 1 - place.c
    homes = ((mine, place.c), (mine, other), (far, place.c), (near, other))

    def row_copy(ar, zs, k):
        chip, core = homes[k]
        source = weighted.at[block_number(chip, core, ar, zs)]
        block = ar * 4 + zs
        window = rows4.at[block, pl.ds(k * SLOTS, SLOTS)]
        if k == 0:
            return pltpu.make_async_copy(source, window, rows_in.at[block, 0])
        return remote(
            source, window, rows_out.at[block, k - 1], rows_in.at[block, k], place.at(chip, core)
        )

    def send_rows(i):
        ar, j = BACK[i]
        for k in (2, 3, 1, 0):
            row_copy(ar, place.ranked(j), k).start()

    for i in range(AHEAD):
        send_rows(i)
    pending = []
    half = total.shape[0] // QUARTERS
    for i, (ar, j) in enumerate(BACK):
        zs = place.ranked(j)
        block = ar * 4 + zs
        for k in range(4):
            copy = row_copy(ar, zs, k)
            if k == 0:
                copy.wait()
            else:
                copy.wait_recv()
                copy.wait_send()
        if i + AHEAD < 8:
            send_rows(i + AHEAD)
        last = not ar and j == 0
        above = (zs <= place.z) & (place.z < 3)
        below = (zs >= place.z) & (place.z > 0)
        below_slot = jnp.where(zs == place.z, 4, zs)
        for h in range(QUARTERS):
            part = pl.ds(h * half, half)
            if not ar:
                window = beside.at[zs, part]
                remote(
                    window, window, beside_out.at[zs, h], beside_in.at[zs, h], place.device("c")
                ).wait_recv()
                for condition, slot in ((above, zs), (below, below_slot)):
                    window = chain.at[slot, part]
                    got = remote(
                        window, window, chain_out.at[0, h], chain_in.at[slot, h], place.device("c")
                    )
                    run(condition, got.wait_recv)

            def tile(t, carry):
                columns = pl.ds(pl.multiple_of(t * 512, 512), 512)
                dense = jnp.dot(
                    sel[block, part], rows4[block, :, columns], preferred_element_type=jnp.float32
                )
                if not ar:
                    dense = dense + beside[zs, part, columns].astype(jnp.float32)
                if last:
                    total[part, columns] = dense
                else:
                    acc[block, part, columns] = dense.astype(jnp.bfloat16)
                return carry

            lax.fori_loop(0, width // 512, tile, 0)
            if not ar:

                def add(slot):
                    def step(t, carry):
                        here = pl.ds(pl.multiple_of(h * half + t * 16, 16), 16)
                        more = chain[slot, here].astype(jnp.float32)
                        if last:
                            total[here] += more
                        else:
                            acc[block, here] = (acc[block, here].astype(jnp.float32) + more).astype(
                                jnp.bfloat16
                            )
                        return carry

                    lax.fori_loop(0, half // 16, step, 0)

                run(above, functools.partial(add, zs))
                run(below, functools.partial(add, below_slot))
            if ar:
                copy = remote(
                    acc.at[block, part], beside.at[zs, part], beside_out.at[zs, h],
                    beside_in.at[zs, h], place.at(near, place.c),
                )
                copy.start()
                pending.append((None, copy))
            elif not last:
                there = jnp.where(zs == place.z + 1, 4, zs)
                for condition, axis, slot in (
                    (zs < place.z, DOWN, zs),
                    (zs > place.z, UP, there),
                ):
                    copy = remote(
                        acc.at[block, part], chain.at[slot, part], chain_out.at[zs, h],
                        chain_in.at[slot, h], place.device(axis),
                    )
                    run(condition, copy.start)
                    pending.append((condition, copy))
            side.event()
    for condition, copy in pending:
        run(condition, copy.wait_send)
    if has_small:
        end_small()


def combine(experts, shards, number, weighted, sel, small=None, extra=None):
    rows = sel.shape[1]
    width = weighted.shape[-1]
    devices = experts * shards
    extra = extra or Extra()
    space = pl.BlockSpec(memory_space=pl.ANY)
    vmem = pl.BlockSpec(memory_space=pltpu.VMEM)
    dma = pltpu.SemaphoreType.DMA
    low = jnp.bfloat16
    has_small = int(small is not None)
    operands, in_specs = [weighted, sel], [space, vmem]
    out_shape, out_specs = [jax.ShapeDtypeStruct((rows, width), jnp.float32)], [vmem]
    scratch = [
        pltpu.VMEM((8, 4 * SLOTS, width), low),
        pltpu.VMEM((8, rows, width), low),
        pltpu.VMEM((4, rows, width), low),
        pltpu.VMEM((5, rows, width), low),
        dma((8, 4)),
        dma((8, 3)),
        dma((4, QUARTERS)),
        dma((4, QUARTERS)),
        dma((5, QUARTERS)),
        dma((4, QUARTERS)),
    ]
    if has_small:
        operands.append(small)
        in_specs.append(space)
        out_shape.append(jax.ShapeDtypeStruct(small.shape, small.dtype))
        out_specs.append(space)
        scratch += [dma((devices,)), dma((devices,)), dma((1,))]
    return pl.pallas_call(
        functools.partial(combine_kernel, (experts, shards), has_small, extra),
        out_shape=out_shape + extra.outs,
        in_specs=in_specs + extra.in_specs,
        out_specs=out_specs + extra.out_specs,
        scratch_shapes=scratch + extra.scratch,
        compiler_params=pltpu.CompilerParams(
            collective_id=number, has_side_effects=True, vmem_limit_bytes=63 * 2**20
        ),
        name="combine",
    )(*operands, *extra.operands)


FLAT = ("zy", "yz")
CHUNKS = 4
PIECES = 8


def flat_parts(rows):
    return (0, rows * 3 // 4), (rows * 3 // 4, rows - rows * 3 // 4)


def send_around(place, experts, shards, src_of, dst, out_sems, in_sems, across):
    count = experts * shards if across else shards
    me = place.e * shards + place.f if across else place.f

    def copy(i, sending):
        other = lax.rem(me + i, count)
        if across:
            device = (other // shards, lax.rem(other, shards))
        else:
            device = (place.e, other)
        source = me if sending else other
        return remote(src_of(other), dst.at[source], out_sems.at[i], in_sems.at[source], device)

    def start(i, carry):
        copy(i, True).start()
        return carry

    def finish(i, carry):
        done = copy(i, False)
        done.wait_send()
        done.wait_recv()
        return carry

    lax.fori_loop(1, count, start, 0)
    return lambda: lax.fori_loop(1, count, finish, 0)


def gather_kernel(
    dims, flat, tall, tok, pack, ids, wide, flat_out_all, tall_out_all, tok_out_all, pack_all, ids_all,
    picks, pick, spread, narrow, wide_held, flat_all, tall_all, tok_all, put_sems,
    flat_in, flat_out, tall_in, tall_out, tok_in, tok_out, pack_in, pack_out, ids_in, ids_out, local,
    ids_held, hits, ranks,
):
    experts, shards = dims
    place = Place()
    greet_all(place, experts, shards)
    me = place.e * shards + place.f
    starts, sizes = flat_parts(flat.shape[0])
    chunk = tall.shape[0] // PIECES
    pending = []
    keeps = [
        pltpu.make_async_copy(flat, flat_all.at[place.f], local.at[0]),
        pltpu.make_async_copy(tok, tok_all.at[place.e], local.at[1]),
        pltpu.make_async_copy(pack, pack_all.at[place.f], local.at[2]),
        pltpu.make_async_copy(ids, ids_all.at[me], local.at[3]),
    ]

    def go(condition, copy):
        run(condition, copy.start)
        pending.append((condition, copy))

    def both(a, b):
        return b if a is None else (a if b is None else a & b)

    puts = []

    def put(src, dst, condition=None):
        copy = pltpu.make_async_copy(src, dst, put_sems.at[len(puts)])
        run(condition, copy.start)
        puts.append((condition, copy))

    def flat_item(p, j, yr):
        zs = place.ranked(j)
        source = zs * 2 + (1 - place.y if yr else place.y)
        first = j == 0 and yr == 0
        window = flat_all.at[source, pl.ds(starts[p], sizes[p])]
        src = window
        if not first:
            remote(
                window, window, flat_out.at[p, source, 0], flat_in.at[p, source], place.device("c")
            ).wait_recv()
        put(window, flat_out_all.at[source, pl.ds(starts[p], sizes[p])])
        for axis, condition in links(place, FLAT[p], j, 0, yr, zs):
            go(
                condition,
                remote(
                    src,
                    window,
                    flat_out.at[p, source, LINK[axis]],
                    flat_in.at[p, source],
                    place.device(axis),
                ),
            )

    owner = place.z == place.e

    distance = jnp.abs(place.z - place.e)

    def tall_round(r):
        k = r - distance
        live = (k >= 0) & (k < PIECES)
        k = jnp.clip(k, 0, PIECES - 1)
        piece = pl.ds(pl.multiple_of(k * chunk, chunk), chunk)
        window = tall_all.at[place.y, piece]

        @pl.when(live & ~owner)
        def _():
            remote(window, window, tall_out.at[k, 0], tall_in.at[0, k], place.device("c")).wait_recv()

        for axis, condition in (
            (UP, (place.z >= place.e) & (place.z < 3)),
            (DOWN, (place.z <= place.e) & (place.z > 0)),
            ("y", None),
        ):
            go(
                both(live, condition),
                remote(
                    window,
                    window,
                    tall_out.at[k, LINK[axis]],
                    tall_in.at[1 if axis == "y" else 0, k],
                    place.device(axis),
                ),
            )
        put(window, tall_out_all.at[place.y, piece], live)

    def rank_rows():
        end_ids()
        keeps[3].wait()
        copy = pltpu.make_async_copy(ids_all, ids_held, local.at[5])
        copy.start()
        copy.wait()
        hits[...] = jnp.zeros_like(hits)

        def hit(i, number):
            found = jnp.where(ids_held[i] == number, 1.0, 0.0)
            return jnp.max(found, 0, keepdims=True)

        def own(i, carry):
            hits[pl.ds(i, 1)] = hit(i, me)
            return carry

        lax.fori_loop(0, experts * shards, own, 0)
        mine, far = (place.x, place.y), place.line()[1]
        for k, (chip, core) in enumerate(
            ((mine, place.c), (mine, 1 - place.c), (far, place.c), (far, 1 - place.c))
        ):
            expert_at, shard_at = place.at(chip, core)
            for ar in range(2):
                for zs in range(4):
                    row = experts * shards + (ar * 4 + zs) * 4 + k
                    at = block_number(mine, place.c, ar, zs)
                    hits[row : row + 1] = hit(at, expert_at * shards + shard_at)
        count = hits.shape[1]
        before = lax.broadcasted_iota(jnp.int32, (count, count), 0)
        after = lax.broadcasted_iota(jnp.int32, (count, count), 1)
        earlier = jnp.where(before < after, 1.0, 0.0).astype(jnp.bfloat16)
        found = jnp.dot(hits[...].astype(jnp.bfloat16), earlier, preferred_element_type=jnp.float32)
        ranks[...] = jnp.where(hits[...] > 0.5, found, -1.0)

    def one_hot_rows():
        shape = (SLOTS, ranks.shape[1])
        slot = lax.broadcasted_iota(jnp.int32, shape, 0).astype(jnp.float32)

        def rows_of(i):
            return jnp.where(ranks[pl.ds(i, 1)] == slot, 1.0, 0.0).astype(jnp.bfloat16)

        def own(i, carry):
            picks[i] = rows_of(i)
            return carry

        def near(i, carry):
            for k in range(4):
                pick[i, k * SLOTS : (k + 1) * SLOTS] = rows_of(experts * shards + i * 4 + k)
            return carry

        lax.fori_loop(0, experts * shards, own, 0)
        lax.fori_loop(0, 8, near, 0)

    def one_hot_columns():
        turned = ranks[...].T
        shape = (turned.shape[0], 4 * SLOTS)
        lane = lax.broadcasted_iota(jnp.int32, shape, 1)
        slot = lax.rem(lane, SLOTS).astype(jnp.float32)
        for i in range(8):
            column = experts * shards + i * 4
            rank = turned[:, column : column + 1]
            for k in range(1, 4):
                rank = jnp.where(lane < k * SLOTS, rank, turned[:, column + k : column + k + 1])
            spread[i] = jnp.where(rank == slot, 1.0, 0.0).astype(jnp.bfloat16)

    for keep in keeps:
        keep.start()
    keep_tall = pltpu.make_async_copy(tall, tall_all.at[place.y], local.at[4])
    run(owner, keep_tall.start)
    keeps[0].wait()
    def narrow_rows():
        fetch.wait()

        def part(i, carry):
            here = pl.ds(pl.multiple_of(i * 16, 16), 16)
            narrow[here] = wide_held[here].astype(narrow.dtype)
            return carry

        lax.fori_loop(0, wide.shape[0] // 16, part, 0)

    fetch = pltpu.make_async_copy(wide, wide_held, local.at[6])
    flat_item(0, 0, 0)
    flat_item(1, 0, 0)
    go(None, remote(tok, tok_all.at[place.e], tok_out.at[0], tok_in.at[place.e], place.device("x")))
    go(None, remote(tok, tok_all.at[place.e], tok_out.at[1], tok_in.at[place.e], place.device("c")))
    end_pack = send_around(
        place, experts, shards, lambda i: pack, pack_all, pack_out, pack_in, False
    )
    end_ids = send_around(place, experts, shards, lambda i: ids, ids_all, ids_out, ids_in, True)
    run(owner, keep_tall.wait)
    keeps[1].wait()
    put(tok_all.at[place.e], tok_out_all.at[place.e])
    fetch.start()
    across = (1 - place.x) * 2 + place.c
    window = tok_all.at[across]
    relay = remote(window, window, tok_out.at[2], tok_in.at[across], place.device("c"))
    tall_round(0)
    flat_item(1, 0, 1)
    flat_item(0, 1, 0)
    tall_round(1)
    rank_rows()
    flat_item(0, 2, 0)
    one_hot_rows()
    tall_round(2)
    one_hot_columns()
    narrow_rows()
    flat_item(1, 1, 0)
    flat_item(1, 1, 1)
    relay.wait_recv()
    go(None, relay)
    put(window, tok_out_all.at[across])
    flat_item(0, 3, 0)
    tall_round(3)
    flat_item(1, 2, 0)
    flat_item(1, 2, 1)
    tall_round(4)
    flat_item(1, 3, 0)
    flat_item(1, 3, 1)
    for r in range(5, PIECES + 3):
        tall_round(r)
    for j in range(4):
        flat_item(0, j, 1)
    for k in range(PIECES):
        window = tall_all.at[1 - place.y, pl.ds(k * chunk, chunk)]
        remote(window, window, tall_out.at[k, 0], tall_in.at[1, k], place.device("c")).wait_recv()
        put(window, tall_out_all.at[1 - place.y, pl.ds(k * chunk, chunk)])
    for source in (place.x * 2 + 1 - place.c, (1 - place.x) * 2 + 1 - place.c):
        window = tok_all.at[source]
        remote(window, window, tok_out.at[2], tok_in.at[source], place.device("c")).wait_recv()
        put(window, tok_out_all.at[source])
    for condition, copy in puts:
        run(condition, copy.wait)
    for condition, copy in pending:
        run(condition, copy.wait_send)
    end_pack()
    keeps[2].wait()


def gather(experts, shards, number, flat, tall, tok, pack, ids, wide):
    space = pl.BlockSpec(memory_space=pl.ANY)
    dma = pltpu.SemaphoreType.DMA
    devices = experts * shards

    def shape(lead, a):
        return jax.ShapeDtypeStruct((lead,) + a.shape, a.dtype)

    return pl.pallas_call(
        functools.partial(gather_kernel, (experts, shards)),
        out_shape=[
            shape(shards, flat),
            shape(2, tall),
            shape(experts, tok),
            shape(shards, pack),
            shape(devices, ids),
            jax.ShapeDtypeStruct((devices, SLOTS, ids.shape[1]), jnp.bfloat16),
            jax.ShapeDtypeStruct((8, 4 * SLOTS, ids.shape[1]), jnp.bfloat16),
            jax.ShapeDtypeStruct((8, ids.shape[1], 4 * SLOTS), jnp.bfloat16),
            jax.ShapeDtypeStruct(wide.shape, jnp.bfloat16),
        ],
        in_specs=[space] * 6,
        out_specs=[space] * 5 + [pl.BlockSpec(memory_space=pltpu.VMEM)] * 4,
        scratch_shapes=[
            pltpu.VMEM(wide.shape, wide.dtype),
            pltpu.VMEM((shards,) + flat.shape, flat.dtype),
            pltpu.VMEM((2,) + tall.shape, tall.dtype),
            pltpu.VMEM((experts,) + tok.shape, tok.dtype),
            dma((64,)),
            dma((2, shards)),
            dma((2, shards, 4)),
            dma((2, PIECES)),
            dma((PIECES, 4)),
            dma((experts,)),
            dma((3,)),
            dma((shards,)),
            dma((shards,)),
            dma((devices,)),
            dma((devices,)),
            dma((7,)),
            pltpu.VMEM((devices,) + ids.shape, ids.dtype),
            pltpu.VMEM((128, ids.shape[1]), jnp.float32),
            pltpu.VMEM((128, ids.shape[1]), jnp.float32),
        ],
        compiler_params=pltpu.CompilerParams(
            collective_id=number, has_side_effects=True, vmem_limit_bytes=60 * 2**20
        ),
        name="gather",
    )(flat, tall, tok, pack, ids, wide)


def add_rows(acc, first, window, rows, step=16):
    def add(i, carry):
        here = pl.ds(pl.multiple_of(i * step, step), step)
        at = pl.ds(pl.multiple_of(first + i * step, step), step)
        acc[at] = (acc[at].astype(jnp.float32) + window[here].astype(jnp.float32)).astype(acc.dtype)
        return carry

    lax.fori_loop(0, rows // step, add, 0)


def reduce_body(
    dims, side, flat, tall, pack, partial, out_q, out_k, out_v, tall_out, pack_all, total,
    acc, tacc, yslot, zslot, yone, zall, ty, tz,
    load, yin, zin, yone_in, zall_in, ty_in, tz_in, flat_send, tall_send, spread_in, spread_out,
    tall_in, keep_tall, local,
    group_acc, group_near, group_cross, group_load, group_out, group_in, cross_out, cross_in,
):
    experts, shards = dims
    place = Place()
    greet(place)
    tall_keeps = []
    owner = place.z == place.e
    home = place.x == place.z // 2
    same = place.c == place.z % 2
    starts, sizes = flat_parts(flat.shape[1])
    sizes = (sizes[0], sizes[1] + pack.shape[1])
    height = tall.shape[1]
    chunk = height // CHUNKS
    part = partial.shape[1] // CHUNKS
    pending = []

    def go(condition, copy):
        run(condition, copy.start)
        pending.append((condition, copy))

    def both(a, b):
        return a if b is None else a & b

    load_tall = pltpu.make_async_copy(tall, tacc, load.at[0])
    load_flat = pltpu.make_async_copy(flat, acc.at[:, pl.ds(0, flat.shape[1])], load.at[1])
    load_pack = pltpu.make_async_copy(
        pack, acc.at[:, pl.ds(flat.shape[1], pack.shape[1])], load.at[2]
    )
    across_y = []
    order = (3, 2, 1, 0)

    def add_tall(k):
        piece = pl.ds(k * chunk, chunk)
        across_y.append(
            remote(
                tall.at[1 - place.y, piece], ty.at[piece], tall_send.at[0, k], ty_in.at[k],
                place.device("y"),
            )
        )

    def add_flat(j):
        target = place.ranked(j) * 2 + 1 - place.y
        across_y.append(
            remote(
                flat.at[target, pl.ds(starts[0], sizes[0])],
                yslot.at[place.ranked(j)],
                flat_send.at[0, target],
                yin.at[place.ranked(j)],
                place.device("y"),
            )
        )

    add_tall(0)
    add_tall(1)
    add_flat(3)
    add_tall(2)
    add_flat(2)
    add_tall(3)
    add_flat(1)
    add_flat(0)
    started = [0]

    def feed(count):
        while started[0] < min(count + 2, len(across_y)):
            if started[0] >= 2:
                across_y[started[0] - 2].wait_send()
            across_y[started[0]].start()
            started[0] += 1

    feed(0)
    load_tall.start()
    load_flat.start()
    load_pack.start()
    group_sends = []
    group_loads = []
    for half in (1 - place.x, place.x):
        for i in range(CHUNKS):
            piece = pl.ds(i * part, part)
            copy = remote(
                partial.at[half * 2 + 1 - place.c, piece], group_near.at[half, piece],
                group_out.at[half, i], group_in.at[half, i], place.device("c"),
            )
            copy.start()
            group_sends.append(copy)
            copy = pltpu.make_async_copy(
                partial.at[half * 2 + place.c, piece], group_acc.at[half, piece],
                group_load.at[half, i],
            )
            copy.start()
            group_loads.append(copy)

    def group_half(index, half):
        for i in range(CHUNKS):
            piece = pl.ds(i * part, part)
            window = group_near.at[half, piece]
            group_loads[index * CHUNKS + i].wait()
            remote(
                window, window, group_out.at[half, i], group_in.at[half, i], place.device("c")
            ).wait_recv()
            add_rows(group_acc.at[half], i * part, window, part)
            if index == 0:
                copy = remote(
                    group_acc.at[half, piece], group_cross.at[piece], cross_out.at[i],
                    cross_in.at[i], place.device("x"),
                )
                copy.start()
                group_sends.append(copy)

    def group_end():
        for i in range(CHUNKS):
            window = group_cross.at[pl.ds(i * part, part)]
            remote(window, window, cross_out.at[i], cross_in.at[i], place.device("c")).wait_recv()

            def add(t, carry):
                here = pl.ds(pl.multiple_of(i * part + t * 16, 16), 16)
                own = group_acc[place.x, here].astype(jnp.float32)
                total[here] = own + group_cross[here].astype(jnp.float32)
                return carry

            lax.fori_loop(0, part // 16, add, 0)

    load_tall.wait()
    load_flat.wait()
    load_pack.wait()

    def into(slots, sems, zd, side):
        index = jnp.where(zd == place.z, 4, zd) if side == BELOW else zd
        return slots.at[index], sems.at[index]

    def out_to(slots, sems, zd, side):
        there = place.z - 1 if side == ABOVE else place.z + 1
        index = jnp.where(zd == there, 4, zd) if side == BELOW else zd
        return slots.at[index], sems.at[index]

    def line(j, p, first, slots, sems, send_sem, target):
        zd = place.ranked(j)
        rows = sizes[p]
        for side, condition in (
            (ABOVE, (zd <= place.z) & (place.z < 3)),
            (BELOW, (zd >= place.z) & (place.z > 0)),
        ):
            window, sem = into(slots, sems, zd, side)

            def take(window=window, sem=sem):
                remote(window, window, send_sem, sem, place.device("c")).wait_recv()
                add_rows(acc.at[target], first, window, rows)

            if j == 0:
                condition = place.z < 3 if side == ABOVE else place.z > 0
            run(condition, take)
        if j == 0:
            return
        for side, axis, condition in ((ABOVE, DOWN, zd < place.z), (BELOW, UP, zd > place.z)):
            window, sem = out_to(slots, sems, zd, side)
            go(
                condition,
                remote(acc.at[target, pl.ds(first, rows)], window, send_sem, sem, place.device(axis)),
            )

    above_e, below_e = place.z > place.e, place.z < place.e
    hops = jnp.where(above_e, 3 - place.z, jnp.where(below_e, place.z, jnp.maximum(place.e, 3 - place.e)))

    def tall_round(r):
        k = r - hops
        live = (k >= 0) & (k < CHUNKS)
        k = jnp.clip(k, 0, CHUNKS - 1)
        first = pl.multiple_of(k * chunk, chunk)
        piece = pl.ds(first, chunk)

        @pl.when(live)
        def _():
            remote(
                ty.at[piece], ty.at[piece], tall_send.at[0, k], ty_in.at[k], place.device("c")
            ).wait_recv()
            add_rows(tacc.at[place.y], first, ty.at[piece], chunk)

        for index, condition in (
            (0, (place.z >= place.e) & (place.z < 3)),
            (1, (place.z <= place.e) & (place.z > 0)),
        ):
            window = tz.at[index, piece]

            def take(window=window, index=index):
                remote(
                    window, window, tall_send.at[1, k], tz_in.at[index, k], place.device("c")
                ).wait_recv()
                add_rows(tacc.at[place.y], first, window, chunk)

            run(live & condition, take)
        for index, axis, condition in ((0, DOWN, above_e), (1, UP, below_e)):
            go(
                live & condition,
                remote(
                    tacc.at[place.y, piece], tz.at[index, piece], tall_send.at[1, k],
                    tz_in.at[index, k], place.device(axis),
                ),
            )
        piece_out = tall_out.at[piece]
        keep = pltpu.make_async_copy(tacc.at[place.y, piece], piece_out, keep_tall.at[k])
        run(live & owner, keep.start)
        tall_keeps.append((live & owner, keep))
        for row, axis in ((2, "x"), (3, "c")):
            go(
                live & owner,
                remote(
                    tacc.at[place.y, piece], piece_out, tall_send.at[row, k], tall_in.at[k],
                    place.device(axis),
                ),
            )

    def flat_first(j):
        zd = place.ranked(j)
        target = zd * 2 + place.y
        window = yslot.at[zd]
        remote(window, window, flat_send.at[0, target], yin.at[zd], place.device("c")).wait_recv()
        add_rows(acc.at[target], starts[0], window, sizes[0])
        line(j, 0, starts[0], zslot, zin, flat_send.at[0, target], target)

    def flat_second(j, yr):
        zd = place.ranked(j)
        target = zd * 2 + (1 - place.y if yr else place.y)
        line(j, 1, starts[1], zall.at[yr], zall_in.at[yr], flat_send.at[1, target], target)

    flat_second(3, 1)
    flat_second(3, 0)
    side.event()
    tall_round(0)
    side.event()
    feed(1)
    tall_round(1)
    side.event()
    feed(2)
    flat_second(2, 1)
    flat_second(2, 0)
    side.event()
    flat_first(3)
    side.event()
    feed(3)
    group_half(0, 1 - place.x)
    tall_round(2)
    side.event()
    feed(4)
    flat_second(1, 1)
    flat_second(1, 0)
    side.event()
    flat_first(2)
    side.event()
    feed(5)
    tall_round(3)
    side.event()
    feed(6)
    flat_first(1)
    side.event()
    group_half(1, place.x)
    flat_second(0, 1)
    other = place.z * 2 + 1 - place.y
    go(
        None,
        remote(
            acc.at[other, pl.ds(starts[1], sizes[1])], yone, flat_send.at[1, other], yone_in.at[0],
            place.device("y"),
        ),
    )
    flat_second(0, 0)
    flat_first(0)
    remote(yone, yone, flat_send.at[1, other], yone_in.at[0], place.device("c")).wait_recv()
    add_rows(acc.at[place.f], starts[1], yone, sizes[1])
    cuts = []
    first = 0
    for out in (out_q, out_k, out_v):
        wide = out.shape[1] // experts
        cuts.append((out, pl.ds(0, flat.shape[1]), pl.ds(first, wide)))
        first += wide
    cuts.append((pack_all, pl.ds(flat.shape[1], pack.shape[1]), pl.ds(0, first)))

    def window_of(i, source):
        out = cuts[i][0]
        if i == 3:
            return out.at[source]
        wide = out.shape[1] // experts
        return out.at[:, pl.ds(pl.multiple_of(source * wide, 128), wide)]

    flat_keeps = []
    for i, (out, high, wide) in enumerate(cuts):
        done = acc.at[place.f, high, wide]
        keep = pltpu.make_async_copy(done, window_of(i, place.e), local.at[1 + i])
        keep.start()
        flat_keeps.append(keep)
        for row, axis in enumerate(("x", "c")):
            go(
                None,
                remote(
                    done, window_of(i, place.e), spread_out.at[row, i], spread_in.at[place.e, i],
                    place.device(axis),
                ),
            )
    tall_round(4)
    side.event()
    tall_round(5)
    side.event()
    tall_round(6)
    side.event()
    group_end()
    across = (1 - place.x) * 2 + place.c
    for i in range(4):
        window = window_of(i, across)
        relay = remote(window, window, spread_out.at[2, i], spread_in.at[across, i], place.device("c"))
        relay.wait_recv()
        go(None, relay)
    for k in range(CHUNKS):
        window = tall_out.at[pl.ds(k * chunk, chunk)]
        tall_relay = remote(window, window, tall_send.at[4, k], tall_in.at[k], place.device("c"))
        run(~owner, tall_relay.wait_recv)
        go(~home & same, tall_relay)
    for source in (place.x * 2 + 1 - place.c, (1 - place.x) * 2 + 1 - place.c):
        for i in range(4):
            window = window_of(i, source)
            remote(
                window, window, spread_out.at[2, i], spread_in.at[source, i], place.device("c")
            ).wait_recv()
    for copy in across_y[-2:]:
        copy.wait_send()
    for condition, copy in pending:
        run(condition, copy.wait_send)
    for keep in flat_keeps:
        keep.wait()
    for condition, keep in tall_keeps:
        run(condition, keep.wait)
    for copy in group_sends:
        copy.wait_send()


def reduce_kernel(dims, extra, *refs):
    more = len(extra.operands), len(extra.outs), len(extra.scratch)
    rest = len(refs) - 10 - sum(more)
    ins, more_in, outs, more_out, scratch, more_scratch = split(
        refs, (4, more[0], 6, more[1], rest, more[2])
    )
    side = Side(extra.steps(*more_in, *more_out, *more_scratch), 13)
    reduce_body(dims, side, *ins, *outs, *scratch)


def reduce(experts, shards, number, flat, tall, pack, partial, extra):
    space = pl.BlockSpec(memory_space=pl.ANY)
    dma = pltpu.SemaphoreType.DMA
    _, sizes = flat_parts(flat.shape[1])
    more = sizes[1] + pack.shape[1]
    width, wide = flat.shape[2], tall.shape[2]
    low = jnp.bfloat16
    return pl.pallas_call(
        functools.partial(reduce_kernel, (experts, shards), extra),
        out_shape=[
            jax.ShapeDtypeStruct((flat.shape[1], experts * (width - 2 * HEAD_SIZE)), low),
            jax.ShapeDtypeStruct((flat.shape[1], experts * HEAD_SIZE), low),
            jax.ShapeDtypeStruct((flat.shape[1], experts * HEAD_SIZE), low),
            jax.ShapeDtypeStruct(tall.shape[1:], low),
            jax.ShapeDtypeStruct((experts,) + pack.shape[1:], low),
            jax.ShapeDtypeStruct(partial.shape[1:], jnp.float32),
        ]
        + extra.outs,
        in_specs=[space] * 4 + extra.in_specs,
        out_specs=[space] * 5 + [pl.BlockSpec(memory_space=pltpu.VMEM)] + extra.out_specs,
        scratch_shapes=[
            pltpu.VMEM((shards, flat.shape[1] + pack.shape[1], width), low),
            pltpu.VMEM(tall.shape, low),
            pltpu.VMEM((4, sizes[0], width), low),
            pltpu.VMEM((5, sizes[0], width), low),
            pltpu.VMEM((more, width), low),
            pltpu.VMEM((2, 5, more, width), low),
            pltpu.VMEM(tall.shape[1:], low),
            pltpu.VMEM((2,) + tall.shape[1:], low),
            dma((3,)),
            dma((4,)),
            dma((5,)),
            dma((1,)),
            dma((2, 5)),
            dma((CHUNKS,)),
            dma((2, CHUNKS)),
            dma((2, shards)),
            dma((5, CHUNKS)),
            dma((experts, 4)),
            dma((3, 4)),
            dma((CHUNKS,)),
            dma((CHUNKS,)),
            dma((5,)),
            pltpu.VMEM((2,) + partial.shape[1:], low),
            pltpu.VMEM((2,) + partial.shape[1:], low),
            pltpu.VMEM(partial.shape[1:], low),
            dma((2, CHUNKS)),
            dma((2, CHUNKS)),
            dma((2, CHUNKS)),
            dma((CHUNKS,)),
            dma((CHUNKS,)),
        ]
        + extra.scratch,
        compiler_params=pltpu.CompilerParams(
            collective_id=number, has_side_effects=True, vmem_limit_bytes=58 * 2**20
        ),
        name="reduce",
    )(flat, tall, pack, partial, *extra.operands)


def branch_scatter_kernel(
    mixed, weight, total, blocks, near, cross, near_out, near_in, x_out, x_in
):
    place = Place()
    greet(place)
    rows, width = total.shape
    chunk = rows // CHUNKS
    sends = []
    for index, half in enumerate((1 - place.x, place.x)):
        for core in (1 - place.c, place.c):
            block = half * 2 + core
            here = pl.ds(pl.multiple_of(block * rows, rows), rows)

            def tile(t, carry):
                columns = pl.ds(pl.multiple_of(t * 512, 512), 512)
                blocks[block, :, columns] = jnp.dot(
                    mixed[here], weight[:, columns], preferred_element_type=jnp.float32
                ).astype(jnp.bfloat16)
                return carry

            lax.fori_loop(0, width // 512, tile, 0)
        for k in range(CHUNKS):
            piece = pl.ds(k * chunk, chunk)
            copy = remote(
                blocks.at[half * 2 + 1 - place.c, piece], near.at[half, piece], near_out.at[half, k],
                near_in.at[half, k], place.device("c"),
            )
            copy.start()
            sends.append(copy)
        for k in range(CHUNKS):
            piece = pl.ds(k * chunk, chunk)
            window = near.at[half, piece]
            remote(window, window, near_out.at[half, k], near_in.at[half, k], place.device("c")).wait_recv()
            add_rows(blocks.at[half * 2 + place.c], k * chunk, window, chunk)
            if index == 0:
                copy = remote(
                    blocks.at[half * 2 + place.c, piece], cross.at[piece], x_out.at[k], x_in.at[k],
                    place.device("x"),
                )
                copy.start()
                sends.append(copy)
    for k in range(CHUNKS):
        window = cross.at[pl.ds(k * chunk, chunk)]
        remote(window, window, x_out.at[k], x_in.at[k], place.device("c")).wait_recv()

        def add(i, carry):
            here = pl.ds(pl.multiple_of(k * chunk + i * 16, 16), 16)
            own = blocks[place.e, here].astype(jnp.float32)
            total[here] = own + cross[here].astype(jnp.float32)
            return carry

        lax.fori_loop(0, chunk // 16, add, 0)
    for copy in sends:
        copy.wait_send()


def branch_scatter(number, mixed, weight):
    dma = pltpu.SemaphoreType.DMA
    rows, width = mixed.shape[0] // 4, weight.shape[1]
    low = jnp.bfloat16
    vmem = pl.BlockSpec(memory_space=pltpu.VMEM)
    return pl.pallas_call(
        branch_scatter_kernel,
        out_shape=jax.ShapeDtypeStruct((rows, width), jnp.float32),
        in_specs=[vmem, vmem],
        out_specs=vmem,
        scratch_shapes=[
            pltpu.VMEM((4, rows, width), low),
            pltpu.VMEM((2, rows, width), low),
            pltpu.VMEM((rows, width), low),
            dma((2, CHUNKS)),
            dma((2, CHUNKS)),
            dma((CHUNKS,)),
            dma((CHUNKS,)),
        ],
        compiler_params=pltpu.CompilerParams(
            collective_id=number, has_side_effects=True, vmem_limit_bytes=32 * 2**20
        ),
        name="branch_scatter",
    )(mixed, weight)


BLOCK = 256


def dot_last(a, b):
    return lax.dot_general(a, b, (((1,), (1,)), ((), ())), preferred_element_type=jnp.float32)


def dot(a, b):
    return jnp.dot(a, b, preferred_element_type=jnp.float32)


def turn(rows):
    lane = lax.broadcasted_iota(jnp.int32, rows.shape, 1)
    half = HEAD_SIZE // 2
    return pltpu.roll(rows, half, 1) * jnp.where(lane < half, -1.0, 1.0)


def mask_block(r, count, ids_column, ids_row, bias):
    queries = pl.ds(r * BLOCK, BLOCK)

    def part(i, carry):
        keys = pl.ds(pl.multiple_of(i * BLOCK, BLOCK), BLOCK)
        key_at = lax.broadcasted_iota(jnp.int32, (BLOCK, BLOCK), 0) + i * BLOCK
        query_at = lax.broadcasted_iota(jnp.int32, (BLOCK, BLOCK), 1) + r * BLOCK
        allowed = (ids_column[keys] == ids_row[:, queries]) & (key_at <= query_at)
        bias[keys] = jnp.where(allowed, 0.0, -1e30)
        return carry

    lax.fori_loop(0, count // BLOCK, part, 0)


def project_steps(
    tok, w_qkv, gain_one, gain_q, gain_k, cosine, sine, normed, raw, query_rot, key_rot, value, inverses
):
    heads = query_rot.shape[1] // HEAD_SIZE
    low = jnp.bfloat16

    def rotated(v, rows, gain):
        u = v * inverse_rms(v) * gain
        return (u * cosine[rows] + turn(u) * sine[rows]).astype(low)

    def norm(r):
        def part(i, carry):
            here = pl.ds(pl.multiple_of(r * BLOCK + i * 16, 16), 16)
            x = tok[here].astype(jnp.float32)
            inverse = inverse_rms(x)
            inverses[here] = inverse
            normed[here] = (x * inverse * gain_one[...]).astype(low)
            return carry

        lax.fori_loop(0, BLOCK // 16, part, 0, unroll=2)

    def multiply(r):
        rows = pl.ds(r * BLOCK, BLOCK)

        def pair(i, carry):
            column = pl.ds(pl.multiple_of(i * 2 * HEAD_SIZE, 2 * HEAD_SIZE), 2 * HEAD_SIZE)
            both = dot(normed[rows], w_qkv[:, column])
            raw[rows, column] = both
            for k in range(2):
                at = pl.ds(pl.multiple_of((2 * i + k) * HEAD_SIZE, HEAD_SIZE), HEAD_SIZE)
                one = both[:, k * HEAD_SIZE : (k + 1) * HEAD_SIZE]
                query_rot[rows, at] = rotated(one, rows, gain_q[...])
            return carry

        lax.fori_loop(0, heads // 2, pair, 0)
        last = pl.ds(heads * HEAD_SIZE, 2 * HEAD_SIZE)
        both = dot(normed[rows], w_qkv[:, last])
        raw[rows, last] = both
        key_rot[rows] = rotated(both[:, :HEAD_SIZE], rows, gain_k[...])
        value[rows] = both[:, HEAD_SIZE:].astype(low)

    steps = []
    for r in range(tok.shape[0] // BLOCK):
        steps.append(functools.partial(norm, r))
        steps.append(functools.partial(multiply, r))
    return steps


def attend_steps(query_rot, key_rot, value, ids_column, ids_row, mixed, bias, value_t):
    length = key_rot.shape[0]
    heads = query_rot.shape[1] // HEAD_SIZE
    scale = HEAD_SIZE ** (-0.5)

    def prepare(r):
        if r == 0:
            value_t[...] = value[...].T
        mask_block(r, (r + 1) * BLOCK, ids_column, ids_row, bias)

    def heads_of(r, first, some):
        rows = pl.ds(r * BLOCK, BLOCK)
        count = (r + 1) * BLOCK

        def head(h, carry):
            column = pl.ds(pl.multiple_of(h * HEAD_SIZE, HEAD_SIZE), HEAD_SIZE)
            scores = dot_last(key_rot[:count], query_rot[rows, column]) * scale + bias[:count]
            shifted = jnp.exp(scores - jnp.max(scores, 0, keepdims=True))
            weights = shifted * (1.0 / jnp.sum(shifted, 0, keepdims=True))
            out = dot(value_t[:, :count], weights.astype(jnp.bfloat16))
            mixed[rows, column] = out.T.astype(jnp.bfloat16)
            return carry

        lax.fori_loop(first, first + some, head, 0, unroll=2)

    steps = []
    for r in range(length // BLOCK):
        steps.append(functools.partial(prepare, r))
        some = heads if r == 0 else heads // 2
        for first in range(0, heads, some):
            steps.append(functools.partial(heads_of, r, first, some))
    return steps


def load(pairs, sems):
    copies = [pltpu.make_async_copy(a, b, sems.at[i]) for i, (a, b) in enumerate(pairs)]
    for copy in copies:
        copy.start()
    return copies


def attention(tokens, w_qkv, gain_one, gain_q, gain_k, cosine, sine, ids_column, ids_row, heads):
    length, width = tokens.shape
    wide = w_qkv.shape[1]
    span = heads * HEAD_SIZE
    low, f32 = jnp.bfloat16, jnp.float32
    space, vmem = pl.BlockSpec(memory_space=pl.ANY), pl.BlockSpec(memory_space=pltpu.VMEM)
    shapes = [
        ((length, width), low),
        ((length, wide), f32),
        ((length, span), low),
        ((length, HEAD_SIZE), low),
        ((length, HEAD_SIZE), low),
        ((length, span), low),
        ((length, 1), f32),
    ]

    def steps(*refs):
        ins, outs, scratch = split(refs, (9, 7, 15))
        tok, weight, cos_held, sin_held, in_sems, out_sems, bias, value_t = scratch[:8]
        results = scratch[8:]
        copies = load(
            [(ins[0], tok), (ins[1], weight), (ins[5], cos_held), (ins[6], sin_held)], in_sems
        )

        def begin():
            for copy in copies:
                copy.wait()

        saved = []

        def save(picks):
            for i in picks:
                copy = pltpu.make_async_copy(results[i], outs[i], out_sems.at[i])
                copy.start()
                saved.append(copy)

        def end():
            save((5, 6))
            for copy in saved:
                copy.wait()

        return (
            [begin]
            + project_steps(tok, weight, *ins[2:5], cos_held, sin_held, *results[:5], results[6])
            + [functools.partial(save, range(5))]
            + attend_steps(*results[2:5], *ins[7:9], results[5], bias, value_t)
            + [end]
        )

    return Extra(
        (tokens, w_qkv, gain_one, gain_q, gain_k, cosine, sine, ids_column, ids_row),
        [space] * 2 + [vmem] * 3 + [space] * 2 + [vmem] * 2,
        [jax.ShapeDtypeStruct(*shape) for shape in shapes],
        [space] * 7,
        [
            pltpu.VMEM(tokens.shape, low),
            pltpu.VMEM(w_qkv.shape, low),
            pltpu.VMEM(cosine.shape, f32),
            pltpu.VMEM(sine.shape, f32),
            pltpu.SemaphoreType.DMA((4,)),
            pltpu.SemaphoreType.DMA((7,)),
            pltpu.VMEM((length, BLOCK), f32),
            pltpu.VMEM((HEAD_SIZE, length), low),
        ]
        + [pltpu.VMEM(*shape) for shape in shapes],
        steps,
    )


def attend_back_steps(
    query_rot, key_rot, value, raw, grad_mixed, ids_column, ids_row, gain_q, gain_k, cosine, sine,
    grad_raw, grad_gains, bias, key_t, grad_key, grad_value, sums,
):
    length = key_rot.shape[0]
    heads = query_rot.shape[1] // HEAD_SIZE
    scale = HEAD_SIZE ** (-0.5)
    low = jnp.bfloat16

    def back(grad, rows, column, gain, index):
        unit = grad * cosine[rows] - turn(grad * sine[rows])
        v = raw[rows, column]
        inverse = inverse_rms(v)
        sums[index] += jnp.sum((unit * v * inverse).reshape(-1, 8, HEAD_SIZE), 0)
        grad_raw[rows, column] = norm_backward(unit, v, inverse, gain).astype(low)

    def prepare(r):
        if r == 0:
            key_t[...] = key_rot[...].T
            grad_key[...] = jnp.zeros_like(grad_key)
            grad_value[...] = jnp.zeros_like(grad_value)
            sums[...] = jnp.zeros_like(sums)
        mask_block(r, (r + 1) * BLOCK, ids_column, ids_row, bias)

    def heads_of(r, first, some):
        rows = pl.ds(r * BLOCK, BLOCK)
        count = (r + 1) * BLOCK

        def head(h, carry):
            column = pl.ds(pl.multiple_of(h * HEAD_SIZE, HEAD_SIZE), HEAD_SIZE)
            query = query_rot[rows, column]
            grad_out = grad_mixed[rows, column]
            scores = dot_last(key_rot[:count], query) * scale + bias[:count]
            shifted = jnp.exp(scores - jnp.max(scores, 0, keepdims=True))
            weights = shifted * (1.0 / jnp.sum(shifted, 0, keepdims=True))
            grad_value[:count] += dot(weights.astype(low), grad_out)
            grad_weights = dot_last(value[:count], grad_out)
            spread = jnp.sum(weights * grad_weights, 0, keepdims=True)
            grad_scores = (weights * (grad_weights - spread)).astype(low)
            grad_key[:count] += dot(grad_scores, query)
            grad_query = dot(key_t[:, :count], grad_scores).T * scale
            back(grad_query, rows, column, gain_q[...], 0)
            return carry

        lax.fori_loop(first, first + some, head, 0, unroll=2)

    def last():
        column = pl.ds(heads * HEAD_SIZE, HEAD_SIZE)
        for r in range(length // BLOCK):
            rows = pl.ds(r * BLOCK, BLOCK)
            back(grad_key[rows] * scale, rows, column, gain_k[...], 1)
            grad_raw[rows, pl.ds((heads + 1) * HEAD_SIZE, HEAD_SIZE)] = grad_value[rows].astype(low)
        grad_gains[...] = jnp.sum(sums[...], 1)

    steps = []
    for r in range(length // BLOCK):
        steps.append(functools.partial(prepare, r))
        some = heads if r == 0 else (heads // 2 if r == 1 else heads // 4)
        for first in range(0, heads, some):
            steps.append(functools.partial(heads_of, r, first, some))
    return steps + [last]


def attention_back(
    query_rot, key_rot, value, raw, mixed, grad_low, w_mix, normed_one, tokens, w_qkv, inverses,
    ids_column, ids_row, gain_q, gain_k, cosine, sine,
):
    length, width = tokens.shape
    span, wide = mixed.shape[1], raw.shape[1]
    tiles = width // BLOCK
    low, f32 = jnp.bfloat16, jnp.float32
    space, vmem = pl.BlockSpec(memory_space=pl.ANY), pl.BlockSpec(memory_space=pltpu.VMEM)
    whole = (query_rot, key_rot, value, raw, mixed, cosine, sine, inverses)
    streamed = (grad_low, w_mix, normed_one, tokens, w_qkv)
    own_rows = grad_low.shape[0]
    piece = own_rows // CHUNKS
    small = (ids_column, ids_row, gain_q, gain_k)

    def dot_first(a, b):
        return lax.dot_general(a, b, (((0,), (0,)), ((), ())), preferred_element_type=f32)

    def steps(*refs):
        ins, outs, scratch = split(refs, (17, 5, 27))
        held, (in_sems, grad_raw), work, tile_refs, group = split(scratch, (8, 2, 5, 4, 8))
        tall_in, tall_out, wide_out, sems = tile_refs
        mine, mix, normed, tok, weight = ins[8:13]
        inverse = held[7]
        branch, grad_mixed, mix_in, mix_sems, x_out, x_in, c_out, c_in = group
        place = Place()
        beside, other = place.at((1 - place.x, place.y), place.c), place.device("c")
        across = (1 - place.x) * 2 + place.c
        gains, grad_mix, grad_qkv, grad_normed, grad_gain = outs
        copies = load(list(zip(ins[:8], held)), in_sems)

        def rows_from(source, k):
            return branch.at[pl.ds(pl.multiple_of(source * own_rows + k * piece, piece), piece)]

        def own(k):
            return mine.at[pl.ds(k * piece, piece)]

        sends = []
        keeps = []
        for k in range(CHUNKS):
            sends.append(remote(own(k), rows_from(place.e, k), x_out.at[k], x_in.at[k], beside))
            sends.append(remote(own(k), rows_from(place.e, k), c_out.at[0, k], c_in.at[0, k], other))
            keeps.append(pltpu.make_async_copy(own(k), rows_from(place.e, k), mix_sems.at[2 + k]))
        for copy in sends + keeps:
            copy.start()

        def relay(k):
            window = rows_from(across, k)
            copy = remote(window, window, c_out.at[1, k], c_in.at[1, k], other)
            remote(window, window, x_out.at[k], x_in.at[k], other).wait_recv()
            copy.start()
            sends.append(copy)

        def mix_tile(t):
            return pltpu.make_async_copy(mix.at[at(t)], mix_in.at[t % 2], mix_sems.at[t % 2])

        def arrived():
            mix_tile(0).start()
            for copy in keeps:
                copy.wait()
            for k in range(CHUNKS):
                window = rows_from(place.x * 2 + 1 - place.c, k)
                remote(window, window, c_out.at[0, k], c_in.at[0, k], other).wait_recv()
                window = rows_from((1 - place.x) * 2 + 1 - place.c, k)
                remote(window, window, c_out.at[1, k], c_in.at[1, k], other).wait_recv()
            for copy in sends:
                copy.wait_send()

        def mixed_grad(t):
            mix_tile(t).wait()
            if t + 1 < span // BLOCK:
                mix_tile(t + 1).start()
            grad_mixed[:, at(t)] = dot_last(branch[...], mix_in[t % 2]).astype(low)

        def at(t):
            return pl.ds(t * BLOCK, BLOCK)

        def fetch(i):
            kind, t, slot = i // tiles, i % tiles, i % 2
            if kind == 0:
                return []
            source = (None, normed, tok)[kind]
            found = [
                pltpu.make_async_copy(source.at[:, at(t)], tall_in.at[slot], sems.at[0, slot])
            ]
            if kind == 2:
                found.append(
                    pltpu.make_async_copy(
                        weight.at[at(t)], mix_in.at[slot, :, pl.ds(0, wide)], sems.at[1, slot]
                    )
                )
            return found

        def store(i):
            kind, t, slot = i // tiles, i % tiles, i % 2
            if kind == 1:
                return pltpu.make_async_copy(
                    wide_out.at[slot], grad_qkv.at[at(t)], sems.at[2, slot]
                )
            target = grad_normed if kind else grad_mix
            return pltpu.make_async_copy(tall_out.at[slot], target.at[:, at(t)], sems.at[2, slot])

        def begin():
            for copy in copies:
                copy.wait()

        def tile(i):
            kind, t, slot = i // tiles, i % tiles, i % 2
            for copy in fetch(i):
                copy.wait()
            if i + 1 < 3 * tiles:
                for copy in fetch(i + 1):
                    copy.start()
            if i >= 2:
                store(i - 2).wait()
            if kind == 0:
                tall_out[slot] = dot_first(held[4][...], branch[:, at(t)]).astype(low)
            elif kind == 1:
                wide_out[slot] = dot_first(tall_in[slot], grad_raw[...]).astype(low)
            else:
                found = dot_last(grad_raw[...], mix_in[slot, :, :wide])
                scaled = tall_in[slot].astype(f32) * inverse[...]
                grad_gain[:, at(t)] = jnp.sum(found * scaled, 0, keepdims=True)
                tall_out[slot] = found.astype(low)
            store(i).start()

        def end():
            for i in (3 * tiles - 2, 3 * tiles - 1):
                store(i).wait()

        jobs = [functools.partial(tile, i) for i in range(3 * tiles)]
        back = attend_back_steps(
            *held[:4], grad_mixed, *ins[13:], *held[5:7], grad_raw, gains, *work
        )
        start = [functools.partial(relay, k) for k in range(CHUNKS)] + [arrived]
        start += [functools.partial(mixed_grad, t) for t in range(span // BLOCK)]
        return [begin] + start + back + jobs + [end]

    return Extra(
        whole + streamed + small,
        [space] * 13 + [vmem] * 4,
        [
            jax.ShapeDtypeStruct((2, HEAD_SIZE), f32),
            jax.ShapeDtypeStruct((span, width), low),
            jax.ShapeDtypeStruct((width, wide), low),
            jax.ShapeDtypeStruct((length, width), low),
            jax.ShapeDtypeStruct((1, width), f32),
        ],
        [vmem, space, space, space, vmem],
        [pltpu.VMEM(a.shape, a.dtype) for a in whole]
        + [
            pltpu.SemaphoreType.DMA((8,)),
            pltpu.VMEM(raw.shape, low),
            pltpu.VMEM((length, BLOCK), f32),
            pltpu.VMEM((HEAD_SIZE, length), low),
            pltpu.VMEM((length, HEAD_SIZE), f32),
            pltpu.VMEM((length, HEAD_SIZE), f32),
            pltpu.VMEM((2, 8, HEAD_SIZE), f32),
            pltpu.VMEM((2, length, BLOCK), low),
            pltpu.VMEM((2, length, BLOCK), low),
            pltpu.VMEM((2, BLOCK, wide), low),
            pltpu.SemaphoreType.DMA((3, 2)),
            pltpu.VMEM((length, width), low),
            pltpu.VMEM((length, span), low),
            pltpu.VMEM((2, BLOCK, width), low),
            pltpu.SemaphoreType.DMA((2 + CHUNKS,)),
            pltpu.SemaphoreType.DMA((CHUNKS,)),
            pltpu.SemaphoreType.DMA((CHUNKS,)),
            pltpu.SemaphoreType.DMA((2, CHUNKS)),
            pltpu.SemaphoreType.DMA((2, CHUNKS)),
        ],
        steps,
    )


def weight_grads(rows, grads, inner, grad_a, grad_b):
    count, width = rows.shape
    inside = inner.shape[1]
    low, f32 = jnp.bfloat16, jnp.float32
    space = pl.BlockSpec(memory_space=pl.ANY)
    tiles = width // BLOCK

    def dot_first(a, b):
        return lax.dot_general(a, b, (((0,), (0,)), ((), ())), preferred_element_type=f32)

    def steps(*refs):
        ins, outs, scratch = split(refs, (5, 3, 9))
        a_held, b_held, inner_held, tile, wide, tall, in_sems, tile_sems, out_sems = scratch
        copies = load([(ins[3], a_held), (ins[4], b_held), (ins[2], inner_held)], in_sems)

        def fetch(i):
            source = ins[0] if i < tiles else ins[1]
            columns = pl.ds((i % tiles) * BLOCK, BLOCK)
            return pltpu.make_async_copy(source.at[:, columns], tile.at[i % 2], tile_sems.at[i % 2])

        def store(i, k):
            at = pl.ds((i % tiles) * BLOCK, BLOCK)
            if i < tiles:
                return pltpu.make_async_copy(wide.at[k, i % 2], outs[k].at[at], out_sems.at[k, i % 2])
            return pltpu.make_async_copy(tall.at[i % 2], outs[2].at[:, at], out_sems.at[2, i % 2])

        def begin():
            fetch(0).start()
            for copy in copies:
                copy.wait()

        def prepare(i):
            fetch(i).wait()
            if i + 1 < 2 * tiles:
                fetch(i + 1).start()

        def first(i, k):
            if k == 0:
                prepare(i)
            if i >= 2:
                store(i - 2, k).wait()
            wide[k, i % 2] = dot_first(tile[i % 2], (a_held, b_held)[k][...])
            store(i, k).start()

        def second(i):
            prepare(i)
            if i >= tiles + 2:
                store(i - 2, 2).wait()
            tall[i % 2] = dot_first(inner_held[...], tile[i % 2])
            store(i, 2).start()

        def end():
            for i in (tiles - 2, tiles - 1):
                store(i, 0).wait()
                store(i, 1).wait()
            for i in (2 * tiles - 2, 2 * tiles - 1):
                store(i, 2).wait()

        found = [begin]
        for i in range(tiles):
            found += [functools.partial(first, i, 0), functools.partial(first, i, 1)]
        for i in range(tiles, 2 * tiles):
            found.append(functools.partial(second, i))
        return found + [end]

    return Extra(
        (rows, grads, inner, grad_a, grad_b),
        [space] * 5,
        [
            jax.ShapeDtypeStruct((width, inside), f32),
            jax.ShapeDtypeStruct((width, inside), f32),
            jax.ShapeDtypeStruct((inside, width), f32),
        ],
        [space] * 3,
        [
            pltpu.VMEM((count, inside), low),
            pltpu.VMEM((count, inside), low),
            pltpu.VMEM((count, inside), low),
            pltpu.VMEM((2, count, BLOCK), low),
            pltpu.VMEM((2, 2, BLOCK, inside), f32),
            pltpu.VMEM((2, inside, BLOCK), f32),
            pltpu.SemaphoreType.DMA((3,)),
            pltpu.SemaphoreType.DMA((2,)),
            pltpu.SemaphoreType.DMA((3, 2)),
        ],
        steps,
    )


def gated_results(inner, w_down):
    count, inside = inner.shape
    width = w_down.shape[1]
    low = jnp.bfloat16
    space = pl.BlockSpec(memory_space=pl.ANY)
    tiles = width // BLOCK

    def steps(*refs):
        ins, outs, scratch = split(refs, (2, 1, 6))
        inner_held, down, result, in_sems, down_sems, result_sems = scratch
        copies = load([(ins[0], inner_held)], in_sems)

        def down_of(i):
            columns = pl.ds(i * BLOCK, BLOCK)
            return pltpu.make_async_copy(ins[1].at[:, columns], down.at[i % 2], down_sems.at[i % 2])

        def result_of(i):
            columns = pl.ds(i * BLOCK, BLOCK)
            return pltpu.make_async_copy(
                result.at[i % 2], outs[0].at[:, columns], result_sems.at[i % 2]
            )

        def third(i):
            if i == 0:
                down_of(0).start()
                copies[0].wait()
            down_of(i).wait()
            if i + 1 < tiles:
                down_of(i + 1).start()
            if i >= 2:
                result_of(i - 2).wait()
            result[i % 2] = dot(inner_held[...], down[i % 2]).astype(low)
            result_of(i).start()

        def end():
            result_of(tiles - 2).wait()
            result_of(tiles - 1).wait()

        return [functools.partial(third, i) for i in range(tiles)] + [end]

    return Extra(
        (inner, w_down),
        [space] * 2,
        [jax.ShapeDtypeStruct((count, width), low)],
        [space],
        [
            pltpu.VMEM(inner.shape, low),
            pltpu.VMEM((2, inside, BLOCK), low),
            pltpu.VMEM((2, count, BLOCK), low),
            pltpu.SemaphoreType.DMA((1,)),
            pltpu.SemaphoreType.DMA((2,)),
            pltpu.SemaphoreType.DMA((2,)),
        ],
        steps,
    )


WIDE = 512


def dispatch_expert_kernel(
    dims, tok, sel, small, grads, picks, ids, w_gate, w_up, w_down,
    small_all, rows_out, inner, grad_a, grad_b, grad_rows, gate_grad,
    held, stage, picked, arrive, leave, pick_out, pick_in, local, small_out, small_in,
    gates, weights_in, gate_held, up_held, down_held, g_held, g_in,
    inner_s, a_s, b_s, rows_s, store_sems, keep_sems,
):
    experts, shards = dims
    low, f32 = jnp.bfloat16, jnp.float32
    place = Place()
    width = tok.shape[1]
    near, far = place.line()
    mine = (place.x, place.y)
    me = place.e * shards + place.f
    greet_all(place, *dims)
    end_small = exchange_small(
        place, dims, lambda i: small, small_all, small_out, small_in, local.at[1]
    )
    keep = pltpu.make_async_copy(tok, held.at[place.z], local.at[0])
    keep.start()
    loads = load([(w_gate.at[0], gate_held), (w_up.at[0], up_held), (w_down.at[0], down_held)], weights_in)
    pending = []
    targets = (place.device("c"), place.at(far, place.c), place.at(far, 1 - place.c))
    half = tok.shape[0] // HALVES

    def pick(ar, zs):
        block = ar * 4 + zs
        number = block_number(mine, place.c, ar, zs)

        def tile(i, carry):
            columns = pl.ds(pl.multiple_of(i * WIDE, WIDE), WIDE)
            chosen = dot(sel[block], held[block, :, columns]).astype(low)
            picked[number, :, columns] = chosen[:SLOTS]
            stage[block, :, columns] = chosen[SLOTS:]
            return carry

        lax.fori_loop(0, width // WIDE, tile, 0)
        for k in (2, 1, 0):
            away = remote(
                stage.at[block, pl.ds(k * SLOTS, SLOTS)], picked.at[number],
                pick_out.at[block, k], pick_in.at[number], targets[k],
            )
            away.start()
            pending.append((None, away))

    def wait_rows(i):
        xs, cs, ys = i // 16, i // 8 % 2, i % 2
        inside = (cs == place.c) & jnp.where(place.c == 0, ys == place.y, xs == place.x)

        @pl.when(~inside)
        def _():
            window = picked.at[i]
            remote(window, window, pick_out.at[0, 0], pick_in.at[i], place.device("c")).wait_recv()

    def sources(n):
        first = n % 2 * 16 + place.ranked(n // 2) * 2
        return first, first + 8

    def grads_of(n):
        return [
            pltpu.make_async_copy(
                grads.at[pl.ds(first, 2)], g_held.at[n % 2, pl.ds(2 * k, 2)], g_in.at[n % 2, k]
            )
            for k, first in enumerate(sources(n))
        ]

    kept = []
    for copy in grads_of(0):
        copy.start()

    def stores(n):
        pairs = ((inner_s, inner), (a_s, grad_a), (b_s, grad_b), (rows_s, grad_rows))
        return [
            pltpu.make_async_copy(
                source.at[pl.ds(2 * k, 2)], target.at[pl.ds(first, 2)], store_sems.at[i, k]
            )
            for i, (source, target) in enumerate(pairs)
            for k, first in enumerate(sources(n))
        ]

    def compute(n):
        first, second = sources(n)
        from_devices = (first, first + 1, second, second + 1)
        if n == 0:
            end_small()
            copy = pltpu.make_async_copy(small_all, gates, local.at[2])
            copy.start()
            for done in loads:
                done.wait()
            copy.wait()
        if n + 1 < 8:
            for copy in grads_of(n + 1):
                copy.start()
        for i in from_devices:
            wait_rows(i)
        for k, start in enumerate((first, second)):
            copy = pltpu.make_async_copy(
                picked.at[pl.ds(start, 2)], rows_out.at[pl.ds(start, 2)], keep_sems.at[n, k]
            )
            copy.start()
            kept.append(copy)
        here = []
        for i in from_devices:
            value = jnp.sum(jnp.where(ids[i] == me, gates[i], 0.0), 0, keepdims=True)
            here.append(jnp.sum(picks[i].astype(f32) * value, -1, keepdims=True))
        here = jnp.concatenate(here, 0)
        count = 4 * SLOTS
        x = jnp.concatenate([picked[i] for i in from_devices], 0)
        a = dot(x, gate_held[...])
        b = dot(x, up_held[...])
        sigmoid = jax.nn.sigmoid(a)
        active = a * sigmoid
        into_a = b * (sigmoid * (1.0 + a * (1.0 - sigmoid)))
        for copy in grads_of(n):
            copy.wait()
        if n:
            for copy in stores(n - 1):
                copy.wait()
        back = dot_last(g_held[n % 2].reshape(count, width), down_held[...])
        product = active * b
        found = jnp.sum(product * back, -1, keepdims=True)
        for k, i in enumerate(from_devices):
            part = picks[i].astype(f32) * found[k * SLOTS : (k + 1) * SLOTS]
            gate_grad[i] = jnp.broadcast_to(jnp.sum(part, 0, keepdims=True), gate_grad.shape[1:])
        inner_s[...] = (product * here).astype(low).reshape(inner_s.shape)
        back = back * here
        a_s[...] = (back * into_a).astype(low).reshape(a_s.shape)
        b_s[...] = (back * active).astype(low).reshape(b_s.shape)

        def backward(t, carry):
            columns = pl.ds(pl.multiple_of(t * WIDE, WIDE), WIDE)
            total = dot_last(a_s[...].reshape(count, -1), gate_held[columns])
            total += dot_last(b_s[...].reshape(count, -1), up_held[columns])
            rows_s[:, :, columns] = total.astype(low).reshape(4, SLOTS, WIDE)
            return carry

        lax.fori_loop(0, width // WIDE, backward, 0)
        for copy in stores(n):
            copy.start()

    work = {3: (0,), 4: (1,), 5: (2,), 6: (3, 4), 7: (5, 6, 7)}
    for event, (ar, j) in enumerate(FAR_FIRST[::-1]):
        zs = place.ranked(j)
        block = ar * 4 + zs
        for h in range(HALVES):
            part = pl.ds(h * half, half)
            window = held.at[block, part]
            if ar or j:
                remote(
                    window, window, leave.at[zs, 0, h], arrive.at[block, h], place.device("c")
                ).wait_recv()
            if ar:
                continue
            source = tok.at[part] if j == 0 else window
            onward = (
                (UP, zs, 0, (zs <= place.z) & (place.z < 3)),
                (DOWN, zs, 1, (zs >= place.z) & (place.z > 0)),
                ("near", 4 + zs, 2, None),
            )
            for axis, there, k, condition in onward:
                device = place.at(near, place.c) if axis == "near" else place.device(axis)
                copy = remote(
                    source, held.at[there, part], leave.at[zs, k, h], arrive.at[there, h], device
                )
                run(condition, copy.start)
                pending.append((condition, copy))
        if not ar and j == 0:
            keep.wait()
        pick(ar, zs)
        for n in work.get(event, ()):
            compute(n)
    for copy in stores(7):
        copy.wait()
    for copy in kept:
        copy.wait()
    for condition, copy in pending:
        run(condition, copy.wait_send)


def dispatch_expert(experts, shards, number, tok, sel, small, grads, picks, ids, w_gate, w_up, w_down):
    rows, width = tok.shape
    devices = experts * shards
    inside = w_gate.shape[2]
    space = pl.BlockSpec(memory_space=pl.ANY)
    vmem = pl.BlockSpec(memory_space=pltpu.VMEM)
    dma = pltpu.SemaphoreType.DMA
    low, f32 = jnp.bfloat16, jnp.float32

    def lots(columns):
        return jax.ShapeDtypeStruct((devices, SLOTS, columns), low)

    def some(columns):
        return pltpu.VMEM((4, SLOTS, columns), low)

    return pl.pallas_call(
        functools.partial(dispatch_expert_kernel, (experts, shards)),
        out_shape=[
            jax.ShapeDtypeStruct((devices,) + small.shape, f32),
            lots(width), lots(inside), lots(inside), lots(inside), lots(width),
            jax.ShapeDtypeStruct((devices, 8, rows), f32),
        ],
        in_specs=[space, vmem, space, space, vmem, vmem, space, space, space],
        out_specs=[space] * 6 + [vmem],
        scratch_shapes=[
            pltpu.VMEM((8, rows, width), low),
            pltpu.VMEM((8, 3 * SLOTS, width), low),
            pltpu.VMEM((devices, SLOTS, width), low),
            dma((8, HALVES)),
            dma((4, 3, HALVES)),
            dma((8, 3)),
            dma((devices,)),
            dma((3,)),
            dma((devices,)),
            dma((devices,)),
            pltpu.VMEM((devices,) + small.shape, f32),
            dma((3,)),
            pltpu.VMEM(w_gate.shape[1:], low),
            pltpu.VMEM(w_up.shape[1:], low),
            pltpu.VMEM(w_down.shape[1:], low),
            pltpu.VMEM((2, 4, SLOTS, width), low),
            dma((2, 2)),
            some(inside), some(inside), some(inside), some(width),
            dma((4, 2)),
            dma((8, 2)),
        ],
        compiler_params=pltpu.CompilerParams(
            collective_id=number, has_side_effects=True, vmem_limit_bytes=62 * 2**20
        ),
        name="dispatch_expert",
    )(tok, sel, small, grads, picks, ids, w_gate, w_up, w_down)


def local(
    layer_input,
    doc_ids,
    expert_ids,
    w_query,
    w_key,
    w_value,
    w_out,
    w_router,
    gain_attn,
    gain_ffn,
    gain_query,
    gain_key,
    w_gate,
    w_up,
    w_down,
    grad_output,
):
    single_float = jnp.float32
    brain_float_half = jnp.bfloat16
    row_count = layer_input.shape[1]
    width = layer_input.shape[2]
    length_total = doc_ids.shape[1]
    query_groups = QUERY_HEADS // KEY_VALUE_HEADS
    scale = HEAD_SIZE ** (-0.5)
    experts = w_router.shape[1]
    capacity = max(2, 6 * row_count * TOP // (5 * experts))
    pairs = row_count * TOP
    (
        full_query,
        gathered_key,
        full_value,
        full_out,
        full_router,
        gain_one,
        gain_two,
        gain_q,
        key_gain_vector,
    ) = (
        lax.all_gather(w_query, FSDP, axis=0, tiled=True),
        lax.all_gather(w_key, FSDP, axis=0, tiled=True),
        lax.all_gather(w_value, FSDP, axis=0, tiled=True),
        lax.all_gather(w_out, FSDP, axis=0, tiled=True),
        lax.all_gather(w_router, FSDP, axis=0, tiled=True),
        lax.all_gather(gain_attn, FSDP, axis=0, tiled=True),
        lax.all_gather(gain_ffn, FSDP, axis=0, tiled=True),
        lax.all_gather(gain_query, FSDP, axis=0, tiled=True),
        lax.all_gather(gain_key, FSDP, axis=0, tiled=True),
    )
    gain_one = gain_one.astype(single_float)
    gain_two = gain_two.astype(single_float)
    gain_q = gain_q.astype(single_float)
    key_gain_vector = key_gain_vector.astype(single_float)
    inputs = layer_input[0].astype(single_float)
    offset = lax.axis_index(EXPERT) * row_count
    own_pos = offset + jnp.arange(row_count, dtype=jnp.int32)
    all_pos = jnp.arange(length_total, dtype=jnp.int32)
    seq_ids = doc_ids[0]
    own_ids = lax.dynamic_slice_in_dim(seq_ids, offset, row_count)
    allowed = (own_ids[:, None] == seq_ids[None, :]) & (own_pos[:, None] >= all_pos[None, :])
    cosine_table, sine_table = angles(own_pos)
    cosine_table = cosine_table[:, None, :]
    sine_table = sine_table[:, None, :]
    scale_one = inverse_rms(inputs)
    normalized_input = (inputs * scale_one * gain_one).astype(brain_float_half)
    query_raw = jnp.dot(normalized_input, full_query, preferred_element_type=single_float).reshape(
        row_count, QUERY_HEADS, HEAD_SIZE
    )
    key_unnormalized = jnp.dot(
        normalized_input, gathered_key, preferred_element_type=single_float
    ).reshape(row_count, KEY_VALUE_HEADS, HEAD_SIZE)
    value_low = jnp.dot(normalized_input, full_value, preferred_element_type=single_float).astype(
        brain_float_half
    )
    query_scale = inverse_rms(query_raw)
    key_norm_scale = inverse_rms(key_unnormalized)
    query_rot = (
        apply_rotary(query_raw * query_scale * gain_q, cosine_table, sine_table)
        .astype(brain_float_half)
        .reshape(row_count, KEY_VALUE_HEADS, query_groups, HEAD_SIZE)
    )
    key_rotated = apply_rotary(
        key_unnormalized * key_norm_scale * key_gain_vector, cosine_table, sine_table
    ).astype(brain_float_half)
    key_gathered_rows, value_gathered_rows = (
        lax.all_gather(
            key_rotated.reshape(row_count, KEY_VALUE_HEADS * HEAD_SIZE),
            EXPERT,
            axis=0,
            tiled=True,
        ),
        lax.all_gather(value_low, EXPERT, axis=0, tiled=True),
    )
    key_gathered_rows = key_gathered_rows.reshape(length_total, KEY_VALUE_HEADS, HEAD_SIZE)
    value_gathered_rows = value_gathered_rows.reshape(length_total, KEY_VALUE_HEADS, HEAD_SIZE)

    def masked_scores():
        raw = (
            jnp.einsum(
                "tkgd,skd->kgts", query_rot, key_gathered_rows, preferred_element_type=single_float
            )
            * scale
        )
        return jnp.where(allowed, raw, -1e30)

    scores = masked_scores()
    peak = jnp.max(scores, -1, keepdims=True)
    shifted = jnp.exp(scores - peak)
    totals = jnp.sum(shifted, -1, keepdims=True)
    weights_low = (shifted / totals).astype(brain_float_half)
    log_total = peak + jnp.log(totals)
    mixed = (
        jnp.einsum(
            "kgts,skd->tkgd", weights_low, value_gathered_rows, preferred_element_type=single_float
        )
        .reshape(row_count, QUERY_HEADS * HEAD_SIZE)
        .astype(brain_float_half)
    )
    hidden = inputs + jnp.dot(mixed, full_out, preferred_element_type=single_float)
    scale_two = inverse_rms(hidden)
    normed_two = (hidden * scale_two * gain_two).astype(brain_float_half)
    logits = jnp.dot(normed_two, full_router, preferred_element_type=single_float)
    selector = (expert_ids[0][:, :, None] == jnp.arange(experts, dtype=jnp.int32)).astype(
        single_float
    )
    chosen = jnp.einsum("tke,te->tk", selector, logits, precision=HIGHEST)
    gates = jax.nn.softmax(chosen, -1)
    flat_routes = expert_ids[0].reshape(pairs)
    hits = (flat_routes[:, None] == jnp.arange(experts, dtype=jnp.int32)).astype(jnp.int32)
    before = jnp.cumsum(hits, 0) - hits
    ranks = jnp.sum(before * hits, 1)
    slot_index = flat_routes * capacity + ranks
    owner_rows = jnp.arange(pairs, dtype=jnp.int32) // TOP
    outgoing = (
        jnp.zeros((experts * capacity, width), brain_float_half)
        .at[slot_index]
        .set(normed_two[owner_rows])
    )
    arrived = lax.all_to_all(
        outgoing.reshape(experts, capacity, width),
        (EXPERT, FSDP),
        split_axis=0,
        concat_axis=0,
        tiled=True,
    ).reshape(experts * capacity, width)
    gate_pre = jnp.dot(arrived, w_gate[0], preferred_element_type=single_float)
    up_pre = jnp.dot(arrived, w_up[0], preferred_element_type=single_float)
    activated = jax.nn.silu(gate_pre)
    inner = (activated * up_pre).astype(brain_float_half)
    result = jnp.dot(inner, w_down[0], preferred_element_type=single_float).astype(brain_float_half)
    returned = lax.all_to_all(
        result.reshape(experts, capacity, width),
        (EXPERT, FSDP),
        split_axis=0,
        concat_axis=0,
        tiled=True,
    ).reshape(experts * capacity, width)
    expert_rows = returned[slot_index].astype(single_float).reshape(row_count, TOP, width)
    output = hidden + jnp.einsum("tk,tkd->td", gates, expert_rows, precision=HIGHEST)
    grad_top = grad_output[0]
    grad_gates = jnp.einsum("tkd,td->tk", expert_rows, grad_top, precision=HIGHEST)
    grad_pairs = (
        (gates[:, :, None] * grad_top[:, None, :]).astype(brain_float_half).reshape(pairs, width)
    )
    grad_send = (
        jnp.zeros((experts * capacity, width), brain_float_half).at[slot_index].set(grad_pairs)
    )
    grad_arrived = lax.all_to_all(
        grad_send.reshape(experts, capacity, width),
        (EXPERT, FSDP),
        split_axis=0,
        concat_axis=0,
        tiled=True,
    ).reshape(experts * capacity, width)
    grad_down = jnp.einsum("rf,rd->fd", inner, grad_arrived, preferred_element_type=single_float)
    grad_inner = jnp.einsum(
        "rd,fd->rf", grad_arrived, w_down[0], preferred_element_type=single_float
    )
    sigmoid_gate = jax.nn.sigmoid(gate_pre)
    slope = sigmoid_gate * (1.0 + gate_pre * (1.0 - sigmoid_gate))
    grad_gate_pre = (grad_inner * up_pre * slope).astype(brain_float_half)
    grad_up_pre = (grad_inner * activated).astype(brain_float_half)
    grad_gate_w = jnp.einsum(
        "rd,rf->df", arrived, grad_gate_pre, preferred_element_type=single_float
    )
    grad_up_w = jnp.einsum("rd,rf->df", arrived, grad_up_pre, preferred_element_type=single_float)
    grad_rows = (
        jnp.einsum("rf,df->rd", grad_gate_pre, w_gate[0], preferred_element_type=single_float)
        + jnp.einsum("rf,df->rd", grad_up_pre, w_up[0], preferred_element_type=single_float)
    ).astype(brain_float_half)
    grad_back = lax.all_to_all(
        grad_rows.reshape(experts, capacity, width),
        (EXPERT, FSDP),
        split_axis=0,
        concat_axis=0,
        tiled=True,
    ).reshape(experts * capacity, width)
    grad_normed_two = jnp.sum(
        grad_back[slot_index].astype(single_float).reshape(row_count, TOP, width), 1
    )
    grad_chosen = gates * (grad_gates - jnp.sum(gates * grad_gates, -1, keepdims=True))
    grad_logits = jnp.einsum("tke,tk->te", selector, grad_chosen, precision=HIGHEST).astype(
        brain_float_half
    )
    grad_normed_two = grad_normed_two + jnp.einsum(
        "te,de->td", grad_logits, full_router, preferred_element_type=single_float
    )
    grad_router = jnp.einsum(
        "td,te->de", normed_two, grad_logits, preferred_element_type=single_float
    )
    grad_gain_two = jnp.sum(grad_normed_two * hidden * scale_two, 0)
    grad_hidden = grad_top + norm_backward(grad_normed_two, hidden, scale_two, gain_two)
    grad_branch = grad_hidden.astype(brain_float_half)
    grad_out_w = jnp.einsum("tq,td->qd", mixed, grad_branch, preferred_element_type=single_float)
    grad_mixed = (
        jnp.einsum("td,qd->tq", grad_branch, full_out, preferred_element_type=single_float)
        .astype(brain_float_half)
        .reshape(row_count, KEY_VALUE_HEADS, query_groups, HEAD_SIZE)
    )
    again = masked_scores()
    weights = jnp.exp(again - log_total)
    weights_again = weights.astype(brain_float_half)
    grad_weights = jnp.einsum(
        "tkgd,skd->kgts", grad_mixed, value_gathered_rows, preferred_element_type=single_float
    )
    spread = jnp.sum(weights * grad_weights, -1, keepdims=True)
    grad_scores = (weights * (grad_weights - spread)).astype(brain_float_half)
    grad_query_rot = (
        jnp.einsum(
            "kgts,skd->tkgd", grad_scores, key_gathered_rows, preferred_element_type=single_float
        )
        * scale
    ).reshape(row_count, QUERY_HEADS, HEAD_SIZE)
    grad_key_all = (
        jnp.einsum("kgts,tkgd->skd", grad_scores, query_rot, preferred_element_type=single_float)
        * scale
    ).reshape(length_total, KEY_VALUE_HEADS * HEAD_SIZE)
    grad_value_all = jnp.einsum(
        "kgts,tkgd->skd", weights_again, grad_mixed, preferred_element_type=single_float
    ).reshape(length_total, KEY_VALUE_HEADS * HEAD_SIZE)
    gradient_key_rotated, grad_value = (
        lax.psum_scatter(
            grad_key_all.astype(jnp.bfloat16), EXPERT, scatter_dimension=0, tiled=True
        ).astype(jnp.float32),
        lax.psum_scatter(
            grad_value_all.astype(jnp.bfloat16), EXPERT, scatter_dimension=0, tiled=True
        ).astype(jnp.float32),
    )
    gradient_key_rotated = gradient_key_rotated.reshape(row_count, KEY_VALUE_HEADS, HEAD_SIZE)
    grad_query_unit = unrotate(grad_query_rot, cosine_table, sine_table)
    gradient_key_normalized = unrotate(gradient_key_rotated, cosine_table, sine_table)
    grad_gain_q = jnp.sum(grad_query_unit * query_raw * query_scale, (0, 1))
    grad_gain_k = jnp.sum(gradient_key_normalized * key_unnormalized * key_norm_scale, (0, 1))
    grad_query = (
        norm_backward(grad_query_unit, query_raw, query_scale, gain_q)
        .reshape(row_count, QUERY_HEADS * HEAD_SIZE)
        .astype(brain_float_half)
    )
    grad_key = (
        norm_backward(gradient_key_normalized, key_unnormalized, key_norm_scale, key_gain_vector)
        .reshape(row_count, KEY_VALUE_HEADS * HEAD_SIZE)
        .astype(brain_float_half)
    )
    grad_value_low = grad_value.astype(brain_float_half)
    grad_query_w = jnp.einsum(
        "td,tq->dq", normalized_input, grad_query, preferred_element_type=single_float
    )
    grad_key_w = jnp.einsum(
        "td,tq->dq", normalized_input, grad_key, preferred_element_type=single_float
    )
    grad_value_w = jnp.einsum(
        "td,tq->dq", normalized_input, grad_value_low, preferred_element_type=single_float
    )
    grad_normed = (
        jnp.einsum("tq,dq->td", grad_query, full_query, preferred_element_type=single_float)
        + jnp.einsum("tq,dq->td", grad_key, gathered_key, preferred_element_type=single_float)
        + jnp.einsum("tq,dq->td", grad_value_low, full_value, preferred_element_type=single_float)
    )
    grad_gain_one = jnp.sum(grad_normed * inputs * scale_one, 0)
    grad_inputs = grad_hidden + norm_backward(grad_normed, inputs, scale_one, gain_one)
    local_grads = (
        grad_query_w,
        grad_key_w,
        grad_value_w,
        grad_out_w,
        grad_router,
        grad_gain_one,
        grad_gain_two,
        grad_gain_q,
        grad_gain_k,
    )
    shards = (
        lax.psum_scatter(
            local_grads[0].astype(jnp.bfloat16), FSDP, scatter_dimension=0, tiled=True
        ).astype(jnp.float32),
        lax.psum_scatter(
            local_grads[1].astype(jnp.bfloat16), FSDP, scatter_dimension=0, tiled=True
        ).astype(jnp.float32),
        lax.psum_scatter(
            local_grads[2].astype(jnp.bfloat16), FSDP, scatter_dimension=0, tiled=True
        ).astype(jnp.float32),
        lax.psum_scatter(
            local_grads[3].astype(jnp.bfloat16), FSDP, scatter_dimension=0, tiled=True
        ).astype(jnp.float32),
        lax.psum_scatter(
            local_grads[4].astype(jnp.bfloat16), FSDP, scatter_dimension=0, tiled=True
        ).astype(jnp.float32),
        lax.psum_scatter(
            local_grads[5].astype(jnp.bfloat16), FSDP, scatter_dimension=0, tiled=True
        ).astype(jnp.float32),
        lax.psum_scatter(
            local_grads[6].astype(jnp.bfloat16), FSDP, scatter_dimension=0, tiled=True
        ).astype(jnp.float32),
        lax.psum_scatter(
            local_grads[7].astype(jnp.bfloat16), FSDP, scatter_dimension=0, tiled=True
        ).astype(jnp.float32),
        lax.psum_scatter(
            local_grads[8].astype(jnp.bfloat16), FSDP, scatter_dimension=0, tiled=True
        ).astype(jnp.float32),
    )
    shards = (
        lax.psum(shards[0].astype(jnp.bfloat16), EXPERT).astype(jnp.float32),
        lax.psum(shards[1].astype(jnp.bfloat16), EXPERT).astype(jnp.float32),
        lax.psum(shards[2].astype(jnp.bfloat16), EXPERT).astype(jnp.float32),
        lax.psum(shards[3].astype(jnp.bfloat16), EXPERT).astype(jnp.float32),
        lax.psum(shards[4].astype(jnp.bfloat16), EXPERT).astype(jnp.float32),
        lax.psum(shards[5].astype(jnp.bfloat16), EXPERT).astype(jnp.float32),
        lax.psum(shards[6].astype(jnp.bfloat16), EXPERT).astype(jnp.float32),
        lax.psum(shards[7].astype(jnp.bfloat16), EXPERT).astype(jnp.float32),
        lax.psum(shards[8].astype(jnp.bfloat16), EXPERT).astype(jnp.float32),
    )
    return (
        output[None],
        grad_inputs[None],
        shards[0],
        shards[1],
        shards[2],
        shards[3],
        shards[4],
        shards[5],
        shards[6],
        shards[7],
        shards[8],
        grad_gate_w[None],
        grad_up_w[None],
        grad_down[None],
    )


def angle_tables(length):
    power = -(np.arange(HEAD_SIZE // 2, dtype=np.float32) * np.float32(2.0)) / np.float32(HEAD_SIZE)
    freq = np.power(np.float32(THETA), power).astype(np.float32)
    turns = np.arange(length, dtype=np.float32)[:, None] * freq[None, :]
    turns = np.concatenate([turns, turns], -1)
    return jnp.asarray(np.cos(turns)), jnp.asarray(np.sin(turns))


def packed(pieces, lead, rows):
    flat = jnp.concatenate([piece.reshape(lead, -1) for piece in pieces], 1)
    flat = jnp.pad(flat, ((0, 0), (0, rows * 128 - flat.shape[1])))
    return flat.reshape(lead, rows, 128)


def local_staged(
    layer_input,
    doc_ids,
    expert_ids,
    w_query,
    w_key,
    w_value,
    w_out,
    w_router,
    gain_attn,
    gain_ffn,
    gain_query,
    gain_key,
    w_gate,
    w_up,
    w_down,
    grad_output,
):
    f32 = jnp.float32
    low = jnp.bfloat16
    rows, width = layer_input.shape[1:]
    length = doc_ids.shape[1]
    depth = w_router.shape[0]
    groups, shards = lax.axis_size(EXPERT), lax.axis_size(FSDP)
    experts = w_router.shape[1]
    heads = QUERY_HEADS // groups
    span = heads * HEAD_SIZE
    mine = lax.axis_index(EXPERT)

    def columns(weight, count):
        return lax.dynamic_slice_in_dim(weight, mine * count, count, 1)

    flat = jnp.concatenate(
        [columns(w_query, span), columns(w_key, HEAD_SIZE), columns(w_value, HEAD_SIZE)], 1
    )
    pack = packed([w_router, gain_attn, gain_ffn, gain_query, gain_key], 1, 80)[0]
    w_qkv, w_mix, tokens, pack_all, ids_all, mine_picks, pick, spread, grad_top_low = gather(
        groups,
        shards,
        5,
        flat,
        w_out,
        layer_input[0],
        pack,
        expert_ids[0].T,
        grad_output[0],
    )
    w_qkv = w_qkv.reshape(width, span + 2 * HEAD_SIZE)
    w_mix = w_mix.reshape(span, width)
    tokens = tokens.reshape(length, width)
    pack_all = pack_all.reshape(shards, -1)
    at = depth * experts
    full_router = pack_all[:, :at].reshape(width, experts)
    gain_one = pack_all[:, at : at + depth].reshape(width).astype(f32)
    gain_two = pack_all[:, at + depth : at + 2 * depth].reshape(width).astype(f32)
    at += 2 * depth
    small = HEAD_SIZE // shards
    gain_q = pack_all[:, at : at + small].reshape(HEAD_SIZE).astype(f32)
    gain_k = pack_all[:, at + small : at + 2 * small].reshape(HEAD_SIZE).astype(f32)
    grad_top = grad_output[0]
    ids_column, ids_row = doc_ids[0][:, None], doc_ids[0][None, :]
    cosine, sine = angle_tables(length)
    gain_q, gain_k = gain_q[None], gain_k[None]
    attend = attention(
        tokens, w_qkv, gain_one[None], gain_q, gain_k, cosine, sine, ids_column, ids_row, heads
    )
    grads_in, normed_one, raw, query_rot, key_rot, value, mixed, inverses = dispatch(
        groups, shards, 1, grad_top_low, pick, extra=attend
    )
    inputs = layer_input[0].astype(f32)
    hidden = inputs + branch_scatter(8, mixed, w_mix)
    scale_two = inverse_rms(hidden)
    normed_two = (hidden * scale_two * gain_two).astype(low)
    logits = jnp.dot(normed_two, full_router, preferred_element_type=f32)
    selector = (expert_ids[0][:, :, None] == jnp.arange(experts, dtype=jnp.int32)).astype(f32)
    gates = jax.nn.softmax(jnp.sum(selector * logits[:, None, :], -1), -1)
    _, arrived, inner, grad_a, grad_b, grad_rows, gate_grads = dispatch_expert(
        groups, shards, 2, normed_two, pick, gates.T, grads_in, mine_picks, ids_all, w_gate, w_up, w_down
    )

    def flat_rows(blocks):
        return blocks.reshape(-1, blocks.shape[-1])

    grad_normed_two, gates_back, weighted = combine(
        groups,
        shards,
        3,
        grad_rows,
        spread,
        gate_grads,
        gated_results(flat_rows(inner), w_down[0]),
    )
    grad_gates = jnp.sum(selector * gates_back[:, 0].T[:, None, :], -1)
    grad_chosen = gates * (grad_gates - jnp.sum(gates * grad_gates, -1, keepdims=True))
    grad_logits = jnp.sum(selector * grad_chosen[:, :, None], 1).astype(low)
    grad_normed_two = grad_normed_two + jnp.einsum(
        "te,de->td", grad_logits, full_router, preferred_element_type=f32
    )
    grad_router = jnp.einsum("td,te->de", normed_two, grad_logits, preferred_element_type=f32)
    grad_gain_two = jnp.sum(grad_normed_two * hidden * scale_two, 0)
    grad_hidden = grad_top + norm_backward(grad_normed_two, hidden, scale_two, gain_two)
    back = attention_back(
        query_rot, key_rot, value, raw, mixed, grad_hidden.astype(low), w_mix, normed_one, tokens, w_qkv,
        inverses, ids_column, ids_row, gain_q, gain_k, cosine, sine,
    )
    combined, gain_grads, grad_mix, grad_qkv, grad_normed_one, grad_gain_one = combine(
        groups, shards, 4, weighted.reshape(experts, SLOTS, width), spread, extra=back
    )
    output = hidden + combined
    sums = [grad_router, grad_gain_one, grad_gain_two, gain_grads[0], gain_grads[1]]
    sums = packed(sums, shards, 16 * (span + 2 * HEAD_SIZE) // 128)
    sums = sums.reshape(shards, 16, -1).astype(low)
    (
        query_sum, key_sum, value_sum, tall_sum, pack_sum, grad_normed_one,
        grad_gate_w, grad_up_w, grad_down,
    ) = reduce(
        groups,
        shards,
        6,
        grad_qkv.reshape(shards, depth, -1),
        grad_mix.reshape(2, -1, width),
        sums,
        grad_normed_one.reshape(groups, rows, width),
        weight_grads(*(flat_rows(a) for a in (arrived, grads_in, inner, grad_a, grad_b))),
    )
    pack_sum = jnp.sum(pack_sum.astype(f32), 0).reshape(-1)
    scale_own = inverse_rms(inputs)
    grad_inputs = grad_hidden + norm_backward(grad_normed_one, inputs, scale_own, gain_one)
    at = depth * experts
    return (
        output[None],
        grad_inputs[None],
        query_sum.astype(f32),
        key_sum.astype(f32),
        value_sum.astype(f32),
        tall_sum.astype(f32),
        pack_sum[:at].reshape(depth, experts),
        pack_sum[at : at + depth],
        pack_sum[at + depth : at + 2 * depth],
        pack_sum[at + 2 * depth : at + 2 * depth + small],
        pack_sum[at + 2 * depth + small : at + 2 * depth + 2 * small],
        grad_gate_w[None],
        grad_up_w[None],
        grad_down[None],
    )


def solution(mesh):
    in_specs = (
        P(FSDP, EXPERT, None),
        P(FSDP, None),
        P(FSDP, EXPERT, None),
        P(FSDP, None),
        P(FSDP, None),
        P(FSDP, None),
        P(FSDP, None),
        P(FSDP, None),
        P(FSDP),
        P(FSDP),
        P(FSDP),
        P(FSDP),
        P((EXPERT, FSDP), None, None),
        P((EXPERT, FSDP), None, None),
        P((EXPERT, FSDP), None, None),
        P(FSDP, EXPERT, None),
    )
    out_specs = (
        P(FSDP, EXPERT, None),
        P(FSDP, EXPERT, None),
        P(FSDP, None),
        P(FSDP, None),
        P(FSDP, None),
        P(FSDP, None),
        P(FSDP, None),
        P(FSDP),
        P(FSDP),
        P(FSDP),
        P(FSDP),
        P((EXPERT, FSDP), None, None),
        P((EXPERT, FSDP), None, None),
        P((EXPERT, FSDP), None, None),
    )
    staged = mesh.shape[EXPERT] == 4 and mesh.shape[FSDP] == 8
    return jax.shard_map(local_staged if staged else local, mesh=mesh, in_specs=in_specs, out_specs=out_specs, check_vma=False)
```
